32 devices in a mesh: sp: 8 (over z, x), bd: 4 (over y, core).
Axes of the slice: x: 2, y: 2, z: 4, core: 2. Of those that a mesh axis runs over, the one named last changes fastest.
Arguments:
- cube: float32 [4, 768, 32, 256], P('bd', 'sp'), may hold values from 0.02 to 25
- taps_x: float32 [4, 768, 25], P('bd', 'sp'), may hold values from 0.1 to 1
- taps_y: float32 [4, 768, 25], P('bd', 'sp'), may hold values from 0.1 to 1
- factor_w: float32 [4, 768, 48], P('bd'), may hold values from 0.1 to 1
- factor_h: float32 [48, 32, 256], P(None, None, 'sp'), may hold values from 0.1 to 1
Outputs:
- w_next: float32 [4, 768, 48], P('bd')
- h_next: float32 [48, 32, 256], P(None, None, 'sp')
The draws below stay inside these ranges and needn't reach their ends.
All inputs are finite; a program needn't handle non-finite values.
Results may differ from the reference program's by a relative error of at most 0.000071.
Values sent between devices are 32-bit elements; how exact they have to be, the bound alone decides.
No kernel may reach another device: no remote copies, remote signals or barrier semaphores. Data moves between devices by JAX's collectives and lax.ppermute only.
A program may use at most 128 MiB of HBM per device.

```python
import math
import jax
import jax.numpy as jnp
from jax import lax

SY = 32
R = 48
TAPS = 25
BANDS = 4
LB = 768
SX = 256


def draw_cube(key, part):
    cube_shape = (BANDS, LB, SY, SX)
    along_strip = jnp.arange(SX, dtype=jnp.float32).reshape(1, 1, 1, SX)
    across_strip = jnp.arange(SY, dtype=jnp.float32).reshape(1, 1, SY, 1)
    continuum_key = jax.random.fold_in(key, 1)
    noise_key = jax.random.fold_in(key, 2)
    continuum = jnp.exp(jax.random.uniform(continuum_key, (BANDS, LB, 1, 1), jnp.float32, math.log(0.2), 0.0))
    summed_flux = continuum
    for source in range(4):
        source_key = jax.random.fold_in(key, 10 + source)
        spectrum_key, scale_key, phase_key = jax.random.split(source_key, 3)
        spectrum = jnp.exp(jax.random.uniform(spectrum_key, (BANDS, LB, 1, 1), jnp.float32, -1.0, 1.0))
        spatial_scales = jnp.exp(jax.random.uniform(scale_key, (3,), jnp.float32, math.log(30.0), math.log(300.0)))
        phases = jax.random.uniform(phase_key, (3,), jnp.float32, 0.0, 2.0 * math.pi)
        profile = jnp.cos(2.0 * math.pi * along_strip / spatial_scales[0] + phases[0])
        profile = profile + jnp.cos(2.0 * math.pi * along_strip / spatial_scales[1] + phases[1])
        profile = profile + jnp.cos(2.0 * math.pi * across_strip / spatial_scales[2] + phases[2])
        summed_flux = summed_flux + spectrum * jnp.exp(0.5 * profile)
    voxel_factor = jnp.exp(jax.random.uniform(noise_key, cube_shape, jnp.float32, math.log(0.5), math.log(2.0)))
    return (0.25 * summed_flux * voxel_factor).astype(jnp.float32)


def steps_of(key, dims, shards, smallest, top_value):
    def one(position, blocks):
        heights = jax.random.uniform(jax.random.fold_in(jax.random.fold_in(key, 6), position), (blocks,), jnp.float32, smallest / len(shards), top_value / len(shards))
        return jnp.repeat(jnp.exp(heights), dims[position] // blocks).reshape((-1,) + (1,) * (len(dims) - position - 1))

    level = one(*shards[0])
    for cut in shards[1:]:
        level = level * one(*cut)
    return level


def setup_inputs(seed: int = 0) -> dict:
    arg_keys = jax.random.split(jax.random.key(seed), 6)
    return {
        "cube": draw_cube(jax.random.fold_in(arg_keys[5], 71), 0),
        "taps_x": jnp.clip(jnp.exp(math.log(1.0) - 2.3025851 * jax.random.uniform(arg_keys[1], (BANDS, LB, TAPS), jnp.float32) ** steps_of(arg_keys[1], (BANDS, LB, TAPS), ((0, 4), (1, 8)), -0.2, 0.2)), 0.1, 1.0),
        "taps_y": jnp.clip(jnp.exp(math.log(1.0) - 2.3025851 * jax.random.uniform(arg_keys[2], (BANDS, LB, TAPS), jnp.float32) ** steps_of(arg_keys[2], (BANDS, LB, TAPS), ((0, 4), (1, 8)), -0.2, 0.2)), 0.1, 1.0),
        "factor_w": jnp.clip(jnp.exp(math.log(1.0) - 2.3025851 * jax.random.uniform(arg_keys[3], (BANDS, LB, R), jnp.float32) ** steps_of(arg_keys[3], (BANDS, LB, R), ((0, 4),), -0.2, 0.2)), 0.1, 1.0),
        "factor_h": jnp.clip(jnp.exp(math.log(1.0) - 2.3025851 * jax.random.uniform(arg_keys[4], (R, SY, SX), jnp.float32) ** steps_of(arg_keys[4], (R, SY, SX), ((2, 8),), -0.2, 0.2)), 0.1, 1.0),
    }


def normalized(kernel):
    return kernel / jnp.sum(kernel, axis=-1, keepdims=True)


def blur_plane(items):
    image_plane, kernel_x, kernel_y = items
    margin = (kernel_x.shape[0] - 1) // 2
    height = image_plane.shape[0]
    length = image_plane.shape[1]
    padded = jnp.pad(image_plane, ((margin, margin), (0, 0)))
    summed = jnp.zeros_like(image_plane)
    for index in range(kernel_y.shape[0]):
        summed = summed + kernel_y[index] * padded[index:index + height, :]
    padded = jnp.pad(summed, ((0, 0), (margin, margin)))
    result = jnp.zeros_like(image_plane)
    for index in range(kernel_x.shape[0]):
        result = result + kernel_x[index] * padded[:, index:index + length]
    return result


def reference(cube, taps_x, taps_y, factor_w, factor_h):
    highest = lax.Precision.HIGHEST
    bands, planes, height, length = cube.shape
    rank = factor_w.shape[2]
    kernel_x = normalized(taps_x).reshape(bands * planes, -1)
    kernel_y = normalized(taps_y).reshape(bands * planes, -1)
    flat_cube = cube.reshape(bands * planes, height, length)
    blurred = lax.map(blur_plane, (flat_cube, kernel_x, kernel_y))
    matrix_x = blurred.reshape(bands * planes, height * length)
    matrix_w = factor_w.reshape(bands * planes, rank)
    matrix_h = factor_h.reshape(rank, height * length)
    numer_h = jnp.dot(matrix_w.T, matrix_x, precision=highest)
    gram_w = jnp.dot(matrix_w.T, matrix_w, precision=highest)
    h_next = matrix_h * numer_h / jnp.dot(gram_w, matrix_h, precision=highest)
    numer_w = jnp.dot(matrix_x, h_next.T, precision=highest)
    gram_h = jnp.dot(h_next, h_next.T, precision=highest)
    w_next = matrix_w * numer_w / jnp.dot(matrix_w, gram_h, precision=highest)
    return w_next.reshape(bands, planes, rank), h_next.reshape(rank, height, length)
```

```python
import functools

import jax
import jax.numpy as jnp
from jax import lax
from jax.experimental import pallas as pl
from jax.experimental.pallas import tpu as pltpu
from jax.sharding import PartitionSpec as P

F32 = jnp.float32
BF16 = jnp.bfloat16
LANES = 128
GROUP = 16
VMEM_LIMIT = 48 * 1024 * 1024


def split(value):
    high = value.astype(BF16)
    low = (value - high.astype(F32)).astype(BF16)
    return high, low


def dot(left, right):
    return lax.dot_general(left, right, (((1,), (0,)), ((), ())), preferred_element_type=F32)


def dot_nt(left, right):
    return lax.dot_general(left, right, (((1,), (1,)), ((), ())), preferred_element_type=F32)


def dot_exact(left, right):
    return lax.dot_general(
        left, right, (((1,), (0,)), ((), ())),
        precision=lax.Precision.HIGHEST, preferred_element_type=F32,
    )


def exchange_blocks(rows, block):
    lane = lax.broadcasted_iota(jnp.int32, rows[0].shape, 1)
    first_half = lane < 2 * block
    even = (lane // block) % 2 == 0
    v0, v1, v2, v3 = rows
    u0 = jnp.where(first_half, v0, pltpu.roll(v2, 2 * block, 1))
    u2 = jnp.where(first_half, pltpu.roll(v0, 2 * block, 1), v2)
    u1 = jnp.where(first_half, v1, pltpu.roll(v3, 2 * block, 1))
    u3 = jnp.where(first_half, pltpu.roll(v1, 2 * block, 1), v3)
    w0 = jnp.where(even, u0, pltpu.roll(u1, block, 1))
    w1 = jnp.where(even, pltpu.roll(u0, 3 * block, 1), u1)
    w2 = jnp.where(even, u2, pltpu.roll(u3, block, 1))
    w3 = jnp.where(even, pltpu.roll(u2, 3 * block, 1), u3)
    return w0, w1, w2, w3


def normalized_taps(taps_ref, reverse, work_ref, out_ref):
    taps = taps_ref.shape[0]
    planes = taps_ref.shape[2]
    work_ref[...] = jnp.zeros_like(work_ref)
    for tap in range(taps):
        row = taps - 1 - tap if reverse else tap
        work_ref[row:row + 1, 0:planes] = taps_ref[tap]
    values = work_ref[...]
    total = jnp.sum(values, axis=0, keepdims=True)
    total = jnp.where(total == 0.0, 1.0, total)
    out_ref[...] = jnp.transpose(values / total)


def column_table(row, margin):
    circulant = pltpu.roll(jnp.broadcast_to(row, (LANES, LANES)), 0, 1, stride=1, stride_axis=0)
    high = circulant.astype(BF16).astype(F32)
    low = circulant - high
    src = lax.broadcasted_iota(jnp.int32, (LANES, LANES), 0)
    dst = lax.broadcasted_iota(jnp.int32, (LANES, LANES), 1)
    near = jnp.abs(dst - src) <= margin
    edge = GROUP
    wraps_up = (src - dst)[LANES - edge:] > LANES // 2
    wraps_down = (dst - src)[:edge] > LANES // 2
    empty = jnp.zeros((LANES - edge, LANES), BF16)

    def table(part):
        middle = jnp.where(near, part, 0.0).astype(BF16)
        upper = jnp.where(wraps_up, part[LANES - edge:], 0.0).astype(BF16)
        lower = jnp.where(wraps_down, part[:edge], 0.0).astype(BF16)
        top = jnp.concatenate([middle, jnp.concatenate([empty, upper], axis=0)], axis=1)
        bottom = jnp.concatenate([jnp.concatenate([lower, empty], axis=0), middle], axis=1)
        return jnp.concatenate([top, bottom], axis=0)

    return table(high), table(low)


def row_table(base, margin, height):
    high = base.astype(BF16).astype(F32)
    low = base - high
    plane = lax.broadcasted_iota(jnp.int32, (8, LANES), 0)
    lane = lax.broadcasted_iota(jnp.int32, (8, LANES), 1)
    per_vector = LANES // height
    own = lane // height == plane % per_vector
    masks = [own & (plane // per_vector == part) for part in range(8 * height // LANES)]

    def table(part):
        strips = []
        for row in range(height):
            rolled = pltpu.roll(part, (row - margin) % LANES, 1)
            strips.append(jnp.concatenate([jnp.where(mask, rolled, 0.0) for mask in masks], axis=1))
        return jnp.concatenate(strips, axis=0).astype(BF16)

    return table(high), table(low)


def blur_kernel(cube_ref, taps_x_ref, taps_y_ref, w_ref, xh_ref, xl_ref, *rest):
    part_refs = rest[:8]
    work_ref, kx_ref, ky_ref = rest[8:]
    step = pl.program_id(0)
    taps = taps_x_ref.shape[0]
    margin = (taps - 1) // 2
    height = cube_ref.shape[1]

    @pl.when(step == 0)
    def _():
        normalized_taps(taps_x_ref, True, work_ref, kx_ref)
        normalized_taps(taps_y_ref, False, work_ref, ky_ref)
        kx_ref[...] = pltpu.roll(kx_ref[...], LANES - margin, 1)
        per_vector = LANES // height
        place = lax.broadcasted_iota(jnp.int32, (LANES, LANES), 0) % per_vector
        values = ky_ref[...]
        placed = values
        for k in range(1, per_vector):
            placed = jnp.where(place == k, pltpu.roll(values, k * height, 1), placed)
        ky_ref[...] = placed

    halves = []
    for half in range(GROUP // 8):
        done = []
        for plane in range(8 * half, 8 * half + 8):
            row = kx_ref[pl.ds(step * GROUP + plane, 1), :]
            table_high, table_low = column_table(row, margin)
            high, low = split(cube_ref[plane])
            both = dot(jnp.concatenate([high, low], axis=0), table_high)
            done.append(both[:height] + (both[height:] + dot(high, table_low)))
        high, low = split(jnp.concatenate(done, axis=0))
        rows = ky_ref[pl.ds(pl.multiple_of(step * GROUP + 8 * half, 8), 8), :]
        table_high, table_low = row_table(rows, margin, height)
        result = dot(table_high, high) + (dot(table_low, high) + dot(table_high, low))
        halves.append(result.reshape(height, 8, result.shape[1]))
    high, low = split(jnp.concatenate(halves, axis=1))
    planes_here = pl.ds(pl.multiple_of(step * GROUP, GROUP), GROUP)
    xh_ref[:, planes_here, :] = high
    xl_ref[:, planes_here, :] = low

    @pl.when(step == pl.num_programs(0) - 1)
    def _():
        planes = xh_ref.shape[1]
        rank, band = w_ref.shape
        me_sp = lax.axis_index("sp")
        me_bd = lax.axis_index("bd")
        bands = lax.axis_size("bd")
        pieces = lax.axis_size("sp")
        tall = height // bands
        wide = xh_ref.shape[2] // pieces
        shift = lax.rem(band - me_sp * planes, band)
        w_high, w_low = split(pltpu.roll(w_ref[...], shift, 1)[:, :planes])
        w_both = jnp.concatenate([w_high, w_low], axis=0)
        for rel_bd in (1, 3, 0, 2):
            first_row = lax.bitwise_xor(me_bd, rel_bd) * tall
            sums = []
            for row in range(tall):
                both = dot(w_both, xh_ref[first_row + row])
                sums.append(both[:rank] + (both[rank:] + dot(w_high, xl_ref[first_row + row])))
            for column in range(2):
                vectors = []
                for quarter in range(2):
                    vectors.append(exchange_blocks(
                        [sums[4 * quarter + k][:, column * LANES:(column + 1) * LANES] for k in range(4)], wide))
                for k in range(4):
                    piece = jnp.concatenate([vectors[0][k], vectors[1][k]], axis=1)
                    owner = column * 4 + k
                    rel_sp = lax.bitwise_xor(me_sp, owner)
                    inner = rel_sp // 2
                    low_bit = rel_sp % 2
                    base = (rel_bd % 2) * 4 + (rel_bd // 2) * 2

                    @pl.when(low_bit == 0)
                    def _():
                        part_refs[base][inner] = piece

                    @pl.when(low_bit == 1)
                    def _():
                        part_refs[base + 1][inner] = piece


def blur_call(cube, taps_x, taps_y, w_rows):
    planes, height, length = cube.shape
    rank = w_rows.shape[0]
    taps = taps_x.shape[0]
    part = jax.ShapeDtypeStruct((4, rank, 256), F32)
    whole = lambda shape: pl.BlockSpec(shape, lambda i: (0,) * len(shape))
    return pl.pallas_call(
        blur_kernel,
        grid=(planes // GROUP,),
        out_shape=[jax.ShapeDtypeStruct((height, planes, length), BF16)] * 2 + [part] * 8,
        in_specs=[
            pl.BlockSpec((GROUP, height, length), lambda i: (i, 0, 0)),
            whole(taps_x.shape), whole(taps_y.shape), whole(w_rows.shape),
        ],
        out_specs=[whole((height, planes, length))] * 2 + [whole(part.shape)] * 8,
        scratch_shapes=[pltpu.VMEM((LANES, LANES), F32)] * 3,
        compiler_params=pltpu.CompilerParams(
            dimension_semantics=("arbitrary",), vmem_limit_bytes=VMEM_LIMIT),
    )(cube, taps_x, taps_y, w_rows)


def gram_kernel(w_ref, out_ref):
    high, low = split(w_ref[...])
    both = jnp.concatenate([high, low], axis=0)
    rank = w_ref.shape[0]
    total = dot_nt(both, both)
    out_ref[...] = total[:rank, :rank] + (total[rank:, :rank] + total[:rank, rank:]) + total[rank:, rank:]


def gram_call(w_rows):
    rank = w_rows.shape[0]
    return pl.pallas_call(
        gram_kernel,
        out_shape=jax.ShapeDtypeStruct((rank, rank), F32),
    )(w_rows)


def update_h_kernel(n0, n1, n2, n3, g0, g1, g2, g3, h_ref, out_ref):
    tall = h_ref.shape[0] // lax.axis_size("bd")
    first = pl.multiple_of(lax.axis_index("bd") * tall, tall)
    here = h_ref[pl.ds(first, tall)]
    here = jnp.transpose(here.reshape(-1, here.shape[2]))
    gram = (g0[...] + g1[...]) + (g2[...] + g3[...])
    numer = (n0[...] + n1[...]) + (n2[...] + n3[...])
    out_ref[...] = here * numer / dot_exact(gram, here)


def update_h_call(numer, gram, h_columns):
    return pl.pallas_call(
        update_h_kernel,
        out_shape=jax.ShapeDtypeStruct(numer[0].shape, F32),
    )(*numer, *gram, h_columns)


def update_w_kernel(xh_ref, xl_ref, w_ref, *rest):
    part_refs = rest[:8]
    w_out, h_out, all_ref = rest[8:]
    height, planes, length = xh_ref.shape
    rank, band = w_ref.shape
    me_sp = lax.axis_index("sp")
    me_bd = lax.axis_index("bd")
    bands = lax.axis_size("bd")
    pieces = lax.axis_size("sp")
    tall = height // bands
    wide = length // pieces
    for rel in range(bands * pieces):
        slot, inner = rel // 4, rel % 4
        rel_bd = (slot // 4) + 2 * ((slot // 2) % 2)
        rel_sp = slot % 2 + 2 * inner
        owner = lax.bitwise_xor(me_bd, rel_bd) * pieces + lax.bitwise_xor(me_sp, rel_sp)
        all_ref[owner] = part_refs[slot][inner]
    for part in range(bands):
        mine = jnp.transpose(all_ref[part * pieces + me_sp])
        h_out[part * tall:(part + 1) * tall] = mine.reshape(tall, wide, rank)
    numer = jnp.zeros((rank, planes), F32)
    gram = jnp.zeros((rank, rank), F32)
    for part in range(bands):
        rows = [[None, None] for _ in range(tall)]
        for column in range(2):
            for quarter in range(2):
                vectors = exchange_blocks(
                    [all_ref[part * pieces + column * 4 + k][:, quarter * LANES:(quarter + 1) * LANES]
                     for k in range(4)], wide)
                for k in range(4):
                    rows[4 * quarter + k][column] = vectors[k]
        for row in range(tall):
            high, low = split(jnp.concatenate(rows[row], axis=1))
            both = jnp.concatenate([high, low], axis=0)
            product = dot_nt(both, xh_ref[part * tall + row])
            numer = numer + (product[:rank] + (product[rank:] + dot_nt(high, xl_ref[part * tall + row])))
            product = dot_nt(both, high)
            gram = gram + (product[:rank] + (product[rank:] + dot_nt(high, low)))
    shift = lax.rem(band - me_sp * planes, band)
    w_here = pltpu.roll(w_ref[...], shift, 1)[:, :planes]
    w_out[...] = w_here * numer / dot_exact(gram, w_here)


def update_w_call(x_high, x_low, w_rows, parts):
    height, planes, length = x_high.shape
    rank = w_rows.shape[0]
    wide = length // lax.axis_size("sp")
    return pl.pallas_call(
        update_w_kernel,
        out_shape=[
            jax.ShapeDtypeStruct((rank, planes), F32),
            jax.ShapeDtypeStruct((height, wide, rank), F32),
        ],
        scratch_shapes=[pltpu.VMEM((4 * len(parts),) + parts[0].shape[1:], F32)],
        compiler_params=pltpu.CompilerParams(vmem_limit_bytes=VMEM_LIMIT),
    )(x_high, x_low, w_rows, *parts)


def gather_w_kernel(*refs):
    part_refs = refs[:-2]
    out_ref, all_ref = refs[-2:]
    planes = part_refs[0].shape[1]
    me_sp = lax.axis_index("sp")
    for rel, part in enumerate(part_refs):
        all_ref[lax.bitwise_xor(me_sp, rel), :, 0:planes] = part[...]
    for owner in range(len(part_refs)):
        out_ref[:, owner * planes:(owner + 1) * planes] = all_ref[owner][:, :planes]


def gather_w_call(parts):
    rank, planes = parts[0].shape
    return pl.pallas_call(
        gather_w_kernel,
        out_shape=jax.ShapeDtypeStruct((rank, planes * len(parts)), F32),
        scratch_shapes=[pltpu.VMEM((len(parts), rank, LANES), F32)],
    )(*parts)


def send(value, mask_sp, mask_bd):
    bands = lax.axis_size("bd")
    pieces = lax.axis_size("sp")
    pairs = []
    for s in range(pieces):
        for b in range(bands):
            pairs.append((s * bands + b, (s ^ mask_sp) * bands + (b ^ mask_bd)))
    return lax.ppermute(value, ("sp", "bd"), pairs)


def local(cube, taps_x, taps_y, factor_w, factor_h):
    bands = lax.axis_size("bd")
    pieces = lax.axis_size("sp")
    w_rows = jnp.transpose(factor_w[0])
    taps_x = jnp.transpose(taps_x, (2, 0, 1))
    taps_y = jnp.transpose(taps_y, (2, 0, 1))
    h_columns = jnp.transpose(factor_h, (1, 2, 0))
    gram = gram_call(w_rows)
    grams = [gram] + [send(gram, 0, mask) for mask in range(1, bands)]
    x_high, x_low, *parts = blur_call(cube[0], taps_x, taps_y, w_rows)
    keep, give = parts[:4], parts[4:]
    taken = [send(value, 0, 1) for value in give]
    chip = [mine + other for mine, other in zip(keep, taken)]
    around = [chip[0]] + [send(chip[k], k % 2, 2 * (k // 2)) for k in range(1, 4)]
    square = [(around[0][k] + around[1][k]) + (around[2][k] + around[3][k]) for k in range(4)]
    line = [square[0]] + [send(square[k], 2 * k, 0) for k in range(1, 4)]
    h_piece = update_h_call(line, grams, h_columns)
    h_line = [h_piece] + [send(h_piece, 2 * k, 0) for k in range(1, 4)]
    h_line = jnp.stack(h_line)
    h_parts = [h_line] + [send(h_line, k % 2, 2 * (k // 2)) for k in range(1, 4)]
    h_parts = h_parts + [send(value, 0, 1) for value in h_parts]
    w_piece, h_next = update_w_call(x_high, x_low, w_rows, h_parts)
    w_pieces = [w_piece] + [send(w_piece, mask, 0) for mask in range(1, pieces)]
    w_next = gather_w_call(w_pieces)
    return jnp.transpose(w_next)[None], jnp.transpose(h_next, (2, 0, 1))


def normalized(kernel):
    return kernel / jnp.sum(kernel, axis=-1, keepdims=True)


def band_weights(kernel, size_in, size_out, offset):
    tap_count = kernel.shape[-1]
    in_index = lax.broadcasted_iota(jnp.int32, (size_in, size_out, tap_count), 0)
    out_index = lax.broadcasted_iota(jnp.int32, (size_in, size_out, tap_count), 1)
    tap_index = lax.broadcasted_iota(jnp.int32, (size_in, size_out, tap_count), 2)
    select = (tap_index == in_index - out_index + offset).astype(jnp.float32)
    return jnp.einsum("pk,iok->pio", kernel, select, precision=lax.Precision.HIGHEST)


def blur_rows(planes, kernel_y):
    margin = (kernel_y.shape[-1] - 1) // 2
    height = planes.shape[1]
    band_table = band_weights(kernel_y, height, height, margin)
    return jnp.einsum("piz,pio->poz", planes, band_table, precision=lax.Precision.HIGHEST)


def blur_columns(planes, kernel_x):
    margin = (kernel_x.shape[-1] - 1) // 2
    count, height, length = planes.shape
    blocks = planes.reshape(count, height, length // 128, 128)
    empty = jnp.zeros((count, height, 1, 128), jnp.float32)
    left_block = jnp.concatenate([empty, blocks[:, :, :-1]], axis=2)
    right_block = jnp.concatenate([blocks[:, :, 1:], empty], axis=2)
    window = jnp.concatenate([left_block, blocks, right_block], axis=3)
    band_table = band_weights(kernel_x, 384, 128, margin - 128)
    result = jnp.einsum("pybi,pio->pybo", window, band_table, precision=lax.Precision.HIGHEST)
    return result.reshape(count, height, length)


def local_any(cube, taps_x, taps_y, factor_w, factor_h):
    highest = lax.Precision.HIGHEST
    kernel_x = normalized(taps_x[0])
    kernel_y = normalized(taps_y[0])
    rows_done = blur_rows(cube[0], kernel_y)
    w_band = factor_w[0]
    blurred = blur_columns(rows_done, kernel_x)[None]
    moved = lax.all_to_all(blurred, "sp", split_axis=3, concat_axis=1, tiled=True)
    numer_part = jnp.einsum("lr,plyx->pryx", w_band, moved, precision=highest)
    gram_part = jnp.dot(w_band.T, w_band, precision=highest)
    numer_h, gram_w = lax.psum((numer_part[0], gram_part), "bd")
    h_next = factor_h * numer_h / jnp.einsum("rq,qyx->ryx", gram_w, factor_h, precision=highest)
    x_band = moved[0]
    gram_h_part = jnp.einsum("ryx,qyx->rq", h_next, h_next, precision=highest)
    numer_w_part = jnp.einsum("lyx,ryx->lr", x_band, h_next, precision=highest)
    numer_w, gram_h = lax.psum((numer_w_part, gram_h_part), "sp")
    w_next = w_band * numer_w / jnp.dot(w_band, gram_h, precision=highest)
    return (w_next[None], h_next)


def solution(mesh):
    in_specs = (
        P("bd", "sp", None, None),
        P("bd", "sp", None),
        P("bd", "sp", None),
        P("bd", None, None),
        P(None, None, "sp"),
    )
    out_specs = (P("bd", None, None), P(None, None, "sp"))

    def body(cube, *rest):
        suits = lax.axis_size("sp") == 8 and lax.axis_size("bd") == 4 and cube.shape[1] % GROUP == 0
        return (local if suits else local_any)(cube, *rest)

    return jax.shard_map(body, mesh=mesh, in_specs=in_specs, out_specs=out_specs, check_vma=False)
```

```python
import functools

import jax
import jax.numpy as jnp
from jax import lax
from jax.experimental import pallas as pl
from jax.experimental.pallas import tpu as pltpu
from jax.sharding import PartitionSpec as P

F32 = jnp.float32
BF16 = jnp.bfloat16
LANES = 128
GROUP = 16
VMEM_LIMIT = 48 * 1024 * 1024


def split(value):
    high = value.astype(BF16)
    low = (value - high.astype(F32)).astype(BF16)
    return high, low


def dot(left, right):
    return lax.dot_general(left, right, (((1,), (0,)), ((), ())), preferred_element_type=F32)


def dot_nt(left, right):
    return lax.dot_general(left, right, (((1,), (1,)), ((), ())), preferred_element_type=F32)


def dot_exact(left, right):
    return lax.dot_general(
        left, right, (((1,), (0,)), ((), ())),
        precision=lax.Precision.HIGHEST, preferred_element_type=F32,
    )


def exchange_blocks(rows, block):
    lane = lax.broadcasted_iota(jnp.int32, rows[0].shape, 1)
    first_half = lane < 2 * block
    even = (lane // block) % 2 == 0
    v0, v1, v2, v3 = rows
    u0 = jnp.where(first_half, v0, pltpu.roll(v2, 2 * block, 1))
    u2 = jnp.where(first_half, pltpu.roll(v0, 2 * block, 1), v2)
    u1 = jnp.where(first_half, v1, pltpu.roll(v3, 2 * block, 1))
    u3 = jnp.where(first_half, pltpu.roll(v1, 2 * block, 1), v3)
    w0 = jnp.where(even, u0, pltpu.roll(u1, block, 1))
    w1 = jnp.where(even, pltpu.roll(u0, 3 * block, 1), u1)
    w2 = jnp.where(even, u2, pltpu.roll(u3, block, 1))
    w3 = jnp.where(even, pltpu.roll(u2, 3 * block, 1), u3)
    return w0, w1, w2, w3


def normalized_taps(taps_ref, reverse, work_ref, out_ref):
    taps = taps_ref.shape[0]
    planes = taps_ref.shape[2]
    work_ref[...] = jnp.zeros_like(work_ref)
    for tap in range(taps):
        row = taps - 1 - tap if reverse else tap
        work_ref[row:row + 1, 0:planes] = taps_ref[tap]
    values = work_ref[...]
    total = jnp.sum(values, axis=0, keepdims=True)
    total = jnp.where(total == 0.0, 1.0, total)
    out_ref[...] = jnp.transpose(values / total)


def column_table(row, margin):
    circulant = pltpu.roll(jnp.broadcast_to(row, (LANES, LANES)), 0, 1, stride=1, stride_axis=0)
    high = circulant.astype(BF16).astype(F32)
    low = circulant - high
    src = lax.broadcasted_iota(jnp.int32, (LANES, LANES), 0)
    dst = lax.broadcasted_iota(jnp.int32, (LANES, LANES), 1)
    near = jnp.abs(dst - src) <= margin
    edge = GROUP
    wraps_up = (src - dst)[LANES - edge:] > LANES // 2
    wraps_down = (dst - src)[:edge] > LANES // 2
    empty = jnp.zeros((LANES - edge, LANES), BF16)

    def table(part):
        middle = jnp.where(near, part, 0.0).astype(BF16)
        upper = jnp.where(wraps_up, part[LANES - edge:], 0.0).astype(BF16)
        lower = jnp.where(wraps_down, part[:edge], 0.0).astype(BF16)
        top = jnp.concatenate([middle, jnp.concatenate([empty, upper], axis=0)], axis=1)
        bottom = jnp.concatenate([jnp.concatenate([lower, empty], axis=0), middle], axis=1)
        return jnp.concatenate([top, bottom], axis=0)

    return table(high), table(low)


def row_table(base, margin, height):
    high = base.astype(BF16).astype(F32)
    low = base - high
    plane = lax.broadcasted_iota(jnp.int32, (8, LANES), 0)
    lane = lax.broadcasted_iota(jnp.int32, (8, LANES), 1)
    per_vector = LANES // height
    own = lane // height == plane % per_vector
    masks = [own & (plane // per_vector == part) for part in range(8 * height // LANES)]

    def table(part):
        strips = []
        for row in range(height):
            rolled = pltpu.roll(part, (row - margin) % LANES, 1)
            strips.append(jnp.concatenate([jnp.where(mask, rolled, 0.0) for mask in masks], axis=1))
        return jnp.concatenate(strips, axis=0).astype(BF16)

    return table(high), table(low)


def band_gram(w_rows):
    high, low = split(w_rows)
    rank = w_rows.shape[0]
    padded = jnp.concatenate([high, jnp.zeros((2 * LANES - rank, high.shape[1]), BF16)], axis=0)
    padded_low = jnp.concatenate([low, jnp.zeros((2 * LANES - rank, low.shape[1]), BF16)], axis=0)
    both = dot_nt(jnp.concatenate([high, low], axis=0), padded)
    return both[:rank] + (both[rank:] + dot_nt(high, padded_low))


def blur_kernel(cube_ref, taps_x_hbm, taps_y_hbm, w_hbm, xh_ref, xl_ref, far_keep, far_give, near_keep, near_give,
                taps_x_ref, taps_y_ref, w_ref, sems, work_ref, kx_ref, ky_ref):
    step = pl.program_id(0)
    taps = taps_x_ref.shape[0]
    margin = (taps - 1) // 2
    height = cube_ref.shape[1]

    @pl.when(step == 0)
    def _():
        copies = [
            pltpu.make_async_copy(taps_x_hbm, taps_x_ref, sems.at[0]),
            pltpu.make_async_copy(taps_y_hbm, taps_y_ref, sems.at[1]),
            pltpu.make_async_copy(w_hbm, w_ref, sems.at[2]),
        ]
        for copy in copies:
            copy.start()
        for copy in copies:
            copy.wait()
        gram = band_gram(w_ref[...])
        near_keep[8] = gram
        near_give[8] = gram
        normalized_taps(taps_x_ref, True, work_ref, kx_ref)
        normalized_taps(taps_y_ref, False, work_ref, ky_ref)
        kx_ref[...] = pltpu.roll(kx_ref[...], LANES - margin, 1)
        per_vector = LANES // height
        place = lax.broadcasted_iota(jnp.int32, (LANES, LANES), 0) % per_vector
        values = ky_ref[...]
        placed = values
        for k in range(1, per_vector):
            placed = jnp.where(place == k, pltpu.roll(values, k * height, 1), placed)
        ky_ref[...] = placed

    halves = []
    for half in range(GROUP // 8):
        done = []
        for plane in range(8 * half, 8 * half + 8):
            row = kx_ref[pl.ds(step * GROUP + plane, 1), :]
            table_high, table_low = column_table(row, margin)
            high, low = split(cube_ref[plane])
            both = dot(jnp.concatenate([high, low], axis=0), table_high)
            done.append(both[:height] + (both[height:] + dot(high, table_low)))
        high, low = split(jnp.concatenate(done, axis=0))
        rows = ky_ref[pl.ds(pl.multiple_of(step * GROUP + 8 * half, 8), 8), :]
        table_high, table_low = row_table(rows, margin, height)
        result = dot(table_high, high) + (dot(table_low, high) + dot(table_high, low))
        halves.append(result.reshape(height, 8, result.shape[1]))
    high, low = split(jnp.concatenate(halves, axis=1))
    planes_here = pl.ds(pl.multiple_of(step * GROUP, GROUP), GROUP)
    for column in range(2):
        xh_ref[column, :, planes_here, :] = high[:, :, column * LANES:(column + 1) * LANES]
        xl_ref[column, :, planes_here, :] = low[:, :, column * LANES:(column + 1) * LANES]

    @pl.when(step == pl.num_programs(0) - 1)
    def _():
        planes = xh_ref.shape[2]
        rank, band = w_ref.shape
        me_sp = lax.axis_index("sp")
        me_bd = lax.axis_index("bd")
        tall = height // lax.axis_size("bd")
        wide = 2 * LANES // lax.axis_size("sp")
        shift = lax.rem(band - me_sp * planes, band)
        w_high, w_low = split(pltpu.roll(w_ref[...], shift, 1)[:, :planes])
        w_both = jnp.concatenate([w_high, w_low], axis=0)
        for rel_bd in range(4):
            first_row = lax.bitwise_xor(me_bd, rel_bd) * tall
            sums = []
            for row in range(tall):
                x_high = jnp.concatenate([xh_ref[0, first_row + row], xh_ref[1, first_row + row]], axis=1)
                x_low = jnp.concatenate([xl_ref[0, first_row + row], xl_ref[1, first_row + row]], axis=1)
                both = dot(w_both, x_high)
                sums.append(both[:rank] + (both[rank:] + dot(w_high, x_low)))
            far_ref, near_ref = (far_keep, near_keep) if rel_bd % 2 == 0 else (far_give, near_give)
            for column in range(2):
                quarters = [
                    exchange_blocks(
                        [sums[4 * quarter + k][:, column * LANES:(column + 1) * LANES] for k in range(4)], wide)
                    for quarter in range(2)]
                for k in range(4):
                    piece = jnp.concatenate([quarters[0][k], quarters[1][k]], axis=1)
                    rel_sp = lax.bitwise_xor(me_sp, column * 4 + k)
                    place = (rel_bd // 2) * 4 + (rel_sp % 2) * 2 + (rel_sp // 2) % 2

                    @pl.when(rel_sp >= 4)
                    def _():
                        far_ref[place] = piece

                    @pl.when(rel_sp < 4)
                    def _():
                        near_ref[place] = piece


def blur_call(cube, taps_x, taps_y, w_rows):
    planes, height, length = cube.shape
    rank = w_rows.shape[0]
    far = jax.ShapeDtypeStruct((8, rank, 2 * LANES), F32)
    near = jax.ShapeDtypeStruct((9, rank, 2 * LANES), F32)
    image = (2, height, planes, LANES)
    whole = lambda shape: pl.BlockSpec(shape, lambda i: (0,) * len(shape))
    return pl.pallas_call(
        blur_kernel,
        grid=(planes // GROUP,),
        out_shape=[jax.ShapeDtypeStruct(image, BF16)] * 2 + [far, far, near, near],
        in_specs=[pl.BlockSpec((GROUP, height, length), lambda i: (i, 0, 0))]
        + [pl.BlockSpec(memory_space=pltpu.HBM)] * 3,
        out_specs=[whole(image)] * 2 + [whole(far.shape)] * 2 + [whole(near.shape)] * 2,
        scratch_shapes=[pltpu.VMEM(value.shape, F32) for value in (taps_x, taps_y, w_rows)]
        + [pltpu.SemaphoreType.DMA((3,))] + [pltpu.VMEM((LANES, LANES), F32)] * 3,
        compiler_params=pltpu.CompilerParams(
            dimension_semantics=("arbitrary",), vmem_limit_bytes=VMEM_LIMIT),
    )(cube, taps_x, taps_y, w_rows)


def ratio_kernel(gram_ref, other_ref, h_ref, out_ref):
    tall = h_ref.shape[0] // lax.axis_size("bd")
    first = pl.multiple_of(lax.axis_index("bd") * tall, tall)
    here = h_ref[pl.ds(first, tall)]
    here = jnp.transpose(here.reshape(-1, here.shape[2]))
    gram = gram_ref[...] + other_ref[...]
    out_ref[...] = here / dot_exact(gram, here)


def ratio_call(gram, gram_other, h_columns):
    rank = h_columns.shape[2]
    columns = h_columns.shape[0] * h_columns.shape[1] // lax.axis_size("bd")
    return pl.pallas_call(
        ratio_kernel,
        out_shape=jax.ShapeDtypeStruct((rank, columns), F32),
    )(gram, gram_other, h_columns)


def accumulate(xh_ref, xl_ref, part_refs, all_ref, column, numer, gram):
    height, rank = xh_ref.shape[1], all_ref.shape[1]
    me_sp = lax.axis_index("sp")
    me_bd = lax.axis_index("bd")
    bands = lax.axis_size("bd")
    tall = height // bands
    wide = 2 * LANES // lax.axis_size("sp")
    for slot in range(8):
        rel_bd = slot // 4 + 2 * ((slot // 2) % 2)
        for inner in range(2):
            owner_sp = lax.bitwise_xor(me_sp, slot % 2 + 2 * inner) % 4
            all_ref[lax.bitwise_xor(me_bd, rel_bd) * 4 + owner_sp] = part_refs[slot][inner]
    for part in range(bands):
        rows = []
        for quarter in range(2):
            rows += exchange_blocks(
                [all_ref[part * 4 + k][:, quarter * LANES:(quarter + 1) * LANES] for k in range(4)], wide)
        for row in range(0, tall, 2):
            high, low = split(jnp.concatenate([rows[row], rows[row + 1]], axis=1))
            both = jnp.concatenate([high, low], axis=0)
            y = part * tall + row
            x_high = jnp.concatenate([xh_ref[column, y], xh_ref[column, y + 1]], axis=1)
            x_low = jnp.concatenate([xl_ref[column, y], xl_ref[column, y + 1]], axis=1)
            product = dot_nt(both, x_high)
            numer = numer + (product[:rank] + (product[rank:] + dot_nt(high, x_low)))
            product = dot_nt(both, high)
            gram = gram + (product[:rank] + (product[rank:] + dot_nt(high, low)))
    return numer, gram


def near_kernel(xh_ref, xl_ref, *rest):
    part_refs = rest[:8]
    numer_out, gram_out, h_out, all_ref = rest[8:]
    planes = xh_ref.shape[2]
    rank = all_ref.shape[1]
    bands = lax.axis_size("bd")
    tall = xh_ref.shape[1] // bands
    wide = 2 * LANES // lax.axis_size("sp")
    me_sp = lax.axis_index("sp")
    numer, gram = accumulate(
        xh_ref, xl_ref, part_refs, all_ref, me_sp // 4,
        jnp.zeros((rank, planes), F32), jnp.zeros((rank, rank), F32))
    numer_out[...] = numer
    gram_out[...] = gram
    for part in range(bands):
        mine = jnp.transpose(all_ref[part * 4 + me_sp % 4])
        h_out[part * tall:(part + 1) * tall] = mine.reshape(tall, wide, rank)


def near_call(x_high, x_low, parts):
    _, height, planes, _ = x_high.shape
    rank = parts[0].shape[1]
    wide = 2 * LANES // lax.axis_size("sp")
    return pl.pallas_call(
        near_kernel,
        out_shape=[
            jax.ShapeDtypeStruct((rank, planes), F32),
            jax.ShapeDtypeStruct((rank, rank), F32),
            jax.ShapeDtypeStruct((height, wide, rank), F32),
        ],
        scratch_shapes=[pltpu.VMEM((16,) + parts[0].shape[1:], F32)],
        compiler_params=pltpu.CompilerParams(vmem_limit_bytes=VMEM_LIMIT),
    )(x_high, x_low, *parts)


def far_kernel(xh_ref, xl_ref, w_ref, numer_ref, gram_ref, *rest):
    part_refs = rest[:8]
    w_out, all_ref = rest[8:]
    planes = xh_ref.shape[2]
    band = w_ref.shape[1]
    me_sp = lax.axis_index("sp")
    numer, gram = accumulate(
        xh_ref, xl_ref, part_refs, all_ref, 1 - me_sp // 4, numer_ref[...], gram_ref[...])
    shift = lax.rem(band - me_sp * planes, band)
    w_here = pltpu.roll(w_ref[...], shift, 1)[:, :planes]
    w_out[...] = w_here * numer / dot_exact(gram, w_here)


def far_call(x_high, x_low, w_rows, numer, gram, parts):
    return pl.pallas_call(
        far_kernel,
        out_shape=jax.ShapeDtypeStruct(numer.shape, F32),
        scratch_shapes=[pltpu.VMEM((16,) + parts[0].shape[1:], F32)],
        compiler_params=pltpu.CompilerParams(vmem_limit_bytes=VMEM_LIMIT),
    )(x_high, x_low, w_rows, numer, gram, *parts)


def gather_w_kernel(mine_ref, other_ref, out_ref, all_ref):
    planes = mine_ref.shape[2]
    me_sp = lax.axis_index("sp")
    for rel in range(8):
        part = mine_ref if rel < 4 else other_ref
        all_ref[lax.bitwise_xor(me_sp, rel), :, 0:planes] = part[rel % 4]
    for owner in range(8):
        out_ref[:, owner * planes:(owner + 1) * planes] = all_ref[owner][:, :planes]


def gather_w_call(mine, other):
    _, rank, planes = mine.shape
    return pl.pallas_call(
        gather_w_kernel,
        out_shape=jax.ShapeDtypeStruct((rank, planes * 8), F32),
        scratch_shapes=[pltpu.VMEM((8, rank, LANES), F32)],
    )(mine, other)


def send(value, mask_sp, mask_bd):
    bands = lax.axis_size("bd")
    pieces = lax.axis_size("sp")
    pairs = []
    for s in range(pieces):
        for b in range(bands):
            pairs.append((s * bands + b, (s ^ mask_sp) * bands + (b ^ mask_bd)))
    return lax.ppermute(value, ("sp", "bd"), pairs)


def around(values):
    return [send(values[k], k % 2, 2 * (k // 2)) for k in range(1, 4)]


def local(cube, taps_x, taps_y, factor_w, factor_h):
    w_rows = jnp.transpose(factor_w[0])
    taps_x = jnp.transpose(taps_x, (2, 0, 1))
    taps_y = jnp.transpose(taps_y, (2, 0, 1))
    h_columns = jnp.transpose(factor_h, (1, 2, 0))
    x_high, x_low, far_keep, far_give, near_keep, near_give = blur_call(cube[0], taps_x, taps_y, w_rows)
    far_taken = send(far_give, 0, 1)
    near_taken = send(near_give, 0, 1)
    far = [far_keep[2 * k:2 * k + 2] + far_taken[2 * k:2 * k + 2] for k in range(4)]
    near = [near_keep[2 * k:2 * k + 2] + near_taken[2 * k:2 * k + 2] for k in range(4)]
    rank = w_rows.shape[0]
    gram = near_keep[8, :, :rank] + near_taken[8, :, :rank]
    gram_other = send(gram, 0, 2)
    far_round = around(far)
    near_round = around(near)
    far_sum = (far[0] + far_round[0]) + (far_round[1] + far_round[2])
    ratio = ratio_call(gram, gram_other, h_columns)
    far_other = send(far_sum, 4, 0)
    far_other, ratio = lax.optimization_barrier((far_other, ratio))
    line = [(near[0][k] + near_round[0][k]) + (near_round[1][k] + near_round[2][k]) + far_other[k] for k in range(2)]
    h_piece = ratio * (line[0] + send(line[1], 2, 0))
    h_near = jnp.stack([h_piece, send(h_piece, 2, 0)])
    h_far = send(h_near, 4, 0)
    near_parts = [h_near] + around([h_near] * 4)
    near_parts = near_parts + [send(value, 0, 1) for value in near_parts]
    numer, gram_h, h_next = near_call(x_high, x_low, near_parts)
    far_parts = [h_far] + around([h_far] * 4)
    numer, *far_parts = lax.optimization_barrier((numer, *far_parts))
    far_parts = far_parts + [send(value, 0, 1) for value in far_parts]
    w_piece = far_call(x_high, x_low, w_rows, numer, gram_h, far_parts)
    w_two = jnp.stack([w_piece, send(w_piece, 1, 0)])
    w_four = jnp.concatenate([w_two, send(w_two, 2, 0)])
    w_next = gather_w_call(w_four, send(w_four, 4, 0))
    return jnp.transpose(w_next)[None], jnp.transpose(h_next, (2, 0, 1))


def normalized(kernel):
    return kernel / jnp.sum(kernel, axis=-1, keepdims=True)


def band_weights(kernel, size_in, size_out, offset):
    tap_count = kernel.shape[-1]
    in_index = lax.broadcasted_iota(jnp.int32, (size_in, size_out, tap_count), 0)
    out_index = lax.broadcasted_iota(jnp.int32, (size_in, size_out, tap_count), 1)
    tap_index = lax.broadcasted_iota(jnp.int32, (size_in, size_out, tap_count), 2)
    select = (tap_index == in_index - out_index + offset).astype(jnp.float32)
    return jnp.einsum("pk,iok->pio", kernel, select, precision=lax.Precision.HIGHEST)


def blur_rows(planes, kernel_y):
    margin = (kernel_y.shape[-1] - 1) // 2
    height = planes.shape[1]
    band_table = band_weights(kernel_y, height, height, margin)
    return jnp.einsum("piz,pio->poz", planes, band_table, precision=lax.Precision.HIGHEST)


def blur_columns(planes, kernel_x):
    margin = (kernel_x.shape[-1] - 1) // 2
    count, height, length = planes.shape
    blocks = planes.reshape(count, height, length // 128, 128)
    empty = jnp.zeros((count, height, 1, 128), jnp.float32)
    left_block = jnp.concatenate([empty, blocks[:, :, :-1]], axis=2)
    right_block = jnp.concatenate([blocks[:, :, 1:], empty], axis=2)
    window = jnp.concatenate([left_block, blocks, right_block], axis=3)
    band_table = band_weights(kernel_x, 384, 128, margin - 128)
    result = jnp.einsum("pybi,pio->pybo", window, band_table, precision=lax.Precision.HIGHEST)
    return result.reshape(count, height, length)


def local_any(cube, taps_x, taps_y, factor_w, factor_h):
    highest = lax.Precision.HIGHEST
    kernel_x = normalized(taps_x[0])
    kernel_y = normalized(taps_y[0])
    rows_done = blur_rows(cube[0], kernel_y)
    w_band = factor_w[0]
    blurred = blur_columns(rows_done, kernel_x)[None]
    moved = lax.all_to_all(blurred, "sp", split_axis=3, concat_axis=1, tiled=True)
    numer_part = jnp.einsum("lr,plyx->pryx", w_band, moved, precision=highest)
    gram_part = jnp.dot(w_band.T, w_band, precision=highest)
    numer_h, gram_w = lax.psum((numer_part[0], gram_part), "bd")
    h_next = factor_h * numer_h / jnp.einsum("rq,qyx->ryx", gram_w, factor_h, precision=highest)
    x_band = moved[0]
    gram_h_part = jnp.einsum("ryx,qyx->rq", h_next, h_next, precision=highest)
    numer_w_part = jnp.einsum("lyx,ryx->lr", x_band, h_next, precision=highest)
    numer_w, gram_h = lax.psum((numer_w_part, gram_h_part), "sp")
    w_next = w_band * numer_w / jnp.dot(w_band, gram_h, precision=highest)
    return (w_next[None], h_next)


def solution(mesh):
    in_specs = (
        P("bd", "sp", None, None),
        P("bd", "sp", None),
        P("bd", "sp", None),
        P("bd", None, None),
        P(None, None, "sp"),
    )
    out_specs = (P("bd", None, None), P(None, None, "sp"))

    def body(cube, *rest):
        suits = lax.axis_size("sp") == 8 and lax.axis_size("bd") == 4 and cube.shape[1] % GROUP == 0
        return (local if suits else local_any)(cube, *rest)

    return jax.shard_map(body, mesh=mesh, in_specs=in_specs, out_specs=out_specs, check_vma=False)
```

```python
import functools

import jax
import jax.numpy as jnp
from jax import lax
from jax.experimental import pallas as pl
from jax.experimental.pallas import tpu as pltpu
from jax.sharding import PartitionSpec as P

F32 = jnp.float32
BF16 = jnp.bfloat16
LANES = 128
GROUP = 16
VMEM_LIMIT = 48 * 1024 * 1024


def split(value):
    high = value.astype(BF16)
    low = (value - high.astype(F32)).astype(BF16)
    return high, low


def dot(left, right):
    return lax.dot_general(left, right, (((1,), (0,)), ((), ())), preferred_element_type=F32)


def dot_nt(left, right):
    return lax.dot_general(left, right, (((1,), (1,)), ((), ())), preferred_element_type=F32)


def dot_exact(left, right):
    return lax.dot_general(
        left, right, (((1,), (0,)), ((), ())),
        precision=lax.Precision.HIGHEST, preferred_element_type=F32,
    )


def exchange_blocks(rows, block):
    lane = lax.broadcasted_iota(jnp.int32, rows[0].shape, 1)
    first_half = lane < 2 * block
    even = (lane // block) % 2 == 0
    v0, v1, v2, v3 = rows
    u0 = jnp.where(first_half, v0, pltpu.roll(v2, 2 * block, 1))
    u2 = jnp.where(first_half, pltpu.roll(v0, 2 * block, 1), v2)
    u1 = jnp.where(first_half, v1, pltpu.roll(v3, 2 * block, 1))
    u3 = jnp.where(first_half, pltpu.roll(v1, 2 * block, 1), v3)
    w0 = jnp.where(even, u0, pltpu.roll(u1, block, 1))
    w1 = jnp.where(even, pltpu.roll(u0, 3 * block, 1), u1)
    w2 = jnp.where(even, u2, pltpu.roll(u3, block, 1))
    w3 = jnp.where(even, pltpu.roll(u2, 3 * block, 1), u3)
    return w0, w1, w2, w3


def normalized_taps(taps_ref, reverse, work_ref, out_ref):
    taps = taps_ref.shape[0]
    planes = taps_ref.shape[2]
    work_ref[...] = jnp.zeros_like(work_ref)
    for tap in range(taps):
        row = taps - 1 - tap if reverse else tap
        work_ref[row:row + 1, 0:planes] = taps_ref[tap]
    values = work_ref[...]
    total = jnp.sum(values, axis=0, keepdims=True)
    total = jnp.where(total == 0.0, 1.0, total)
    out_ref[...] = jnp.transpose(values / total)


def column_table(row, margin):
    circulant = pltpu.roll(jnp.broadcast_to(row, (LANES, LANES)), 0, 1, stride=1, stride_axis=0)
    high = circulant.astype(BF16).astype(F32)
    low = circulant - high
    src = lax.broadcasted_iota(jnp.int32, (LANES, LANES), 0)
    dst = lax.broadcasted_iota(jnp.int32, (LANES, LANES), 1)
    near = jnp.abs(dst - src) <= margin
    edge = GROUP
    wraps_up = (src - dst)[LANES - edge:] > LANES // 2
    wraps_down = (dst - src)[:edge] > LANES // 2
    empty = jnp.zeros((LANES - edge, LANES), BF16)

    def table(part):
        middle = jnp.where(near, part, 0.0).astype(BF16)
        upper = jnp.where(wraps_up, part[LANES - edge:], 0.0).astype(BF16)
        lower = jnp.where(wraps_down, part[:edge], 0.0).astype(BF16)
        top = jnp.concatenate([middle, jnp.concatenate([empty, upper], axis=0)], axis=1)
        bottom = jnp.concatenate([jnp.concatenate([lower, empty], axis=0), middle], axis=1)
        return jnp.concatenate([top, bottom], axis=0)

    return table(high), table(low)


def row_table(base, margin, height):
    high = base.astype(BF16).astype(F32)
    low = base - high
    plane = lax.broadcasted_iota(jnp.int32, (8, LANES), 0)
    lane = lax.broadcasted_iota(jnp.int32, (8, LANES), 1)
    per_vector = LANES // height
    own = lane // height == plane % per_vector
    masks = [own & (plane // per_vector == part) for part in range(8 * height // LANES)]

    def table(part):
        strips = []
        for row in range(height):
            rolled = pltpu.roll(part, (row - margin) % LANES, 1)
            strips.append(jnp.concatenate([jnp.where(mask, rolled, 0.0) for mask in masks], axis=1))
        return jnp.concatenate(strips, axis=0).astype(BF16)

    return table(high), table(low)


def fold(square):
    side = square.shape[0]
    across = 2 * LANES // side
    blocks = [square[first:first + 8] for first in range(0, side, 8)]
    blocks += [jnp.zeros_like(blocks[0])] * (2 * across - len(blocks))
    rest = jnp.zeros((8, 2 * LANES - across * side), F32)
    return jnp.concatenate(
        [jnp.concatenate(blocks[first:first + across] + [rest], axis=1) for first in (0, across)], axis=0)


def unfold(folded, side):
    across = 2 * LANES // side
    blocks = []
    for block in range(side // 8):
        row, lane = 8 * (block // across), side * (block % across)
        blocks.append(folded[row:row + 8, lane:lane + side])
    return jnp.concatenate(blocks, axis=0)


def in_vmem(count):
    return [pl.BlockSpec(memory_space=pltpu.VMEM)] * count


def band_gram(w_rows):
    high, low = split(w_rows)
    rank = w_rows.shape[0]
    padded = jnp.concatenate([high, jnp.zeros((2 * LANES - rank, high.shape[1]), BF16)], axis=0)
    padded_low = jnp.concatenate([low, jnp.zeros((2 * LANES - rank, low.shape[1]), BF16)], axis=0)
    both = dot_nt(jnp.concatenate([high, low], axis=0), padded)
    return both[:rank] + (both[rank:] + dot_nt(high, padded_low))


def blur_kernel(cube_ref, taps_x_hbm, taps_y_hbm, w_hbm, xh_ref, xl_ref, far_keep, far_give, near_keep, near_give,
                taps_x_ref, taps_y_ref, w_ref, sems, work_ref, kx_ref, ky_ref):
    step = pl.program_id(0)
    taps = taps_x_ref.shape[0]
    margin = (taps - 1) // 2
    height = cube_ref.shape[1]
    rank = w_ref.shape[0]

    @pl.when(step == 0)
    def _():
        copies = [
            pltpu.make_async_copy(taps_x_hbm, taps_x_ref, sems.at[0]),
            pltpu.make_async_copy(taps_y_hbm, taps_y_ref, sems.at[1]),
            pltpu.make_async_copy(w_hbm, w_ref, sems.at[2]),
        ]
        for copy in copies:
            copy.start()
        for copy in copies:
            copy.wait()
        gram = fold(band_gram(w_ref[...])[:, :rank])
        far_keep[8 * rank:] = gram
        far_give[8 * rank:] = gram
        normalized_taps(taps_x_ref, True, work_ref, kx_ref)
        normalized_taps(taps_y_ref, False, work_ref, ky_ref)
        kx_ref[...] = pltpu.roll(kx_ref[...], LANES - margin, 1)
        per_vector = LANES // height
        place = lax.broadcasted_iota(jnp.int32, (LANES, LANES), 0) % per_vector
        values = ky_ref[...]
        placed = values
        for k in range(1, per_vector):
            placed = jnp.where(place == k, pltpu.roll(values, k * height, 1), placed)
        ky_ref[...] = placed

    halves = []
    for half in range(GROUP // 8):
        done = []
        for plane in range(8 * half, 8 * half + 8):
            row = kx_ref[pl.ds(step * GROUP + plane, 1), :]
            table_high, table_low = column_table(row, margin)
            high, low = split(cube_ref[plane])
            both = dot(jnp.concatenate([high, low], axis=0), table_high)
            done.append(both[:height] + (both[height:] + dot(high, table_low)))
        high, low = split(jnp.concatenate(done, axis=0))
        rows = ky_ref[pl.ds(pl.multiple_of(step * GROUP + 8 * half, 8), 8), :]
        table_high, table_low = row_table(rows, margin, height)
        result = dot(table_high, high) + (dot(table_low, high) + dot(table_high, low))
        halves.append(result.reshape(height, 8, result.shape[1]))
    high, low = split(jnp.concatenate(halves, axis=1))
    planes_here = pl.ds(pl.multiple_of(step * GROUP, GROUP), GROUP)
    for column in range(2):
        xh_ref[column, :, planes_here, :] = high[:, :, column * LANES:(column + 1) * LANES]
        xl_ref[column, :, planes_here, :] = low[:, :, column * LANES:(column + 1) * LANES]

    @pl.when(step == pl.num_programs(0) - 1)
    def _():
        planes = xh_ref.shape[2]
        band = w_ref.shape[1]
        me_sp = lax.axis_index("sp")
        me_bd = lax.axis_index("bd")
        tall = height // lax.axis_size("bd")
        wide = 2 * LANES // lax.axis_size("sp")
        shift = lax.rem(band - me_sp * planes, band)
        w_high, w_low = split(pltpu.roll(w_ref[...], shift, 1)[:, :planes])
        w_both = jnp.concatenate([w_high, w_low], axis=0)
        for rel_bd in range(4):
            first_row = lax.bitwise_xor(me_bd, rel_bd) * tall
            sums = []
            for row in range(tall):
                x_high = jnp.concatenate([xh_ref[0, first_row + row], xh_ref[1, first_row + row]], axis=1)
                x_low = jnp.concatenate([xl_ref[0, first_row + row], xl_ref[1, first_row + row]], axis=1)
                both = dot(w_both, x_high)
                sums.append(both[:rank] + (both[rank:] + dot(w_high, x_low)))
            far_ref, near_ref = (far_keep, near_keep) if rel_bd % 2 == 0 else (far_give, near_give)
            for column in range(2):
                quarters = [
                    exchange_blocks(
                        [sums[4 * quarter + k][:, column * LANES:(column + 1) * LANES] for k in range(4)], wide)
                    for quarter in range(2)]
                for k in range(4):
                    piece = jnp.concatenate([quarters[0][k], quarters[1][k]], axis=1)
                    rel_sp = lax.bitwise_xor(me_sp, column * 4 + k)
                    near_side = rel_sp % 2
                    if rel_bd // 2:
                        near_side = 1 - near_side
                    place = (rel_bd // 2) * 4 + near_side * 2 + (rel_sp // 2) % 2
                    first = pl.multiple_of(place * rank, 8)

                    @pl.when(rel_sp >= 4)
                    def _():
                        far_ref[pl.ds(first, rank)] = piece

                    @pl.when(rel_sp < 4)
                    def _():
                        near_ref[pl.ds(first, rank)] = piece


def blur_call(cube, taps_x, taps_y, w_rows):
    planes, height, length = cube.shape
    rank = w_rows.shape[0]
    far = jax.ShapeDtypeStruct((8 * rank + 16, 2 * LANES), F32)
    near = jax.ShapeDtypeStruct((8 * rank, 2 * LANES), F32)
    image = (2, height, planes, LANES)
    whole = lambda shape: pl.BlockSpec(shape, lambda i: (0,) * len(shape))
    return pl.pallas_call(
        blur_kernel,
        grid=(planes // GROUP,),
        out_shape=[jax.ShapeDtypeStruct(image, BF16)] * 2 + [far, far, near, near],
        in_specs=[pl.BlockSpec((GROUP, height, length), lambda i: (i, 0, 0))]
        + [pl.BlockSpec(memory_space=pltpu.HBM)] * 3,
        out_specs=[whole(image)] * 2 + [whole(far.shape)] * 2 + [whole(near.shape)] * 2,
        scratch_shapes=[pltpu.VMEM(value.shape, F32) for value in (taps_x, taps_y, w_rows)]
        + [pltpu.SemaphoreType.DMA((3,))] + [pltpu.VMEM((LANES, LANES), F32)] * 3,
        compiler_params=pltpu.CompilerParams(
            dimension_semantics=("arbitrary",), vmem_limit_bytes=VMEM_LIMIT),
    )(cube, taps_x, taps_y, w_rows)


def ratio_kernel(gram_ref, other_ref, h_ref, out_ref):
    tall = h_ref.shape[0] // lax.axis_size("bd")
    first = pl.multiple_of(lax.axis_index("bd") * tall, tall)
    here = h_ref[pl.ds(first, tall)]
    here = jnp.transpose(here.reshape(-1, here.shape[2]))
    gram = unfold(gram_ref[...] + other_ref[...], here.shape[0])
    out_ref[...] = here / dot_exact(gram, here)


def ratio_call(gram, gram_other, h_columns):
    rank = h_columns.shape[2]
    columns = h_columns.shape[0] * h_columns.shape[1] // lax.axis_size("bd")
    return pl.pallas_call(
        ratio_kernel,
        out_shape=jax.ShapeDtypeStruct((rank, columns), F32),
        in_specs=in_vmem(3),
    )(gram, gram_other, h_columns)


def accumulate(xh_ref, xl_ref, part_refs, all_ref, column, numer, gram):
    height, rank = xh_ref.shape[1], all_ref.shape[1]
    me_sp = lax.axis_index("sp")
    me_bd = lax.axis_index("bd")
    bands = lax.axis_size("bd")
    tall = height // bands
    wide = 2 * LANES // lax.axis_size("sp")
    for slot in range(8):
        rel_bd = slot // 4 + 2 * ((slot // 2) % 2)
        for inner in range(2):
            owner_sp = lax.bitwise_xor(me_sp, slot % 2 + 2 * inner) % 4
            all_ref[lax.bitwise_xor(me_bd, rel_bd) * 4 + owner_sp] = part_refs[slot][inner]
    for part in range(bands):
        rows = []
        for quarter in range(2):
            rows += exchange_blocks(
                [all_ref[part * 4 + k][:, quarter * LANES:(quarter + 1) * LANES] for k in range(4)], wide)
        for row in range(0, tall, 2):
            high, low = split(jnp.concatenate([rows[row], rows[row + 1]], axis=1))
            both = jnp.concatenate([high, low], axis=0)
            y = part * tall + row
            x_high = jnp.concatenate([xh_ref[column, y], xh_ref[column, y + 1]], axis=1)
            x_low = jnp.concatenate([xl_ref[column, y], xl_ref[column, y + 1]], axis=1)
            product = dot_nt(both, x_high)
            numer = numer + (product[:rank] + (product[rank:] + dot_nt(high, x_low)))
            product = dot_nt(both, high)
            gram = gram + (product[:rank] + (product[rank:] + dot_nt(high, low)))
    return numer, gram


def near_kernel(xh_ref, xl_ref, *rest):
    part_refs = rest[:8]
    numer_out, gram_out, h_out, all_ref = rest[8:]
    planes = xh_ref.shape[2]
    rank = all_ref.shape[1]
    bands = lax.axis_size("bd")
    tall = xh_ref.shape[1] // bands
    wide = 2 * LANES // lax.axis_size("sp")
    me_sp = lax.axis_index("sp")
    numer, gram = accumulate(
        xh_ref, xl_ref, part_refs, all_ref, me_sp // 4,
        jnp.zeros((rank, planes), F32), jnp.zeros((rank, rank), F32))
    numer_out[...] = numer
    gram_out[...] = gram
    for part in range(bands):
        mine = jnp.transpose(all_ref[part * 4 + me_sp % 4])
        h_out[part * tall:(part + 1) * tall] = mine.reshape(tall, wide, rank)


def near_call(x_high, x_low, parts):
    _, height, planes, _ = x_high.shape
    rank = parts[0].shape[1]
    wide = 2 * LANES // lax.axis_size("sp")
    return pl.pallas_call(
        near_kernel,
        out_shape=[
            jax.ShapeDtypeStruct((rank, planes), F32),
            jax.ShapeDtypeStruct((rank, rank), F32),
            jax.ShapeDtypeStruct((height, wide, rank), F32),
        ],
        in_specs=in_vmem(len(parts) + 2),
        scratch_shapes=[pltpu.VMEM((16,) + parts[0].shape[1:], F32)],
        compiler_params=pltpu.CompilerParams(vmem_limit_bytes=VMEM_LIMIT),
    )(x_high, x_low, *parts)


def far_kernel(xh_ref, xl_ref, w_ref, numer_ref, gram_ref, *rest):
    part_refs = rest[:8]
    w_out, all_ref = rest[8:]
    planes = xh_ref.shape[2]
    band = w_ref.shape[1]
    me_sp = lax.axis_index("sp")
    numer, gram = accumulate(
        xh_ref, xl_ref, part_refs, all_ref, 1 - me_sp // 4, numer_ref[...], gram_ref[...])
    shift = lax.rem(band - me_sp * planes, band)
    w_here = pltpu.roll(w_ref[...], shift, 1)[:, :planes]
    w_out[...] = w_here * numer / dot_exact(gram, w_here)


def far_call(x_high, x_low, w_rows, numer, gram, parts):
    return pl.pallas_call(
        far_kernel,
        out_shape=jax.ShapeDtypeStruct(numer.shape, F32),
        in_specs=in_vmem(len(parts) + 5),
        scratch_shapes=[pltpu.VMEM((16,) + parts[0].shape[1:], F32)],
        compiler_params=pltpu.CompilerParams(vmem_limit_bytes=VMEM_LIMIT),
    )(x_high, x_low, w_rows, numer, gram, *parts)


def gather_w_kernel(*refs):
    part_refs = refs[:-2]
    out_ref, all_ref = refs[-2:]
    planes = out_ref.shape[1] // 8
    me_sp = lax.axis_index("sp")
    rel = 0
    for part_ref in part_refs:
        for inner in range(part_ref.shape[0]):
            all_ref[lax.bitwise_xor(me_sp, RING[rel]), :, 0:planes] = part_ref[inner]
            rel += 1
    for owner in range(8):
        out_ref[:, owner * planes:(owner + 1) * planes] = all_ref[owner][:, :planes]


RING = (0, 1, 2, 4, 6, 3, 5, 7)


def gather_w_call(parts):
    _, rank, planes = parts[0].shape
    return pl.pallas_call(
        gather_w_kernel,
        out_shape=jax.ShapeDtypeStruct((rank, planes * 8), F32),
        in_specs=in_vmem(len(parts)),
        scratch_shapes=[pltpu.VMEM((8, rank, LANES), F32)],
    )(*parts)


def send(value, mask_sp, mask_bd):
    bands = lax.axis_size("bd")
    pieces = lax.axis_size("sp")
    pairs = []
    for s in range(pieces):
        for b in range(bands):
            pairs.append((s * bands + b, (s ^ mask_sp) * bands + (b ^ mask_bd)))
    return lax.ppermute(value, ("sp", "bd"), pairs)


def around(values):
    return [send(values[k], k % 2, 2 * (k // 2)) for k in range(1, 4)]


def local(cube, taps_x, taps_y, factor_w, factor_h):
    w_rows = jnp.transpose(factor_w[0])
    taps_x = jnp.transpose(taps_x, (2, 0, 1))
    taps_y = jnp.transpose(taps_y, (2, 0, 1))
    h_columns = jnp.transpose(factor_h, (1, 2, 0))
    rank = w_rows.shape[0]
    x_high, x_low, far_keep, far_give, near_keep, near_give = blur_call(cube[0], taps_x, taps_y, w_rows)
    far_taken = send(far_give, 0, 1)
    near_taken = send(near_give, 0, 1)
    spans = [(0, 2), (2, 4), (6, 8), (4, 6)]
    rows = [(first * rank, last * rank) for first, last in spans]
    near = [near_keep[first:last] + near_taken[first:last] for first, last in rows]
    rows[2] = (rows[2][0], far_keep.shape[0])
    far = [far_keep[first:last] + far_taken[first:last] for first, last in rows]
    gram = far[2][2 * rank:]
    far_round = around(far)
    near_round = around(near)
    ratio = ratio_call(gram, far_round[1][2 * rank:], h_columns)

    def total(first, others, k):
        part = slice(k * rank, (k + 1) * rank)
        return (first[part] + others[0][part]) + (others[1][part] + others[2][part])

    across = [send(total(far[0], far_round, 0), 4, 0), send(total(far[0], far_round, 1), 6, 0)]
    along = send(total(near[0], near_round, 1), 2, 0)
    h_piece = ratio * ((total(near[0], near_round, 0) + along) + (across[0] + across[1]))
    h_near = jnp.stack([h_piece, send(h_piece, 2, 0)])
    h_far = jnp.stack([send(h_piece, 4, 0), send(h_piece, 6, 0)])
    near_parts = [h_near] + around([h_near] * 4)
    near_parts = near_parts + [send(value, 0, 1) for value in near_parts]
    numer, gram_h, h_next = near_call(x_high, x_low, near_parts)
    far_parts = [h_far] + around([h_far] * 4)
    numer, *far_parts = lax.optimization_barrier((numer, *far_parts))
    far_parts = far_parts + [send(value, 0, 1) for value in far_parts]
    w_piece = far_call(x_high, x_low, w_rows, numer, gram_h, far_parts)[None]
    w_line = jnp.concatenate([send(w_piece, mask, 0) for mask in (2, 4, 6)])
    w_next = gather_w_call([w_piece, send(w_piece, 1, 0), w_line, send(w_line, 1, 0)])
    return jnp.transpose(w_next)[None], jnp.transpose(h_next, (2, 0, 1))


def normalized(kernel):
    return kernel / jnp.sum(kernel, axis=-1, keepdims=True)


def band_weights(kernel, size_in, size_out, offset):
    tap_count = kernel.shape[-1]
    in_index = lax.broadcasted_iota(jnp.int32, (size_in, size_out, tap_count), 0)
    out_index = lax.broadcasted_iota(jnp.int32, (size_in, size_out, tap_count), 1)
    tap_index = lax.broadcasted_iota(jnp.int32, (size_in, size_out, tap_count), 2)
    select = (tap_index == in_index - out_index + offset).astype(jnp.float32)
    return jnp.einsum("pk,iok->pio", kernel, select, precision=lax.Precision.HIGHEST)


def blur_rows(planes, kernel_y):
    margin = (kernel_y.shape[-1] - 1) // 2
    height = planes.shape[1]
    band_table = band_weights(kernel_y, height, height, margin)
    return jnp.einsum("piz,pio->poz", planes, band_table, precision=lax.Precision.HIGHEST)


def blur_columns(planes, kernel_x):
    margin = (kernel_x.shape[-1] - 1) // 2
    count, height, length = planes.shape
    blocks = planes.reshape(count, height, length // 128, 128)
    empty = jnp.zeros((count, height, 1, 128), jnp.float32)
    left_block = jnp.concatenate([empty, blocks[:, :, :-1]], axis=2)
    right_block = jnp.concatenate([blocks[:, :, 1:], empty], axis=2)
    window = jnp.concatenate([left_block, blocks, right_block], axis=3)
    band_table = band_weights(kernel_x, 384, 128, margin - 128)
    result = jnp.einsum("pybi,pio->pybo", window, band_table, precision=lax.Precision.HIGHEST)
    return result.reshape(count, height, length)


def local_any(cube, taps_x, taps_y, factor_w, factor_h):
    highest = lax.Precision.HIGHEST
    kernel_x = normalized(taps_x[0])
    kernel_y = normalized(taps_y[0])
    rows_done = blur_rows(cube[0], kernel_y)
    w_band = factor_w[0]
    blurred = blur_columns(rows_done, kernel_x)[None]
    moved = lax.all_to_all(blurred, "sp", split_axis=3, concat_axis=1, tiled=True)
    numer_part = jnp.einsum("lr,plyx->pryx", w_band, moved, precision=highest)
    gram_part = jnp.dot(w_band.T, w_band, precision=highest)
    numer_h, gram_w = lax.psum((numer_part[0], gram_part), "bd")
    h_next = factor_h * numer_h / jnp.einsum("rq,qyx->ryx", gram_w, factor_h, precision=highest)
    x_band = moved[0]
    gram_h_part = jnp.einsum("ryx,qyx->rq", h_next, h_next, precision=highest)
    numer_w_part = jnp.einsum("lyx,ryx->lr", x_band, h_next, precision=highest)
    numer_w, gram_h = lax.psum((numer_w_part, gram_h_part), "sp")
    w_next = w_band * numer_w / jnp.dot(w_band, gram_h, precision=highest)
    return (w_next[None], h_next)


def solution(mesh):
    in_specs = (
        P("bd", "sp", None, None),
        P("bd", "sp", None),
        P("bd", "sp", None),
        P("bd", None, None),
        P(None, None, "sp"),
    )
    out_specs = (P("bd", None, None), P(None, None, "sp"))

    def body(cube, *rest):
        suits = lax.axis_size("sp") == 8 and lax.axis_size("bd") == 4 and cube.shape[1] % GROUP == 0
        return (local if suits else local_any)(cube, *rest)

    return jax.shard_map(body, mesh=mesh, in_specs=in_specs, out_specs=out_specs, check_vma=False)
```

```python
import functools

import jax
import jax.numpy as jnp
from jax import lax
from jax.experimental import pallas as pl
from jax.experimental.pallas import tpu as pltpu
from jax.sharding import PartitionSpec as P

F32 = jnp.float32
BF16 = jnp.bfloat16
LANES = 128
GROUP = 16
PIECES = 16
FOLDED = 24
VMEM_LIMIT = 48 * 1024 * 1024


def split(value):
    high = value.astype(BF16)
    low = (value - high.astype(F32)).astype(BF16)
    return high, low


def dot(left, right):
    return lax.dot_general(left, right, (((1,), (0,)), ((), ())), preferred_element_type=F32)


def dot_nt(left, right):
    return lax.dot_general(left, right, (((1,), (1,)), ((), ())), preferred_element_type=F32)


def dot_exact(left, right):
    return lax.dot_general(
        left, right, (((1,), (0,)), ((), ())),
        precision=lax.Precision.HIGHEST, preferred_element_type=F32,
    )


def exchange_blocks(rows, block):
    lane = lax.broadcasted_iota(jnp.int32, rows[0].shape, 1)
    first_half = lane < 2 * block
    even = (lane // block) % 2 == 0
    v0, v1, v2, v3 = rows
    u0 = jnp.where(first_half, v0, pltpu.roll(v2, 2 * block, 1))
    u2 = jnp.where(first_half, pltpu.roll(v0, 2 * block, 1), v2)
    u1 = jnp.where(first_half, v1, pltpu.roll(v3, 2 * block, 1))
    u3 = jnp.where(first_half, pltpu.roll(v1, 2 * block, 1), v3)
    w0 = jnp.where(even, u0, pltpu.roll(u1, block, 1))
    w1 = jnp.where(even, pltpu.roll(u0, 3 * block, 1), u1)
    w2 = jnp.where(even, u2, pltpu.roll(u3, block, 1))
    w3 = jnp.where(even, pltpu.roll(u2, 3 * block, 1), u3)
    return w0, w1, w2, w3


def normalized_taps(taps_ref, reverse, work_ref, out_ref):
    taps = taps_ref.shape[0]
    planes = taps_ref.shape[2]
    work_ref[...] = jnp.zeros_like(work_ref)
    for tap in range(taps):
        row = taps - 1 - tap if reverse else tap
        work_ref[row:row + 1, 0:planes] = taps_ref[tap]
    values = work_ref[...]
    total = jnp.sum(values, axis=0, keepdims=True)
    total = jnp.where(total == 0.0, 1.0, total)
    out_ref[...] = jnp.transpose(values / total)


def column_table(row, margin):
    circulant = pltpu.roll(jnp.broadcast_to(row, (LANES, LANES)), 0, 1, stride=1, stride_axis=0)
    high = circulant.astype(BF16).astype(F32)
    low = circulant - high
    src = lax.broadcasted_iota(jnp.int32, (LANES, LANES), 0)
    dst = lax.broadcasted_iota(jnp.int32, (LANES, LANES), 1)
    near = jnp.abs(dst - src) <= margin
    edge = GROUP
    wraps_up = (src - dst)[LANES - edge:] > LANES // 2
    wraps_down = (dst - src)[:edge] > LANES // 2
    empty = jnp.zeros((LANES - edge, LANES), BF16)

    def table(part):
        middle = jnp.where(near, part, 0.0).astype(BF16)
        upper = jnp.where(wraps_up, part[LANES - edge:], 0.0).astype(BF16)
        lower = jnp.where(wraps_down, part[:edge], 0.0).astype(BF16)
        top = jnp.concatenate([middle, jnp.concatenate([empty, upper], axis=0)], axis=1)
        bottom = jnp.concatenate([jnp.concatenate([lower, empty], axis=0), middle], axis=1)
        return jnp.concatenate([top, bottom], axis=0)

    return table(high), table(low)


def row_table(base, margin, height):
    high = base.astype(BF16).astype(F32)
    low = base - high
    plane = lax.broadcasted_iota(jnp.int32, (8, LANES), 0)
    lane = lax.broadcasted_iota(jnp.int32, (8, LANES), 1)
    per_vector = LANES // height
    own = lane // height == plane % per_vector
    masks = [own & (plane // per_vector == part) for part in range(8 * height // LANES)]

    def table(part):
        strips = []
        for row in range(height):
            rolled = pltpu.roll(part, (row - margin) % LANES, 1)
            strips.append(jnp.concatenate([jnp.where(mask, rolled, 0.0) for mask in masks], axis=1))
        return jnp.concatenate(strips, axis=0).astype(BF16)

    return table(high), table(low)


def fold(square):
    side = square.shape[0]
    rest = jnp.zeros((8, LANES - 2 * side), F32)
    return jnp.concatenate(
        [jnp.concatenate([square[first:first + 8], square[first + 8:first + 16], rest], axis=1)
         for first in range(0, side, 16)], axis=0)


def unfold(folded, side):
    blocks = []
    for first in range(0, folded.shape[0], 8):
        blocks += [folded[first:first + 8, :side], folded[first:first + 8, side:2 * side]]
    return jnp.concatenate(blocks, axis=0)


def in_vmem(count):
    return [pl.BlockSpec(memory_space=pltpu.VMEM)] * count


def band_gram(w_rows):
    high, low = split(w_rows)
    rank = w_rows.shape[0]
    padded = jnp.concatenate([high, jnp.zeros((2 * LANES - rank, high.shape[1]), BF16)], axis=0)
    padded_low = jnp.concatenate([low, jnp.zeros((2 * LANES - rank, low.shape[1]), BF16)], axis=0)
    both = dot_nt(jnp.concatenate([high, low], axis=0), padded)
    return both[:rank] + (both[rank:] + dot_nt(high, padded_low))


def blur_kernel(cube_ref, taps_x_hbm, taps_y_hbm, w_hbm, xh_ref, xl_ref, keep_0, give_0, keep_1, give_1,
                taps_x_ref, taps_y_ref, w_ref, sems, work_ref, kx_ref, ky_ref):
    step = pl.program_id(0)
    taps = taps_x_ref.shape[0]
    margin = (taps - 1) // 2
    height = cube_ref.shape[1]
    rank = w_ref.shape[0]

    @pl.when(step == 0)
    def _():
        copies = [
            pltpu.make_async_copy(taps_x_hbm, taps_x_ref, sems.at[0]),
            pltpu.make_async_copy(taps_y_hbm, taps_y_ref, sems.at[1]),
            pltpu.make_async_copy(w_hbm, w_ref, sems.at[2]),
        ]
        for copy in copies:
            copy.start()
        for copy in copies:
            copy.wait()
        gram = fold(band_gram(w_ref[...])[:, :rank])
        keep_0[PIECES * rank:] = gram
        give_0[PIECES * rank:] = gram
        normalized_taps(taps_x_ref, True, work_ref, kx_ref)
        normalized_taps(taps_y_ref, False, work_ref, ky_ref)
        kx_ref[...] = pltpu.roll(kx_ref[...], LANES - margin, 1)
        per_vector = LANES // height
        place = lax.broadcasted_iota(jnp.int32, (LANES, LANES), 0) % per_vector
        values = ky_ref[...]
        placed = values
        for k in range(1, per_vector):
            placed = jnp.where(place == k, pltpu.roll(values, k * height, 1), placed)
        ky_ref[...] = placed

    halves = []
    for half in range(GROUP // 8):
        done = []
        for plane in range(8 * half, 8 * half + 8):
            row = kx_ref[pl.ds(step * GROUP + plane, 1), :]
            table_high, table_low = column_table(row, margin)
            high, low = split(cube_ref[plane])
            both = dot(jnp.concatenate([high, low], axis=0), table_high)
            done.append(both[:height] + (both[height:] + dot(high, table_low)))
        high, low = split(jnp.concatenate(done, axis=0))
        rows = ky_ref[pl.ds(pl.multiple_of(step * GROUP + 8 * half, 8), 8), :]
        table_high, table_low = row_table(rows, margin, height)
        result = dot(table_high, high) + (dot(table_low, high) + dot(table_high, low))
        halves.append(result.reshape(height, 8, result.shape[1]))
    high, low = split(jnp.concatenate(halves, axis=1))
    planes_here = pl.ds(pl.multiple_of(step * GROUP, GROUP), GROUP)
    xh_ref[:, planes_here, :] = high
    xl_ref[:, planes_here, :] = low

    @pl.when(step == pl.num_programs(0) - 1)
    def _():
        planes = xh_ref.shape[1]
        band = w_ref.shape[1]
        me_sp = lax.axis_index("sp")
        me_bd = lax.axis_index("bd")
        tall = height // lax.axis_size("bd")
        wide = 2 * LANES // lax.axis_size("sp")
        shift = lax.rem(band - me_sp * planes, band)
        w_high, w_low = split(pltpu.roll(w_ref[...], shift, 1)[:, :planes])
        w_both = jnp.concatenate([w_high, w_low], axis=0)
        for chain in range(2):
            for rel_bd in (1, 3, 0, 2):
                first_row = lax.bitwise_xor(me_bd, rel_bd) * tall + 4 * chain
                sums = []
                for row in range(4):
                    both = dot(w_both, xh_ref[first_row + row])
                    sums.append(both[:rank] + (both[rank:] + dot(w_high, xl_ref[first_row + row])))
                refs = ((keep_0, give_0), (keep_1, give_1))[chain]
                for column in range(2):
                    pieces = exchange_blocks(
                        [value[:, column * LANES:(column + 1) * LANES] for value in sums], wide)
                    for k in range(4):
                        rel_sp = lax.bitwise_xor(me_sp, column * 4 + k)
                        side = 3 - rel_sp % 2 if rel_bd // 2 else rel_sp % 2
                        first = pl.multiple_of((side * 4 + rel_sp // 2) * rank, 8)
                        refs[rel_bd % 2][pl.ds(first, rank)] = pieces[k]


def blur_call(cube, taps_x, taps_y, w_rows):
    planes, height, length = cube.shape
    rank = w_rows.shape[0]
    first = jax.ShapeDtypeStruct((PIECES * rank + FOLDED, LANES), F32)
    second = jax.ShapeDtypeStruct((PIECES * rank, LANES), F32)
    image = (height, planes, length)
    whole = lambda shape: pl.BlockSpec(shape, lambda i: (0,) * len(shape))
    return pl.pallas_call(
        blur_kernel,
        grid=(planes // GROUP,),
        out_shape=[jax.ShapeDtypeStruct(image, BF16)] * 2 + [first, first, second, second],
        in_specs=[pl.BlockSpec((GROUP, height, length), lambda i: (i, 0, 0))]
        + [pl.BlockSpec(memory_space=pltpu.HBM)] * 3,
        out_specs=[whole(image)] * 2 + [whole(first.shape)] * 2 + [whole(second.shape)] * 2,
        scratch_shapes=[pltpu.VMEM(value.shape, F32) for value in (taps_x, taps_y, w_rows)]
        + [pltpu.SemaphoreType.DMA((3,))] + [pltpu.VMEM((LANES, LANES), F32)] * 3,
        compiler_params=pltpu.CompilerParams(
            dimension_semantics=("arbitrary",), vmem_limit_bytes=VMEM_LIMIT),
    )(cube, taps_x, taps_y, w_rows)


def ratio_kernel(mine_ref, other_ref, h_ref, out_0, out_1):
    tall = h_ref.shape[0] // lax.axis_size("bd")
    first = pl.multiple_of(lax.axis_index("bd") * tall, tall)
    here = h_ref[pl.ds(first, tall)]
    here = jnp.transpose(here.reshape(-1, here.shape[2]))
    rows = mine_ref.shape[0]
    gram = unfold(mine_ref[rows - FOLDED:rows] + other_ref[rows - FOLDED:rows], here.shape[0])
    ratio = here / dot_exact(gram, here)
    out_0[...] = ratio[:, :LANES]
    out_1[...] = ratio[:, LANES:]


def ratio_call(mine, other, h_columns):
    piece = jax.ShapeDtypeStruct((h_columns.shape[2], LANES), F32)
    return pl.pallas_call(
        ratio_kernel,
        out_shape=[piece, piece],
        in_specs=in_vmem(3),
        compiler_params=pltpu.CompilerParams(vmem_limit_bytes=VMEM_LIMIT),
    )(mine, other, h_columns)


def accumulate(xh_ref, xl_ref, part_refs, all_ref, h_out, chain, numer, gram):
    height, rank = xh_ref.shape[0], all_ref.shape[1]
    me_sp = lax.axis_index("sp")
    me_bd = lax.axis_index("bd")
    bands = lax.axis_size("bd")
    pieces = lax.axis_size("sp")
    tall = height // bands
    wide = 2 * LANES // pieces
    for slot, part_ref in enumerate(part_refs):
        rel_bd = slot // 4 + 2 * ((slot // 2) % 2)
        for inner in range(4):
            rel_sp = slot % 2 + 2 * inner
            owner = lax.bitwise_xor(me_bd, rel_bd) * pieces + lax.bitwise_xor(me_sp, rel_sp)
            all_ref[owner] = part_ref[inner]
    for part in range(bands):
        first_row = part * tall + 4 * chain
        halves = [
            exchange_blocks([all_ref[part * pieces + column * 4 + k] for k in range(4)], wide)
            for column in range(2)]
        for row in range(4):
            high, low = split(jnp.concatenate([halves[0][row], halves[1][row]], axis=1))
            both = jnp.concatenate([high, low], axis=0)
            product = dot_nt(both, xh_ref[first_row + row])
            numer = numer + (product[:rank] + (product[rank:] + dot_nt(high, xl_ref[first_row + row])))
            product = dot_nt(both, high)
            gram = gram + (product[:rank] + (product[rank:] + dot_nt(high, low)))
        mine = jnp.transpose(all_ref[part * pieces + me_sp])
        h_out[first_row:first_row + 4] = mine.reshape(4, wide, rank)
    return numer, gram


def first_kernel(xh_ref, xl_ref, *rest):
    part_refs = rest[:8]
    numer_out, gram_out, h_out, all_ref = rest[8:]
    planes, rank = xh_ref.shape[1], all_ref.shape[1]
    numer, gram = accumulate(
        xh_ref, xl_ref, part_refs, all_ref, h_out, 0,
        jnp.zeros((rank, planes), F32), jnp.zeros((rank, rank), F32))
    numer_out[...] = numer
    gram_out[...] = gram
    tall = xh_ref.shape[0] // lax.axis_size("bd")
    for part in range(lax.axis_size("bd")):
        h_out[part * tall + 4:(part + 1) * tall] = jnp.zeros((tall - 4,) + h_out.shape[1:], F32)


def first_call(x_high, x_low, parts):
    height, planes, length = x_high.shape
    rank = parts[0].shape[1]
    return pl.pallas_call(
        first_kernel,
        out_shape=[
            jax.ShapeDtypeStruct((rank, planes), F32),
            jax.ShapeDtypeStruct((rank, rank), F32),
            jax.ShapeDtypeStruct((height, length // lax.axis_size("sp"), rank), F32),
        ],
        in_specs=in_vmem(2 + len(parts)),
        scratch_shapes=[pltpu.VMEM((32,) + parts[0].shape[1:], F32)],
        compiler_params=pltpu.CompilerParams(vmem_limit_bytes=VMEM_LIMIT),
    )(x_high, x_low, *parts)


def second_kernel(xh_ref, xl_ref, w_ref, numer_ref, gram_ref, h_ref, *rest):
    part_refs = rest[:8]
    w_out, h_out, all_ref = rest[8:]
    planes = xh_ref.shape[1]
    band = w_ref.shape[1]
    me_sp = lax.axis_index("sp")
    h_out[...] = h_ref[...]
    numer, gram = accumulate(
        xh_ref, xl_ref, part_refs, all_ref, h_out, 1, numer_ref[...], gram_ref[...])
    shift = lax.rem(band - me_sp * planes, band)
    w_here = pltpu.roll(w_ref[...], shift, 1)[:, :planes]
    w_out[...] = w_here * numer / dot_exact(gram, w_here)


def second_call(x_high, x_low, w_rows, numer, gram, h_half, parts):
    return pl.pallas_call(
        second_kernel,
        out_shape=[
            jax.ShapeDtypeStruct(numer.shape, F32),
            jax.ShapeDtypeStruct(h_half.shape, F32),
        ],
        in_specs=in_vmem(6 + len(parts)),
        scratch_shapes=[pltpu.VMEM((32,) + parts[0].shape[1:], F32)],
        compiler_params=pltpu.CompilerParams(vmem_limit_bytes=VMEM_LIMIT),
    )(x_high, x_low, w_rows, numer, gram, h_half, *parts)


def gather_w_kernel(*refs):
    part_refs = refs[:-2]
    out_ref, all_ref = refs[-2:]
    planes = out_ref.shape[1] // 8
    me_sp = lax.axis_index("sp")
    rel = 0
    for part_ref in part_refs:
        for inner in range(part_ref.shape[0]):
            all_ref[lax.bitwise_xor(me_sp, RING[rel]), :, 0:planes] = part_ref[inner]
            rel += 1
    for owner in range(8):
        out_ref[:, owner * planes:(owner + 1) * planes] = all_ref[owner][:, :planes]


RING = (0, 1, 2, 4, 6, 3, 5, 7)


def gather_w_call(parts):
    _, rank, planes = parts[0].shape
    return pl.pallas_call(
        gather_w_kernel,
        out_shape=jax.ShapeDtypeStruct((rank, planes * 8), F32),
        in_specs=in_vmem(len(parts)),
        scratch_shapes=[pltpu.VMEM((8, rank, LANES), F32)],
        compiler_params=pltpu.CompilerParams(vmem_limit_bytes=VMEM_LIMIT),
    )(*parts)


def send(value, mask_sp, mask_bd):
    bands = lax.axis_size("bd")
    pieces = lax.axis_size("sp")
    pairs = []
    for s in range(pieces):
        for b in range(bands):
            pairs.append((s * bands + b, (s ^ mask_sp) * bands + (b ^ mask_bd)))
    return lax.ppermute(value, ("sp", "bd"), pairs)


def around(values):
    return [send(values[k], k % 2, 2 * (k // 2)) for k in range(1, 4)]


def local(cube, taps_x, taps_y, factor_w, factor_h):
    w_rows = jnp.transpose(factor_w[0])
    taps_x = jnp.transpose(taps_x, (2, 0, 1))
    taps_y = jnp.transpose(taps_y, (2, 0, 1))
    h_columns = jnp.transpose(factor_h, (1, 2, 0))
    rank = w_rows.shape[0]
    x_high, x_low, keep_0, give_0, keep_1, give_1 = blur_call(cube[0], taps_x, taps_y, w_rows)
    chains = []
    for keep, give in ((keep_0, give_0), (keep_1, give_1)):
        taken = send(give, 0, 1)
        bounds = [place * 4 * rank for place in (0, 1, 3, 2)]
        sides = []
        for first in bounds:
            last = keep.shape[0] if first == max(bounds) else first + 4 * rank
            sides.append(keep[first:last] + taken[first:last])
        chains.append((sides, around(sides)))
    ratios = ratio_call(chains[0][0][2], chains[0][1][1], h_columns)
    rounds = []
    for (sides, others), ratio in zip(chains, ratios):
        line = []
        for k in range(4):
            part = slice(k * rank, (k + 1) * rank)
            line.append((sides[0][part] + others[0][part]) + (others[1][part] + others[2][part]))
        line = [line[0]] + [send(line[k], 2 * k, 0) for k in range(1, 4)]
        h_piece = ratio * ((line[0] + line[1]) + (line[2] + line[3]))
        h_line = jnp.stack([h_piece] + [send(h_piece, 2 * k, 0) for k in range(1, 4)])
        parts = [h_line] + around([h_line] * 4)
        rounds.append(parts + [send(value, 0, 1) for value in parts])
    numer, gram_h, h_half = first_call(x_high, x_low, rounds[0])
    w_piece, h_next = second_call(x_high, x_low, w_rows, numer, gram_h, h_half, rounds[1])
    w_piece = w_piece[None]
    w_line = jnp.concatenate([send(w_piece, mask, 0) for mask in (2, 4, 6)])
    w_next = gather_w_call([w_piece, send(w_piece, 1, 0), w_line, send(w_line, 1, 0)])
    return jnp.transpose(w_next)[None], jnp.transpose(h_next, (2, 0, 1))


def normalized(kernel):
    return kernel / jnp.sum(kernel, axis=-1, keepdims=True)


def band_weights(kernel, size_in, size_out, offset):
    tap_count = kernel.shape[-1]
    in_index = lax.broadcasted_iota(jnp.int32, (size_in, size_out, tap_count), 0)
    out_index = lax.broadcasted_iota(jnp.int32, (size_in, size_out, tap_count), 1)
    tap_index = lax.broadcasted_iota(jnp.int32, (size_in, size_out, tap_count), 2)
    select = (tap_index == in_index - out_index + offset).astype(jnp.float32)
    return jnp.einsum("pk,iok->pio", kernel, select, precision=lax.Precision.HIGHEST)


def blur_rows(planes, kernel_y):
    margin = (kernel_y.shape[-1] - 1) // 2
    height = planes.shape[1]
    band_table = band_weights(kernel_y, height, height, margin)
    return jnp.einsum("piz,pio->poz", planes, band_table, precision=lax.Precision.HIGHEST)


def blur_columns(planes, kernel_x):
    margin = (kernel_x.shape[-1] - 1) // 2
    count, height, length = planes.shape
    blocks = planes.reshape(count, height, length // 128, 128)
    empty = jnp.zeros((count, height, 1, 128), jnp.float32)
    left_block = jnp.concatenate([empty, blocks[:, :, :-1]], axis=2)
    right_block = jnp.concatenate([blocks[:, :, 1:], empty], axis=2)
    window = jnp.concatenate([left_block, blocks, right_block], axis=3)
    band_table = band_weights(kernel_x, 384, 128, margin - 128)
    result = jnp.einsum("pybi,pio->pybo", window, band_table, precision=lax.Precision.HIGHEST)
    return result.reshape(count, height, length)


def local_any(cube, taps_x, taps_y, factor_w, factor_h):
    highest = lax.Precision.HIGHEST
    kernel_x = normalized(taps_x[0])
    kernel_y = normalized(taps_y[0])
    rows_done = blur_rows(cube[0], kernel_y)
    w_band = factor_w[0]
    blurred = blur_columns(rows_done, kernel_x)[None]
    moved = lax.all_to_all(blurred, "sp", split_axis=3, concat_axis=1, tiled=True)
    numer_part = jnp.einsum("lr,plyx->pryx", w_band, moved, precision=highest)
    gram_part = jnp.dot(w_band.T, w_band, precision=highest)
    numer_h, gram_w = lax.psum((numer_part[0], gram_part), "bd")
    h_next = factor_h * numer_h / jnp.einsum("rq,qyx->ryx", gram_w, factor_h, precision=highest)
    x_band = moved[0]
    gram_h_part = jnp.einsum("ryx,qyx->rq", h_next, h_next, precision=highest)
    numer_w_part = jnp.einsum("lyx,ryx->lr", x_band, h_next, precision=highest)
    numer_w, gram_h = lax.psum((numer_w_part, gram_h_part), "sp")
    w_next = w_band * numer_w / jnp.dot(w_band, gram_h, precision=highest)
    return (w_next[None], h_next)


def solution(mesh):
    in_specs = (
        P("bd", "sp", None, None),
        P("bd", "sp", None),
        P("bd", "sp", None),
        P("bd", None, None),
        P(None, None, "sp"),
    )
    out_specs = (P("bd", None, None), P(None, None, "sp"))

    def body(cube, *rest):
        suits = lax.axis_size("sp") == 8 and lax.axis_size("bd") == 4 and cube.shape[1] % GROUP == 0
        return (local if suits else local_any)(cube, *rest)

    return jax.shard_map(body, mesh=mesh, in_specs=in_specs, out_specs=out_specs, check_vma=False)
```

```python
import functools

import jax
import jax.numpy as jnp
from jax import lax
from jax.experimental import pallas as pl
from jax.experimental.pallas import tpu as pltpu
from jax.sharding import PartitionSpec as P

F32 = jnp.float32
BF16 = jnp.bfloat16
LANES = 128
GROUP = 16
FOLDED = 16
VMEM_LIMIT = 48 * 1024 * 1024


def split(value):
    high = value.astype(BF16)
    low = (value - high.astype(F32)).astype(BF16)
    return high, low


def dot(left, right):
    return lax.dot_general(left, right, (((1,), (0,)), ((), ())), preferred_element_type=F32)


def dot_nt(left, right):
    return lax.dot_general(left, right, (((1,), (1,)), ((), ())), preferred_element_type=F32)


def dot_exact(left, right):
    return lax.dot_general(
        left, right, (((1,), (0,)), ((), ())),
        precision=lax.Precision.HIGHEST, preferred_element_type=F32,
    )


def exchange_blocks(rows, block):
    lane = lax.broadcasted_iota(jnp.int32, rows[0].shape, 1)
    first_half = lane < 2 * block
    even = (lane // block) % 2 == 0
    v0, v1, v2, v3 = rows
    u0 = jnp.where(first_half, v0, pltpu.roll(v2, 2 * block, 1))
    u2 = jnp.where(first_half, pltpu.roll(v0, 2 * block, 1), v2)
    u1 = jnp.where(first_half, v1, pltpu.roll(v3, 2 * block, 1))
    u3 = jnp.where(first_half, pltpu.roll(v1, 2 * block, 1), v3)
    w0 = jnp.where(even, u0, pltpu.roll(u1, block, 1))
    w1 = jnp.where(even, pltpu.roll(u0, 3 * block, 1), u1)
    w2 = jnp.where(even, u2, pltpu.roll(u3, block, 1))
    w3 = jnp.where(even, pltpu.roll(u2, 3 * block, 1), u3)
    return w0, w1, w2, w3


def normalized_taps(taps_ref, reverse, work_ref, out_ref):
    taps = taps_ref.shape[0]
    planes = taps_ref.shape[2]
    work_ref[...] = jnp.zeros_like(work_ref)
    for tap in range(taps):
        row = taps - 1 - tap if reverse else tap
        work_ref[row:row + 1, 0:planes] = taps_ref[tap]
    values = work_ref[...]
    total = jnp.sum(values, axis=0, keepdims=True)
    total = jnp.where(total == 0.0, 1.0, total)
    out_ref[...] = jnp.transpose(values / total)


def column_table(row, margin):
    circulant = pltpu.roll(jnp.broadcast_to(row, (LANES, LANES)), 0, 1, stride=1, stride_axis=0)
    high = circulant.astype(BF16).astype(F32)
    low = circulant - high
    src = lax.broadcasted_iota(jnp.int32, (LANES, LANES), 0)
    dst = lax.broadcasted_iota(jnp.int32, (LANES, LANES), 1)
    near = jnp.abs(dst - src) <= margin
    edge = GROUP
    wraps_up = (src - dst)[LANES - edge:] > LANES // 2
    wraps_down = (dst - src)[:edge] > LANES // 2
    empty = jnp.zeros((LANES - edge, LANES), BF16)

    def table(part):
        middle = jnp.where(near, part, 0.0).astype(BF16)
        upper = jnp.where(wraps_up, part[LANES - edge:], 0.0).astype(BF16)
        lower = jnp.where(wraps_down, part[:edge], 0.0).astype(BF16)
        top = jnp.concatenate([middle, jnp.concatenate([empty, upper], axis=0)], axis=1)
        bottom = jnp.concatenate([jnp.concatenate([lower, empty], axis=0), middle], axis=1)
        return jnp.concatenate([top, bottom], axis=0)

    return table(high), table(low)


def row_table(base, margin, height):
    high = base.astype(BF16).astype(F32)
    low = base - high
    plane = lax.broadcasted_iota(jnp.int32, (8, LANES), 0)
    lane = lax.broadcasted_iota(jnp.int32, (8, LANES), 1)
    per_vector = LANES // height
    own = lane // height == plane % per_vector
    masks = [own & (plane // per_vector == part) for part in range(8 * height // LANES)]

    def table(part):
        strips = []
        for row in range(height):
            rolled = pltpu.roll(part, (row - margin) % LANES, 1)
            strips.append(jnp.concatenate([jnp.where(mask, rolled, 0.0) for mask in masks], axis=1))
        return jnp.concatenate(strips, axis=0).astype(BF16)

    return table(high), table(low)


def fold(square):
    side = square.shape[0]
    across = 2 * LANES // side
    blocks = [square[first:first + 8] for first in range(0, side, 8)]
    blocks += [jnp.zeros_like(blocks[0])] * (2 * across - len(blocks))
    rest = jnp.zeros((8, 2 * LANES - across * side), F32)
    return jnp.concatenate(
        [jnp.concatenate(blocks[first:first + across] + [rest], axis=1) for first in (0, across)], axis=0)


def unfold(folded, side):
    across = 2 * LANES // side
    blocks = []
    for block in range(side // 8):
        row, lane = 8 * (block // across), side * (block % across)
        blocks.append(folded[row:row + 8, lane:lane + side])
    return jnp.concatenate(blocks, axis=0)


def in_vmem(count):
    return [pl.BlockSpec(memory_space=pltpu.VMEM)] * count


def band_gram(w_rows):
    high, low = split(w_rows)
    rank = w_rows.shape[0]
    padded = jnp.concatenate([high, jnp.zeros((2 * LANES - rank, high.shape[1]), BF16)], axis=0)
    padded_low = jnp.concatenate([low, jnp.zeros((2 * LANES - rank, low.shape[1]), BF16)], axis=0)
    both = dot_nt(jnp.concatenate([high, low], axis=0), padded)
    return both[:rank] + (both[rank:] + dot_nt(high, padded_low))


def blur_kernel(cube_ref, taps_x_hbm, taps_y_hbm, w_hbm, xh_ref, xl_ref, keep_ref, give_ref,
                taps_x_ref, taps_y_ref, w_ref, sems, work_ref, kx_ref, ky_ref):
    step = pl.program_id(0)
    taps = taps_x_ref.shape[0]
    margin = (taps - 1) // 2
    height = cube_ref.shape[1]
    rank = w_ref.shape[0]

    @pl.when(step == 0)
    def _():
        copies = [
            pltpu.make_async_copy(taps_x_hbm, taps_x_ref, sems.at[0]),
            pltpu.make_async_copy(taps_y_hbm, taps_y_ref, sems.at[1]),
            pltpu.make_async_copy(w_hbm, w_ref, sems.at[2]),
        ]
        for copy in copies:
            copy.start()
        for copy in copies:
            copy.wait()
        gram = fold(band_gram(w_ref[...])[:, :rank])
        for side in range(4):
            keep_ref[side, 4 * rank:] = gram
            give_ref[side, 4 * rank:] = gram
        normalized_taps(taps_x_ref, True, work_ref, kx_ref)
        normalized_taps(taps_y_ref, False, work_ref, ky_ref)
        kx_ref[...] = pltpu.roll(kx_ref[...], LANES - margin, 1)
        per_vector = LANES // height
        place = lax.broadcasted_iota(jnp.int32, (LANES, LANES), 0) % per_vector
        values = ky_ref[...]
        placed = values
        for k in range(1, per_vector):
            placed = jnp.where(place == k, pltpu.roll(values, k * height, 1), placed)
        ky_ref[...] = placed

    halves = []
    for half in range(GROUP // 8):
        done = []
        for plane in range(8 * half, 8 * half + 8):
            row = kx_ref[pl.ds(step * GROUP + plane, 1), :]
            table_high, table_low = column_table(row, margin)
            high, low = split(cube_ref[plane])
            both = dot(jnp.concatenate([high, low], axis=0), table_high)
            done.append(both[:height] + (both[height:] + dot(high, table_low)))
        high, low = split(jnp.concatenate(done, axis=0))
        rows = ky_ref[pl.ds(pl.multiple_of(step * GROUP + 8 * half, 8), 8), :]
        table_high, table_low = row_table(rows, margin, height)
        result = dot(table_high, high) + (dot(table_low, high) + dot(table_high, low))
        halves.append(result.reshape(height, 8, result.shape[1]))
    high, low = split(jnp.concatenate(halves, axis=1))
    planes_here = pl.ds(pl.multiple_of(step * GROUP, GROUP), GROUP)
    xh_ref[:, planes_here, :] = high
    xl_ref[:, planes_here, :] = low

    @pl.when(step == pl.num_programs(0) - 1)
    def _():
        planes = xh_ref.shape[1]
        band = w_ref.shape[1]
        me_sp = lax.axis_index("sp")
        me_bd = lax.axis_index("bd")
        tall = height // lax.axis_size("bd")
        wide = 2 * LANES // lax.axis_size("sp")
        shift = lax.rem(band - me_sp * planes, band)
        w_high, w_low = split(pltpu.roll(w_ref[...], shift, 1)[:, :planes])
        w_both = jnp.concatenate([w_high, w_low], axis=0)
        for rel, part_ref in ((1, give_ref), (0, keep_ref)):
            for row_side in range(2):
                first_row = (2 * row_side + lax.bitwise_xor(me_bd % 2, rel)) * tall
                sums = []
                for row in range(tall):
                    both = dot(w_both, xh_ref[first_row + row])
                    sums.append(both[:rank] + (both[rank:] + dot(w_high, xl_ref[first_row + row])))
                for column in range(2):
                    quarters = [
                        exchange_blocks(
                            [value[:, column * LANES:(column + 1) * LANES] for value in sums[first:first + 4]], wide)
                        for first in (0, 4)]
                    for k in range(4):
                        owner = column * 4 + k
                        first = (owner // 2) * rank
                        part_ref[2 * row_side + owner % 2, first:first + rank] = jnp.concatenate(
                            [quarters[0][k], quarters[1][k]], axis=1)


def blur_call(cube, taps_x, taps_y, w_rows):
    planes, height, length = cube.shape
    rank = w_rows.shape[0]
    part = jax.ShapeDtypeStruct((4, 4 * rank + FOLDED, 2 * LANES), F32)
    image = (height, planes, length)
    whole = lambda shape: pl.BlockSpec(shape, lambda i: (0,) * len(shape))
    return pl.pallas_call(
        blur_kernel,
        grid=(planes // GROUP,),
        out_shape=[jax.ShapeDtypeStruct(image, BF16)] * 2 + [part, part],
        in_specs=[pl.BlockSpec((GROUP, height, length), lambda i: (i, 0, 0))]
        + [pl.BlockSpec(memory_space=pltpu.HBM)] * 3,
        out_specs=[whole(image)] * 2 + [whole(part.shape)] * 2,
        scratch_shapes=[pltpu.VMEM(value.shape, F32) for value in (taps_x, taps_y, w_rows)]
        + [pltpu.SemaphoreType.DMA((3,))] + [pltpu.VMEM((LANES, LANES), F32)] * 3,
        compiler_params=pltpu.CompilerParams(
            dimension_semantics=("arbitrary",), vmem_limit_bytes=VMEM_LIMIT),
    )(cube, taps_x, taps_y, w_rows)


def ratio_kernel(parts_ref, h_ref, out_ref):
    tall = h_ref.shape[0] // lax.axis_size("bd")
    first = pl.multiple_of(lax.axis_index("bd") * tall, tall)
    here = h_ref[pl.ds(first, tall)]
    here = jnp.transpose(here.reshape(-1, here.shape[2]))
    rows = parts_ref.shape[1]
    folded = [parts_ref[k, rows - FOLDED:rows] for k in range(4)]
    gram = 0.5 * unfold((folded[0] + folded[1]) + (folded[2] + folded[3]), here.shape[0])
    out_ref[...] = here / dot_exact(gram, here)


def ratio_call(parts, h_columns):
    return pl.pallas_call(
        ratio_kernel,
        out_shape=jax.ShapeDtypeStruct((h_columns.shape[2], 2 * LANES), F32),
        in_specs=in_vmem(2),
        compiler_params=pltpu.CompilerParams(vmem_limit_bytes=VMEM_LIMIT),
    )(parts, h_columns)


def update_w_kernel(xh_ref, xl_ref, w_ref, all_ref, w_out, h_out):
    height, planes, _ = xh_ref.shape
    rank, band = w_ref.shape
    me_sp = lax.axis_index("sp")
    bands = lax.axis_size("bd")
    tall = height // bands
    wide = 2 * LANES // lax.axis_size("sp")
    numer = jnp.zeros((rank, planes), F32)
    gram = jnp.zeros((rank, rank), F32)
    for part in range(bands):
        rows = [[None, None] for _ in range(tall)]
        for column in range(2):
            for quarter in range(2):
                vectors = exchange_blocks(
                    [all_ref[(column * 4 + k) * bands + part][:, quarter * LANES:(quarter + 1) * LANES]
                     for k in range(4)], wide)
                for k in range(4):
                    rows[4 * quarter + k][column] = vectors[k]
        for row in range(tall):
            high, low = split(jnp.concatenate(rows[row], axis=1))
            both = jnp.concatenate([high, low], axis=0)
            product = dot_nt(both, xh_ref[part * tall + row])
            numer = numer + (product[:rank] + (product[rank:] + dot_nt(high, xl_ref[part * tall + row])))
            product = dot_nt(both, high)
            gram = gram + (product[:rank] + (product[rank:] + dot_nt(high, low)))
        mine = jnp.transpose(all_ref[me_sp * bands + part])
        h_out[part * tall:(part + 1) * tall] = mine.reshape(tall, wide, rank)
    shift = lax.rem(band - me_sp * planes, band)
    w_here = pltpu.roll(w_ref[...], shift, 1)[:, :planes]
    w_here = w_here * numer / dot_exact(gram, w_here)
    for owner in range(w_out.shape[0]):
        w_out[owner] = w_here


def update_w_call(x_high, x_low, w_rows, gathered):
    height, planes, length = x_high.shape
    rank = w_rows.shape[0]
    pieces = lax.axis_size("sp")
    return pl.pallas_call(
        update_w_kernel,
        out_shape=[
            jax.ShapeDtypeStruct((pieces, rank, planes), F32),
            jax.ShapeDtypeStruct((height, length // pieces, rank), F32),
        ],
        in_specs=in_vmem(4),
        compiler_params=pltpu.CompilerParams(vmem_limit_bytes=VMEM_LIMIT),
    )(x_high, x_low, w_rows, gathered)


def join_w_kernel(parts_ref, out_ref):
    planes = parts_ref.shape[2]
    for owner in range(parts_ref.shape[0]):
        out_ref[:, owner * planes:(owner + 1) * planes] = parts_ref[owner]


def join_w_call(parts):
    pieces, rank, planes = parts.shape
    return pl.pallas_call(
        join_w_kernel,
        out_shape=jax.ShapeDtypeStruct((rank, planes * pieces), F32),
        in_specs=in_vmem(1),
        compiler_params=pltpu.CompilerParams(vmem_limit_bytes=VMEM_LIMIT),
    )(parts)


def send(value, mask_sp, mask_bd):
    bands = lax.axis_size("bd")
    pieces = lax.axis_size("sp")
    pairs = []
    for s in range(pieces):
        for b in range(bands):
            pairs.append((s * bands + b, (s ^ mask_sp) * bands + (b ^ mask_bd)))
    return lax.ppermute(value, ("sp", "bd"), pairs)


def exchange(value, square):
    pieces, bands = lax.axis_size("sp"), lax.axis_size("bd")
    if square:
        groups = [[(2 * z + s) * bands + 2 * b + core for b in range(2) for s in range(2)]
                  for z in range(pieces // 2) for core in range(2)]
    else:
        groups = [[(2 * z + s) * bands + b for z in range(pieces // 2)] for s in range(2) for b in range(bands)]
    return lax.all_to_all(value, ("sp", "bd"), 0, 0, axis_index_groups=groups, tiled=True)


def local(cube, taps_x, taps_y, factor_w, factor_h):
    w_rows = jnp.transpose(factor_w[0])
    taps_x = jnp.transpose(taps_x, (2, 0, 1))
    taps_y = jnp.transpose(taps_y, (2, 0, 1))
    h_columns = jnp.transpose(factor_h, (1, 2, 0))
    rank = w_rows.shape[0]
    x_high, x_low, keep, give = blur_call(cube[0], taps_x, taps_y, w_rows)
    square = exchange(keep + send(give, 0, 1), True)
    line = jnp.sum(square[:, :4 * rank], axis=0).reshape(4, rank, 2 * LANES)
    numer = jnp.sum(exchange(line, False), axis=0)
    h_piece = ratio_call(square, h_columns) * numer
    gathered = lax.all_gather(h_piece, ("sp", "bd"))
    w_piece, h_next = update_w_call(x_high, x_low, w_rows, gathered)
    w_next = join_w_call(lax.all_to_all(w_piece, "sp", 0, 0, tiled=True))
    return jnp.transpose(w_next)[None], jnp.transpose(h_next, (2, 0, 1))


def normalized(kernel):
    return kernel / jnp.sum(kernel, axis=-1, keepdims=True)


def band_weights(kernel, size_in, size_out, offset):
    tap_count = kernel.shape[-1]
    in_index = lax.broadcasted_iota(jnp.int32, (size_in, size_out, tap_count), 0)
    out_index = lax.broadcasted_iota(jnp.int32, (size_in, size_out, tap_count), 1)
    tap_index = lax.broadcasted_iota(jnp.int32, (size_in, size_out, tap_count), 2)
    select = (tap_index == in_index - out_index + offset).astype(jnp.float32)
    return jnp.einsum("pk,iok->pio", kernel, select, precision=lax.Precision.HIGHEST)


def blur_rows(planes, kernel_y):
    margin = (kernel_y.shape[-1] - 1) // 2
    height = planes.shape[1]
    band_table = band_weights(kernel_y, height, height, margin)
    return jnp.einsum("piz,pio->poz", planes, band_table, precision=lax.Precision.HIGHEST)


def blur_columns(planes, kernel_x):
    margin = (kernel_x.shape[-1] - 1) // 2
    count, height, length = planes.shape
    blocks = planes.reshape(count, height, length // 128, 128)
    empty = jnp.zeros((count, height, 1, 128), jnp.float32)
    left_block = jnp.concatenate([empty, blocks[:, :, :-1]], axis=2)
    right_block = jnp.concatenate([blocks[:, :, 1:], empty], axis=2)
    window = jnp.concatenate([left_block, blocks, right_block], axis=3)
    band_table = band_weights(kernel_x, 384, 128, margin - 128)
    result = jnp.einsum("pybi,pio->pybo", window, band_table, precision=lax.Precision.HIGHEST)
    return result.reshape(count, height, length)


def local_any(cube, taps_x, taps_y, factor_w, factor_h):
    highest = lax.Precision.HIGHEST
    kernel_x = normalized(taps_x[0])
    kernel_y = normalized(taps_y[0])
    rows_done = blur_rows(cube[0], kernel_y)
    w_band = factor_w[0]
    blurred = blur_columns(rows_done, kernel_x)[None]
    moved = lax.all_to_all(blurred, "sp", split_axis=3, concat_axis=1, tiled=True)
    numer_part = jnp.einsum("lr,plyx->pryx", w_band, moved, precision=highest)
    gram_part = jnp.dot(w_band.T, w_band, precision=highest)
    numer_h, gram_w = lax.psum((numer_part[0], gram_part), "bd")
    h_next = factor_h * numer_h / jnp.einsum("rq,qyx->ryx", gram_w, factor_h, precision=highest)
    x_band = moved[0]
    gram_h_part = jnp.einsum("ryx,qyx->rq", h_next, h_next, precision=highest)
    numer_w_part = jnp.einsum("lyx,ryx->lr", x_band, h_next, precision=highest)
    numer_w, gram_h = lax.psum((numer_w_part, gram_h_part), "sp")
    w_next = w_band * numer_w / jnp.dot(w_band, gram_h, precision=highest)
    return (w_next[None], h_next)


def solution(mesh):
    in_specs = (
        P("bd", "sp", None, None),
        P("bd", "sp", None),
        P("bd", "sp", None),
        P("bd", None, None),
        P(None, None, "sp"),
    )
    out_specs = (P("bd", None, None), P(None, None, "sp"))

    def body(cube, *rest):
        suits = lax.axis_size("sp") == 8 and lax.axis_size("bd") == 4 and cube.shape[1] % GROUP == 0
        return (local if suits else local_any)(cube, *rest)

    return jax.shard_map(body, mesh=mesh, in_specs=in_specs, out_specs=out_specs, check_vma=False)
```

```python
import functools

import jax
import jax.numpy as jnp
from jax import lax
from jax.experimental import pallas as pl
from jax.experimental.pallas import tpu as pltpu
from jax.sharding import PartitionSpec as P

F32 = jnp.float32
BF16 = jnp.bfloat16
LANES = 128
GROUP = 16
PIECES = 16
FOLDED = 24
VMEM_LIMIT = 48 * 1024 * 1024


def split(value):
    high = value.astype(BF16)
    low = (value - high.astype(F32)).astype(BF16)
    return high, low


def dot(left, right):
    return lax.dot_general(left, right, (((1,), (0,)), ((), ())), preferred_element_type=F32)


def dot_nt(left, right):
    return lax.dot_general(left, right, (((1,), (1,)), ((), ())), preferred_element_type=F32)


def dot_exact(left, right):
    return lax.dot_general(
        left, right, (((1,), (0,)), ((), ())),
        precision=lax.Precision.HIGHEST, preferred_element_type=F32,
    )


def exchange_blocks(rows, block):
    lane = lax.broadcasted_iota(jnp.int32, rows[0].shape, 1)
    first_half = lane < 2 * block
    even = (lane // block) % 2 == 0
    v0, v1, v2, v3 = rows
    u0 = jnp.where(first_half, v0, pltpu.roll(v2, 2 * block, 1))
    u2 = jnp.where(first_half, pltpu.roll(v0, 2 * block, 1), v2)
    u1 = jnp.where(first_half, v1, pltpu.roll(v3, 2 * block, 1))
    u3 = jnp.where(first_half, pltpu.roll(v1, 2 * block, 1), v3)
    w0 = jnp.where(even, u0, pltpu.roll(u1, block, 1))
    w1 = jnp.where(even, pltpu.roll(u0, 3 * block, 1), u1)
    w2 = jnp.where(even, u2, pltpu.roll(u3, block, 1))
    w3 = jnp.where(even, pltpu.roll(u2, 3 * block, 1), u3)
    return w0, w1, w2, w3


def normalized_taps(taps_ref, reverse, work_ref, out_ref):
    taps = taps_ref.shape[0]
    planes = taps_ref.shape[2]
    work_ref[...] = jnp.zeros_like(work_ref)
    for tap in range(taps):
        row = taps - 1 - tap if reverse else tap
        work_ref[row:row + 1, 0:planes] = taps_ref[tap]
    values = work_ref[...]
    total = jnp.sum(values, axis=0, keepdims=True)
    total = jnp.where(total == 0.0, 1.0, total)
    out_ref[...] = jnp.transpose(values / total)


def blur_plane(plane, row, taps):
    margin = (taps - 1) // 2
    step = LANES - 2 * margin
    table = pltpu.roll(jnp.broadcast_to(row, (LANES, LANES)), 0, 1, stride=1, stride_axis=0)
    table = jnp.concatenate(split(table), axis=1)
    left, right = plane[:, :LANES], plane[:, LANES:]
    lane = lax.broadcasted_iota(jnp.int32, left.shape, 1)
    zero = jnp.zeros_like(left)
    windows = [
        jnp.where(lane >= margin, pltpu.roll(left, margin, 1), zero),
        jnp.where(lane < 3 * margin, pltpu.roll(left, 3 * margin, 1), pltpu.roll(right, 3 * margin, 1)),
        jnp.where(lane < 5 * margin, pltpu.roll(right, 5 * margin, 1), zero),
    ]
    high, low = split(jnp.concatenate(windows, axis=0))
    product = dot(jnp.concatenate([high, low], axis=0), table)
    rows = high.shape[0]
    blocks = product[:rows, :LANES] + (product[:rows, LANES:] + product[rows:, :LANES])
    height = plane.shape[0]
    first, second, third = [blocks[k * height:(k + 1) * height] for k in range(3)]
    second = pltpu.roll(second, step, 1)
    third = pltpu.roll(third, 2 * step - LANES, 1)
    return jnp.concatenate(
        [jnp.where(lane < step, first, second), jnp.where(lane < 2 * step - LANES, second, third)], axis=1)


def row_table(base, margin, height):
    high = base.astype(BF16).astype(F32)
    low = base - high
    plane = lax.broadcasted_iota(jnp.int32, (8, LANES), 0)
    lane = lax.broadcasted_iota(jnp.int32, (8, LANES), 1)
    per_vector = LANES // height
    own = lane // height == plane % per_vector
    masks = [own & (plane // per_vector == part) for part in range(8 * height // LANES)]

    def table(part):
        strips = []
        for row in range(height):
            rolled = pltpu.roll(part, (row - margin) % LANES, 1)
            strips.append(jnp.concatenate([jnp.where(mask, rolled, 0.0) for mask in masks], axis=1))
        return jnp.concatenate(strips, axis=0).astype(BF16)

    return table(high), table(low)


def fold(square):
    side = square.shape[0]
    rest = jnp.zeros((8, LANES - 2 * side), F32)
    return jnp.concatenate(
        [jnp.concatenate([square[first:first + 8], square[first + 8:first + 16], rest], axis=1)
         for first in range(0, side, 16)], axis=0)


def unfold(folded, side):
    blocks = []
    for first in range(0, folded.shape[0], 8):
        blocks += [folded[first:first + 8, :side], folded[first:first + 8, side:2 * side]]
    return jnp.concatenate(blocks, axis=0)


def in_vmem(count):
    return [pl.BlockSpec(memory_space=pltpu.VMEM)] * count


def band_gram(w_rows):
    high, low = split(w_rows)
    rank = w_rows.shape[0]
    padded = jnp.concatenate([high, jnp.zeros((2 * LANES - rank, high.shape[1]), BF16)], axis=0)
    padded_low = jnp.concatenate([low, jnp.zeros((2 * LANES - rank, low.shape[1]), BF16)], axis=0)
    both = dot_nt(jnp.concatenate([high, low], axis=0), padded)
    return both[:rank] + (both[rank:] + dot_nt(high, padded_low))


def blur_kernel(cube_ref, taps_x_hbm, taps_y_hbm, w_hbm, xh_ref, xl_ref, keep_0, give_0, keep_1, give_1,
                taps_x_ref, taps_y_ref, w_ref, sems, work_ref, kx_ref, ky_ref):
    step = pl.program_id(0)
    taps = taps_x_ref.shape[0]
    margin = (taps - 1) // 2
    height = cube_ref.shape[1]
    rank = w_ref.shape[0]

    @pl.when(step == 0)
    def _():
        copies = [
            pltpu.make_async_copy(taps_x_hbm, taps_x_ref, sems.at[0]),
            pltpu.make_async_copy(taps_y_hbm, taps_y_ref, sems.at[1]),
            pltpu.make_async_copy(w_hbm, w_ref, sems.at[2]),
        ]
        for copy in copies:
            copy.start()
        for copy in copies:
            copy.wait()
        gram = fold(band_gram(w_ref[...])[:, :rank])
        keep_0[PIECES * rank:] = gram
        give_0[PIECES * rank:] = gram
        normalized_taps(taps_x_ref, True, work_ref, kx_ref)
        normalized_taps(taps_y_ref, False, work_ref, ky_ref)
        kx_ref[...] = pltpu.roll(kx_ref[...], LANES - 2 * margin, 1)
        per_vector = LANES // height
        place = lax.broadcasted_iota(jnp.int32, (LANES, LANES), 0) % per_vector
        values = ky_ref[...]
        placed = values
        for k in range(1, per_vector):
            placed = jnp.where(place == k, pltpu.roll(values, k * height, 1), placed)
        ky_ref[...] = placed

    halves = []
    for half in range(GROUP // 8):
        done = []
        for plane in range(8 * half, 8 * half + 8):
            row = kx_ref[pl.ds(step * GROUP + plane, 1), :]
            done.append(blur_plane(cube_ref[plane], row, taps))
        high, low = split(jnp.concatenate(done, axis=0))
        rows = ky_ref[pl.ds(pl.multiple_of(step * GROUP + 8 * half, 8), 8), :]
        table_high, table_low = row_table(rows, margin, height)
        result = dot(table_high, high) + (dot(table_low, high) + dot(table_high, low))
        halves.append(result.reshape(height, 8, result.shape[1]))
    high, low = split(jnp.concatenate(halves, axis=1))
    planes_here = pl.ds(pl.multiple_of(step * GROUP, GROUP), GROUP)
    xh_ref[:, planes_here, :] = high
    xl_ref[:, planes_here, :] = low

    @pl.when(step == pl.num_programs(0) - 1)
    def _():
        planes = xh_ref.shape[1]
        band = w_ref.shape[1]
        me_sp = lax.axis_index("sp")
        me_bd = lax.axis_index("bd")
        tall = height // lax.axis_size("bd")
        wide = 2 * LANES // lax.axis_size("sp")
        shift = lax.rem(band - me_sp * planes, band)
        w_here = pltpu.roll(w_ref[...], shift, 1)[:, :2 * LANES]
        lane = lax.broadcasted_iota(jnp.int32, w_here.shape, 1)
        w_here = jnp.where(lane < planes, w_here, 0.0)
        w_high = w_here.astype(BF16).astype(F32)
        w_both = jnp.concatenate([w_high + pltpu.roll(w_high, planes, 1), w_here - w_high], axis=0)
        w_both = w_both.astype(BF16)[:, :2 * planes]
        for chain in range(2):
            for rel_bd in (1, 3, 0, 2):
                first_row = lax.bitwise_xor(me_bd, rel_bd) * tall + 4 * chain
                sums = []
                for row in range(4):
                    image = jnp.concatenate([xh_ref[first_row + row], xl_ref[first_row + row]], axis=0)
                    both = dot(w_both, image)
                    sums.append(both[:rank] + both[rank:])
                refs = ((keep_0, give_0), (keep_1, give_1))[chain]
                for column in range(2):
                    pieces = exchange_blocks(
                        [value[:, column * LANES:(column + 1) * LANES] for value in sums], wide)
                    for k in range(4):
                        rel_sp = lax.bitwise_xor(me_sp, column * 4 + k)
                        side = 3 - rel_sp % 2 if rel_bd // 2 else rel_sp % 2
                        first = pl.multiple_of((side * 4 + rel_sp // 2) * rank, 8)
                        refs[rel_bd % 2][pl.ds(first, rank)] = pieces[k]


def blur_call(cube, taps_x, taps_y, w_rows):
    planes, height, length = cube.shape
    rank = w_rows.shape[0]
    first = jax.ShapeDtypeStruct((PIECES * rank + FOLDED, LANES), F32)
    second = jax.ShapeDtypeStruct((PIECES * rank, LANES), F32)
    image = (height, planes, length)
    whole = lambda shape: pl.BlockSpec(shape, lambda i: (0,) * len(shape))
    return pl.pallas_call(
        blur_kernel,
        grid=(planes // GROUP,),
        out_shape=[jax.ShapeDtypeStruct(image, BF16)] * 2 + [first, first, second, second],
        in_specs=[pl.BlockSpec((GROUP, height, length), lambda i: (i, 0, 0))]
        + [pl.BlockSpec(memory_space=pltpu.HBM)] * 3,
        out_specs=[whole(image)] * 2 + [whole(first.shape)] * 2 + [whole(second.shape)] * 2,
        scratch_shapes=[pltpu.VMEM(value.shape, F32) for value in (taps_x, taps_y, w_rows)]
        + [pltpu.SemaphoreType.DMA((3,))] + [pltpu.VMEM((LANES, LANES), F32)] * 3,
        compiler_params=pltpu.CompilerParams(
            dimension_semantics=("arbitrary",), vmem_limit_bytes=VMEM_LIMIT),
    )(cube, taps_x, taps_y, w_rows)


def ratio_kernel(mine_ref, other_ref, h_ref, out_0, out_1):
    tall = h_ref.shape[0] // lax.axis_size("bd")
    first = pl.multiple_of(lax.axis_index("bd") * tall, tall)
    here = h_ref[pl.ds(first, tall)]
    here = jnp.transpose(here.reshape(-1, here.shape[2]))
    rows = mine_ref.shape[0]
    gram = unfold(mine_ref[rows - FOLDED:rows] + other_ref[rows - FOLDED:rows], here.shape[0])
    ratio = here / dot_exact(gram, here)
    out_0[...] = ratio[:, :LANES]
    out_1[...] = ratio[:, LANES:]


def ratio_call(mine, other, h_columns):
    piece = jax.ShapeDtypeStruct((h_columns.shape[2], LANES), F32)
    return pl.pallas_call(
        ratio_kernel,
        out_shape=[piece, piece],
        in_specs=in_vmem(3),
        compiler_params=pltpu.CompilerParams(vmem_limit_bytes=VMEM_LIMIT),
    )(mine, other, h_columns)


def accumulate(xh_ref, xl_ref, part_refs, all_ref, h_out, chain, total):
    height, planes, _ = xh_ref.shape
    rank = all_ref.shape[1]
    me_sp = lax.axis_index("sp")
    me_bd = lax.axis_index("bd")
    bands = lax.axis_size("bd")
    pieces = lax.axis_size("sp")
    tall = height // bands
    wide = 2 * LANES // pieces
    for slot, part_ref in enumerate(part_refs):
        rel_bd = slot // 4 + 2 * ((slot // 2) % 2)
        for inner in range(4):
            rel_sp = slot % 2 + 2 * inner
            owner = lax.bitwise_xor(me_bd, rel_bd) * pieces + lax.bitwise_xor(me_sp, rel_sp)
            all_ref[owner] = part_ref[inner]
    for part in range(bands):
        first_row = part * tall + 4 * chain
        halves = [
            exchange_blocks([all_ref[part * pieces + column * 4 + k] for k in range(4)], wide)
            for column in range(2)]
        rows = jnp.concatenate([halves[column][row] for row in range(4) for column in range(2)], axis=1)
        high, low = split(rows)
        here = jnp.concatenate([high, low], axis=0)
        image = [
            jnp.concatenate([ref[first_row + row] for row in range(4)], axis=1) for ref in (xh_ref, xl_ref)]
        total = total + dot_nt(jnp.concatenate(image + [here], axis=0), here)
        mine = jnp.transpose(all_ref[part * pieces + me_sp])
        h_out[first_row:first_row + 4] = mine.reshape(4, wide, rank)
    return total


def first_kernel(xh_ref, xl_ref, *rest):
    part_refs = rest[:8]
    total_out, h_out, all_ref = rest[8:]
    total_out[...] = accumulate(
        xh_ref, xl_ref, part_refs, all_ref, h_out, 0, jnp.zeros(total_out.shape, F32))
    tall = xh_ref.shape[0] // lax.axis_size("bd")
    for part in range(lax.axis_size("bd")):
        h_out[part * tall + 4:(part + 1) * tall] = jnp.zeros((tall - 4,) + h_out.shape[1:], F32)


def first_call(x_high, x_low, parts):
    height, planes, length = x_high.shape
    rank = parts[0].shape[1]
    return pl.pallas_call(
        first_kernel,
        out_shape=[
            jax.ShapeDtypeStruct((2 * (planes + rank), 2 * rank), F32),
            jax.ShapeDtypeStruct((height, length // lax.axis_size("sp"), rank), F32),
        ],
        in_specs=in_vmem(2 + len(parts)),
        scratch_shapes=[pltpu.VMEM((32,) + parts[0].shape[1:], F32)],
        compiler_params=pltpu.CompilerParams(vmem_limit_bytes=VMEM_LIMIT),
    )(x_high, x_low, *parts)


def second_kernel(xh_ref, xl_ref, w_ref, total_ref, h_ref, *rest):
    part_refs = rest[:8]
    w_out, h_out, all_ref = rest[8:]
    planes = xh_ref.shape[1]
    rank, band = w_ref.shape
    me_sp = lax.axis_index("sp")
    h_out[...] = h_ref[...]
    total = accumulate(xh_ref, xl_ref, part_refs, all_ref, h_out, 1, total_ref[...])
    numer = total[:planes, :rank] + (total[:planes, rank:] + total[planes:2 * planes, :rank])
    gram = total[2 * planes:]
    gram = gram[:rank, :rank] + (gram[:rank, rank:] + gram[rank:, :rank])
    shift = lax.rem(band - me_sp * planes, band)
    w_here = pltpu.roll(w_ref[...], shift, 1)[:, :planes]
    w_out[...] = w_here * jnp.transpose(numer) / dot_exact(gram, w_here)


def second_call(x_high, x_low, w_rows, total, h_half, parts):
    planes, rank = x_high.shape[1], w_rows.shape[0]
    return pl.pallas_call(
        second_kernel,
        out_shape=[
            jax.ShapeDtypeStruct((rank, planes), F32),
            jax.ShapeDtypeStruct(h_half.shape, F32),
        ],
        in_specs=in_vmem(5 + len(parts)),
        scratch_shapes=[pltpu.VMEM((32,) + parts[0].shape[1:], F32)],
        compiler_params=pltpu.CompilerParams(vmem_limit_bytes=VMEM_LIMIT),
    )(x_high, x_low, w_rows, total, h_half, *parts)


def gather_w_kernel(*refs):
    part_refs = refs[:-2]
    out_ref, all_ref = refs[-2:]
    planes = out_ref.shape[1] // 8
    me_sp = lax.axis_index("sp")
    rel = 0
    for part_ref in part_refs:
        for inner in range(part_ref.shape[0]):
            all_ref[lax.bitwise_xor(me_sp, RING[rel]), :, 0:planes] = part_ref[inner]
            rel += 1
    for owner in range(8):
        out_ref[:, owner * planes:(owner + 1) * planes] = all_ref[owner][:, :planes]


RING = (0, 1, 2, 3, 4, 5, 6, 7)


def gather_w_call(parts):
    _, rank, planes = parts[0].shape
    return pl.pallas_call(
        gather_w_kernel,
        out_shape=jax.ShapeDtypeStruct((rank, planes * 8), F32),
        in_specs=in_vmem(len(parts)),
        scratch_shapes=[pltpu.VMEM((8, rank, LANES), F32)],
        compiler_params=pltpu.CompilerParams(vmem_limit_bytes=VMEM_LIMIT),
    )(*parts)


def send(value, mask_sp, mask_bd):
    bands = lax.axis_size("bd")
    pieces = lax.axis_size("sp")
    pairs = []
    for s in range(pieces):
        for b in range(bands):
            pairs.append((s * bands + b, (s ^ mask_sp) * bands + (b ^ mask_bd)))
    return lax.ppermute(value, ("sp", "bd"), pairs)


def around(values):
    return [send(values[k], k % 2, 2 * (k // 2)) for k in range(1, 4)]


def local(cube, taps_x, taps_y, factor_w, factor_h):
    w_rows = jnp.transpose(factor_w[0])
    taps_x = jnp.transpose(taps_x, (2, 0, 1))
    taps_y = jnp.transpose(taps_y, (2, 0, 1))
    h_columns = jnp.transpose(factor_h, (1, 2, 0))
    rank = w_rows.shape[0]
    x_high, x_low, keep_0, give_0, keep_1, give_1 = blur_call(cube[0], taps_x, taps_y, w_rows)
    chains = []
    for keep, give in ((keep_0, give_0), (keep_1, give_1)):
        taken = send(give, 0, 1)
        bounds = [place * 4 * rank for place in (0, 1, 3, 2)]
        sides = []
        for first in bounds:
            last = keep.shape[0] if first == max(bounds) else first + 4 * rank
            sides.append(keep[first:last] + taken[first:last])
        chains.append((sides, around(sides)))
    ratios = ratio_call(chains[0][0][2], chains[0][1][1], h_columns)
    rounds = []
    for (sides, others), ratio in zip(chains, ratios):
        line = []
        for k in range(4):
            part = slice(k * rank, (k + 1) * rank)
            line.append((sides[0][part] + others[0][part]) + (others[1][part] + others[2][part]))
        line = [line[0]] + [send(line[k], 2 * k, 0) for k in range(1, 4)]
        h_piece = ratio * ((line[0] + line[1]) + (line[2] + line[3]))
        h_line = jnp.stack([h_piece] + [send(h_piece, 2 * k, 0) for k in range(1, 4)])
        parts = [h_line] + around([h_line] * 4)
        rounds.append(parts + [send(value, 0, 1) for value in parts])
    total, h_half = first_call(x_high, x_low, rounds[0])
    w_piece, h_next = second_call(x_high, x_low, w_rows, total, h_half, rounds[1])
    w_pair = jnp.stack([w_piece, send(w_piece, 1, 0)])
    w_next = gather_w_call([w_pair] + [send(w_pair, 2 * k, 0) for k in range(1, 4)])
    return jnp.transpose(w_next)[None], jnp.transpose(h_next, (2, 0, 1))


def normalized(kernel):
    return kernel / jnp.sum(kernel, axis=-1, keepdims=True)


def band_weights(kernel, size_in, size_out, offset):
    tap_count = kernel.shape[-1]
    in_index = lax.broadcasted_iota(jnp.int32, (size_in, size_out, tap_count), 0)
    out_index = lax.broadcasted_iota(jnp.int32, (size_in, size_out, tap_count), 1)
    tap_index = lax.broadcasted_iota(jnp.int32, (size_in, size_out, tap_count), 2)
    select = (tap_index == in_index - out_index + offset).astype(jnp.float32)
    return jnp.einsum("pk,iok->pio", kernel, select, precision=lax.Precision.HIGHEST)


def blur_rows(planes, kernel_y):
    margin = (kernel_y.shape[-1] - 1) // 2
    height = planes.shape[1]
    band_table = band_weights(kernel_y, height, height, margin)
    return jnp.einsum("piz,pio->poz", planes, band_table, precision=lax.Precision.HIGHEST)


def blur_columns(planes, kernel_x):
    margin = (kernel_x.shape[-1] - 1) // 2
    count, height, length = planes.shape
    blocks = planes.reshape(count, height, length // 128, 128)
    empty = jnp.zeros((count, height, 1, 128), jnp.float32)
    left_block = jnp.concatenate([empty, blocks[:, :, :-1]], axis=2)
    right_block = jnp.concatenate([blocks[:, :, 1:], empty], axis=2)
    window = jnp.concatenate([left_block, blocks, right_block], axis=3)
    band_table = band_weights(kernel_x, 384, 128, margin - 128)
    result = jnp.einsum("pybi,pio->pybo", window, band_table, precision=lax.Precision.HIGHEST)
    return result.reshape(count, height, length)


def local_any(cube, taps_x, taps_y, factor_w, factor_h):
    highest = lax.Precision.HIGHEST
    kernel_x = normalized(taps_x[0])
    kernel_y = normalized(taps_y[0])
    rows_done = blur_rows(cube[0], kernel_y)
    w_band = factor_w[0]
    blurred = blur_columns(rows_done, kernel_x)[None]
    moved = lax.all_to_all(blurred, "sp", split_axis=3, concat_axis=1, tiled=True)
    numer_part = jnp.einsum("lr,plyx->pryx", w_band, moved, precision=highest)
    gram_part = jnp.dot(w_band.T, w_band, precision=highest)
    numer_h, gram_w = lax.psum((numer_part[0], gram_part), "bd")
    h_next = factor_h * numer_h / jnp.einsum("rq,qyx->ryx", gram_w, factor_h, precision=highest)
    x_band = moved[0]
    gram_h_part = jnp.einsum("ryx,qyx->rq", h_next, h_next, precision=highest)
    numer_w_part = jnp.einsum("lyx,ryx->lr", x_band, h_next, precision=highest)
    numer_w, gram_h = lax.psum((numer_w_part, gram_h_part), "sp")
    w_next = w_band * numer_w / jnp.dot(w_band, gram_h, precision=highest)
    return (w_next[None], h_next)


def solution(mesh):
    in_specs = (
        P("bd", "sp", None, None),
        P("bd", "sp", None),
        P("bd", "sp", None),
        P("bd", None, None),
        P(None, None, "sp"),
    )
    out_specs = (P("bd", None, None), P(None, None, "sp"))

    def body(cube, *rest):
        suits = lax.axis_size("sp") == 8 and lax.axis_size("bd") == 4 and cube.shape[1] % GROUP == 0
        return (local if suits else local_any)(cube, *rest)

    return jax.shard_map(body, mesh=mesh, in_specs=in_specs, out_specs=out_specs, check_vma=False)
```

```python
import functools

import jax
import jax.numpy as jnp
from jax import lax
from jax.experimental import pallas as pl
from jax.experimental.pallas import tpu as pltpu
from jax.sharding import PartitionSpec as P

F32 = jnp.float32
BF16 = jnp.bfloat16
LANES = 128
GROUP = 16
PIECES = 16
FOLDED = 24
VMEM_LIMIT = 48 * 1024 * 1024


def split(value):
    high = value.astype(BF16)
    low = (value - high.astype(F32)).astype(BF16)
    return high, low


def dot(left, right):
    return lax.dot_general(left, right, (((1,), (0,)), ((), ())), preferred_element_type=F32)


def dot_nt(left, right):
    return lax.dot_general(left, right, (((1,), (1,)), ((), ())), preferred_element_type=F32)


def dot_exact(left, right):
    return lax.dot_general(
        left, right, (((1,), (0,)), ((), ())),
        precision=lax.Precision.HIGHEST, preferred_element_type=F32,
    )


def exchange_blocks(rows, block):
    lane = lax.broadcasted_iota(jnp.int32, rows[0].shape, 1)
    first_half = lane < 2 * block
    even = (lane // block) % 2 == 0
    v0, v1, v2, v3 = rows
    u0 = jnp.where(first_half, v0, pltpu.roll(v2, 2 * block, 1))
    u2 = jnp.where(first_half, pltpu.roll(v0, 2 * block, 1), v2)
    u1 = jnp.where(first_half, v1, pltpu.roll(v3, 2 * block, 1))
    u3 = jnp.where(first_half, pltpu.roll(v1, 2 * block, 1), v3)
    w0 = jnp.where(even, u0, pltpu.roll(u1, block, 1))
    w1 = jnp.where(even, pltpu.roll(u0, 3 * block, 1), u1)
    w2 = jnp.where(even, u2, pltpu.roll(u3, block, 1))
    w3 = jnp.where(even, pltpu.roll(u2, 3 * block, 1), u3)
    return w0, w1, w2, w3


def normalized_taps(taps_ref, reverse, work_ref, out_ref):
    taps = taps_ref.shape[0]
    planes = taps_ref.shape[2]
    work_ref[...] = jnp.zeros_like(work_ref)
    for tap in range(taps):
        row = taps - 1 - tap if reverse else tap
        work_ref[row:row + 1, 0:planes] = taps_ref[tap]
    values = work_ref[...]
    total = jnp.sum(values, axis=0, keepdims=True)
    total = jnp.where(total == 0.0, 1.0, total)
    out_ref[...] = jnp.transpose(values / total)


def column_table(row, margin):
    table = pltpu.roll(jnp.broadcast_to(row, (LANES, LANES)), 0, 1, stride=1, stride_axis=0)
    high = table.astype(BF16).astype(F32)
    src = lax.broadcasted_iota(jnp.int32, (GROUP, LANES), 0)
    dst = lax.broadcasted_iota(jnp.int32, (GROUP, LANES), 1)
    first, last = slice(0, GROUP), slice(LANES - GROUP, LANES)
    above = dst - src <= LANES // 2
    below = src + LANES - GROUP - dst <= LANES // 2
    empty = jnp.zeros((LANES - 2 * GROUP, LANES), F32)
    main, edge = [], []
    for part in (high, table - high):
        main.append(jnp.concatenate(
            [jnp.where(above, part[first], 0.0), part[GROUP:LANES - GROUP], jnp.where(below, part[last], 0.0)],
            axis=0).astype(BF16))
        edge.append(jnp.concatenate(
            [jnp.where(above, 0.0, part[first]), empty, jnp.where(below, 0.0, part[last])],
            axis=0).astype(BF16))
    return jnp.concatenate([jnp.concatenate(main, axis=1), jnp.concatenate(edge, axis=1)], axis=0)


def blur_plane(plane, row, margin):
    height = plane.shape[0]
    table = column_table(row, margin)
    left, right = plane[:, :LANES], plane[:, LANES:]
    lane = lax.broadcasted_iota(jnp.int32, left.shape, 1)
    main = jnp.concatenate([left, right], axis=0)
    edge = jnp.concatenate(
        [jnp.where(lane < LANES // 2, right, 0.0), jnp.where(lane < LANES // 2, 0.0, left)], axis=0)
    high, low = split(jnp.concatenate([main, edge], axis=1))
    product = dot(jnp.concatenate([high, low], axis=0), table)
    rows = 2 * height
    blocks = product[:rows, :LANES] + (product[:rows, LANES:] + product[rows:, :LANES])
    return jnp.concatenate([blocks[:height], blocks[height:]], axis=1)


def row_table(base, margin, height):
    high = base.astype(BF16).astype(F32)
    low = base - high
    plane = lax.broadcasted_iota(jnp.int32, (8, LANES), 0)
    lane = lax.broadcasted_iota(jnp.int32, (8, LANES), 1)
    per_vector = LANES // height
    own = lane // height == plane % per_vector
    masks = [own & (plane // per_vector == part) for part in range(8 * height // LANES)]

    def table(part):
        strips = []
        for row in range(height):
            rolled = pltpu.roll(part, (row - margin) % LANES, 1)
            strips.append(jnp.concatenate([jnp.where(mask, rolled, 0.0) for mask in masks], axis=1))
        return jnp.concatenate(strips, axis=0).astype(BF16)

    return table(high), table(low)


def fold(square):
    side = square.shape[0]
    rest = jnp.zeros((8, LANES - 2 * side), F32)
    return jnp.concatenate(
        [jnp.concatenate([square[first:first + 8], square[first + 8:first + 16], rest], axis=1)
         for first in range(0, side, 16)], axis=0)


def unfold(folded, side):
    blocks = []
    for first in range(0, folded.shape[0], 8):
        blocks += [folded[first:first + 8, :side], folded[first:first + 8, side:2 * side]]
    return jnp.concatenate(blocks, axis=0)


def in_vmem(count):
    return [pl.BlockSpec(memory_space=pltpu.VMEM)] * count


def band_gram(w_rows):
    high, low = split(w_rows)
    rank = w_rows.shape[0]
    padded = jnp.concatenate([high, jnp.zeros((2 * LANES - rank, high.shape[1]), BF16)], axis=0)
    padded_low = jnp.concatenate([low, jnp.zeros((2 * LANES - rank, low.shape[1]), BF16)], axis=0)
    both = dot_nt(jnp.concatenate([high, low], axis=0), padded)
    return both[:rank] + (both[rank:] + dot_nt(high, padded_low))


def blur_kernel(cube_ref, taps_x_hbm, taps_y_hbm, w_hbm, xh_ref, xl_ref, w_here_ref, keep_0, give_0, keep_1, give_1,
                taps_x_ref, taps_y_ref, w_ref, sems, work_ref, kx_ref, ky_ref):
    step = pl.program_id(0)
    taps = taps_x_ref.shape[0]
    margin = (taps - 1) // 2
    height = cube_ref.shape[1]
    rank = w_ref.shape[0]

    @pl.when(step == 0)
    def _():
        copies = [
            pltpu.make_async_copy(taps_x_hbm, taps_x_ref, sems.at[0]),
            pltpu.make_async_copy(taps_y_hbm, taps_y_ref, sems.at[1]),
            pltpu.make_async_copy(w_hbm, w_ref, sems.at[2]),
        ]
        for copy in copies:
            copy.start()
        for copy in copies:
            copy.wait()
        gram = fold(band_gram(w_ref[...])[:, :rank])
        keep_0[PIECES * rank:] = gram
        give_0[PIECES * rank:] = gram
        normalized_taps(taps_x_ref, True, work_ref, kx_ref)
        normalized_taps(taps_y_ref, False, work_ref, ky_ref)
        kx_ref[...] = pltpu.roll(kx_ref[...], LANES - margin, 1)
        per_vector = LANES // height
        place = lax.broadcasted_iota(jnp.int32, (LANES, LANES), 0) % per_vector
        values = ky_ref[...]
        placed = values
        for k in range(1, per_vector):
            placed = jnp.where(place == k, pltpu.roll(values, k * height, 1), placed)
        ky_ref[...] = placed

    halves = []
    for half in range(GROUP // 8):
        done = []
        for plane in range(8 * half, 8 * half + 8):
            row = kx_ref[pl.ds(step * GROUP + plane, 1), :]
            done.append(blur_plane(cube_ref[plane], row, margin))
        high, low = split(jnp.concatenate(done, axis=0))
        rows = ky_ref[pl.ds(pl.multiple_of(step * GROUP + 8 * half, 8), 8), :]
        table_high, table_low = row_table(rows, margin, height)
        result = dot(table_high, high) + (dot(table_low, high) + dot(table_high, low))
        halves.append(result.reshape(height, 8, result.shape[1]))
    high, low = split(jnp.concatenate(halves, axis=1))
    planes_here = pl.ds(pl.multiple_of(step * GROUP, GROUP), GROUP)
    xh_ref[:, planes_here, :] = high
    xl_ref[:, planes_here, :] = low

    @pl.when(step == pl.num_programs(0) - 1)
    def _():
        planes = xh_ref.shape[1]
        band = w_ref.shape[1]
        me_sp = lax.axis_index("sp")
        me_bd = lax.axis_index("bd")
        tall = height // lax.axis_size("bd")
        wide = 2 * LANES // lax.axis_size("sp")
        shift = lax.rem(band - me_sp * planes, band)
        w_here = pltpu.roll(w_ref[...], shift, 1)[:, :2 * LANES]
        w_here_ref[...] = w_here[:, :planes]
        lane = lax.broadcasted_iota(jnp.int32, w_here.shape, 1)
        w_here = jnp.where(lane < planes, w_here, 0.0)
        w_high = w_here.astype(BF16).astype(F32)
        w_both = jnp.concatenate([w_high + pltpu.roll(w_high, planes, 1), w_here - w_high], axis=0)
        w_both = w_both.astype(BF16)[:, :2 * planes]
        for chain in range(2):
            for rel_bd in (1, 3, 0, 2):
                first_row = lax.bitwise_xor(me_bd, rel_bd) * tall + 4 * chain
                sums = []
                for row in range(4):
                    image = jnp.concatenate([xh_ref[first_row + row], xl_ref[first_row + row]], axis=0)
                    both = dot(w_both, image)
                    sums.append(both[:rank] + both[rank:])
                refs = ((keep_0, give_0), (keep_1, give_1))[chain]
                for column in range(2):
                    pieces = exchange_blocks(
                        [value[:, column * LANES:(column + 1) * LANES] for value in sums], wide)
                    for k in range(4):
                        rel_sp = lax.bitwise_xor(me_sp, column * 4 + k)
                        side = 3 - rel_sp % 2 if rel_bd // 2 else rel_sp % 2
                        first = pl.multiple_of((side * 4 + rel_sp // 2) * rank, 8)
                        refs[rel_bd % 2][pl.ds(first, rank)] = pieces[k]


def blur_call(cube, taps_x, taps_y, w_rows):
    planes, height, length = cube.shape
    rank = w_rows.shape[0]
    first = jax.ShapeDtypeStruct((PIECES * rank + FOLDED, LANES), F32)
    second = jax.ShapeDtypeStruct((PIECES * rank, LANES), F32)
    image = (height, planes, length)
    mine = jax.ShapeDtypeStruct((rank, planes), F32)
    whole = lambda shape: pl.BlockSpec(shape, lambda i: (0,) * len(shape))
    return pl.pallas_call(
        blur_kernel,
        grid=(planes // GROUP,),
        out_shape=[jax.ShapeDtypeStruct(image, BF16)] * 2 + [mine, first, first, second, second],
        in_specs=[pl.BlockSpec((GROUP, height, length), lambda i: (i, 0, 0))]
        + [pl.BlockSpec(memory_space=pltpu.HBM)] * 3,
        out_specs=[whole(image)] * 2 + [whole(mine.shape)] + [whole(first.shape)] * 2 + [whole(second.shape)] * 2,
        scratch_shapes=[pltpu.VMEM(value.shape, F32) for value in (taps_x, taps_y, w_rows)]
        + [pltpu.SemaphoreType.DMA((3,))] + [pltpu.VMEM((LANES, LANES), F32)] * 3,
        compiler_params=pltpu.CompilerParams(
            dimension_semantics=("arbitrary",), vmem_limit_bytes=VMEM_LIMIT),
    )(cube, taps_x, taps_y, w_rows)


def ratio_kernel(mine_ref, other_ref, h_ref, out_ref):
    tall = h_ref.shape[0] // lax.axis_size("bd")
    first = pl.multiple_of(lax.axis_index("bd") * tall, tall)
    here = h_ref[pl.ds(first, tall)]
    here = jnp.transpose(here.reshape(-1, here.shape[2]))
    rows = mine_ref.shape[0]
    gram = unfold(mine_ref[rows - FOLDED:rows] + other_ref[rows - FOLDED:rows], here.shape[0])
    out_ref[...] = here / dot_exact(gram, here)


def ratio_call(mine, other, h_columns):
    piece = jax.ShapeDtypeStruct((h_columns.shape[2], 2 * LANES), F32)
    return pl.pallas_call(
        ratio_kernel,
        out_shape=piece,
        in_specs=in_vmem(3),
        compiler_params=pltpu.CompilerParams(vmem_limit_bytes=VMEM_LIMIT),
    )(mine, other, h_columns)


def accumulate(xh_ref, xl_ref, part_refs, all_ref, h_out, chain, total):
    height, planes, _ = xh_ref.shape
    rank = all_ref.shape[1]
    me_sp = lax.axis_index("sp")
    me_bd = lax.axis_index("bd")
    bands = lax.axis_size("bd")
    pieces = lax.axis_size("sp")
    tall = height // bands
    wide = 2 * LANES // pieces
    for slot, part_ref in enumerate(part_refs):
        rel_bd = slot // 4 + 2 * ((slot // 2) % 2)
        for inner in range(4):
            rel_sp = slot % 2 + 2 * inner
            owner = lax.bitwise_xor(me_bd, rel_bd) * pieces + lax.bitwise_xor(me_sp, rel_sp)
            all_ref[owner] = part_ref[inner]
    for part in range(bands):
        first_row = part * tall + 4 * chain
        halves = [
            exchange_blocks([all_ref[part * pieces + column * 4 + k] for k in range(4)], wide)
            for column in range(2)]
        rows = jnp.concatenate([halves[column][row] for row in range(4) for column in range(2)], axis=1)
        high, low = split(rows)
        here = jnp.concatenate([high, low], axis=0)
        image = [
            jnp.concatenate([ref[first_row + row] for row in range(4)], axis=1) for ref in (xh_ref, xl_ref)]
        total = total + dot_nt(jnp.concatenate(image + [here], axis=0), here)
        mine = jnp.transpose(all_ref[part * pieces + me_sp])
        h_out[first_row:first_row + 4] = mine.reshape(4, wide, rank)
    return total


def first_kernel(xh_ref, xl_ref, *rest):
    part_refs = rest[:8]
    total_out, h_out, all_ref = rest[8:]
    total_out[...] = accumulate(
        xh_ref, xl_ref, part_refs, all_ref, h_out, 0, jnp.zeros(total_out.shape, F32))
    tall = xh_ref.shape[0] // lax.axis_size("bd")
    for part in range(lax.axis_size("bd")):
        h_out[part * tall + 4:(part + 1) * tall] = jnp.zeros((tall - 4,) + h_out.shape[1:], F32)


def first_call(x_high, x_low, parts):
    height, planes, length = x_high.shape
    rank = parts[0].shape[1]
    return pl.pallas_call(
        first_kernel,
        out_shape=[
            jax.ShapeDtypeStruct((2 * (planes + rank), 2 * rank), F32),
            jax.ShapeDtypeStruct((height, length // lax.axis_size("sp"), rank), F32),
        ],
        in_specs=in_vmem(2 + len(parts)),
        scratch_shapes=[pltpu.VMEM((32,) + parts[0].shape[1:], F32)],
        compiler_params=pltpu.CompilerParams(vmem_limit_bytes=VMEM_LIMIT),
    )(x_high, x_low, *parts)


def second_kernel(xh_ref, xl_ref, w_ref, total_ref, h_ref, *rest):
    part_refs = rest[:8]
    w_out, h_out, all_ref = rest[8:]
    planes = xh_ref.shape[1]
    rank = w_ref.shape[0]
    h_out[...] = h_ref[...]
    total = accumulate(xh_ref, xl_ref, part_refs, all_ref, h_out, 1, total_ref[...])
    numer = total[:planes, :rank] + (total[:planes, rank:] + total[planes:2 * planes, :rank])
    gram = total[2 * planes:]
    gram = gram[:rank, :rank] + (gram[:rank, rank:] + gram[rank:, :rank])
    w_here = w_ref[...]
    w_out[...] = w_here * jnp.transpose(numer) / dot_exact(gram, w_here)


def second_call(x_high, x_low, w_here, total, h_half, parts):
    return pl.pallas_call(
        second_kernel,
        out_shape=[
            jax.ShapeDtypeStruct(w_here.shape, F32),
            jax.ShapeDtypeStruct(h_half.shape, F32),
        ],
        in_specs=in_vmem(5 + len(parts)),
        scratch_shapes=[pltpu.VMEM((32,) + parts[0].shape[1:], F32)],
        compiler_params=pltpu.CompilerParams(vmem_limit_bytes=VMEM_LIMIT),
    )(x_high, x_low, w_here, total, h_half, *parts)


def gather_w_kernel(*refs):
    part_refs = refs[:-2]
    out_ref, all_ref = refs[-2:]
    planes = out_ref.shape[1] // 8
    me_sp = lax.axis_index("sp")
    rel = 0
    for part_ref in part_refs:
        for inner in range(part_ref.shape[0]):
            all_ref[lax.bitwise_xor(me_sp, RING[rel]), :, 0:planes] = part_ref[inner]
            rel += 1
    for owner in range(8):
        out_ref[:, owner * planes:(owner + 1) * planes] = all_ref[owner][:, :planes]


RING = (0, 1, 2, 3, 4, 5, 6, 7)


def gather_w_call(parts):
    _, rank, planes = parts[0].shape
    return pl.pallas_call(
        gather_w_kernel,
        out_shape=jax.ShapeDtypeStruct((rank, planes * 8), F32),
        in_specs=in_vmem(len(parts)),
        scratch_shapes=[pltpu.VMEM((8, rank, LANES), F32)],
        compiler_params=pltpu.CompilerParams(vmem_limit_bytes=VMEM_LIMIT),
    )(*parts)


def send(value, mask_sp, mask_bd):
    bands = lax.axis_size("bd")
    pieces = lax.axis_size("sp")
    pairs = []
    for s in range(pieces):
        for b in range(bands):
            pairs.append((s * bands + b, (s ^ mask_sp) * bands + (b ^ mask_bd)))
    return lax.ppermute(value, ("sp", "bd"), pairs)


def around(values):
    return [send(values[k], k % 2, 2 * (k // 2)) for k in range(1, 4)]


def local(cube, taps_x, taps_y, factor_w, factor_h):
    w_rows = jnp.transpose(factor_w[0])
    taps_x = jnp.transpose(taps_x, (2, 0, 1))
    taps_y = jnp.transpose(taps_y, (2, 0, 1))
    h_columns = jnp.transpose(factor_h, (1, 2, 0))
    rank = w_rows.shape[0]
    x_high, x_low, w_here, keep_0, give_0, keep_1, give_1 = blur_call(cube[0], taps_x, taps_y, w_rows)
    chains = []
    for keep, give in ((keep_0, give_0), (keep_1, give_1)):
        taken = send(give, 0, 1)
        bounds = [place * 4 * rank for place in (0, 1, 3, 2)]
        sides = []
        for first in bounds:
            last = keep.shape[0] if first == max(bounds) else first + 4 * rank
            sides.append(keep[first:last] + taken[first:last])
        chains.append((sides, around(sides)))
    ratio = ratio_call(chains[0][0][2], chains[0][1][1], h_columns)
    line = []
    for k in range(4):
        part = slice(k * rank, (k + 1) * rank)
        line.append(jnp.concatenate(
            [(sides[0][part] + others[0][part]) + (others[1][part] + others[2][part]) for sides, others in chains],
            axis=1))
    line = [line[0]] + [send(line[k], 2 * k, 0) for k in range(1, 4)]
    h_piece = ratio * ((line[0] + line[1]) + (line[2] + line[3]))
    h_line = [h_piece] + [send(h_piece, 2 * k, 0) for k in range(1, 4)]
    rounds = []
    for first in (0, LANES):
        mine = jnp.stack([value[:, first:first + LANES] for value in h_line])
        parts = [mine] + around([mine] * 4)
        rounds.append(parts + [send(value, 0, 1) for value in parts])
    total, h_half = first_call(x_high, x_low, rounds[0])
    w_piece, h_next = second_call(x_high, x_low, w_here, total, h_half, rounds[1])
    w_pair = jnp.stack([w_piece, send(w_piece, 1, 0)])
    w_next = gather_w_call([w_pair] + [send(w_pair, 2 * k, 0) for k in range(1, 4)])
    return jnp.transpose(w_next)[None], jnp.transpose(h_next, (2, 0, 1))


def normalized(kernel):
    return kernel / jnp.sum(kernel, axis=-1, keepdims=True)


def band_weights(kernel, size_in, size_out, offset):
    tap_count = kernel.shape[-1]
    in_index = lax.broadcasted_iota(jnp.int32, (size_in, size_out, tap_count), 0)
    out_index = lax.broadcasted_iota(jnp.int32, (size_in, size_out, tap_count), 1)
    tap_index = lax.broadcasted_iota(jnp.int32, (size_in, size_out, tap_count), 2)
    select = (tap_index == in_index - out_index + offset).astype(jnp.float32)
    return jnp.einsum("pk,iok->pio", kernel, select, precision=lax.Precision.HIGHEST)


def blur_rows(planes, kernel_y):
    margin = (kernel_y.shape[-1] - 1) // 2
    height = planes.shape[1]
    band_table = band_weights(kernel_y, height, height, margin)
    return jnp.einsum("piz,pio->poz", planes, band_table, precision=lax.Precision.HIGHEST)


def blur_columns(planes, kernel_x):
    margin = (kernel_x.shape[-1] - 1) // 2
    count, height, length = planes.shape
    blocks = planes.reshape(count, height, length // 128, 128)
    empty = jnp.zeros((count, height, 1, 128), jnp.float32)
    left_block = jnp.concatenate([empty, blocks[:, :, :-1]], axis=2)
    right_block = jnp.concatenate([blocks[:, :, 1:], empty], axis=2)
    window = jnp.concatenate([left_block, blocks, right_block], axis=3)
    band_table = band_weights(kernel_x, 384, 128, margin - 128)
    result = jnp.einsum("pybi,pio->pybo", window, band_table, precision=lax.Precision.HIGHEST)
    return result.reshape(count, height, length)


def local_any(cube, taps_x, taps_y, factor_w, factor_h):
    highest = lax.Precision.HIGHEST
    kernel_x = normalized(taps_x[0])
    kernel_y = normalized(taps_y[0])
    rows_done = blur_rows(cube[0], kernel_y)
    w_band = factor_w[0]
    blurred = blur_columns(rows_done, kernel_x)[None]
    moved = lax.all_to_all(blurred, "sp", split_axis=3, concat_axis=1, tiled=True)
    numer_part = jnp.einsum("lr,plyx->pryx", w_band, moved, precision=highest)
    gram_part = jnp.dot(w_band.T, w_band, precision=highest)
    numer_h, gram_w = lax.psum((numer_part[0], gram_part), "bd")
    h_next = factor_h * numer_h / jnp.einsum("rq,qyx->ryx", gram_w, factor_h, precision=highest)
    x_band = moved[0]
    gram_h_part = jnp.einsum("ryx,qyx->rq", h_next, h_next, precision=highest)
    numer_w_part = jnp.einsum("lyx,ryx->lr", x_band, h_next, precision=highest)
    numer_w, gram_h = lax.psum((numer_w_part, gram_h_part), "sp")
    w_next = w_band * numer_w / jnp.dot(w_band, gram_h, precision=highest)
    return (w_next[None], h_next)


def solution(mesh):
    in_specs = (
        P("bd", "sp", None, None),
        P("bd", "sp", None),
        P("bd", "sp", None),
        P("bd", None, None),
        P(None, None, "sp"),
    )
    out_specs = (P("bd", None, None), P(None, None, "sp"))

    def body(cube, *rest):
        suits = lax.axis_size("sp") == 8 and lax.axis_size("bd") == 4 and cube.shape[1] % GROUP == 0
        return (local if suits else local_any)(cube, *rest)

    return jax.shard_map(body, mesh=mesh, in_specs=in_specs, out_specs=out_specs, check_vma=False)
```

```python
import functools

import jax
import jax.numpy as jnp
from jax import lax
from jax.experimental import pallas as pl
from jax.experimental.pallas import tpu as pltpu
from jax.sharding import PartitionSpec as P

F32 = jnp.float32
BF16 = jnp.bfloat16
LANES = 128
GROUP = 16
PIECES = 16
FOLDED = 24
VMEM_LIMIT = 48 * 1024 * 1024


def split(value):
    high = value.astype(BF16)
    low = (value - high.astype(F32)).astype(BF16)
    return high, low


def dot(left, right):
    return lax.dot_general(left, right, (((1,), (0,)), ((), ())), preferred_element_type=F32)


def dot_nt(left, right):
    return lax.dot_general(left, right, (((1,), (1,)), ((), ())), preferred_element_type=F32)


def dot_exact(left, right):
    return lax.dot_general(
        left, right, (((1,), (0,)), ((), ())),
        precision=lax.Precision.HIGHEST, preferred_element_type=F32,
    )


def exchange_blocks(rows, block):
    lane = lax.broadcasted_iota(jnp.int32, rows[0].shape, 1)
    first_half = lane < 2 * block
    even = (lane // block) % 2 == 0
    v0, v1, v2, v3 = rows
    u0 = jnp.where(first_half, v0, pltpu.roll(v2, 2 * block, 1))
    u2 = jnp.where(first_half, pltpu.roll(v0, 2 * block, 1), v2)
    u1 = jnp.where(first_half, v1, pltpu.roll(v3, 2 * block, 1))
    u3 = jnp.where(first_half, pltpu.roll(v1, 2 * block, 1), v3)
    w0 = jnp.where(even, u0, pltpu.roll(u1, block, 1))
    w1 = jnp.where(even, pltpu.roll(u0, 3 * block, 1), u1)
    w2 = jnp.where(even, u2, pltpu.roll(u3, block, 1))
    w3 = jnp.where(even, pltpu.roll(u2, 3 * block, 1), u3)
    return w0, w1, w2, w3


def normalized_taps(taps_ref, reverse, work_ref, out_ref):
    taps = taps_ref.shape[0]
    planes = taps_ref.shape[2]
    work_ref[...] = jnp.zeros_like(work_ref)
    for tap in range(taps):
        row = taps - 1 - tap if reverse else tap
        work_ref[row:row + 1, 0:planes] = taps_ref[tap]
    values = work_ref[...]
    total = jnp.sum(values, axis=0, keepdims=True)
    total = jnp.where(total == 0.0, 1.0, total)
    out_ref[...] = jnp.transpose(values / total)


def column_table(row, margin):
    table = pltpu.roll(jnp.broadcast_to(row, (LANES, LANES)), 0, 1, stride=1, stride_axis=0)
    high = table.astype(BF16).astype(F32)
    src = lax.broadcasted_iota(jnp.int32, (GROUP, LANES), 0)
    dst = lax.broadcasted_iota(jnp.int32, (GROUP, LANES), 1)
    first, last = slice(0, GROUP), slice(LANES - GROUP, LANES)
    above = dst - src <= LANES // 2
    below = src + LANES - GROUP - dst <= LANES // 2
    empty = jnp.zeros((LANES - 2 * GROUP, LANES), F32)
    main, edge = [], []
    for part in (high, table - high):
        main.append(jnp.concatenate(
            [jnp.where(above, part[first], 0.0), part[GROUP:LANES - GROUP], jnp.where(below, part[last], 0.0)],
            axis=0).astype(BF16))
        edge.append(jnp.concatenate(
            [jnp.where(above, 0.0, part[first]), empty, jnp.where(below, 0.0, part[last])],
            axis=0).astype(BF16))
    return jnp.concatenate([jnp.concatenate(main, axis=1), jnp.concatenate(edge, axis=1)], axis=0)


def blur_plane(plane, row, margin):
    height = plane.shape[0]
    table = column_table(row, margin)
    left, right = plane[:, :LANES], plane[:, LANES:]
    lane = lax.broadcasted_iota(jnp.int32, left.shape, 1)
    main = jnp.concatenate([left, right], axis=0)
    edge = jnp.concatenate(
        [jnp.where(lane < LANES // 2, right, 0.0), jnp.where(lane < LANES // 2, 0.0, left)], axis=0)
    high, low = split(jnp.concatenate([main, edge], axis=1))
    product = dot(jnp.concatenate([high, low], axis=0), table)
    rows = 2 * height
    blocks = product[:rows, :LANES] + (product[:rows, LANES:] + product[rows:, :LANES])
    return jnp.concatenate([blocks[:height], blocks[height:]], axis=1)


def row_table(base, margin, height):
    high = base.astype(BF16).astype(F32)
    low = base - high
    plane = lax.broadcasted_iota(jnp.int32, (8, LANES), 0)
    lane = lax.broadcasted_iota(jnp.int32, (8, LANES), 1)
    per_vector = LANES // height
    own = lane // height == plane % per_vector
    masks = [own & (plane // per_vector == part) for part in range(8 * height // LANES)]

    def table(part):
        strips = []
        for row in range(height):
            rolled = pltpu.roll(part, (row - margin) % LANES, 1)
            strips.append(jnp.concatenate([jnp.where(mask, rolled, 0.0) for mask in masks], axis=1))
        return jnp.concatenate(strips, axis=0).astype(BF16)

    return table(high), table(low)


def fold(square):
    side = square.shape[0]
    rest = jnp.zeros((8, LANES - 2 * side), F32)
    return jnp.concatenate(
        [jnp.concatenate([square[first:first + 8], square[first + 8:first + 16], rest], axis=1)
         for first in range(0, side, 16)], axis=0)


def unfold(folded, side):
    blocks = []
    for first in range(0, folded.shape[0], 8):
        blocks += [folded[first:first + 8, :side], folded[first:first + 8, side:2 * side]]
    return jnp.concatenate(blocks, axis=0)


def in_vmem(count):
    return [pl.BlockSpec(memory_space=pltpu.VMEM)] * count


def band_gram(w_rows):
    high, low = split(w_rows)
    rank = w_rows.shape[0]
    padded = jnp.concatenate([high, jnp.zeros((2 * LANES - rank, high.shape[1]), BF16)], axis=0)
    padded_low = jnp.concatenate([low, jnp.zeros((2 * LANES - rank, low.shape[1]), BF16)], axis=0)
    both = dot_nt(jnp.concatenate([high, low], axis=0), padded)
    return both[:rank] + (both[rank:] + dot_nt(high, padded_low))


def blur_group(step, cube_ref, kx_ref, ky_ref, xh_ref, xl_ref, margin):
    height = cube_ref.shape[1]
    halves = []
    for half in range(GROUP // 8):
        done = []
        for k in range(8 * half, 8 * half + 8):
            plane = step * GROUP + k
            done.append(blur_plane(cube_ref[plane], kx_ref[pl.ds(plane, 1), :], margin))
        high, low = split(jnp.concatenate(done, axis=0))
        rows = ky_ref[pl.ds(pl.multiple_of(step * GROUP + 8 * half, 8), 8), :]
        table_high, table_low = row_table(rows, margin, height)
        result = dot(table_high, high) + (dot(table_low, high) + dot(table_high, low))
        halves.append(result.reshape(height, 8, result.shape[1]))
    high, low = split(jnp.concatenate(halves, axis=1))
    planes_here = pl.ds(pl.multiple_of(step * GROUP, GROUP), GROUP)
    xh_ref[:, planes_here, :] = high
    xl_ref[:, planes_here, :] = low


def blur_kernel(cube_hbm, taps_x_hbm, taps_y_hbm, w_hbm, xh_ref, xl_ref, w_here_ref, keep_0, give_0, keep_1, give_1,
                cube_ref, taps_x_ref, taps_y_ref, w_ref, sems, chunk_sems, work_ref, kx_ref, ky_ref):
    taps = taps_x_ref.shape[0]
    margin = (taps - 1) // 2
    height = cube_ref.shape[1]
    rank = w_ref.shape[0]
    groups = cube_ref.shape[0] // GROUP

    def chunk(step):
        here = pl.ds(step * GROUP, GROUP)
        return pltpu.make_async_copy(cube_hbm.at[here], cube_ref.at[here], chunk_sems.at[step])

    copies = [
        pltpu.make_async_copy(taps_x_hbm, taps_x_ref, sems.at[0]),
        pltpu.make_async_copy(taps_y_hbm, taps_y_ref, sems.at[1]),
        pltpu.make_async_copy(w_hbm, w_ref, sems.at[2]),
    ]
    for copy in copies:
        copy.start()
    for step in range(groups):
        chunk(step).start()
    copies[0].wait()
    normalized_taps(taps_x_ref, True, work_ref, kx_ref)
    kx_ref[...] = pltpu.roll(kx_ref[...], LANES - margin, 1)
    copies[1].wait()
    normalized_taps(taps_y_ref, False, work_ref, ky_ref)
    per_vector = LANES // height
    place = lax.broadcasted_iota(jnp.int32, (LANES, LANES), 0) % per_vector
    values = ky_ref[...]
    placed = values
    for k in range(1, per_vector):
        placed = jnp.where(place == k, pltpu.roll(values, k * height, 1), placed)
    ky_ref[...] = placed
    copies[2].wait()

    def body(step, carry):
        chunk(step).wait()
        blur_group(step, cube_ref, kx_ref, ky_ref, xh_ref, xl_ref, margin)
        return carry

    lax.fori_loop(0, groups, body, 0)
    gram = fold(band_gram(w_ref[...])[:, :rank])
    keep_0[PIECES * rank:] = gram
    give_0[PIECES * rank:] = gram
    planes = xh_ref.shape[1]
    band = w_ref.shape[1]
    me_sp = lax.axis_index("sp")
    me_bd = lax.axis_index("bd")
    tall = height // lax.axis_size("bd")
    wide = 2 * LANES // lax.axis_size("sp")
    shift = lax.rem(band - me_sp * planes, band)
    w_here = pltpu.roll(w_ref[...], shift, 1)[:, :2 * LANES]
    w_here_ref[...] = w_here[:, :planes]
    lane = lax.broadcasted_iota(jnp.int32, w_here.shape, 1)
    w_here = jnp.where(lane < planes, w_here, 0.0)
    w_high = w_here.astype(BF16).astype(F32)
    w_both = jnp.concatenate([w_high + pltpu.roll(w_high, planes, 1), w_here - w_high], axis=0)
    w_both = w_both.astype(BF16)[:, :2 * planes]
    for chain in range(2):
        for rel_bd in (1, 3, 0, 2):
            first_row = lax.bitwise_xor(me_bd, rel_bd) * tall + 4 * chain
            sums = []
            for row in range(4):
                image = jnp.concatenate([xh_ref[first_row + row], xl_ref[first_row + row]], axis=0)
                both = dot(w_both, image)
                sums.append(both[:rank] + both[rank:])
            refs = ((keep_0, give_0), (keep_1, give_1))[chain]
            for column in range(2):
                pieces = exchange_blocks(
                    [value[:, column * LANES:(column + 1) * LANES] for value in sums], wide)
                for k in range(4):
                    rel_sp = lax.bitwise_xor(me_sp, column * 4 + k)
                    side = 3 - rel_sp % 2 if rel_bd // 2 else rel_sp % 2
                    first = pl.multiple_of((side * 4 + rel_sp // 2) * rank, 8)
                    refs[rel_bd % 2][pl.ds(first, rank)] = pieces[k]


def blur_call(cube, taps_x, taps_y, w_rows):
    planes, height, length = cube.shape
    rank = w_rows.shape[0]
    first = jax.ShapeDtypeStruct((PIECES * rank + FOLDED, LANES), F32)
    second = jax.ShapeDtypeStruct((PIECES * rank, LANES), F32)
    image = (height, planes, length)
    mine = jax.ShapeDtypeStruct((rank, planes), F32)
    in_hbm = [pltpu.with_memory_space_constraint(value, pltpu.HBM) for value in (cube, taps_x, taps_y, w_rows)]
    return pl.pallas_call(
        blur_kernel,
        out_shape=[jax.ShapeDtypeStruct(image, BF16)] * 2 + [mine, first, first, second, second],
        in_specs=[pl.BlockSpec(memory_space=pltpu.HBM)] * 4,
        out_specs=in_vmem(7),
        scratch_shapes=[pltpu.VMEM(value.shape, F32) for value in (cube, taps_x, taps_y, w_rows)]
        + [pltpu.SemaphoreType.DMA((3,)), pltpu.SemaphoreType.DMA((planes // GROUP,))]
        + [pltpu.VMEM((LANES, LANES), F32)] * 3,
        compiler_params=pltpu.CompilerParams(vmem_limit_bytes=VMEM_LIMIT),
    )(*in_hbm)


def ratio_kernel(mine_ref, other_ref, h_ref, out_ref):
    tall = h_ref.shape[0] // lax.axis_size("bd")
    first = pl.multiple_of(lax.axis_index("bd") * tall, tall)
    here = h_ref[pl.ds(first, tall)]
    here = jnp.transpose(here.reshape(-1, here.shape[2]))
    rows = mine_ref.shape[0]
    gram = unfold(mine_ref[rows - FOLDED:rows] + other_ref[rows - FOLDED:rows], here.shape[0])
    out_ref[...] = here / dot_exact(gram, here)


def ratio_call(mine, other, h_columns):
    piece = jax.ShapeDtypeStruct((h_columns.shape[2], 2 * LANES), F32)
    return pl.pallas_call(
        ratio_kernel,
        out_shape=piece,
        in_specs=in_vmem(3),
        compiler_params=pltpu.CompilerParams(vmem_limit_bytes=VMEM_LIMIT),
    )(mine, other, h_columns)


def accumulate(xh_ref, xl_ref, part_refs, all_ref, h_out, chain, total):
    height, planes, _ = xh_ref.shape
    rank = all_ref.shape[1]
    me_sp = lax.axis_index("sp")
    me_bd = lax.axis_index("bd")
    bands = lax.axis_size("bd")
    pieces = lax.axis_size("sp")
    tall = height // bands
    wide = 2 * LANES // pieces
    for slot, part_ref in enumerate(part_refs):
        rel_bd = slot // 4 + 2 * ((slot // 2) % 2)
        for inner in range(4):
            rel_sp = slot % 2 + 2 * inner
            owner = lax.bitwise_xor(me_bd, rel_bd) * pieces + lax.bitwise_xor(me_sp, rel_sp)
            all_ref[owner] = part_ref[inner]
    for part in range(bands):
        first_row = part * tall + 4 * chain
        halves = [
            exchange_blocks([all_ref[part * pieces + column * 4 + k] for k in range(4)], wide)
            for column in range(2)]
        rows = jnp.concatenate([halves[column][row] for row in range(4) for column in range(2)], axis=1)
        high, low = split(rows)
        here = jnp.concatenate([high, low], axis=0)
        image = [
            jnp.concatenate([ref[first_row + row] for row in range(4)], axis=1) for ref in (xh_ref, xl_ref)]
        total = total + dot_nt(jnp.concatenate(image + [here], axis=0), here)
        mine = jnp.transpose(all_ref[part * pieces + me_sp])
        h_out[first_row:first_row + 4] = mine.reshape(4, wide, rank)
    return total


def first_kernel(xh_ref, xl_ref, *rest):
    part_refs = rest[:8]
    total_out, h_out, all_ref = rest[8:]
    total_out[...] = accumulate(
        xh_ref, xl_ref, part_refs, all_ref, h_out, 0, jnp.zeros(total_out.shape, F32))
    tall = xh_ref.shape[0] // lax.axis_size("bd")
    for part in range(lax.axis_size("bd")):
        h_out[part * tall + 4:(part + 1) * tall] = jnp.zeros((tall - 4,) + h_out.shape[1:], F32)


def first_call(x_high, x_low, parts):
    height, planes, length = x_high.shape
    rank = parts[0].shape[1]
    return pl.pallas_call(
        first_kernel,
        out_shape=[
            jax.ShapeDtypeStruct((2 * (planes + rank), 2 * rank), F32),
            jax.ShapeDtypeStruct((height, length // lax.axis_size("sp"), rank), F32),
        ],
        in_specs=in_vmem(2 + len(parts)),
        scratch_shapes=[pltpu.VMEM((32,) + parts[0].shape[1:], F32)],
        compiler_params=pltpu.CompilerParams(vmem_limit_bytes=VMEM_LIMIT),
    )(x_high, x_low, *parts)


def second_kernel(xh_ref, xl_ref, w_ref, total_ref, h_ref, *rest):
    part_refs = rest[:8]
    w_out, h_out, all_ref = rest[8:]
    planes = xh_ref.shape[1]
    rank = w_ref.shape[0]
    h_out[...] = h_ref[...]
    total = accumulate(xh_ref, xl_ref, part_refs, all_ref, h_out, 1, total_ref[...])
    numer = total[:planes, :rank] + (total[:planes, rank:] + total[planes:2 * planes, :rank])
    gram = total[2 * planes:]
    gram = gram[:rank, :rank] + (gram[:rank, rank:] + gram[rank:, :rank])
    w_here = w_ref[...]
    w_out[...] = w_here * jnp.transpose(numer) / dot_exact(gram, w_here)


def second_call(x_high, x_low, w_here, total, h_half, parts):
    return pl.pallas_call(
        second_kernel,
        out_shape=[
            jax.ShapeDtypeStruct(w_here.shape, F32),
            jax.ShapeDtypeStruct(h_half.shape, F32),
        ],
        in_specs=in_vmem(5 + len(parts)),
        scratch_shapes=[pltpu.VMEM((32,) + parts[0].shape[1:], F32)],
        compiler_params=pltpu.CompilerParams(vmem_limit_bytes=VMEM_LIMIT),
    )(x_high, x_low, w_here, total, h_half, *parts)


def gather_w_kernel(*refs):
    part_refs = refs[:-2]
    out_ref, all_ref = refs[-2:]
    planes = out_ref.shape[1] // 8
    me_sp = lax.axis_index("sp")
    rel = 0
    for part_ref in part_refs:
        for inner in range(part_ref.shape[0]):
            all_ref[lax.bitwise_xor(me_sp, RING[rel]), :, 0:planes] = part_ref[inner]
            rel += 1
    for owner in range(8):
        out_ref[:, owner * planes:(owner + 1) * planes] = all_ref[owner][:, :planes]


RING = (0, 1, 2, 3, 4, 5, 6, 7)


def gather_w_call(parts):
    _, rank, planes = parts[0].shape
    return pl.pallas_call(
        gather_w_kernel,
        out_shape=jax.ShapeDtypeStruct((rank, planes * 8), F32),
        in_specs=in_vmem(len(parts)),
        scratch_shapes=[pltpu.VMEM((8, rank, LANES), F32)],
        compiler_params=pltpu.CompilerParams(vmem_limit_bytes=VMEM_LIMIT),
    )(*parts)


def send(value, mask_sp, mask_bd):
    bands = lax.axis_size("bd")
    pieces = lax.axis_size("sp")
    pairs = []
    for s in range(pieces):
        for b in range(bands):
            pairs.append((s * bands + b, (s ^ mask_sp) * bands + (b ^ mask_bd)))
    return lax.ppermute(value, ("sp", "bd"), pairs)


def around(values):
    return [send(values[k], k % 2, 2 * (k // 2)) for k in range(1, 4)]


def local(cube, taps_x, taps_y, factor_w, factor_h):
    w_rows = jnp.transpose(factor_w[0])
    taps_x = jnp.transpose(taps_x, (2, 0, 1))
    taps_y = jnp.transpose(taps_y, (2, 0, 1))
    h_columns = jnp.transpose(factor_h, (1, 2, 0))
    rank = w_rows.shape[0]
    x_high, x_low, w_here, keep_0, give_0, keep_1, give_1 = blur_call(cube[0], taps_x, taps_y, w_rows)
    chains = []
    for keep, give in ((keep_0, give_0), (keep_1, give_1)):
        taken = send(give, 0, 1)
        bounds = [place * 4 * rank for place in (0, 1, 3, 2)]
        sides = []
        for first in bounds:
            last = keep.shape[0] if first == max(bounds) else first + 4 * rank
            sides.append(keep[first:last] + taken[first:last])
        chains.append((sides, around(sides)))
    ratio = ratio_call(chains[0][0][2], chains[0][1][1], h_columns)
    line = []
    for k in range(4):
        part = slice(k * rank, (k + 1) * rank)
        line.append(jnp.concatenate(
            [(sides[0][part] + others[0][part]) + (others[1][part] + others[2][part]) for sides, others in chains],
            axis=1))
    line = [line[0]] + [send(line[k], 2 * k, 0) for k in range(1, 4)]
    h_piece = ratio * ((line[0] + line[1]) + (line[2] + line[3]))
    h_line = [h_piece] + [send(h_piece, 2 * k, 0) for k in range(1, 4)]
    rounds = []
    for first in (0, LANES):
        mine = jnp.stack([value[:, first:first + LANES] for value in h_line])
        parts = [mine] + around([mine] * 4)
        rounds.append(parts + [send(value, 0, 1) for value in parts])
    total, h_half = first_call(x_high, x_low, rounds[0])
    w_piece, h_next = second_call(x_high, x_low, w_here, total, h_half, rounds[1])
    w_pair = jnp.stack([w_piece, send(w_piece, 1, 0)])
    w_next = gather_w_call([w_pair] + [send(w_pair, 2 * k, 0) for k in range(1, 4)])
    return jnp.transpose(w_next)[None], jnp.transpose(h_next, (2, 0, 1))


def normalized(kernel):
    return kernel / jnp.sum(kernel, axis=-1, keepdims=True)


def band_weights(kernel, size_in, size_out, offset):
    tap_count = kernel.shape[-1]
    in_index = lax.broadcasted_iota(jnp.int32, (size_in, size_out, tap_count), 0)
    out_index = lax.broadcasted_iota(jnp.int32, (size_in, size_out, tap_count), 1)
    tap_index = lax.broadcasted_iota(jnp.int32, (size_in, size_out, tap_count), 2)
    select = (tap_index == in_index - out_index + offset).astype(jnp.float32)
    return jnp.einsum("pk,iok->pio", kernel, select, precision=lax.Precision.HIGHEST)


def blur_rows(planes, kernel_y):
    margin = (kernel_y.shape[-1] - 1) // 2
    height = planes.shape[1]
    band_table = band_weights(kernel_y, height, height, margin)
    return jnp.einsum("piz,pio->poz", planes, band_table, precision=lax.Precision.HIGHEST)


def blur_columns(planes, kernel_x):
    margin = (kernel_x.shape[-1] - 1) // 2
    count, height, length = planes.shape
    blocks = planes.reshape(count, height, length // 128, 128)
    empty = jnp.zeros((count, height, 1, 128), jnp.float32)
    left_block = jnp.concatenate([empty, blocks[:, :, :-1]], axis=2)
    right_block = jnp.concatenate([blocks[:, :, 1:], empty], axis=2)
    window = jnp.concatenate([left_block, blocks, right_block], axis=3)
    band_table = band_weights(kernel_x, 384, 128, margin - 128)
    result = jnp.einsum("pybi,pio->pybo", window, band_table, precision=lax.Precision.HIGHEST)
    return result.reshape(count, height, length)


def local_any(cube, taps_x, taps_y, factor_w, factor_h):
    highest = lax.Precision.HIGHEST
    kernel_x = normalized(taps_x[0])
    kernel_y = normalized(taps_y[0])
    rows_done = blur_rows(cube[0], kernel_y)
    w_band = factor_w[0]
    blurred = blur_columns(rows_done, kernel_x)[None]
    moved = lax.all_to_all(blurred, "sp", split_axis=3, concat_axis=1, tiled=True)
    numer_part = jnp.einsum("lr,plyx->pryx", w_band, moved, precision=highest)
    gram_part = jnp.dot(w_band.T, w_band, precision=highest)
    numer_h, gram_w = lax.psum((numer_part[0], gram_part), "bd")
    h_next = factor_h * numer_h / jnp.einsum("rq,qyx->ryx", gram_w, factor_h, precision=highest)
    x_band = moved[0]
    gram_h_part = jnp.einsum("ryx,qyx->rq", h_next, h_next, precision=highest)
    numer_w_part = jnp.einsum("lyx,ryx->lr", x_band, h_next, precision=highest)
    numer_w, gram_h = lax.psum((numer_w_part, gram_h_part), "sp")
    w_next = w_band * numer_w / jnp.dot(w_band, gram_h, precision=highest)
    return (w_next[None], h_next)


def solution(mesh):
    in_specs = (
        P("bd", "sp", None, None),
        P("bd", "sp", None),
        P("bd", "sp", None),
        P("bd", None, None),
        P(None, None, "sp"),
    )
    out_specs = (P("bd", None, None), P(None, None, "sp"))

    def body(cube, *rest):
        suits = lax.axis_size("sp") == 8 and lax.axis_size("bd") == 4 and cube.shape[1] % GROUP == 0
        return (local if suits else local_any)(cube, *rest)

    return jax.shard_map(body, mesh=mesh, in_specs=in_specs, out_specs=out_specs, check_vma=False)
```

```python
import functools

import jax
import jax.numpy as jnp
from jax import lax
from jax.experimental import pallas as pl
from jax.experimental.pallas import tpu as pltpu
from jax.sharding import PartitionSpec as P

F32 = jnp.float32
BF16 = jnp.bfloat16
LANES = 128
GROUP = 16
PIECES = 16
FOLDED = 24
VMEM_LIMIT = 48 * 1024 * 1024


def split(value):
    high = value.astype(BF16)
    low = (value - high.astype(F32)).astype(BF16)
    return high, low


def dot(left, right):
    return lax.dot_general(left, right, (((1,), (0,)), ((), ())), preferred_element_type=F32)


def dot_nt(left, right):
    return lax.dot_general(left, right, (((1,), (1,)), ((), ())), preferred_element_type=F32)


def dot_exact(left, right):
    return lax.dot_general(
        left, right, (((1,), (0,)), ((), ())),
        precision=lax.Precision.HIGHEST, preferred_element_type=F32,
    )


def exchange_blocks(rows, block):
    lane = lax.broadcasted_iota(jnp.int32, rows[0].shape, 1)
    first_half = lane < 2 * block
    even = (lane // block) % 2 == 0
    v0, v1, v2, v3 = rows
    u0 = jnp.where(first_half, v0, pltpu.roll(v2, 2 * block, 1))
    u2 = jnp.where(first_half, pltpu.roll(v0, 2 * block, 1), v2)
    u1 = jnp.where(first_half, v1, pltpu.roll(v3, 2 * block, 1))
    u3 = jnp.where(first_half, pltpu.roll(v1, 2 * block, 1), v3)
    w0 = jnp.where(even, u0, pltpu.roll(u1, block, 1))
    w1 = jnp.where(even, pltpu.roll(u0, 3 * block, 1), u1)
    w2 = jnp.where(even, u2, pltpu.roll(u3, block, 1))
    w3 = jnp.where(even, pltpu.roll(u2, 3 * block, 1), u3)
    return w0, w1, w2, w3


def normalized_taps(taps_ref, reverse, work_ref, out_ref):
    taps = taps_ref.shape[0]
    planes = taps_ref.shape[2]
    work_ref[...] = jnp.zeros_like(work_ref)
    for tap in range(taps):
        row = taps - 1 - tap if reverse else tap
        work_ref[row:row + 1, 0:planes] = taps_ref[tap]
    values = work_ref[...]
    total = jnp.sum(values, axis=0, keepdims=True)
    total = jnp.where(total == 0.0, 1.0, total)
    out_ref[...] = jnp.transpose(values / total)


def column_table(row, margin):
    table = pltpu.roll(jnp.broadcast_to(row, (LANES, LANES)), 0, 1, stride=1, stride_axis=0)
    high = table.astype(BF16).astype(F32)
    src = lax.broadcasted_iota(jnp.int32, (GROUP, LANES), 0)
    dst = lax.broadcasted_iota(jnp.int32, (GROUP, LANES), 1)
    first, last = slice(0, GROUP), slice(LANES - GROUP, LANES)
    above = dst - src <= LANES // 2
    below = src + LANES - GROUP - dst <= LANES // 2
    empty = jnp.zeros((LANES - 2 * GROUP, LANES), F32)
    main, edge = [], []
    for part in (high, table - high):
        main.append(jnp.concatenate(
            [jnp.where(above, part[first], 0.0), part[GROUP:LANES - GROUP], jnp.where(below, part[last], 0.0)],
            axis=0).astype(BF16))
        edge.append(jnp.concatenate(
            [jnp.where(above, 0.0, part[first]), empty, jnp.where(below, 0.0, part[last])],
            axis=0).astype(BF16))
    return jnp.concatenate([jnp.concatenate(main, axis=1), jnp.concatenate(edge, axis=1)], axis=0)


def blur_plane(plane, row, margin):
    height = plane.shape[0]
    table = column_table(row, margin)
    left, right = plane[:, :LANES], plane[:, LANES:]
    lane = lax.broadcasted_iota(jnp.int32, left.shape, 1)
    main = jnp.concatenate([left, right], axis=0)
    edge = jnp.concatenate(
        [jnp.where(lane < LANES // 2, right, 0.0), jnp.where(lane < LANES // 2, 0.0, left)], axis=0)
    high, low = split(jnp.concatenate([main, edge], axis=1))
    product = dot(jnp.concatenate([high, low], axis=0), table)
    rows = 2 * height
    blocks = product[:rows, :LANES] + (product[:rows, LANES:] + product[rows:, :LANES])
    return jnp.concatenate([blocks[:height], blocks[height:]], axis=1)


def row_table(base, margin, height):
    high = base.astype(BF16).astype(F32)
    low = base - high
    plane = lax.broadcasted_iota(jnp.int32, (8, LANES), 0)
    lane = lax.broadcasted_iota(jnp.int32, (8, LANES), 1)
    per_vector = LANES // height
    own = lane // height == plane % per_vector
    masks = [own & (plane // per_vector == part) for part in range(8 * height // LANES)]

    def table(part):
        strips = []
        for row in range(height):
            rolled = pltpu.roll(part, (row - margin) % LANES, 1)
            strips.append(jnp.concatenate([jnp.where(mask, rolled, 0.0) for mask in masks], axis=1))
        return jnp.concatenate(strips, axis=0).astype(BF16)

    return table(high), table(low)


def fold(square):
    side = square.shape[0]
    rest = jnp.zeros((8, LANES - 2 * side), F32)
    return jnp.concatenate(
        [jnp.concatenate([square[first:first + 8], square[first + 8:first + 16], rest], axis=1)
         for first in range(0, side, 16)], axis=0)


def unfold(folded, side):
    blocks = []
    for first in range(0, folded.shape[0], 8):
        blocks += [folded[first:first + 8, :side], folded[first:first + 8, side:2 * side]]
    return jnp.concatenate(blocks, axis=0)


def in_vmem(count):
    return [pl.BlockSpec(memory_space=pltpu.VMEM)] * count


def stage_bits(row, column, swapped):
    return row + swapped * (column - row), column + swapped * (row - column)


def band_gram(w_rows):
    high, low = split(w_rows)
    rank = w_rows.shape[0]
    padded = jnp.concatenate([high, jnp.zeros((2 * LANES - rank, high.shape[1]), BF16)], axis=0)
    padded_low = jnp.concatenate([low, jnp.zeros((2 * LANES - rank, low.shape[1]), BF16)], axis=0)
    both = dot_nt(jnp.concatenate([high, low], axis=0), padded)
    return both[:rank] + (both[rank:] + dot_nt(high, padded_low))


def blur_group(step, cube_ref, kx_ref, ky_ref, xh_ref, xl_ref, margin):
    height = cube_ref.shape[1]
    halves = []
    for half in range(GROUP // 8):
        done = []
        for k in range(8 * half, 8 * half + 8):
            plane = step * GROUP + k
            done.append(blur_plane(cube_ref[plane], kx_ref[pl.ds(plane, 1), :], margin))
        high, low = split(jnp.concatenate(done, axis=0))
        rows = ky_ref[pl.ds(pl.multiple_of(step * GROUP + 8 * half, 8), 8), :]
        table_high, table_low = row_table(rows, margin, height)
        result = dot(table_high, high) + (dot(table_low, high) + dot(table_high, low))
        halves.append(result.reshape(height, 8, result.shape[1]))
    high, low = split(jnp.concatenate(halves, axis=1))
    planes_here = pl.ds(pl.multiple_of(step * GROUP, GROUP), GROUP)
    xh_ref[:, planes_here, :] = high
    xl_ref[:, planes_here, :] = low


def blur_kernel(cube_hbm, taps_x_hbm, taps_y_hbm, w_hbm, xh_ref, xl_ref, w_here_ref, keep_0, give_0, keep_1, give_1,
                cube_ref, taps_x_ref, taps_y_ref, w_ref, sems, chunk_sems, work_ref, kx_ref, ky_ref):
    taps = taps_x_ref.shape[0]
    margin = (taps - 1) // 2
    height = cube_ref.shape[1]
    rank = w_ref.shape[0]
    groups = cube_ref.shape[0] // GROUP

    def chunk(step):
        here = pl.ds(step * GROUP, GROUP)
        return pltpu.make_async_copy(cube_hbm.at[here], cube_ref.at[here], chunk_sems.at[step])

    copies = [
        pltpu.make_async_copy(taps_x_hbm, taps_x_ref, sems.at[0]),
        pltpu.make_async_copy(taps_y_hbm, taps_y_ref, sems.at[1]),
        pltpu.make_async_copy(w_hbm, w_ref, sems.at[2]),
    ]
    for copy in copies:
        copy.start()
    for step in range(groups):
        chunk(step).start()
    copies[0].wait()
    normalized_taps(taps_x_ref, True, work_ref, kx_ref)
    kx_ref[...] = pltpu.roll(kx_ref[...], LANES - margin, 1)
    copies[1].wait()
    normalized_taps(taps_y_ref, False, work_ref, ky_ref)
    per_vector = LANES // height
    place = lax.broadcasted_iota(jnp.int32, (LANES, LANES), 0) % per_vector
    values = ky_ref[...]
    placed = values
    for k in range(1, per_vector):
        placed = jnp.where(place == k, pltpu.roll(values, k * height, 1), placed)
    ky_ref[...] = placed
    copies[2].wait()

    def body(step, carry):
        chunk(step).wait()
        blur_group(step, cube_ref, kx_ref, ky_ref, xh_ref, xl_ref, margin)
        return carry

    lax.fori_loop(0, groups, body, 0)
    gram = fold(band_gram(w_ref[...])[:, :rank])
    span = PIECES // 2 * rank
    for ref in (keep_0, give_0):
        ref[span:span + FOLDED] = gram
        ref[2 * span + FOLDED:] = gram
    planes = xh_ref.shape[1]
    band = w_ref.shape[1]
    me_sp = lax.axis_index("sp")
    me_bd = lax.axis_index("bd")
    tall = height // lax.axis_size("bd")
    wide = 2 * LANES // lax.axis_size("sp")
    shift = lax.rem(band - me_sp * planes, band)
    w_here = pltpu.roll(w_ref[...], shift, 1)[:, :2 * LANES]
    w_here_ref[...] = w_here[:, :planes]
    lane = lax.broadcasted_iota(jnp.int32, w_here.shape, 1)
    w_here = jnp.where(lane < planes, w_here, 0.0)
    w_high = w_here.astype(BF16).astype(F32)
    w_both = jnp.concatenate([w_high + pltpu.roll(w_high, planes, 1), w_here - w_high], axis=0)
    w_both = w_both.astype(BF16)[:, :2 * planes]
    for chain in range(2):
        for rel_bd in (1, 3, 0, 2):
            first_row = lax.bitwise_xor(me_bd, rel_bd) * tall + 4 * chain
            sums = []
            for row in range(4):
                image = jnp.concatenate([xh_ref[first_row + row], xl_ref[first_row + row]], axis=0)
                both = dot(w_both, image)
                sums.append(both[:rank] + both[rank:])
            refs = ((keep_0, give_0), (keep_1, give_1))[chain]
            for column in range(2):
                pieces = exchange_blocks(
                    [value[:, column * LANES:(column + 1) * LANES] for value in sums], wide)
                for k in range(4):
                    rel_sp = lax.bitwise_xor(me_sp, column * 4 + k)
                    outer, inner = stage_bits(rel_bd // 2, rel_sp % 2, (me_bd + rel_bd + chain) % 2)
                    first = ((outer * 2 + inner) * 4 + rel_sp // 2) * rank
                    first = first + outer * FOLDED if chain == 0 else first
                    refs[rel_bd % 2][pl.ds(pl.multiple_of(first, 8), rank)] = pieces[k]


def blur_call(cube, taps_x, taps_y, w_rows):
    planes, height, length = cube.shape
    rank = w_rows.shape[0]
    first = jax.ShapeDtypeStruct((PIECES * rank + 2 * FOLDED, LANES), F32)
    second = jax.ShapeDtypeStruct((PIECES * rank, LANES), F32)
    image = (height, planes, length)
    mine = jax.ShapeDtypeStruct((rank, planes), F32)
    in_hbm = [pltpu.with_memory_space_constraint(value, pltpu.HBM) for value in (cube, taps_x, taps_y, w_rows)]
    return pl.pallas_call(
        blur_kernel,
        out_shape=[jax.ShapeDtypeStruct(image, BF16)] * 2 + [mine, first, first, second, second],
        in_specs=[pl.BlockSpec(memory_space=pltpu.HBM)] * 4,
        out_specs=in_vmem(7),
        scratch_shapes=[pltpu.VMEM(value.shape, F32) for value in (cube, taps_x, taps_y, w_rows)]
        + [pltpu.SemaphoreType.DMA((3,)), pltpu.SemaphoreType.DMA((planes // GROUP,))]
        + [pltpu.VMEM((LANES, LANES), F32)] * 3,
        compiler_params=pltpu.CompilerParams(vmem_limit_bytes=VMEM_LIMIT),
    )(*in_hbm)


def ratio_kernel(mine_ref, other_ref, h_ref, out_ref):
    tall = h_ref.shape[0] // lax.axis_size("bd")
    first = pl.multiple_of(lax.axis_index("bd") * tall, tall)
    here = h_ref[pl.ds(first, tall)]
    here = jnp.transpose(here.reshape(-1, here.shape[2]))
    rows = mine_ref.shape[0]
    gram = 0.5 * unfold(mine_ref[rows - FOLDED:rows] + other_ref[rows - FOLDED:rows], here.shape[0])
    out_ref[...] = here / dot_exact(gram, here)


def ratio_call(mine, other, h_columns):
    piece = jax.ShapeDtypeStruct((h_columns.shape[2], 2 * LANES), F32)
    return pl.pallas_call(
        ratio_kernel,
        out_shape=piece,
        in_specs=in_vmem(3),
        compiler_params=pltpu.CompilerParams(vmem_limit_bytes=VMEM_LIMIT),
    )(mine, other, h_columns)


def accumulate(xh_ref, xl_ref, part_refs, all_ref, chain, total):
    height, planes, _ = xh_ref.shape
    me_sp = lax.axis_index("sp")
    me_bd = lax.axis_index("bd")
    bands = lax.axis_size("bd")
    pieces = lax.axis_size("sp")
    tall = height // bands
    wide = 2 * LANES // pieces
    for slot, part_ref in enumerate(part_refs):
        core, outer = slot // 2, slot % 2
        for inner in range(2):
            row, column = stage_bits(outer, inner, (me_bd + core + chain) % 2)
            for step in range(4):
                owner_bd = lax.bitwise_xor(me_bd, core + 2 * row)
                owner_sp = lax.bitwise_xor(me_sp, column + 2 * step)
                all_ref[owner_bd * pieces + owner_sp] = part_ref[inner, step]
    for part in range(bands):
        first_row = part * tall + 4 * chain
        halves = [
            exchange_blocks([all_ref[part * pieces + column * 4 + k] for k in range(4)], wide)
            for column in range(2)]
        rows = jnp.concatenate([halves[column][row] for row in range(4) for column in range(2)], axis=1)
        high, low = split(rows)
        here = jnp.concatenate([high, low], axis=0)
        image = [
            jnp.concatenate([ref[first_row + row] for row in range(4)], axis=1) for ref in (xh_ref, xl_ref)]
        total = total + dot_nt(jnp.concatenate(image + [here], axis=0), here)
    return total


def first_kernel(xh_ref, xl_ref, *rest):
    part_refs = rest[:4]
    total_out, all_ref = rest[4:]
    total_out[...] = accumulate(xh_ref, xl_ref, part_refs, all_ref, 0, jnp.zeros(total_out.shape, F32))


def first_call(x_high, x_low, parts):
    _, planes, _ = x_high.shape
    rank = parts[0].shape[2]
    return pl.pallas_call(
        first_kernel,
        out_shape=jax.ShapeDtypeStruct((2 * (planes + rank), 2 * rank), F32),
        in_specs=in_vmem(2 + len(parts)),
        scratch_shapes=[pltpu.VMEM((32, rank, LANES), F32)],
        compiler_params=pltpu.CompilerParams(vmem_limit_bytes=VMEM_LIMIT),
    )(x_high, x_low, *parts)


def second_kernel(xh_ref, xl_ref, w_ref, total_ref, *rest):
    part_refs = rest[:4]
    w_out, all_ref = rest[4:]
    planes = xh_ref.shape[1]
    rank = w_ref.shape[0]
    total = accumulate(xh_ref, xl_ref, part_refs, all_ref, 1, total_ref[...])
    numer = total[:planes, :rank] + (total[:planes, rank:] + total[planes:2 * planes, :rank])
    gram = total[2 * planes:]
    gram = gram[:rank, :rank] + (gram[:rank, rank:] + gram[rank:, :rank])
    w_here = w_ref[...]
    w_out[...] = w_here * jnp.transpose(numer) / dot_exact(gram, w_here)


def second_call(x_high, x_low, w_here, total, parts):
    rank = w_here.shape[0]
    return pl.pallas_call(
        second_kernel,
        out_shape=jax.ShapeDtypeStruct(w_here.shape, F32),
        in_specs=in_vmem(4 + len(parts)),
        scratch_shapes=[pltpu.VMEM((32, rank, LANES), F32)],
        compiler_params=pltpu.CompilerParams(vmem_limit_bytes=VMEM_LIMIT),
    )(x_high, x_low, w_here, total, *parts)


def place_h_kernel(*refs):
    h_out = refs[-1]
    me_bd = lax.axis_index("bd")
    tall = h_out.shape[0] // lax.axis_size("bd")
    for chain in range(2):
        for core in range(2):
            near_ref, far_ref = refs[4 * chain + 2 * core:4 * chain + 2 * core + 2]
            swapped = (me_bd + core + chain) % 2
            across = jnp.where(swapped == 0, far_ref[0, 0], near_ref[1, 0])
            for row, piece in ((0, near_ref[0, 0]), (1, across)):
                first = lax.bitwise_xor(me_bd, core + 2 * row) * tall + 4 * chain
                h_out[pl.ds(first, 4)] = jnp.transpose(piece).reshape((4,) + h_out.shape[1:])


def place_h_call(parts, shape):
    return pl.pallas_call(
        place_h_kernel,
        out_shape=jax.ShapeDtypeStruct(shape, F32),
        in_specs=in_vmem(len(parts)),
        compiler_params=pltpu.CompilerParams(vmem_limit_bytes=VMEM_LIMIT),
    )(*parts)


def gather_w_kernel(*refs):
    part_refs = refs[:-2]
    out_ref, all_ref = refs[-2:]
    planes = out_ref.shape[1] // 8
    me_sp = lax.axis_index("sp")
    rel = 0
    for part_ref in part_refs:
        for inner in range(part_ref.shape[0]):
            all_ref[lax.bitwise_xor(me_sp, RING[rel]), :, 0:planes] = part_ref[inner]
            rel += 1
    for owner in range(8):
        out_ref[:, owner * planes:(owner + 1) * planes] = all_ref[owner][:, :planes]


ORDER = (3, 2, 1)
RING = (0, 1, 2, 3, 4, 5, 6, 7)


def gather_w_call(parts):
    _, rank, planes = parts[0].shape
    return pl.pallas_call(
        gather_w_kernel,
        out_shape=jax.ShapeDtypeStruct((rank, planes * 8), F32),
        in_specs=in_vmem(len(parts)),
        scratch_shapes=[pltpu.VMEM((8, rank, LANES), F32)],
        compiler_params=pltpu.CompilerParams(vmem_limit_bytes=VMEM_LIMIT),
    )(*parts)


def send(value, mask_sp, mask_bd):
    bands = lax.axis_size("bd")
    pieces = lax.axis_size("sp")
    pairs = []
    for s in range(pieces):
        for b in range(bands):
            pairs.append((s * bands + b, (s ^ mask_sp) * bands + (b ^ mask_bd)))
    return lax.ppermute(value, ("sp", "bd"), pairs)


def send_across(value, chain, outer):
    bands = lax.axis_size("bd")
    pieces = lax.axis_size("sp")
    pairs = []
    for s in range(pieces):
        for b in range(bands):
            if (b + chain + outer) % 2:
                target = s * bands + (b ^ 2)
            else:
                target = (s ^ 1) * bands + b
            pairs.append((s * bands + b, target))
    return lax.ppermute(value, ("sp", "bd"), pairs)


def local(cube, taps_x, taps_y, factor_w, factor_h):
    w_rows = jnp.transpose(factor_w[0])
    taps_x = jnp.transpose(taps_x, (2, 0, 1))
    taps_y = jnp.transpose(taps_y, (2, 0, 1))
    h_columns = jnp.transpose(factor_h, (1, 2, 0))
    rank = w_rows.shape[0]
    x_high, x_low, w_here, keep_0, give_0, keep_1, give_1 = blur_call(cube[0], taps_x, taps_y, w_rows)
    sums = []
    for chain, (keep, give) in enumerate(((keep_0, give_0), (keep_1, give_1))):
        taken = send(give, 0, 1)
        half = keep.shape[0] // 2
        outer = send_across(keep[half:] + taken[half:], chain, 1)
        near = keep[:half] + taken[:half] + outer
        quarter = 4 * rank
        across = near[quarter:]
        inner = send_across(across, chain, 0)
        if chain == 0:
            ratio = ratio_call(across, inner, h_columns)
        sums.append(near[:quarter] + inner[:quarter])
    line = [jnp.concatenate([value[k * rank:(k + 1) * rank] for value in sums], axis=1) for k in range(4)]
    line = [line[0]] + [send(line[k], 2 * k, 0) for k in ORDER]
    h_piece = ratio * ((line[0] + line[1]) + (line[2] + line[3]))
    h_line = [h_piece] + [send(h_piece, 2 * k, 0) for k in range(1, 4)]
    chains = []
    for chain, first in enumerate((0, LANES)):
        mine = jnp.stack([value[:, first:first + LANES] for value in h_line])
        near = jnp.stack([mine, send_across(mine, chain, 0)])
        chains.append([near, send_across(near, chain, 1)])
    first_parts = chains[0] + [send(value, 0, 1) for value in chains[0]]
    total = first_call(x_high, x_low, first_parts)
    total, far = lax.optimization_barrier((total, chains[1][1]))
    second_parts = [chains[1][0], far]
    second_parts = second_parts + [send(value, 0, 1) for value in second_parts]
    w_piece = second_call(x_high, x_low, w_here, total, second_parts)
    h_next = place_h_call(first_parts + second_parts, h_columns.shape)
    w_pair = jnp.stack([w_piece, send(w_piece, 1, 0)])
    w_next = gather_w_call([w_pair] + [send(w_pair, 2 * k, 0) for k in range(1, 4)])
    return jnp.transpose(w_next)[None], jnp.transpose(h_next, (2, 0, 1))


def normalized(kernel):
    return kernel / jnp.sum(kernel, axis=-1, keepdims=True)


def band_weights(kernel, size_in, size_out, offset):
    tap_count = kernel.shape[-1]
    in_index = lax.broadcasted_iota(jnp.int32, (size_in, size_out, tap_count), 0)
    out_index = lax.broadcasted_iota(jnp.int32, (size_in, size_out, tap_count), 1)
    tap_index = lax.broadcasted_iota(jnp.int32, (size_in, size_out, tap_count), 2)
    select = (tap_index == in_index - out_index + offset).astype(jnp.float32)
    return jnp.einsum("pk,iok->pio", kernel, select, precision=lax.Precision.HIGHEST)


def blur_rows(planes, kernel_y):
    margin = (kernel_y.shape[-1] - 1) // 2
    height = planes.shape[1]
    band_table = band_weights(kernel_y, height, height, margin)
    return jnp.einsum("piz,pio->poz", planes, band_table, precision=lax.Precision.HIGHEST)


def blur_columns(planes, kernel_x):
    margin = (kernel_x.shape[-1] - 1) // 2
    count, height, length = planes.shape
    blocks = planes.reshape(count, height, length // 128, 128)
    empty = jnp.zeros((count, height, 1, 128), jnp.float32)
    left_block = jnp.concatenate([empty, blocks[:, :, :-1]], axis=2)
    right_block = jnp.concatenate([blocks[:, :, 1:], empty], axis=2)
    window = jnp.concatenate([left_block, blocks, right_block], axis=3)
    band_table = band_weights(kernel_x, 384, 128, margin - 128)
    result = jnp.einsum("pybi,pio->pybo", window, band_table, precision=lax.Precision.HIGHEST)
    return result.reshape(count, height, length)


def local_any(cube, taps_x, taps_y, factor_w, factor_h):
    highest = lax.Precision.HIGHEST
    kernel_x = normalized(taps_x[0])
    kernel_y = normalized(taps_y[0])
    rows_done = blur_rows(cube[0], kernel_y)
    w_band = factor_w[0]
    blurred = blur_columns(rows_done, kernel_x)[None]
    moved = lax.all_to_all(blurred, "sp", split_axis=3, concat_axis=1, tiled=True)
    numer_part = jnp.einsum("lr,plyx->pryx", w_band, moved, precision=highest)
    gram_part = jnp.dot(w_band.T, w_band, precision=highest)
    numer_h, gram_w = lax.psum((numer_part[0], gram_part), "bd")
    h_next = factor_h * numer_h / jnp.einsum("rq,qyx->ryx", gram_w, factor_h, precision=highest)
    x_band = moved[0]
    gram_h_part = jnp.einsum("ryx,qyx->rq", h_next, h_next, precision=highest)
    numer_w_part = jnp.einsum("lyx,ryx->lr", x_band, h_next, precision=highest)
    numer_w, gram_h = lax.psum((numer_w_part, gram_h_part), "sp")
    w_next = w_band * numer_w / jnp.dot(w_band, gram_h, precision=highest)
    return (w_next[None], h_next)


def solution(mesh):
    in_specs = (
        P("bd", "sp", None, None),
        P("bd", "sp", None),
        P("bd", "sp", None),
        P("bd", None, None),
        P(None, None, "sp"),
    )
    out_specs = (P("bd", None, None), P(None, None, "sp"))

    def body(cube, *rest):
        suits = lax.axis_size("sp") == 8 and lax.axis_size("bd") == 4 and cube.shape[1] % GROUP == 0
        return (local if suits else local_any)(cube, *rest)

    return jax.shard_map(body, mesh=mesh, in_specs=in_specs, out_specs=out_specs, check_vma=False)
```

```python
import functools

import jax
import jax.numpy as jnp
from jax import lax
from jax.experimental import pallas as pl
from jax.experimental.pallas import tpu as pltpu
from jax.sharding import PartitionSpec as P

F32 = jnp.float32
BF16 = jnp.bfloat16
LANES = 128
GROUP = 16
PIECES = 16
FOLDED = 24
VMEM_LIMIT = 48 * 1024 * 1024


def split(value):
    high = value.astype(BF16)
    low = (value - high.astype(F32)).astype(BF16)
    return high, low


def dot(left, right):
    return lax.dot_general(left, right, (((1,), (0,)), ((), ())), preferred_element_type=F32)


def dot_nt(left, right):
    return lax.dot_general(left, right, (((1,), (1,)), ((), ())), preferred_element_type=F32)


def dot_exact(left, right):
    return lax.dot_general(
        left, right, (((1,), (0,)), ((), ())),
        precision=lax.Precision.HIGHEST, preferred_element_type=F32,
    )


def exchange_blocks(rows, block):
    lane = lax.broadcasted_iota(jnp.int32, rows[0].shape, 1)
    first_half = lane < 2 * block
    even = (lane // block) % 2 == 0
    v0, v1, v2, v3 = rows
    u0 = jnp.where(first_half, v0, pltpu.roll(v2, 2 * block, 1))
    u2 = jnp.where(first_half, pltpu.roll(v0, 2 * block, 1), v2)
    u1 = jnp.where(first_half, v1, pltpu.roll(v3, 2 * block, 1))
    u3 = jnp.where(first_half, pltpu.roll(v1, 2 * block, 1), v3)
    w0 = jnp.where(even, u0, pltpu.roll(u1, block, 1))
    w1 = jnp.where(even, pltpu.roll(u0, 3 * block, 1), u1)
    w2 = jnp.where(even, u2, pltpu.roll(u3, block, 1))
    w3 = jnp.where(even, pltpu.roll(u2, 3 * block, 1), u3)
    return w0, w1, w2, w3


def normalized_taps(taps_ref, reverse, work_ref, out_ref):
    taps = taps_ref.shape[0]
    planes = taps_ref.shape[2]
    work_ref[...] = jnp.zeros_like(work_ref)
    for tap in range(taps):
        row = taps - 1 - tap if reverse else tap
        work_ref[row:row + 1, 0:planes] = taps_ref[tap]
    values = work_ref[...]
    total = jnp.sum(values, axis=0, keepdims=True)
    total = jnp.where(total == 0.0, 1.0, total)
    out_ref[...] = jnp.transpose(values / total)


def column_table(row, margin):
    table = pltpu.roll(jnp.broadcast_to(row, (LANES, LANES)), 0, 1, stride=1, stride_axis=0)
    high = table.astype(BF16).astype(F32)
    src = lax.broadcasted_iota(jnp.int32, (GROUP, LANES), 0)
    dst = lax.broadcasted_iota(jnp.int32, (GROUP, LANES), 1)
    first, last = slice(0, GROUP), slice(LANES - GROUP, LANES)
    above = dst - src <= LANES // 2
    below = src + LANES - GROUP - dst <= LANES // 2
    empty = jnp.zeros((LANES - 2 * GROUP, LANES), F32)
    main, edge = [], []
    for part in (high, table - high):
        main.append(jnp.concatenate(
            [jnp.where(above, part[first], 0.0), part[GROUP:LANES - GROUP], jnp.where(below, part[last], 0.0)],
            axis=0).astype(BF16))
        edge.append(jnp.concatenate(
            [jnp.where(above, 0.0, part[first]), empty, jnp.where(below, 0.0, part[last])],
            axis=0).astype(BF16))
    return jnp.concatenate([jnp.concatenate(main, axis=1), jnp.concatenate(edge, axis=1)], axis=0)


def blur_plane(plane, row, margin):
    height = plane.shape[0]
    table = column_table(row, margin)
    left, right = plane[:, :LANES], plane[:, LANES:]
    lane = lax.broadcasted_iota(jnp.int32, left.shape, 1)
    main = jnp.concatenate([left, right], axis=0)
    edge = jnp.concatenate(
        [jnp.where(lane < LANES // 2, right, 0.0), jnp.where(lane < LANES // 2, 0.0, left)], axis=0)
    high, low = split(jnp.concatenate([main, edge], axis=1))
    product = dot(jnp.concatenate([high, low], axis=0), table)
    rows = 2 * height
    blocks = product[:rows, :LANES] + (product[:rows, LANES:] + product[rows:, :LANES])
    return jnp.concatenate([blocks[:height], blocks[height:]], axis=1)


def row_table(base, margin, height):
    high = base.astype(BF16).astype(F32)
    low = base - high
    plane = lax.broadcasted_iota(jnp.int32, (8, LANES), 0)
    lane = lax.broadcasted_iota(jnp.int32, (8, LANES), 1)
    per_vector = LANES // height
    own = lane // height == plane % per_vector
    masks = [own & (plane // per_vector == part) for part in range(8 * height // LANES)]

    def table(part):
        strips = []
        for row in range(height):
            rolled = pltpu.roll(part, (row - margin) % LANES, 1)
            strips.append(jnp.concatenate([jnp.where(mask, rolled, 0.0) for mask in masks], axis=1))
        return jnp.concatenate(strips, axis=0).astype(BF16)

    return table(high), table(low)


def fold(square):
    side = square.shape[0]
    rest = jnp.zeros((8, LANES - 2 * side), F32)
    return jnp.concatenate(
        [jnp.concatenate([square[first:first + 8], square[first + 8:first + 16], rest], axis=1)
         for first in range(0, side, 16)], axis=0)


def unfold(folded, side):
    blocks = []
    for first in range(0, folded.shape[0], 8):
        blocks += [folded[first:first + 8, :side], folded[first:first + 8, side:2 * side]]
    return jnp.concatenate(blocks, axis=0)


def in_vmem(count):
    return [pl.BlockSpec(memory_space=pltpu.VMEM)] * count


def band_gram(w_rows):
    high, low = split(w_rows)
    rank = w_rows.shape[0]
    padded = jnp.concatenate([high, jnp.zeros((2 * LANES - rank, high.shape[1]), BF16)], axis=0)
    padded_low = jnp.concatenate([low, jnp.zeros((2 * LANES - rank, low.shape[1]), BF16)], axis=0)
    both = dot_nt(jnp.concatenate([high, low], axis=0), padded)
    return both[:rank] + (both[rank:] + dot_nt(high, padded_low))


def blur_group(step, cube_ref, kx_ref, ky_ref, xh_ref, xl_ref, margin):
    height = cube_ref.shape[1]
    halves = []
    for half in range(GROUP // 8):
        done = []
        for k in range(8 * half, 8 * half + 8):
            plane = step * GROUP + k
            done.append(blur_plane(cube_ref[plane], kx_ref[pl.ds(plane, 1), :], margin))
        high, low = split(jnp.concatenate(done, axis=0))
        rows = ky_ref[pl.ds(pl.multiple_of(step * GROUP + 8 * half, 8), 8), :]
        table_high, table_low = row_table(rows, margin, height)
        result = dot(table_high, high) + (dot(table_low, high) + dot(table_high, low))
        halves.append(result.reshape(height, 8, result.shape[1]))
    high, low = split(jnp.concatenate(halves, axis=1))
    planes_here = pl.ds(pl.multiple_of(step * GROUP, GROUP), GROUP)
    xh_ref[:, planes_here, :] = high
    xl_ref[:, planes_here, :] = low


def blur_kernel(cube_hbm, taps_x_hbm, taps_y_hbm, w_hbm, xh_ref, xl_ref, w_here_ref, keep_0, give_0, keep_1, give_1,
                cube_ref, taps_x_ref, taps_y_ref, w_ref, sems, chunk_sems, work_ref, kx_ref, ky_ref):
    taps = taps_x_ref.shape[0]
    margin = (taps - 1) // 2
    height = cube_ref.shape[1]
    rank = w_ref.shape[0]
    groups = cube_ref.shape[0] // GROUP

    def chunk(step):
        here = pl.ds(step * GROUP, GROUP)
        return pltpu.make_async_copy(cube_hbm.at[here], cube_ref.at[here], chunk_sems.at[step])

    copies = [
        pltpu.make_async_copy(taps_x_hbm, taps_x_ref, sems.at[0]),
        pltpu.make_async_copy(taps_y_hbm, taps_y_ref, sems.at[1]),
        pltpu.make_async_copy(w_hbm, w_ref, sems.at[2]),
    ]
    for copy in copies:
        copy.start()
    for step in range(groups):
        chunk(step).start()
    copies[0].wait()
    normalized_taps(taps_x_ref, True, work_ref, kx_ref)
    kx_ref[...] = pltpu.roll(kx_ref[...], LANES - margin, 1)
    copies[1].wait()
    normalized_taps(taps_y_ref, False, work_ref, ky_ref)
    per_vector = LANES // height
    place = lax.broadcasted_iota(jnp.int32, (LANES, LANES), 0) % per_vector
    values = ky_ref[...]
    placed = values
    for k in range(1, per_vector):
        placed = jnp.where(place == k, pltpu.roll(values, k * height, 1), placed)
    ky_ref[...] = placed
    copies[2].wait()

    def body(step, carry):
        chunk(step).wait()
        blur_group(step, cube_ref, kx_ref, ky_ref, xh_ref, xl_ref, margin)
        return carry

    lax.fori_loop(0, groups, body, 0)
    gram = fold(band_gram(w_ref[...])[:, :rank])
    keep_0[PIECES * rank:] = gram
    give_0[PIECES * rank:] = gram
    planes = xh_ref.shape[1]
    band = w_ref.shape[1]
    me_sp = lax.axis_index("sp")
    me_bd = lax.axis_index("bd")
    tall = height // lax.axis_size("bd")
    wide = 2 * LANES // lax.axis_size("sp")
    shift = lax.rem(band - me_sp * planes, band)
    w_here = pltpu.roll(w_ref[...], shift, 1)[:, :2 * LANES]
    w_here_ref[...] = w_here[:, :planes]
    lane = lax.broadcasted_iota(jnp.int32, w_here.shape, 1)
    w_here = jnp.where(lane < planes, w_here, 0.0)
    w_high = w_here.astype(BF16).astype(F32)
    w_both = jnp.concatenate([w_high + pltpu.roll(w_high, planes, 1), w_here - w_high], axis=0)
    w_both = w_both.astype(BF16)[:, :2 * planes]
    for chain in range(2):
        for rel_bd in (1, 3, 0, 2):
            first_row = lax.bitwise_xor(me_bd, rel_bd) * tall + 4 * chain
            sums = []
            for row in range(4):
                image = jnp.concatenate([xh_ref[first_row + row], xl_ref[first_row + row]], axis=0)
                both = dot(w_both, image)
                sums.append(both[:rank] + both[rank:])
            refs = ((keep_0, give_0), (keep_1, give_1))[chain]
            for column in range(2):
                pieces = exchange_blocks(
                    [value[:, column * LANES:(column + 1) * LANES] for value in sums], wide)
                for k in range(4):
                    rel_sp = lax.bitwise_xor(me_sp, column * 4 + k)
                    side = 3 - rel_sp % 2 if rel_bd // 2 else rel_sp % 2
                    first = pl.multiple_of((side * 4 + rel_sp // 2) * rank, 8)
                    refs[rel_bd % 2][pl.ds(first, rank)] = pieces[k]


def blur_call(cube, taps_x, taps_y, w_rows):
    planes, height, length = cube.shape
    rank = w_rows.shape[0]
    first = jax.ShapeDtypeStruct((PIECES * rank + FOLDED, LANES), F32)
    second = jax.ShapeDtypeStruct((PIECES * rank, LANES), F32)
    image = (height, planes, length)
    mine = jax.ShapeDtypeStruct((rank, planes), F32)
    in_hbm = [pltpu.with_memory_space_constraint(value, pltpu.HBM) for value in (cube, taps_x, taps_y, w_rows)]
    return pl.pallas_call(
        blur_kernel,
        out_shape=[jax.ShapeDtypeStruct(image, BF16)] * 2 + [mine, first, first, second, second],
        in_specs=[pl.BlockSpec(memory_space=pltpu.HBM)] * 4,
        out_specs=in_vmem(7),
        scratch_shapes=[pltpu.VMEM(value.shape, F32) for value in (cube, taps_x, taps_y, w_rows)]
        + [pltpu.SemaphoreType.DMA((3,)), pltpu.SemaphoreType.DMA((planes // GROUP,))]
        + [pltpu.VMEM((LANES, LANES), F32)] * 3,
        compiler_params=pltpu.CompilerParams(vmem_limit_bytes=VMEM_LIMIT),
    )(*in_hbm)


def ratio_kernel(mine_ref, other_ref, h_ref, out_ref):
    tall = h_ref.shape[0] // lax.axis_size("bd")
    first = pl.multiple_of(lax.axis_index("bd") * tall, tall)
    here = h_ref[pl.ds(first, tall)]
    here = jnp.transpose(here.reshape(-1, here.shape[2]))
    rows = mine_ref.shape[0]
    gram = unfold(mine_ref[rows - FOLDED:rows] + other_ref[rows - FOLDED:rows], here.shape[0])
    out_ref[...] = here / dot_exact(gram, here)


def ratio_call(mine, other, h_columns):
    piece = jax.ShapeDtypeStruct((h_columns.shape[2], 2 * LANES), F32)
    return pl.pallas_call(
        ratio_kernel,
        out_shape=piece,
        in_specs=in_vmem(3),
        compiler_params=pltpu.CompilerParams(vmem_limit_bytes=VMEM_LIMIT),
    )(mine, other, h_columns)


def accumulate(xh_ref, xl_ref, part_refs, all_ref, chain, total):
    height, planes, _ = xh_ref.shape
    me_sp = lax.axis_index("sp")
    me_bd = lax.axis_index("bd")
    bands = lax.axis_size("bd")
    pieces = lax.axis_size("sp")
    tall = height // bands
    wide = 2 * LANES // pieces
    for slot, part_ref in enumerate(part_refs):
        rel_bd = slot // 4 + 2 * ((slot // 2) % 2)
        for inner in range(4):
            rel_sp = slot % 2 + 2 * inner
            owner = lax.bitwise_xor(me_bd, rel_bd) * pieces + lax.bitwise_xor(me_sp, rel_sp)
            all_ref[owner] = part_ref[inner]
    for part in range(bands):
        first_row = part * tall + 4 * chain
        halves = [
            exchange_blocks([all_ref[part * pieces + column * 4 + k] for k in range(4)], wide)
            for column in range(2)]
        rows = jnp.concatenate([halves[column][row] for row in range(4) for column in range(2)], axis=1)
        high, low = split(rows)
        here = jnp.concatenate([high, low], axis=0)
        image = [
            jnp.concatenate([ref[first_row + row] for row in range(4)], axis=1) for ref in (xh_ref, xl_ref)]
        total = total + dot_nt(jnp.concatenate(image + [here], axis=0), here)
    return total


def first_kernel(xh_ref, xl_ref, *rest):
    part_refs = rest[:8]
    total_out, all_ref = rest[8:]
    total_out[...] = accumulate(xh_ref, xl_ref, part_refs, all_ref, 0, jnp.zeros(total_out.shape, F32))


def first_call(x_high, x_low, parts):
    _, planes, _ = x_high.shape
    rank = parts[0].shape[1]
    return pl.pallas_call(
        first_kernel,
        out_shape=jax.ShapeDtypeStruct((2 * (planes + rank), 2 * rank), F32),
        in_specs=in_vmem(2 + len(parts)),
        scratch_shapes=[pltpu.VMEM((32, rank, LANES), F32)],
        compiler_params=pltpu.CompilerParams(vmem_limit_bytes=VMEM_LIMIT),
    )(x_high, x_low, *parts)


def second_kernel(xh_ref, xl_ref, w_ref, total_ref, *rest):
    part_refs = rest[:8]
    w_out, all_ref = rest[8:]
    planes = xh_ref.shape[1]
    rank = w_ref.shape[0]
    total = accumulate(xh_ref, xl_ref, part_refs, all_ref, 1, total_ref[...])
    numer = total[:planes, :rank] + (total[:planes, rank:] + total[planes:2 * planes, :rank])
    gram = total[2 * planes:]
    gram = gram[:rank, :rank] + (gram[:rank, rank:] + gram[rank:, :rank])
    w_here = w_ref[...]
    w_out[...] = w_here * jnp.transpose(numer) / dot_exact(gram, w_here)


def second_call(x_high, x_low, w_here, total, parts):
    rank = w_here.shape[0]
    return pl.pallas_call(
        second_kernel,
        out_shape=jax.ShapeDtypeStruct(w_here.shape, F32),
        in_specs=in_vmem(4 + len(parts)),
        scratch_shapes=[pltpu.VMEM((32, rank, LANES), F32)],
        compiler_params=pltpu.CompilerParams(vmem_limit_bytes=VMEM_LIMIT),
    )(x_high, x_low, w_here, total, *parts)


def place_h_kernel(*refs):
    h_out = refs[-1]
    me_bd = lax.axis_index("bd")
    tall = h_out.shape[0] // lax.axis_size("bd")
    for chain in range(2):
        for rel_bd in range(4):
            piece = refs[4 * chain + rel_bd][0]
            first = lax.bitwise_xor(me_bd, rel_bd) * tall + 4 * chain
            h_out[pl.ds(first, 4)] = jnp.transpose(piece).reshape((4,) + h_out.shape[1:])


def place_h_call(parts, shape):
    return pl.pallas_call(
        place_h_kernel,
        out_shape=jax.ShapeDtypeStruct(shape, F32),
        in_specs=in_vmem(len(parts)),
        compiler_params=pltpu.CompilerParams(vmem_limit_bytes=VMEM_LIMIT),
    )(*parts)


def gather_w_kernel(*refs):
    part_refs = refs[:-2]
    out_ref, all_ref = refs[-2:]
    planes = out_ref.shape[1] // 8
    me_sp = lax.axis_index("sp")
    rel = 0
    for part_ref in part_refs:
        for inner in range(part_ref.shape[0]):
            all_ref[lax.bitwise_xor(me_sp, RING[rel]), :, 0:planes] = part_ref[inner]
            rel += 1
    for owner in range(8):
        out_ref[:, owner * planes:(owner + 1) * planes] = all_ref[owner][:, :planes]


RING = (0, 1, 2, 3, 4, 5, 6, 7)


def gather_w_call(parts):
    _, rank, planes = parts[0].shape
    return pl.pallas_call(
        gather_w_kernel,
        out_shape=jax.ShapeDtypeStruct((rank, planes * 8), F32),
        in_specs=in_vmem(len(parts)),
        scratch_shapes=[pltpu.VMEM((8, rank, LANES), F32)],
        compiler_params=pltpu.CompilerParams(vmem_limit_bytes=VMEM_LIMIT),
    )(*parts)


def send(value, mask_sp, mask_bd):
    bands = lax.axis_size("bd")
    pieces = lax.axis_size("sp")
    pairs = []
    for s in range(pieces):
        for b in range(bands):
            pairs.append((s * bands + b, (s ^ mask_sp) * bands + (b ^ mask_bd)))
    return lax.ppermute(value, ("sp", "bd"), pairs)


def around(values):
    return [send(values[k], k % 2, 2 * (k // 2)) for k in range(1, 4)]


def local(cube, taps_x, taps_y, factor_w, factor_h):
    w_rows = jnp.transpose(factor_w[0])
    taps_x = jnp.transpose(taps_x, (2, 0, 1))
    taps_y = jnp.transpose(taps_y, (2, 0, 1))
    h_columns = jnp.transpose(factor_h, (1, 2, 0))
    rank = w_rows.shape[0]
    x_high, x_low, w_here, keep_0, give_0, keep_1, give_1 = blur_call(cube[0], taps_x, taps_y, w_rows)
    chains = []
    for keep, give in ((keep_0, give_0), (keep_1, give_1)):
        taken = send(give, 0, 1)
        bounds = [place * 4 * rank for place in (0, 1, 3, 2)]
        sides = []
        for first in bounds:
            last = keep.shape[0] if first == max(bounds) else first + 4 * rank
            sides.append(keep[first:last] + taken[first:last])
        chains.append((sides, around(sides)))
    ratio = ratio_call(chains[0][0][2], chains[0][1][1], h_columns)
    line = []
    for k in range(4):
        part = slice(k * rank, (k + 1) * rank)
        line.append(jnp.concatenate(
            [(sides[0][part] + others[0][part]) + (others[1][part] + others[2][part]) for sides, others in chains],
            axis=1))
    line = [line[0]] + [send(line[k], 2 * k, 0) for k in (3, 2, 1)]
    h_piece = ratio * ((line[0] + line[1]) + (line[2] + line[3]))
    h_line = [h_piece] + [send(h_piece, 2 * k, 0) for k in range(1, 4)]
    chains = []
    for first in (0, LANES):
        mine = jnp.stack([value[:, first:first + LANES] for value in h_line])
        chains.append([mine] + around([mine] * 4))
    first_parts = chains[0] + [send(value, 0, 1) for value in chains[0]]
    total = first_call(x_high, x_low, first_parts)
    second_parts = chains[1] + [send(value, 0, 1) for value in chains[1]]
    w_piece = second_call(x_high, x_low, w_here, total, second_parts)
    own = [parts[k] for parts in (first_parts, second_parts) for k in (0, 4, 2, 6)]
    h_next = place_h_call(own, h_columns.shape)
    w_pair = jnp.stack([w_piece, send(w_piece, 1, 0)])
    w_next = gather_w_call([w_pair] + [send(w_pair, 2 * k, 0) for k in range(1, 4)])
    return jnp.transpose(w_next)[None], jnp.transpose(h_next, (2, 0, 1))


def normalized(kernel):
    return kernel / jnp.sum(kernel, axis=-1, keepdims=True)


def band_weights(kernel, size_in, size_out, offset):
    tap_count = kernel.shape[-1]
    in_index = lax.broadcasted_iota(jnp.int32, (size_in, size_out, tap_count), 0)
    out_index = lax.broadcasted_iota(jnp.int32, (size_in, size_out, tap_count), 1)
    tap_index = lax.broadcasted_iota(jnp.int32, (size_in, size_out, tap_count), 2)
    select = (tap_index == in_index - out_index + offset).astype(jnp.float32)
    return jnp.einsum("pk,iok->pio", kernel, select, precision=lax.Precision.HIGHEST)


def blur_rows(planes, kernel_y):
    margin = (kernel_y.shape[-1] - 1) // 2
    height = planes.shape[1]
    band_table = band_weights(kernel_y, height, height, margin)
    return jnp.einsum("piz,pio->poz", planes, band_table, precision=lax.Precision.HIGHEST)


def blur_columns(planes, kernel_x):
    margin = (kernel_x.shape[-1] - 1) // 2
    count, height, length = planes.shape
    blocks = planes.reshape(count, height, length // 128, 128)
    empty = jnp.zeros((count, height, 1, 128), jnp.float32)
    left_block = jnp.concatenate([empty, blocks[:, :, :-1]], axis=2)
    right_block = jnp.concatenate([blocks[:, :, 1:], empty], axis=2)
    window = jnp.concatenate([left_block, blocks, right_block], axis=3)
    band_table = band_weights(kernel_x, 384, 128, margin - 128)
    result = jnp.einsum("pybi,pio->pybo", window, band_table, precision=lax.Precision.HIGHEST)
    return result.reshape(count, height, length)


def local_any(cube, taps_x, taps_y, factor_w, factor_h):
    highest = lax.Precision.HIGHEST
    kernel_x = normalized(taps_x[0])
    kernel_y = normalized(taps_y[0])
    rows_done = blur_rows(cube[0], kernel_y)
    w_band = factor_w[0]
    blurred = blur_columns(rows_done, kernel_x)[None]
    moved = lax.all_to_all(blurred, "sp", split_axis=3, concat_axis=1, tiled=True)
    numer_part = jnp.einsum("lr,plyx->pryx", w_band, moved, precision=highest)
    gram_part = jnp.dot(w_band.T, w_band, precision=highest)
    numer_h, gram_w = lax.psum((numer_part[0], gram_part), "bd")
    h_next = factor_h * numer_h / jnp.einsum("rq,qyx->ryx", gram_w, factor_h, precision=highest)
    x_band = moved[0]
    gram_h_part = jnp.einsum("ryx,qyx->rq", h_next, h_next, precision=highest)
    numer_w_part = jnp.einsum("lyx,ryx->lr", x_band, h_next, precision=highest)
    numer_w, gram_h = lax.psum((numer_w_part, gram_h_part), "sp")
    w_next = w_band * numer_w / jnp.dot(w_band, gram_h, precision=highest)
    return (w_next[None], h_next)


def solution(mesh):
    in_specs = (
        P("bd", "sp", None, None),
        P("bd", "sp", None),
        P("bd", "sp", None),
        P("bd", None, None),
        P(None, None, "sp"),
    )
    out_specs = (P("bd", None, None), P(None, None, "sp"))

    def body(cube, *rest):
        suits = lax.axis_size("sp") == 8 and lax.axis_size("bd") == 4 and cube.shape[1] % GROUP == 0
        return (local if suits else local_any)(cube, *rest)

    return jax.shard_map(body, mesh=mesh, in_specs=in_specs, out_specs=out_specs, check_vma=False)
```

```python
import functools

import jax
import jax.numpy as jnp
from jax import lax
from jax.experimental import pallas as pl
from jax.experimental.pallas import tpu as pltpu
from jax.sharding import PartitionSpec as P

F32 = jnp.float32
BF16 = jnp.bfloat16
LANES = 128
GROUP = 16
PIECES = 16
FOLDED = 24
VMEM_LIMIT = 48 * 1024 * 1024


def split(value):
    high = value.astype(BF16)
    low = (value - high.astype(F32)).astype(BF16)
    return high, low


def dot(left, right):
    return lax.dot_general(left, right, (((1,), (0,)), ((), ())), preferred_element_type=F32)


def dot_nt(left, right):
    return lax.dot_general(left, right, (((1,), (1,)), ((), ())), preferred_element_type=F32)


def dot_exact(left, right):
    return lax.dot_general(
        left, right, (((1,), (0,)), ((), ())),
        precision=lax.Precision.HIGHEST, preferred_element_type=F32,
    )


def exchange_blocks(rows, block):
    lane = lax.broadcasted_iota(jnp.int32, rows[0].shape, 1)
    first_half = lane < 2 * block
    even = (lane // block) % 2 == 0
    v0, v1, v2, v3 = rows
    u0 = jnp.where(first_half, v0, pltpu.roll(v2, 2 * block, 1))
    u2 = jnp.where(first_half, pltpu.roll(v0, 2 * block, 1), v2)
    u1 = jnp.where(first_half, v1, pltpu.roll(v3, 2 * block, 1))
    u3 = jnp.where(first_half, pltpu.roll(v1, 2 * block, 1), v3)
    w0 = jnp.where(even, u0, pltpu.roll(u1, block, 1))
    w1 = jnp.where(even, pltpu.roll(u0, 3 * block, 1), u1)
    w2 = jnp.where(even, u2, pltpu.roll(u3, block, 1))
    w3 = jnp.where(even, pltpu.roll(u2, 3 * block, 1), u3)
    return w0, w1, w2, w3


def normalized_taps(taps_ref, reverse, work_ref, out_ref):
    taps = taps_ref.shape[0]
    planes = taps_ref.shape[2]
    work_ref[...] = jnp.zeros_like(work_ref)
    for tap in range(taps):
        row = taps - 1 - tap if reverse else tap
        work_ref[row:row + 1, 0:planes] = taps_ref[tap]
    values = work_ref[...]
    total = jnp.sum(values, axis=0, keepdims=True)
    total = jnp.where(total == 0.0, 1.0, total)
    out_ref[...] = jnp.transpose(values / total)


def blur_plane(plane, row, taps):
    margin = (taps - 1) // 2
    step = LANES - 2 * margin
    height = plane.shape[0]
    table = pltpu.roll(jnp.broadcast_to(row, (LANES, LANES)), 0, 1, stride=1, stride_axis=0)
    table = jnp.concatenate(split(table), axis=1)
    left, right = plane[:, :LANES], plane[:, LANES:]
    lane = lax.broadcasted_iota(jnp.int32, left.shape, 1)
    windows = [
        jnp.where(lane >= margin, pltpu.roll(left, margin, 1), 0.0),
        pltpu.roll(jnp.where(lane < LANES - 3 * margin, right, left), 3 * margin, 1),
        jnp.where(lane < 5 * margin, pltpu.roll(right, 5 * margin, 1), 0.0),
    ]
    image = jnp.concatenate(split(jnp.concatenate(windows, axis=0)), axis=1)
    product = dot(image, jnp.concatenate([table, table], axis=0))
    blocks = product[:, :LANES] + product[:, LANES:]
    first, second, third = [blocks[k * height:(k + 1) * height] for k in range(3)]
    second = pltpu.roll(second, step, 1)
    third = pltpu.roll(third, 2 * step - LANES, 1)
    return jnp.concatenate(
        [jnp.where(lane < step, first, second), jnp.where(lane < 2 * step - LANES, second, third)], axis=1)


def blur_rows_of(images, rows, margin):
    height = images[0].shape[0]
    sub = lax.broadcasted_iota(jnp.int32, (8, LANES), 0)
    lane = lax.broadcasted_iota(jnp.int32, (8, LANES), 1)
    lower = sub < 4
    own = lane // height == sub % 4
    moved = pltpu.roll(pltpu.roll(rows, 4, 0), 1, 1)
    results = []
    for group, base in ((0, jnp.where(lower, rows, moved)), (1, jnp.where(lower, moved, rows))):
        high = base.astype(BF16).astype(F32)
        strips = [
            jnp.where(own, pltpu.roll(part, (2 * pair - margin) % LANES, 1), 0.0)
            for part in (high, base - high) for pair in range(height // 2)]
        table = jnp.concatenate(strips, axis=0).astype(BF16)
        table = jnp.concatenate([table, table], axis=1)
        image = jnp.concatenate(split(jnp.concatenate(images[4 * group:4 * group + 4], axis=0)), axis=0)
        product = dot(table, image)
        half = product.shape[0] // 2
        results.append(product[:half] + product[half:])
    lower = lax.broadcasted_iota(jnp.int32, (8, results[0].shape[1]), 0) < 4
    out = []
    for pair in range(height // 2):
        here = slice(8 * pair, 8 * pair + 8)
        one, two = results[0][here], results[1][here]
        out.append(jnp.where(lower, one, two))
        out.append(pltpu.roll(jnp.where(lower, two, one), 4, 0))
    return jnp.concatenate(out, axis=0).reshape(height, 8, results[0].shape[1])


def fold(square):
    side = square.shape[0]
    rest = jnp.zeros((8, LANES - 2 * side), F32)
    return jnp.concatenate(
        [jnp.concatenate([square[first:first + 8], square[first + 8:first + 16], rest], axis=1)
         for first in range(0, side, 16)], axis=0)


def unfold(folded, side):
    blocks = []
    for first in range(0, folded.shape[0], 8):
        blocks += [folded[first:first + 8, :side], folded[first:first + 8, side:2 * side]]
    return jnp.concatenate(blocks, axis=0)


def in_vmem(count):
    return [pl.BlockSpec(memory_space=pltpu.VMEM)] * count


def band_gram(w_rows):
    high, low = split(w_rows)
    rank = w_rows.shape[0]
    padded = jnp.concatenate([high, jnp.zeros((2 * LANES - rank, high.shape[1]), BF16)], axis=0)
    padded_low = jnp.concatenate([low, jnp.zeros((2 * LANES - rank, low.shape[1]), BF16)], axis=0)
    both = dot_nt(jnp.concatenate([high, low], axis=0), padded)
    return both[:rank] + (both[rank:] + dot_nt(high, padded_low))


def blur_group(step, cube_ref, kx_ref, ky_ref, xh_ref, xl_ref, taps):
    halves = []
    for half in range(GROUP // 8):
        done = []
        for k in range(8 * half, 8 * half + 8):
            plane = step * GROUP + k
            done.append(blur_plane(cube_ref[plane], kx_ref[pl.ds(plane, 1), :], taps))
        rows = ky_ref[pl.ds(pl.multiple_of(step * GROUP + 8 * half, 8), 8), :]
        halves.append(blur_rows_of(done, rows, (taps - 1) // 2))
    high, low = split(jnp.concatenate(halves, axis=1))
    planes_here = pl.ds(pl.multiple_of(step * GROUP, GROUP), GROUP)
    xh_ref[:, planes_here, :] = high
    xl_ref[:, planes_here, :] = low


def blur_kernel(cube_hbm, taps_x_hbm, taps_y_hbm, w_hbm, xh_ref, xl_ref, w_here_ref, keep_0, give_0, keep_1, give_1,
                cube_ref, taps_x_ref, taps_y_ref, w_ref, sems, chunk_sems, work_ref, kx_ref, ky_ref):
    taps = taps_x_ref.shape[0]
    margin = (taps - 1) // 2
    height = cube_ref.shape[1]
    rank = w_ref.shape[0]
    groups = cube_ref.shape[0] // GROUP

    def chunk(step):
        here = pl.ds(step * GROUP, GROUP)
        return pltpu.make_async_copy(cube_hbm.at[here], cube_ref.at[here], chunk_sems.at[step])

    copies = [
        pltpu.make_async_copy(taps_x_hbm, taps_x_ref, sems.at[0]),
        pltpu.make_async_copy(taps_y_hbm, taps_y_ref, sems.at[1]),
        pltpu.make_async_copy(w_hbm, w_ref, sems.at[2]),
    ]
    for copy in copies:
        copy.start()
    for step in range(groups):
        chunk(step).start()
    copies[0].wait()
    normalized_taps(taps_x_ref, True, work_ref, kx_ref)
    kx_ref[...] = pltpu.roll(kx_ref[...], LANES - 2 * margin, 1)
    copies[1].wait()
    normalized_taps(taps_y_ref, False, work_ref, ky_ref)
    per_vector = LANES // height
    place = lax.broadcasted_iota(jnp.int32, (LANES, LANES), 0) % per_vector
    values = ky_ref[...]
    placed = values
    for k in range(1, per_vector):
        placed = jnp.where(place == k, pltpu.roll(values, k * height, 1), placed)
    ky_ref[...] = placed
    copies[2].wait()

    def body(step, carry):
        chunk(step).wait()
        blur_group(step, cube_ref, kx_ref, ky_ref, xh_ref, xl_ref, taps)
        return carry

    lax.fori_loop(0, groups, body, 0)
    gram = fold(band_gram(w_ref[...])[:, :rank])
    keep_0[PIECES * rank:] = gram
    give_0[PIECES * rank:] = gram
    planes = xh_ref.shape[1]
    band = w_ref.shape[1]
    me_sp = lax.axis_index("sp")
    me_bd = lax.axis_index("bd")
    tall = height // lax.axis_size("bd")
    wide = 2 * LANES // lax.axis_size("sp")
    shift = lax.rem(band - me_sp * planes, band)
    w_here = pltpu.roll(w_ref[...], shift, 1)[:, :2 * LANES]
    w_here_ref[...] = w_here[:, :planes]
    lane = lax.broadcasted_iota(jnp.int32, w_here.shape, 1)
    w_here = jnp.where(lane < planes, w_here, 0.0)
    w_high = w_here.astype(BF16).astype(F32)
    w_both = jnp.concatenate([w_high + pltpu.roll(w_high, planes, 1), w_here - w_high], axis=0)
    w_both = w_both.astype(BF16)[:, :2 * planes]
    for chain in range(2):
        for rel_bd in (1, 3, 0, 2):
            first_row = lax.bitwise_xor(me_bd, rel_bd) * tall + 4 * chain
            sums = []
            for row in range(4):
                image = jnp.concatenate([xh_ref[first_row + row], xl_ref[first_row + row]], axis=0)
                both = dot(w_both, image)
                sums.append(both[:rank] + both[rank:])
            refs = ((keep_0, give_0), (keep_1, give_1))[chain]
            for column in range(2):
                pieces = exchange_blocks(
                    [value[:, column * LANES:(column + 1) * LANES] for value in sums], wide)
                for k in range(4):
                    rel_sp = lax.bitwise_xor(me_sp, column * 4 + k)
                    side = 3 - rel_sp % 2 if rel_bd // 2 else rel_sp % 2
                    first = pl.multiple_of((side * 4 + rel_sp // 2) * rank, 8)
                    refs[rel_bd % 2][pl.ds(first, rank)] = pieces[k]


def blur_call(cube, taps_x, taps_y, w_rows):
    planes, height, length = cube.shape
    rank = w_rows.shape[0]
    first = jax.ShapeDtypeStruct((PIECES * rank + FOLDED, LANES), F32)
    second = jax.ShapeDtypeStruct((PIECES * rank, LANES), F32)
    image = (height, planes, length)
    mine = jax.ShapeDtypeStruct((rank, planes), F32)
    in_hbm = [pltpu.with_memory_space_constraint(value, pltpu.HBM) for value in (cube, taps_x, taps_y, w_rows)]
    return pl.pallas_call(
        blur_kernel,
        out_shape=[jax.ShapeDtypeStruct(image, BF16)] * 2 + [mine, first, first, second, second],
        in_specs=[pl.BlockSpec(memory_space=pltpu.HBM)] * 4,
        out_specs=in_vmem(7),
        scratch_shapes=[pltpu.VMEM(value.shape, F32) for value in (cube, taps_x, taps_y, w_rows)]
        + [pltpu.SemaphoreType.DMA((3,)), pltpu.SemaphoreType.DMA((planes // GROUP,))]
        + [pltpu.VMEM((LANES, LANES), F32)] * 3,
        compiler_params=pltpu.CompilerParams(vmem_limit_bytes=VMEM_LIMIT),
    )(*in_hbm)


def ratio_kernel(mine_ref, other_ref, h_ref, out_ref):
    tall = h_ref.shape[0] // lax.axis_size("bd")
    first = pl.multiple_of(lax.axis_index("bd") * tall, tall)
    here = h_ref[pl.ds(first, tall)]
    here = jnp.transpose(here.reshape(-1, here.shape[2]))
    rows = mine_ref.shape[0]
    gram = unfold(mine_ref[rows - FOLDED:rows] + other_ref[rows - FOLDED:rows], here.shape[0])
    out_ref[...] = here / dot_exact(gram, here)


def ratio_call(mine, other, h_columns):
    piece = jax.ShapeDtypeStruct((h_columns.shape[2], 2 * LANES), F32)
    return pl.pallas_call(
        ratio_kernel,
        out_shape=piece,
        in_specs=in_vmem(3),
        compiler_params=pltpu.CompilerParams(vmem_limit_bytes=VMEM_LIMIT),
    )(mine, other, h_columns)


def accumulate(xh_ref, xl_ref, part_refs, all_ref, chain, total):
    height, planes, _ = xh_ref.shape
    me_sp = lax.axis_index("sp")
    me_bd = lax.axis_index("bd")
    bands = lax.axis_size("bd")
    pieces = lax.axis_size("sp")
    tall = height // bands
    wide = 2 * LANES // pieces
    for slot, part_ref in enumerate(part_refs):
        rel_bd = slot // 4 + 2 * ((slot // 2) % 2)
        for inner in range(4):
            rel_sp = slot % 2 + 2 * inner
            owner = lax.bitwise_xor(me_bd, rel_bd) * pieces + lax.bitwise_xor(me_sp, rel_sp)
            all_ref[owner] = part_ref[inner]
    for part in range(bands):
        first_row = part * tall + 4 * chain
        halves = [
            exchange_blocks([all_ref[part * pieces + column * 4 + k] for k in range(4)], wide)
            for column in range(2)]
        rows = jnp.concatenate([halves[column][row] for row in range(4) for column in range(2)], axis=1)
        high, low = split(rows)
        here = jnp.concatenate([high, low], axis=0)
        image = [
            jnp.concatenate([ref[first_row + row] for row in range(4)], axis=1) for ref in (xh_ref, xl_ref)]
        total = total + dot_nt(jnp.concatenate(image + [here], axis=0), here)
    return total


def first_kernel(xh_ref, xl_ref, *rest):
    part_refs = rest[:8]
    total_out, all_ref = rest[8:]
    total_out[...] = accumulate(xh_ref, xl_ref, part_refs, all_ref, 0, jnp.zeros(total_out.shape, F32))


def first_call(x_high, x_low, parts):
    _, planes, _ = x_high.shape
    rank = parts[0].shape[1]
    return pl.pallas_call(
        first_kernel,
        out_shape=jax.ShapeDtypeStruct((2 * (planes + rank), 2 * rank), F32),
        in_specs=in_vmem(2 + len(parts)),
        scratch_shapes=[pltpu.VMEM((32, rank, LANES), F32)],
        compiler_params=pltpu.CompilerParams(vmem_limit_bytes=VMEM_LIMIT),
    )(x_high, x_low, *parts)


def second_kernel(xh_ref, xl_ref, w_ref, total_ref, *rest):
    part_refs = rest[:8]
    w_out, all_ref = rest[8:]
    planes = xh_ref.shape[1]
    rank = w_ref.shape[0]
    total = accumulate(xh_ref, xl_ref, part_refs, all_ref, 1, total_ref[...])
    numer = total[:planes, :rank] + (total[:planes, rank:] + total[planes:2 * planes, :rank])
    gram = total[2 * planes:]
    gram = gram[:rank, :rank] + (gram[:rank, rank:] + gram[rank:, :rank])
    w_here = w_ref[...]
    w_out[...] = w_here * jnp.transpose(numer) / dot_exact(gram, w_here)


def second_call(x_high, x_low, w_here, total, parts):
    rank = w_here.shape[0]
    return pl.pallas_call(
        second_kernel,
        out_shape=jax.ShapeDtypeStruct(w_here.shape, F32),
        in_specs=in_vmem(4 + len(parts)),
        scratch_shapes=[pltpu.VMEM((32, rank, LANES), F32)],
        compiler_params=pltpu.CompilerParams(vmem_limit_bytes=VMEM_LIMIT),
    )(x_high, x_low, w_here, total, *parts)


def place_h_kernel(*refs):
    h_out = refs[-1]
    me_bd = lax.axis_index("bd")
    tall = h_out.shape[0] // lax.axis_size("bd")
    for chain in range(2):
        for rel_bd in range(4):
            piece = refs[4 * chain + rel_bd][0]
            first = lax.bitwise_xor(me_bd, rel_bd) * tall + 4 * chain
            h_out[pl.ds(first, 4)] = jnp.transpose(piece).reshape((4,) + h_out.shape[1:])


def place_h_call(parts, shape):
    return pl.pallas_call(
        place_h_kernel,
        out_shape=jax.ShapeDtypeStruct(shape, F32),
        in_specs=in_vmem(len(parts)),
        compiler_params=pltpu.CompilerParams(vmem_limit_bytes=VMEM_LIMIT),
    )(*parts)


def gather_w_kernel(*refs):
    part_refs = refs[:-2]
    out_ref, all_ref = refs[-2:]
    planes = out_ref.shape[1] // 8
    me_sp = lax.axis_index("sp")
    rel = 0
    for part_ref in part_refs:
        for inner in range(part_ref.shape[0]):
            all_ref[lax.bitwise_xor(me_sp, RING[rel]), :, 0:planes] = part_ref[inner]
            rel += 1
    for owner in range(8):
        out_ref[:, owner * planes:(owner + 1) * planes] = all_ref[owner][:, :planes]


RING = (0, 1, 2, 3, 4, 5, 6, 7)


def gather_w_call(parts):
    _, rank, planes = parts[0].shape
    return pl.pallas_call(
        gather_w_kernel,
        out_shape=jax.ShapeDtypeStruct((rank, planes * 8), F32),
        in_specs=in_vmem(len(parts)),
        scratch_shapes=[pltpu.VMEM((8, rank, LANES), F32)],
        compiler_params=pltpu.CompilerParams(vmem_limit_bytes=VMEM_LIMIT),
    )(*parts)


def send(value, mask_sp, mask_bd):
    bands = lax.axis_size("bd")
    pieces = lax.axis_size("sp")
    pairs = []
    for s in range(pieces):
        for b in range(bands):
            pairs.append((s * bands + b, (s ^ mask_sp) * bands + (b ^ mask_bd)))
    return lax.ppermute(value, ("sp", "bd"), pairs)


def around(values):
    return [send(values[k], k % 2, 2 * (k // 2)) for k in range(1, 4)]


def local(cube, taps_x, taps_y, factor_w, factor_h):
    w_rows = jnp.transpose(factor_w[0])
    taps_x = jnp.transpose(taps_x, (2, 0, 1))
    taps_y = jnp.transpose(taps_y, (2, 0, 1))
    h_columns = jnp.transpose(factor_h, (1, 2, 0))
    rank = w_rows.shape[0]
    x_high, x_low, w_here, keep_0, give_0, keep_1, give_1 = blur_call(cube[0], taps_x, taps_y, w_rows)
    chains = []
    for keep, give in ((keep_0, give_0), (keep_1, give_1)):
        taken = send(give, 0, 1)
        bounds = [place * 4 * rank for place in (0, 1, 3, 2)]
        sides = []
        for first in bounds:
            last = keep.shape[0] if first == max(bounds) else first + 4 * rank
            sides.append(keep[first:last] + taken[first:last])
        chains.append((sides, around(sides)))
    ratio = ratio_call(chains[0][0][2], chains[0][1][1], h_columns)
    line = []
    for k in range(4):
        part = slice(k * rank, (k + 1) * rank)
        line.append(jnp.concatenate(
            [(sides[0][part] + others[0][part]) + (others[1][part] + others[2][part]) for sides, others in chains],
            axis=1))
    line = [line[0]] + [send(line[k], 2 * k, 0) for k in (3, 2, 1)]
    h_piece = ratio * ((line[0] + line[1]) + (line[2] + line[3]))
    h_line = [h_piece] + [send(h_piece, 2 * k, 0) for k in range(1, 4)]
    chains = []
    for first in (0, LANES):
        mine = jnp.stack([value[:, first:first + LANES] for value in h_line])
        chains.append([mine] + around([mine] * 4))
    first_parts = chains[0] + [send(value, 0, 1) for value in chains[0]]
    total = first_call(x_high, x_low, first_parts)
    second_parts = chains[1] + [send(value, 0, 1) for value in chains[1]]
    w_piece = second_call(x_high, x_low, w_here, total, second_parts)
    own = [parts[k] for parts in (first_parts, second_parts) for k in (0, 4, 2, 6)]
    h_next = place_h_call(own, h_columns.shape)
    w_pair = jnp.stack([w_piece, send(w_piece, 1, 0)])
    w_next = gather_w_call([w_pair] + [send(w_pair, 2 * k, 0) for k in range(1, 4)])
    return jnp.transpose(w_next)[None], jnp.transpose(h_next, (2, 0, 1))


def normalized(kernel):
    return kernel / jnp.sum(kernel, axis=-1, keepdims=True)


def band_weights(kernel, size_in, size_out, offset):
    tap_count = kernel.shape[-1]
    in_index = lax.broadcasted_iota(jnp.int32, (size_in, size_out, tap_count), 0)
    out_index = lax.broadcasted_iota(jnp.int32, (size_in, size_out, tap_count), 1)
    tap_index = lax.broadcasted_iota(jnp.int32, (size_in, size_out, tap_count), 2)
    select = (tap_index == in_index - out_index + offset).astype(jnp.float32)
    return jnp.einsum("pk,iok->pio", kernel, select, precision=lax.Precision.HIGHEST)


def blur_rows(planes, kernel_y):
    margin = (kernel_y.shape[-1] - 1) // 2
    height = planes.shape[1]
    band_table = band_weights(kernel_y, height, height, margin)
    return jnp.einsum("piz,pio->poz", planes, band_table, precision=lax.Precision.HIGHEST)


def blur_columns(planes, kernel_x):
    margin = (kernel_x.shape[-1] - 1) // 2
    count, height, length = planes.shape
    blocks = planes.reshape(count, height, length // 128, 128)
    empty = jnp.zeros((count, height, 1, 128), jnp.float32)
    left_block = jnp.concatenate([empty, blocks[:, :, :-1]], axis=2)
    right_block = jnp.concatenate([blocks[:, :, 1:], empty], axis=2)
    window = jnp.concatenate([left_block, blocks, right_block], axis=3)
    band_table = band_weights(kernel_x, 384, 128, margin - 128)
    result = jnp.einsum("pybi,pio->pybo", window, band_table, precision=lax.Precision.HIGHEST)
    return result.reshape(count, height, length)


def local_any(cube, taps_x, taps_y, factor_w, factor_h):
    highest = lax.Precision.HIGHEST
    kernel_x = normalized(taps_x[0])
    kernel_y = normalized(taps_y[0])
    rows_done = blur_rows(cube[0], kernel_y)
    w_band = factor_w[0]
    blurred = blur_columns(rows_done, kernel_x)[None]
    moved = lax.all_to_all(blurred, "sp", split_axis=3, concat_axis=1, tiled=True)
    numer_part = jnp.einsum("lr,plyx->pryx", w_band, moved, precision=highest)
    gram_part = jnp.dot(w_band.T, w_band, precision=highest)
    numer_h, gram_w = lax.psum((numer_part[0], gram_part), "bd")
    h_next = factor_h * numer_h / jnp.einsum("rq,qyx->ryx", gram_w, factor_h, precision=highest)
    x_band = moved[0]
    gram_h_part = jnp.einsum("ryx,qyx->rq", h_next, h_next, precision=highest)
    numer_w_part = jnp.einsum("lyx,ryx->lr", x_band, h_next, precision=highest)
    numer_w, gram_h = lax.psum((numer_w_part, gram_h_part), "sp")
    w_next = w_band * numer_w / jnp.dot(w_band, gram_h, precision=highest)
    return (w_next[None], h_next)


def solution(mesh):
    in_specs = (
        P("bd", "sp", None, None),
        P("bd", "sp", None),
        P("bd", "sp", None),
        P("bd", None, None),
        P(None, None, "sp"),
    )
    out_specs = (P("bd", None, None), P(None, None, "sp"))

    def body(cube, *rest):
        suits = lax.axis_size("sp") == 8 and lax.axis_size("bd") == 4 and cube.shape[1] % GROUP == 0
        return (local if suits else local_any)(cube, *rest)

    return jax.shard_map(body, mesh=mesh, in_specs=in_specs, out_specs=out_specs, check_vma=False)
```

```python
import functools

import jax
import jax.numpy as jnp
from jax import lax
from jax.experimental import pallas as pl
from jax.experimental.pallas import tpu as pltpu
from jax.sharding import PartitionSpec as P

F32 = jnp.float32
BF16 = jnp.bfloat16
LANES = 128
GROUP = 16
PIECES = 16
FOLDED = 24
VMEM_LIMIT = 48 * 1024 * 1024


def split(value):
    high = value.astype(BF16)
    low = (value - high.astype(F32)).astype(BF16)
    return high, low


def dot(left, right):
    return lax.dot_general(left, right, (((1,), (0,)), ((), ())), preferred_element_type=F32)


def dot_nt(left, right):
    return lax.dot_general(left, right, (((1,), (1,)), ((), ())), preferred_element_type=F32)


def dot_exact(left, right):
    return lax.dot_general(
        left, right, (((1,), (0,)), ((), ())),
        precision=lax.Precision.HIGHEST, preferred_element_type=F32,
    )


def exchange_blocks(rows, block):
    lane = lax.broadcasted_iota(jnp.int32, rows[0].shape, 1)
    first_half = lane < 2 * block
    even = (lane // block) % 2 == 0
    v0, v1, v2, v3 = rows
    u0 = jnp.where(first_half, v0, pltpu.roll(v2, 2 * block, 1))
    u2 = jnp.where(first_half, pltpu.roll(v0, 2 * block, 1), v2)
    u1 = jnp.where(first_half, v1, pltpu.roll(v3, 2 * block, 1))
    u3 = jnp.where(first_half, pltpu.roll(v1, 2 * block, 1), v3)
    w0 = jnp.where(even, u0, pltpu.roll(u1, block, 1))
    w1 = jnp.where(even, pltpu.roll(u0, 3 * block, 1), u1)
    w2 = jnp.where(even, u2, pltpu.roll(u3, block, 1))
    w3 = jnp.where(even, pltpu.roll(u2, 3 * block, 1), u3)
    return w0, w1, w2, w3


def normalized_taps(taps_ref, reverse, work_ref, out_ref):
    taps = taps_ref.shape[0]
    planes = taps_ref.shape[2]
    work_ref[...] = jnp.zeros_like(work_ref)
    for tap in range(taps):
        row = taps - 1 - tap if reverse else tap
        work_ref[row:row + 1, 0:planes] = taps_ref[tap]
    values = work_ref[...]
    total = jnp.sum(values, axis=0, keepdims=True)
    total = jnp.where(total == 0.0, 1.0, total)
    out_ref[...] = jnp.transpose(values / total)


def column_table(row, margin):
    table = pltpu.roll(jnp.broadcast_to(row, (LANES, LANES)), 0, 1, stride=1, stride_axis=0)
    high = table.astype(BF16).astype(F32)
    src = lax.broadcasted_iota(jnp.int32, (GROUP, LANES), 0)
    dst = lax.broadcasted_iota(jnp.int32, (GROUP, LANES), 1)
    first, last = slice(0, GROUP), slice(LANES - GROUP, LANES)
    above = dst - src <= LANES // 2
    below = src + LANES - GROUP - dst <= LANES // 2
    empty = jnp.zeros((LANES - 2 * GROUP, LANES), F32)
    main, edge = [], []
    for part in (high, table - high):
        main.append(jnp.concatenate(
            [jnp.where(above, part[first], 0.0), part[GROUP:LANES - GROUP], jnp.where(below, part[last], 0.0)],
            axis=0).astype(BF16))
        edge.append(jnp.concatenate(
            [jnp.where(above, 0.0, part[first]), empty, jnp.where(below, 0.0, part[last])],
            axis=0).astype(BF16))
    return jnp.concatenate([jnp.concatenate(main, axis=1), jnp.concatenate(edge, axis=1)], axis=0)


def blur_plane(plane, row, margin):
    height = plane.shape[0]
    table = column_table(row, margin)
    left, right = plane[:, :LANES], plane[:, LANES:]
    lane = lax.broadcasted_iota(jnp.int32, left.shape, 1)
    main = jnp.concatenate([left, right], axis=0)
    edge = jnp.concatenate(
        [jnp.where(lane < LANES // 2, right, 0.0), jnp.where(lane < LANES // 2, 0.0, left)], axis=0)
    high, low = split(jnp.concatenate([main, edge], axis=1))
    product = dot(jnp.concatenate([high, low], axis=0), table)
    rows = 2 * height
    blocks = product[:rows, :LANES] + (product[:rows, LANES:] + product[rows:, :LANES])
    return jnp.concatenate([blocks[:height], blocks[height:]], axis=1)


def row_table(base, margin, height):
    high = base.astype(BF16).astype(F32)
    low = base - high
    plane = lax.broadcasted_iota(jnp.int32, (8, LANES), 0)
    lane = lax.broadcasted_iota(jnp.int32, (8, LANES), 1)
    per_vector = LANES // height
    own = lane // height == plane % per_vector
    masks = [own & (plane // per_vector == part) for part in range(8 * height // LANES)]

    def table(part):
        strips = []
        for row in range(height):
            rolled = pltpu.roll(part, (row - margin) % LANES, 1)
            strips.append(jnp.concatenate([jnp.where(mask, rolled, 0.0) for mask in masks], axis=1))
        return jnp.concatenate(strips, axis=0).astype(BF16)

    return table(high), table(low)


def fold(square):
    side = square.shape[0]
    rest = jnp.zeros((8, LANES - 2 * side), F32)
    return jnp.concatenate(
        [jnp.concatenate([square[first:first + 8], square[first + 8:first + 16], rest], axis=1)
         for first in range(0, side, 16)], axis=0)


def unfold(folded, side):
    blocks = []
    for first in range(0, folded.shape[0], 8):
        blocks += [folded[first:first + 8, :side], folded[first:first + 8, side:2 * side]]
    return jnp.concatenate(blocks, axis=0)


def in_vmem(count):
    return [pl.BlockSpec(memory_space=pltpu.VMEM)] * count


def band_gram(w_rows):
    high, low = split(w_rows)
    rank = w_rows.shape[0]
    padded = jnp.concatenate([high, jnp.zeros((2 * LANES - rank, high.shape[1]), BF16)], axis=0)
    padded_low = jnp.concatenate([low, jnp.zeros((2 * LANES - rank, low.shape[1]), BF16)], axis=0)
    both = dot_nt(jnp.concatenate([high, low], axis=0), padded)
    return both[:rank] + (both[rank:] + dot_nt(high, padded_low))


def blur_group(step, cube_ref, kx_ref, ky_ref, xh_ref, xl_ref, margin):
    height = cube_ref.shape[1]
    halves = []
    for half in range(GROUP // 8):
        done = []
        for k in range(8 * half, 8 * half + 8):
            plane = step * GROUP + k
            done.append(blur_plane(cube_ref[plane], kx_ref[pl.ds(plane, 1), :], margin))
        high, low = split(jnp.concatenate(done, axis=0))
        rows = ky_ref[pl.ds(pl.multiple_of(step * GROUP + 8 * half, 8), 8), :]
        table_high, table_low = row_table(rows, margin, height)
        result = dot(table_high, high) + (dot(table_low, high) + dot(table_high, low))
        halves.append(result.reshape(height, 8, result.shape[1]))
    high, low = split(jnp.concatenate(halves, axis=1))
    planes_here = pl.ds(pl.multiple_of(step * GROUP, GROUP), GROUP)
    xh_ref[:, planes_here, :] = high
    xl_ref[:, planes_here, :] = low


def blur_kernel(cube_hbm, taps_x_hbm, taps_y_hbm, w_hbm, xh_ref, xl_ref, w_here_ref, w_both_ref, keep_ref, give_ref,
                cube_ref, taps_x_ref, taps_y_ref, w_ref, sems, chunk_sems, work_ref, kx_ref, ky_ref):
    taps = taps_x_ref.shape[0]
    margin = (taps - 1) // 2
    height = cube_ref.shape[1]
    rank = w_ref.shape[0]
    groups = cube_ref.shape[0] // GROUP

    def chunk(step):
        here = pl.ds(step * GROUP, GROUP)
        return pltpu.make_async_copy(cube_hbm.at[here], cube_ref.at[here], chunk_sems.at[step])

    copies = [
        pltpu.make_async_copy(taps_x_hbm, taps_x_ref, sems.at[0]),
        pltpu.make_async_copy(taps_y_hbm, taps_y_ref, sems.at[1]),
        pltpu.make_async_copy(w_hbm, w_ref, sems.at[2]),
    ]
    for copy in copies:
        copy.start()
    for step in range(groups):
        chunk(step).start()
    copies[0].wait()
    normalized_taps(taps_x_ref, True, work_ref, kx_ref)
    kx_ref[...] = pltpu.roll(kx_ref[...], LANES - margin, 1)
    copies[1].wait()
    normalized_taps(taps_y_ref, False, work_ref, ky_ref)
    per_vector = LANES // height
    place = lax.broadcasted_iota(jnp.int32, (LANES, LANES), 0) % per_vector
    values = ky_ref[...]
    placed = values
    for k in range(1, per_vector):
        placed = jnp.where(place == k, pltpu.roll(values, k * height, 1), placed)
    ky_ref[...] = placed
    copies[2].wait()

    def body(step, carry):
        chunk(step).wait()
        blur_group(step, cube_ref, kx_ref, ky_ref, xh_ref, xl_ref, margin)
        return carry

    lax.fori_loop(0, groups, body, 0)
    gram = fold(band_gram(w_ref[...])[:, :rank])
    keep_ref[PIECES * rank:] = gram
    give_ref[PIECES * rank:] = gram
    planes = xh_ref.shape[1]
    band = w_ref.shape[1]
    shift = lax.rem(band - lax.axis_index("sp") * planes, band)
    w_here = pltpu.roll(w_ref[...], shift, 1)[:, :2 * LANES]
    w_here_ref[...] = w_here[:, :planes]
    lane = lax.broadcasted_iota(jnp.int32, w_here.shape, 1)
    w_here = jnp.where(lane < planes, w_here, 0.0)
    w_high = w_here.astype(BF16).astype(F32)
    w_both = jnp.concatenate([w_high + pltpu.roll(w_high, planes, 1), w_here - w_high], axis=0).astype(BF16)
    w_both_ref[...] = w_both
    project(xh_ref, xl_ref, w_both[:, :2 * planes], keep_ref, give_ref, 0)


def project(xh_ref, xl_ref, w_both, keep_ref, give_ref, chain):
    height = xh_ref.shape[0]
    rank = w_both.shape[0] // 2
    me_sp = lax.axis_index("sp")
    me_bd = lax.axis_index("bd")
    tall = height // lax.axis_size("bd")
    wide = 2 * LANES // lax.axis_size("sp")
    for rel_bd in (1, 3, 0, 2):
        first_row = lax.bitwise_xor(me_bd, rel_bd) * tall + 4 * chain
        sums = []
        for row in range(4):
            image = jnp.concatenate([xh_ref[first_row + row], xl_ref[first_row + row]], axis=0)
            both = dot(w_both, image)
            sums.append(both[:rank] + both[rank:])
        part_ref = (keep_ref, give_ref)[rel_bd % 2]
        for column in range(2):
            pieces = exchange_blocks(
                [value[:, column * LANES:(column + 1) * LANES] for value in sums], wide)
            for k in range(4):
                rel_sp = lax.bitwise_xor(me_sp, column * 4 + k)
                side = 3 - rel_sp % 2 if rel_bd // 2 else rel_sp % 2
                first = pl.multiple_of((side * 4 + rel_sp // 2) * rank, 8)
                part_ref[pl.ds(first, rank)] = pieces[k]


def project_kernel(xh_ref, xl_ref, w_both_ref, keep_ref, give_ref):
    planes = xh_ref.shape[1]
    project(xh_ref, xl_ref, w_both_ref[:, :2 * planes], keep_ref, give_ref, 1)


def project_call(x_high, x_low, w_both):
    part = jax.ShapeDtypeStruct((PIECES * w_both.shape[0] // 2, LANES), F32)
    return pl.pallas_call(
        project_kernel,
        out_shape=[part, part],
        in_specs=in_vmem(3),
        out_specs=in_vmem(2),
        compiler_params=pltpu.CompilerParams(vmem_limit_bytes=VMEM_LIMIT),
    )(x_high, x_low, w_both)


def blur_call(cube, taps_x, taps_y, w_rows):
    planes, height, length = cube.shape
    rank = w_rows.shape[0]
    first = jax.ShapeDtypeStruct((PIECES * rank + FOLDED, LANES), F32)
    image = (height, planes, length)
    mine = jax.ShapeDtypeStruct((rank, planes), F32)
    both = jax.ShapeDtypeStruct((2 * rank, 2 * LANES), BF16)
    in_hbm = [pltpu.with_memory_space_constraint(value, pltpu.HBM) for value in (cube, taps_x, taps_y, w_rows)]
    return pl.pallas_call(
        blur_kernel,
        out_shape=[jax.ShapeDtypeStruct(image, BF16)] * 2 + [mine, both, first, first],
        in_specs=[pl.BlockSpec(memory_space=pltpu.HBM)] * 4,
        out_specs=in_vmem(6),
        scratch_shapes=[pltpu.VMEM(value.shape, F32) for value in (cube, taps_x, taps_y, w_rows)]
        + [pltpu.SemaphoreType.DMA((3,)), pltpu.SemaphoreType.DMA((planes // GROUP,))]
        + [pltpu.VMEM((LANES, LANES), F32)] * 3,
        compiler_params=pltpu.CompilerParams(vmem_limit_bytes=VMEM_LIMIT),
    )(*in_hbm)


def ratio_kernel(mine_ref, other_ref, h_ref, out_ref):
    tall = h_ref.shape[0] // lax.axis_size("bd")
    first = pl.multiple_of(lax.axis_index("bd") * tall, tall)
    here = h_ref[pl.ds(first, tall)]
    here = jnp.transpose(here.reshape(-1, here.shape[2]))
    rows = mine_ref.shape[0]
    gram = unfold(mine_ref[rows - FOLDED:rows] + other_ref[rows - FOLDED:rows], here.shape[0])
    out_ref[...] = here / dot_exact(gram, here)


def ratio_call(mine, other, h_columns):
    piece = jax.ShapeDtypeStruct((h_columns.shape[2], 2 * LANES), F32)
    return pl.pallas_call(
        ratio_kernel,
        out_shape=piece,
        in_specs=in_vmem(3),
        compiler_params=pltpu.CompilerParams(vmem_limit_bytes=VMEM_LIMIT),
    )(mine, other, h_columns)


def accumulate(xh_ref, xl_ref, part_refs, all_ref, chain, total):
    height, planes, _ = xh_ref.shape
    me_sp = lax.axis_index("sp")
    me_bd = lax.axis_index("bd")
    bands = lax.axis_size("bd")
    pieces = lax.axis_size("sp")
    tall = height // bands
    wide = 2 * LANES // pieces
    for slot, part_ref in enumerate(part_refs):
        rel_bd = slot // 4 + 2 * ((slot // 2) % 2)
        for inner in range(4):
            rel_sp = slot % 2 + 2 * inner
            owner = lax.bitwise_xor(me_bd, rel_bd) * pieces + lax.bitwise_xor(me_sp, rel_sp)
            all_ref[owner] = part_ref[inner]
    for part in range(bands):
        first_row = part * tall + 4 * chain
        halves = [
            exchange_blocks([all_ref[part * pieces + column * 4 + k] for k in range(4)], wide)
            for column in range(2)]
        rows = jnp.concatenate([halves[column][row] for row in range(4) for column in range(2)], axis=1)
        high, low = split(rows)
        here = jnp.concatenate([high, low], axis=0)
        image = [
            jnp.concatenate([ref[first_row + row] for row in range(4)], axis=1) for ref in (xh_ref, xl_ref)]
        total = total + dot_nt(jnp.concatenate(image + [here], axis=0), here)
    return total


def first_kernel(xh_ref, xl_ref, *rest):
    part_refs = rest[:8]
    total_out, all_ref = rest[8:]
    total_out[...] = accumulate(xh_ref, xl_ref, part_refs, all_ref, 0, jnp.zeros(total_out.shape, F32))


def first_call(x_high, x_low, parts):
    _, planes, _ = x_high.shape
    rank = parts[0].shape[1]
    return pl.pallas_call(
        first_kernel,
        out_shape=jax.ShapeDtypeStruct((2 * (planes + rank), 2 * rank), F32),
        in_specs=in_vmem(2 + len(parts)),
        scratch_shapes=[pltpu.VMEM((32, rank, LANES), F32)],
        compiler_params=pltpu.CompilerParams(vmem_limit_bytes=VMEM_LIMIT),
    )(x_high, x_low, *parts)


def second_kernel(xh_ref, xl_ref, w_ref, total_ref, *rest):
    part_refs = rest[:8]
    w_out, all_ref = rest[8:]
    planes = xh_ref.shape[1]
    rank = w_ref.shape[0]
    total = accumulate(xh_ref, xl_ref, part_refs, all_ref, 1, total_ref[...])
    numer = total[:planes, :rank] + (total[:planes, rank:] + total[planes:2 * planes, :rank])
    gram = total[2 * planes:]
    gram = gram[:rank, :rank] + (gram[:rank, rank:] + gram[rank:, :rank])
    w_here = w_ref[...]
    w_out[...] = w_here * jnp.transpose(numer) / dot_exact(gram, w_here)


def second_call(x_high, x_low, w_here, total, parts):
    rank = w_here.shape[0]
    return pl.pallas_call(
        second_kernel,
        out_shape=jax.ShapeDtypeStruct(w_here.shape, F32),
        in_specs=in_vmem(4 + len(parts)),
        scratch_shapes=[pltpu.VMEM((32, rank, LANES), F32)],
        compiler_params=pltpu.CompilerParams(vmem_limit_bytes=VMEM_LIMIT),
    )(x_high, x_low, w_here, total, *parts)


def place_h_kernel(*refs):
    h_out = refs[-1]
    me_bd = lax.axis_index("bd")
    tall = h_out.shape[0] // lax.axis_size("bd")
    for chain in range(2):
        for rel_bd in range(4):
            piece = refs[4 * chain + rel_bd][0]
            first = lax.bitwise_xor(me_bd, rel_bd) * tall + 4 * chain
            h_out[pl.ds(first, 4)] = jnp.transpose(piece).reshape((4,) + h_out.shape[1:])


def place_h_call(parts, shape):
    return pl.pallas_call(
        place_h_kernel,
        out_shape=jax.ShapeDtypeStruct(shape, F32),
        in_specs=in_vmem(len(parts)),
        compiler_params=pltpu.CompilerParams(vmem_limit_bytes=VMEM_LIMIT),
    )(*parts)


def gather_w_kernel(*refs):
    part_refs = refs[:-2]
    out_ref, all_ref = refs[-2:]
    planes = out_ref.shape[1] // 8
    me_sp = lax.axis_index("sp")
    rel = 0
    for part_ref in part_refs:
        for inner in range(part_ref.shape[0]):
            all_ref[lax.bitwise_xor(me_sp, RING[rel]), :, 0:planes] = part_ref[inner]
            rel += 1
    for owner in range(8):
        out_ref[:, owner * planes:(owner + 1) * planes] = all_ref[owner][:, :planes]


RING = (0, 1, 2, 3, 4, 5, 6, 7)


def gather_w_call(parts):
    _, rank, planes = parts[0].shape
    return pl.pallas_call(
        gather_w_kernel,
        out_shape=jax.ShapeDtypeStruct((rank, planes * 8), F32),
        in_specs=in_vmem(len(parts)),
        scratch_shapes=[pltpu.VMEM((8, rank, LANES), F32)],
        compiler_params=pltpu.CompilerParams(vmem_limit_bytes=VMEM_LIMIT),
    )(*parts)


def send(value, mask_sp, mask_bd):
    bands = lax.axis_size("bd")
    pieces = lax.axis_size("sp")
    pairs = []
    for s in range(pieces):
        for b in range(bands):
            pairs.append((s * bands + b, (s ^ mask_sp) * bands + (b ^ mask_bd)))
    return lax.ppermute(value, ("sp", "bd"), pairs)


def around(values):
    return [send(values[k], k % 2, 2 * (k // 2)) for k in range(1, 4)]


def spread(value, chain):
    if chain == 0:
        column, row = send(value, 1, 0), send(value, 0, 2)
        corner = send(row, 1, 0)
    else:
        row, column = send(value, 0, 2), send(value, 1, 0)
        corner = send(column, 0, 2)
    return [value, column, row, corner]


def local(cube, taps_x, taps_y, factor_w, factor_h):
    w_rows = jnp.transpose(factor_w[0])
    taps_x = jnp.transpose(taps_x, (2, 0, 1))
    taps_y = jnp.transpose(taps_y, (2, 0, 1))
    h_columns = jnp.transpose(factor_h, (1, 2, 0))
    rank = w_rows.shape[0]
    x_high, x_low, w_here, w_both, keep_0, give_0 = blur_call(cube[0], taps_x, taps_y, w_rows)
    chains = []
    taken_0 = send(give_0, 0, 1)
    keep_1, give_1 = project_call(x_high, x_low, w_both)
    taken_0, keep_1, give_1 = lax.optimization_barrier((taken_0, keep_1, give_1))
    for keep, taken in ((keep_0, taken_0), (keep_1, send(give_1, 0, 1))):
        bounds = [place * 4 * rank for place in (0, 1, 3, 2)]
        sides = []
        for first in bounds:
            last = keep.shape[0] if first == max(bounds) else first + 4 * rank
            sides.append(keep[first:last] + taken[first:last])
        chains.append((sides, around(sides)))
    ratio = ratio_call(chains[0][0][2], chains[0][1][1], h_columns)
    line = []
    for k in range(4):
        part = slice(k * rank, (k + 1) * rank)
        line.append(jnp.concatenate(
            [(sides[0][part] + others[0][part]) + (others[1][part] + others[2][part]) for sides, others in chains],
            axis=1))
    line = [line[0]] + [send(line[k], 2 * k, 0) for k in (3, 2, 1)]
    h_piece = ratio * ((line[0] + line[1]) + (line[2] + line[3]))
    h_line = [h_piece] + [send(h_piece, 2 * k, 0) for k in range(1, 4)]
    chains = []
    for first in (0, LANES):
        mine = jnp.stack([value[:, first:first + LANES] for value in h_line])
        chains.append(spread(mine, len(chains)))
    first_parts = chains[0] + [send(value, 0, 1) for value in chains[0]]
    total = first_call(x_high, x_low, first_parts)
    second_parts = chains[1] + [send(value, 0, 1) for value in chains[1]]
    w_piece = second_call(x_high, x_low, w_here, total, second_parts)
    own = [parts[k] for parts in (first_parts, second_parts) for k in (0, 4, 2, 6)]
    h_next = place_h_call(own, h_columns.shape)
    w_pair = jnp.stack([w_piece, send(w_piece, 1, 0)])
    w_next = gather_w_call([w_pair] + [send(w_pair, 2 * k, 0) for k in range(1, 4)])
    return jnp.transpose(w_next)[None], jnp.transpose(h_next, (2, 0, 1))


def normalized(kernel):
    return kernel / jnp.sum(kernel, axis=-1, keepdims=True)


def band_weights(kernel, size_in, size_out, offset):
    tap_count = kernel.shape[-1]
    in_index = lax.broadcasted_iota(jnp.int32, (size_in, size_out, tap_count), 0)
    out_index = lax.broadcasted_iota(jnp.int32, (size_in, size_out, tap_count), 1)
    tap_index = lax.broadcasted_iota(jnp.int32, (size_in, size_out, tap_count), 2)
    select = (tap_index == in_index - out_index + offset).astype(jnp.float32)
    return jnp.einsum("pk,iok->pio", kernel, select, precision=lax.Precision.HIGHEST)


def blur_rows(planes, kernel_y):
    margin = (kernel_y.shape[-1] - 1) // 2
    height = planes.shape[1]
    band_table = band_weights(kernel_y, height, height, margin)
    return jnp.einsum("piz,pio->poz", planes, band_table, precision=lax.Precision.HIGHEST)


def blur_columns(planes, kernel_x):
    margin = (kernel_x.shape[-1] - 1) // 2
    count, height, length = planes.shape
    blocks = planes.reshape(count, height, length // 128, 128)
    empty = jnp.zeros((count, height, 1, 128), jnp.float32)
    left_block = jnp.concatenate([empty, blocks[:, :, :-1]], axis=2)
    right_block = jnp.concatenate([blocks[:, :, 1:], empty], axis=2)
    window = jnp.concatenate([left_block, blocks, right_block], axis=3)
    band_table = band_weights(kernel_x, 384, 128, margin - 128)
    result = jnp.einsum("pybi,pio->pybo", window, band_table, precision=lax.Precision.HIGHEST)
    return result.reshape(count, height, length)


def local_any(cube, taps_x, taps_y, factor_w, factor_h):
    highest = lax.Precision.HIGHEST
    kernel_x = normalized(taps_x[0])
    kernel_y = normalized(taps_y[0])
    rows_done = blur_rows(cube[0], kernel_y)
    w_band = factor_w[0]
    blurred = blur_columns(rows_done, kernel_x)[None]
    moved = lax.all_to_all(blurred, "sp", split_axis=3, concat_axis=1, tiled=True)
    numer_part = jnp.einsum("lr,plyx->pryx", w_band, moved, precision=highest)
    gram_part = jnp.dot(w_band.T, w_band, precision=highest)
    numer_h, gram_w = lax.psum((numer_part[0], gram_part), "bd")
    h_next = factor_h * numer_h / jnp.einsum("rq,qyx->ryx", gram_w, factor_h, precision=highest)
    x_band = moved[0]
    gram_h_part = jnp.einsum("ryx,qyx->rq", h_next, h_next, precision=highest)
    numer_w_part = jnp.einsum("lyx,ryx->lr", x_band, h_next, precision=highest)
    numer_w, gram_h = lax.psum((numer_w_part, gram_h_part), "sp")
    w_next = w_band * numer_w / jnp.dot(w_band, gram_h, precision=highest)
    return (w_next[None], h_next)


def solution(mesh):
    in_specs = (
        P("bd", "sp", None, None),
        P("bd", "sp", None),
        P("bd", "sp", None),
        P("bd", None, None),
        P(None, None, "sp"),
    )
    out_specs = (P("bd", None, None), P(None, None, "sp"))

    def body(cube, *rest):
        suits = lax.axis_size("sp") == 8 and lax.axis_size("bd") == 4 and cube.shape[1] % GROUP == 0
        return (local if suits else local_any)(cube, *rest)

    return jax.shard_map(body, mesh=mesh, in_specs=in_specs, out_specs=out_specs, check_vma=False)
```

```python
import functools

import jax
import jax.numpy as jnp
from jax import lax
from jax.experimental import pallas as pl
from jax.experimental.pallas import tpu as pltpu
from jax.sharding import PartitionSpec as P

F32 = jnp.float32
BF16 = jnp.bfloat16
LANES = 128
GROUP = 16
PIECES = 16
FOLDED = 24
VMEM_LIMIT = 48 * 1024 * 1024


def split(value):
    high = value.astype(BF16)
    low = (value - high.astype(F32)).astype(BF16)
    return high, low


def dot(left, right):
    return lax.dot_general(left, right, (((1,), (0,)), ((), ())), preferred_element_type=F32)


def dot_nt(left, right):
    return lax.dot_general(left, right, (((1,), (1,)), ((), ())), preferred_element_type=F32)


def dot_exact(left, right):
    return lax.dot_general(
        left, right, (((1,), (0,)), ((), ())),
        precision=lax.Precision.HIGHEST, preferred_element_type=F32,
    )


def exchange_blocks(rows, block):
    lane = lax.broadcasted_iota(jnp.int32, rows[0].shape, 1)
    first_half = lane < 2 * block
    even = (lane // block) % 2 == 0
    v0, v1, v2, v3 = rows
    u0 = jnp.where(first_half, v0, pltpu.roll(v2, 2 * block, 1))
    u2 = jnp.where(first_half, pltpu.roll(v0, 2 * block, 1), v2)
    u1 = jnp.where(first_half, v1, pltpu.roll(v3, 2 * block, 1))
    u3 = jnp.where(first_half, pltpu.roll(v1, 2 * block, 1), v3)
    w0 = jnp.where(even, u0, pltpu.roll(u1, block, 1))
    w1 = jnp.where(even, pltpu.roll(u0, 3 * block, 1), u1)
    w2 = jnp.where(even, u2, pltpu.roll(u3, block, 1))
    w3 = jnp.where(even, pltpu.roll(u2, 3 * block, 1), u3)
    return w0, w1, w2, w3


def normalized_taps(taps_ref, reverse, work_ref, out_ref):
    taps = taps_ref.shape[0]
    planes = taps_ref.shape[2]
    work_ref[...] = jnp.zeros_like(work_ref)
    for tap in range(taps):
        row = taps - 1 - tap if reverse else tap
        work_ref[row:row + 1, 0:planes] = taps_ref[tap]
    values = work_ref[...]
    total = jnp.sum(values, axis=0, keepdims=True)
    total = jnp.where(total == 0.0, 1.0, total)
    out_ref[...] = jnp.transpose(values / total)


def column_table(row, margin):
    table = pltpu.roll(jnp.broadcast_to(row, (LANES, LANES)), 0, 1, stride=1, stride_axis=0)
    high = table.astype(BF16).astype(F32)
    src = lax.broadcasted_iota(jnp.int32, (GROUP, LANES), 0)
    dst = lax.broadcasted_iota(jnp.int32, (GROUP, LANES), 1)
    first, last = slice(0, GROUP), slice(LANES - GROUP, LANES)
    above = dst - src <= LANES // 2
    below = src + LANES - GROUP - dst <= LANES // 2
    empty = jnp.zeros((LANES - 2 * GROUP, LANES), F32)
    main, edge = [], []
    for part in (high, table - high):
        main.append(jnp.concatenate(
            [jnp.where(above, part[first], 0.0), part[GROUP:LANES - GROUP], jnp.where(below, part[last], 0.0)],
            axis=0).astype(BF16))
        edge.append(jnp.concatenate(
            [jnp.where(above, 0.0, part[first]), empty, jnp.where(below, 0.0, part[last])],
            axis=0).astype(BF16))
    return jnp.concatenate([jnp.concatenate(main, axis=1), jnp.concatenate(edge, axis=1)], axis=0)


def blur_plane(plane, row, margin):
    height = plane.shape[0]
    table = column_table(row, margin)
    left, right = plane[:, :LANES], plane[:, LANES:]
    lane = lax.broadcasted_iota(jnp.int32, left.shape, 1)
    main = jnp.concatenate([left, right], axis=0)
    edge = jnp.concatenate(
        [jnp.where(lane < LANES // 2, right, 0.0), jnp.where(lane < LANES // 2, 0.0, left)], axis=0)
    high, low = split(jnp.concatenate([main, edge], axis=1))
    product = dot(jnp.concatenate([high, low], axis=0), table)
    rows = 2 * height
    blocks = product[:rows, :LANES] + (product[:rows, LANES:] + product[rows:, :LANES])
    return jnp.concatenate([blocks[:height], blocks[height:]], axis=1)


def row_table(base, margin, height):
    high = base.astype(BF16).astype(F32)
    low = base - high
    plane = lax.broadcasted_iota(jnp.int32, (8, LANES), 0)
    lane = lax.broadcasted_iota(jnp.int32, (8, LANES), 1)
    per_vector = LANES // height
    own = lane // height == plane % per_vector
    masks = [own & (plane // per_vector == part) for part in range(8 * height // LANES)]

    def table(part):
        strips = []
        for row in range(height):
            rolled = pltpu.roll(part, (row - margin) % LANES, 1)
            strips.append(jnp.concatenate([jnp.where(mask, rolled, 0.0) for mask in masks], axis=1))
        return jnp.concatenate(strips, axis=0).astype(BF16)

    return table(high), table(low)


def fold(square):
    side = square.shape[0]
    rest = jnp.zeros((8, LANES - 2 * side), F32)
    return jnp.concatenate(
        [jnp.concatenate([square[first:first + 8], square[first + 8:first + 16], rest], axis=1)
         for first in range(0, side, 16)], axis=0)


def unfold(folded, side):
    blocks = []
    for first in range(0, folded.shape[0], 8):
        blocks += [folded[first:first + 8, :side], folded[first:first + 8, side:2 * side]]
    return jnp.concatenate(blocks, axis=0)


def in_vmem(count):
    return [pl.BlockSpec(memory_space=pltpu.VMEM)] * count


def band_gram(w_rows):
    high, low = split(w_rows)
    rank = w_rows.shape[0]
    padded = jnp.concatenate([high, jnp.zeros((2 * LANES - rank, high.shape[1]), BF16)], axis=0)
    padded_low = jnp.concatenate([low, jnp.zeros((2 * LANES - rank, low.shape[1]), BF16)], axis=0)
    both = dot_nt(jnp.concatenate([high, low], axis=0), padded)
    return both[:rank] + (both[rank:] + dot_nt(high, padded_low))


def blur_group(step, cube_ref, kx_ref, ky_ref, xh_ref, xl_ref, margin):
    height = cube_ref.shape[1]
    halves = []
    for half in range(GROUP // 8):
        done = []
        for k in range(8 * half, 8 * half + 8):
            plane = step * GROUP + k
            done.append(blur_plane(cube_ref[plane], kx_ref[pl.ds(plane, 1), :], margin))
        high, low = split(jnp.concatenate(done, axis=0))
        rows = ky_ref[pl.ds(pl.multiple_of(step * GROUP + 8 * half, 8), 8), :]
        table_high, table_low = row_table(rows, margin, height)
        result = dot(table_high, high) + (dot(table_low, high) + dot(table_high, low))
        halves.append(result.reshape(height, 8, result.shape[1]))
    high, low = split(jnp.concatenate(halves, axis=1))
    planes_here = pl.ds(pl.multiple_of(step * GROUP, GROUP), GROUP)
    xh_ref[:, planes_here, :] = high
    xl_ref[:, planes_here, :] = low


def blur_kernel(cube_hbm, taps_x_hbm, taps_y_hbm, w_hbm, xh_ref, xl_ref, w_here_ref, w_both_ref, keep_ref, give_ref,
                cube_ref, taps_x_ref, taps_y_ref, w_ref, sems, chunk_sems, work_ref, kx_ref, ky_ref):
    taps = taps_x_ref.shape[0]
    margin = (taps - 1) // 2
    height = cube_ref.shape[1]
    rank = w_ref.shape[0]
    groups = cube_ref.shape[0] // GROUP

    def chunk(step):
        here = pl.ds(step * GROUP, GROUP)
        return pltpu.make_async_copy(cube_hbm.at[here], cube_ref.at[here], chunk_sems.at[step])

    copies = [
        pltpu.make_async_copy(taps_x_hbm, taps_x_ref, sems.at[0]),
        pltpu.make_async_copy(taps_y_hbm, taps_y_ref, sems.at[1]),
        pltpu.make_async_copy(w_hbm, w_ref, sems.at[2]),
    ]
    for copy in copies:
        copy.start()
    for step in range(groups):
        chunk(step).start()
    copies[0].wait()
    normalized_taps(taps_x_ref, True, work_ref, kx_ref)
    kx_ref[...] = pltpu.roll(kx_ref[...], LANES - margin, 1)
    copies[1].wait()
    normalized_taps(taps_y_ref, False, work_ref, ky_ref)
    per_vector = LANES // height
    place = lax.broadcasted_iota(jnp.int32, (LANES, LANES), 0) % per_vector
    values = ky_ref[...]
    placed = values
    for k in range(1, per_vector):
        placed = jnp.where(place == k, pltpu.roll(values, k * height, 1), placed)
    ky_ref[...] = placed
    copies[2].wait()

    def body(step, carry):
        chunk(step).wait()
        blur_group(step, cube_ref, kx_ref, ky_ref, xh_ref, xl_ref, margin)
        return carry

    lax.fori_loop(0, groups, body, 0)
    gram = fold(band_gram(w_ref[...])[:, :rank])
    keep_ref[PIECES * rank:] = gram
    give_ref[PIECES * rank:] = gram
    planes = xh_ref.shape[1]
    band = w_ref.shape[1]
    shift = lax.rem(band - lax.axis_index("sp") * planes, band)
    w_here = pltpu.roll(w_ref[...], shift, 1)[:, :2 * LANES]
    w_here_ref[...] = w_here[:, :planes]
    lane = lax.broadcasted_iota(jnp.int32, w_here.shape, 1)
    w_here = jnp.where(lane < planes, w_here, 0.0)
    w_high = w_here.astype(BF16).astype(F32)
    w_both = jnp.concatenate([w_high + pltpu.roll(w_high, planes, 1), w_here - w_high], axis=0).astype(BF16)
    w_both_ref[...] = w_both
    project(xh_ref, xl_ref, w_both[:, :2 * planes], keep_ref, give_ref, 0)


def project(xh_ref, xl_ref, w_both, keep_ref, give_ref, chain):
    height = xh_ref.shape[0]
    rank = w_both.shape[0] // 2
    me_sp = lax.axis_index("sp")
    me_bd = lax.axis_index("bd")
    tall = height // lax.axis_size("bd")
    wide = 2 * LANES // lax.axis_size("sp")
    for rel_bd in (1, 3, 0, 2):
        first_row = lax.bitwise_xor(me_bd, rel_bd) * tall + 4 * chain
        sums = []
        for row in range(4):
            image = jnp.concatenate([xh_ref[first_row + row], xl_ref[first_row + row]], axis=0)
            both = dot(w_both, image)
            sums.append(both[:rank] + both[rank:])
        part_ref = (keep_ref, give_ref)[rel_bd % 2]
        for column in range(2):
            pieces = exchange_blocks(
                [value[:, column * LANES:(column + 1) * LANES] for value in sums], wide)
            for k in range(4):
                rel_sp = lax.bitwise_xor(me_sp, column * 4 + k)
                side = 3 - rel_sp % 2 if rel_bd // 2 else rel_sp % 2
                first = pl.multiple_of((side * 4 + rel_sp // 2) * rank, 8)
                part_ref[pl.ds(first, rank)] = pieces[k]


def project_kernel(xh_ref, xl_ref, w_both_ref, keep_ref, give_ref):
    planes = xh_ref.shape[1]
    project(xh_ref, xl_ref, w_both_ref[:, :2 * planes], keep_ref, give_ref, 1)


def project_call(x_high, x_low, w_both):
    part = jax.ShapeDtypeStruct((PIECES * w_both.shape[0] // 2, LANES), F32)
    return pl.pallas_call(
        project_kernel,
        out_shape=[part, part],
        in_specs=in_vmem(3),
        out_specs=in_vmem(2),
        compiler_params=pltpu.CompilerParams(vmem_limit_bytes=VMEM_LIMIT),
    )(x_high, x_low, w_both)


def blur_call(cube, taps_x, taps_y, w_rows):
    planes, height, length = cube.shape
    rank = w_rows.shape[0]
    first = jax.ShapeDtypeStruct((PIECES * rank + FOLDED, LANES), F32)
    image = (height, planes, length)
    mine = jax.ShapeDtypeStruct((rank, planes), F32)
    both = jax.ShapeDtypeStruct((2 * rank, 2 * LANES), BF16)
    in_hbm = [pltpu.with_memory_space_constraint(value, pltpu.HBM) for value in (cube, taps_x, taps_y, w_rows)]
    return pl.pallas_call(
        blur_kernel,
        out_shape=[jax.ShapeDtypeStruct(image, BF16)] * 2 + [mine, both, first, first],
        in_specs=[pl.BlockSpec(memory_space=pltpu.HBM)] * 4,
        out_specs=in_vmem(6),
        scratch_shapes=[pltpu.VMEM(value.shape, F32) for value in (cube, taps_x, taps_y, w_rows)]
        + [pltpu.SemaphoreType.DMA((3,)), pltpu.SemaphoreType.DMA((planes // GROUP,))]
        + [pltpu.VMEM((LANES, LANES), F32)] * 3,
        compiler_params=pltpu.CompilerParams(vmem_limit_bytes=VMEM_LIMIT),
    )(*in_hbm)


def ratio_kernel(mine_ref, other_ref, h_ref, out_ref):
    tall = h_ref.shape[0] // lax.axis_size("bd")
    first = pl.multiple_of(lax.axis_index("bd") * tall, tall)
    here = h_ref[pl.ds(first, tall)]
    here = jnp.transpose(here.reshape(-1, here.shape[2]))
    rows = mine_ref.shape[0]
    gram = unfold(mine_ref[rows - FOLDED:rows] + other_ref[rows - FOLDED:rows], here.shape[0])
    out_ref[...] = here / dot_exact(gram, here)


def ratio_call(mine, other, h_columns):
    piece = jax.ShapeDtypeStruct((h_columns.shape[2], 2 * LANES), F32)
    return pl.pallas_call(
        ratio_kernel,
        out_shape=piece,
        in_specs=in_vmem(3),
        compiler_params=pltpu.CompilerParams(vmem_limit_bytes=VMEM_LIMIT),
    )(mine, other, h_columns)


def accumulate(xh_ref, xl_ref, part_refs, all_ref, chain, total):
    height, planes, _ = xh_ref.shape
    me_sp = lax.axis_index("sp")
    me_bd = lax.axis_index("bd")
    bands = lax.axis_size("bd")
    pieces = lax.axis_size("sp")
    tall = height // bands
    wide = 2 * LANES // pieces
    for slot, part_ref in enumerate(part_refs):
        partner = ((0,) + PARTNERS[chain])[slot % 4]
        rel_bd = slot // 4 + 2 * (partner // 2)
        for inner in range(4):
            rel_sp = partner % 2 + 2 * inner
            owner = lax.bitwise_xor(me_bd, rel_bd) * pieces + lax.bitwise_xor(me_sp, rel_sp)
            all_ref[owner] = part_ref[inner]
    for part in range(bands):
        first_row = part * tall + 4 * chain
        halves = [
            exchange_blocks([all_ref[part * pieces + column * 4 + k] for k in range(4)], wide)
            for column in range(2)]
        rows = jnp.concatenate([halves[column][row] for row in range(4) for column in range(2)], axis=1)
        high, low = split(rows)
        here = jnp.concatenate([high, low], axis=0)
        image = [
            jnp.concatenate([ref[first_row + row] for row in range(4)], axis=1) for ref in (xh_ref, xl_ref)]
        total = total + dot_nt(jnp.concatenate(image + [here], axis=0), here)
    return total


def first_kernel(xh_ref, xl_ref, *rest):
    part_refs = rest[:8]
    total_out, all_ref = rest[8:]
    total_out[...] = accumulate(xh_ref, xl_ref, part_refs, all_ref, 0, jnp.zeros(total_out.shape, F32))


def first_call(x_high, x_low, parts):
    _, planes, _ = x_high.shape
    rank = parts[0].shape[1]
    return pl.pallas_call(
        first_kernel,
        out_shape=jax.ShapeDtypeStruct((2 * (planes + rank), 2 * rank), F32),
        in_specs=in_vmem(2 + len(parts)),
        scratch_shapes=[pltpu.VMEM((32, rank, LANES), F32)],
        compiler_params=pltpu.CompilerParams(vmem_limit_bytes=VMEM_LIMIT),
    )(x_high, x_low, *parts)


def second_kernel(xh_ref, xl_ref, w_ref, total_ref, *rest):
    part_refs = rest[:8]
    w_out, all_ref = rest[8:]
    planes = xh_ref.shape[1]
    rank = w_ref.shape[0]
    total = accumulate(xh_ref, xl_ref, part_refs, all_ref, 1, total_ref[...])
    numer = total[:planes, :rank] + (total[:planes, rank:] + total[planes:2 * planes, :rank])
    gram = total[2 * planes:]
    gram = gram[:rank, :rank] + (gram[:rank, rank:] + gram[rank:, :rank])
    w_here = w_ref[...]
    w_out[...] = w_here * jnp.transpose(numer) / dot_exact(gram, w_here)


def second_call(x_high, x_low, w_here, total, parts):
    rank = w_here.shape[0]
    return pl.pallas_call(
        second_kernel,
        out_shape=jax.ShapeDtypeStruct(w_here.shape, F32),
        in_specs=in_vmem(4 + len(parts)),
        scratch_shapes=[pltpu.VMEM((32, rank, LANES), F32)],
        compiler_params=pltpu.CompilerParams(vmem_limit_bytes=VMEM_LIMIT),
    )(x_high, x_low, w_here, total, *parts)


def place_h_kernel(*refs):
    h_out = refs[-1]
    me_bd = lax.axis_index("bd")
    tall = h_out.shape[0] // lax.axis_size("bd")
    for chain in range(2):
        for rel_bd in range(4):
            piece = refs[4 * chain + rel_bd][0]
            first = lax.bitwise_xor(me_bd, rel_bd) * tall + 4 * chain
            h_out[pl.ds(first, 4)] = jnp.transpose(piece).reshape((4,) + h_out.shape[1:])


def place_h_call(parts, shape):
    return pl.pallas_call(
        place_h_kernel,
        out_shape=jax.ShapeDtypeStruct(shape, F32),
        in_specs=in_vmem(len(parts)),
        compiler_params=pltpu.CompilerParams(vmem_limit_bytes=VMEM_LIMIT),
    )(*parts)


def gather_w_kernel(*refs):
    part_refs = refs[:-2]
    out_ref, all_ref = refs[-2:]
    planes = out_ref.shape[1] // 8
    me_sp = lax.axis_index("sp")
    rel = 0
    for part_ref in part_refs:
        for inner in range(part_ref.shape[0]):
            all_ref[lax.bitwise_xor(me_sp, RING[rel]), :, 0:planes] = part_ref[inner]
            rel += 1
    for owner in range(8):
        out_ref[:, owner * planes:(owner + 1) * planes] = all_ref[owner][:, :planes]


PARTNERS = ((3, 1, 2), (1, 2, 3))
RING = (0, 1, 2, 3, 4, 5, 6, 7)


def gather_w_call(parts):
    _, rank, planes = parts[0].shape
    return pl.pallas_call(
        gather_w_kernel,
        out_shape=jax.ShapeDtypeStruct((rank, planes * 8), F32),
        in_specs=in_vmem(len(parts)),
        scratch_shapes=[pltpu.VMEM((8, rank, LANES), F32)],
        compiler_params=pltpu.CompilerParams(vmem_limit_bytes=VMEM_LIMIT),
    )(*parts)


def send(value, mask_sp, mask_bd):
    bands = lax.axis_size("bd")
    pieces = lax.axis_size("sp")
    pairs = []
    for s in range(pieces):
        for b in range(bands):
            pairs.append((s * bands + b, (s ^ mask_sp) * bands + (b ^ mask_bd)))
    return lax.ppermute(value, ("sp", "bd"), pairs)


def around(values):
    return [send(values[k], k % 2, 2 * (k // 2)) for k in range(1, 4)]


def local(cube, taps_x, taps_y, factor_w, factor_h):
    w_rows = jnp.transpose(factor_w[0])
    taps_x = jnp.transpose(taps_x, (2, 0, 1))
    taps_y = jnp.transpose(taps_y, (2, 0, 1))
    h_columns = jnp.transpose(factor_h, (1, 2, 0))
    rank = w_rows.shape[0]
    x_high, x_low, w_here, w_both, keep_0, give_0 = blur_call(cube[0], taps_x, taps_y, w_rows)
    chains = []
    taken_0 = send(give_0, 0, 1)
    keep_1, give_1 = project_call(x_high, x_low, w_both)
    taken_0, keep_1, give_1 = lax.optimization_barrier((taken_0, keep_1, give_1))
    for keep, taken in ((keep_0, taken_0), (keep_1, send(give_1, 0, 1))):
        bounds = [place * 4 * rank for place in (0, 1, 3, 2)]
        sides = []
        for first in bounds:
            last = keep.shape[0] if first == max(bounds) else first + 4 * rank
            sides.append(keep[first:last] + taken[first:last])
        chains.append((sides, around(sides)))
    ratio = ratio_call(chains[0][0][2], chains[0][1][1], h_columns)
    line = []
    for k in range(4):
        part = slice(k * rank, (k + 1) * rank)
        halves = []
        for order, (sides, others) in zip(PARTNERS, chains):
            one, two, three = [others[partner - 1][part] for partner in order]
            halves.append((sides[0][part] + one) + (two + three))
        line.append(jnp.concatenate(halves, axis=1))
    line = [line[0]] + [send(line[k], 2 * k, 0) for k in (3, 2, 1)]
    h_piece = ratio * ((line[0] + line[1]) + (line[2] + line[3]))
    h_line = [h_piece] + [send(h_piece, 2 * k, 0) for k in range(1, 4)]
    chains = []
    for first in (0, LANES):
        mine = jnp.stack([value[:, first:first + LANES] for value in h_line])
        others = around([mine] * 4)
        chains.append([mine] + [others[k - 1] for k in PARTNERS[len(chains)]])
    first_parts = chains[0] + [send(value, 0, 1) for value in chains[0]]
    total = first_call(x_high, x_low, first_parts)
    second_parts = chains[1] + [send(value, 0, 1) for value in chains[1]]
    w_piece = second_call(x_high, x_low, w_here, total, second_parts)
    own = []
    for order, parts in zip(PARTNERS, (first_parts, second_parts)):
        row = 1 + order.index(2)
        own += [parts[0], parts[4], parts[row], parts[4 + row]]
    h_next = place_h_call(own, h_columns.shape)
    w_pair = jnp.stack([w_piece, send(w_piece, 1, 0)])
    w_next = gather_w_call([w_pair] + [send(w_pair, 2 * k, 0) for k in range(1, 4)])
    return jnp.transpose(w_next)[None], jnp.transpose(h_next, (2, 0, 1))


def normalized(kernel):
    return kernel / jnp.sum(kernel, axis=-1, keepdims=True)


def band_weights(kernel, size_in, size_out, offset):
    tap_count = kernel.shape[-1]
    in_index = lax.broadcasted_iota(jnp.int32, (size_in, size_out, tap_count), 0)
    out_index = lax.broadcasted_iota(jnp.int32, (size_in, size_out, tap_count), 1)
    tap_index = lax.broadcasted_iota(jnp.int32, (size_in, size_out, tap_count), 2)
    select = (tap_index == in_index - out_index + offset).astype(jnp.float32)
    return jnp.einsum("pk,iok->pio", kernel, select, precision=lax.Precision.HIGHEST)


def blur_rows(planes, kernel_y):
    margin = (kernel_y.shape[-1] - 1) // 2
    height = planes.shape[1]
    band_table = band_weights(kernel_y, height, height, margin)
    return jnp.einsum("piz,pio->poz", planes, band_table, precision=lax.Precision.HIGHEST)


def blur_columns(planes, kernel_x):
    margin = (kernel_x.shape[-1] - 1) // 2
    count, height, length = planes.shape
    blocks = planes.reshape(count, height, length // 128, 128)
    empty = jnp.zeros((count, height, 1, 128), jnp.float32)
    left_block = jnp.concatenate([empty, blocks[:, :, :-1]], axis=2)
    right_block = jnp.concatenate([blocks[:, :, 1:], empty], axis=2)
    window = jnp.concatenate([left_block, blocks, right_block], axis=3)
    band_table = band_weights(kernel_x, 384, 128, margin - 128)
    result = jnp.einsum("pybi,pio->pybo", window, band_table, precision=lax.Precision.HIGHEST)
    return result.reshape(count, height, length)


def local_any(cube, taps_x, taps_y, factor_w, factor_h):
    highest = lax.Precision.HIGHEST
    kernel_x = normalized(taps_x[0])
    kernel_y = normalized(taps_y[0])
    rows_done = blur_rows(cube[0], kernel_y)
    w_band = factor_w[0]
    blurred = blur_columns(rows_done, kernel_x)[None]
    moved = lax.all_to_all(blurred, "sp", split_axis=3, concat_axis=1, tiled=True)
    numer_part = jnp.einsum("lr,plyx->pryx", w_band, moved, precision=highest)
    gram_part = jnp.dot(w_band.T, w_band, precision=highest)
    numer_h, gram_w = lax.psum((numer_part[0], gram_part), "bd")
    h_next = factor_h * numer_h / jnp.einsum("rq,qyx->ryx", gram_w, factor_h, precision=highest)
    x_band = moved[0]
    gram_h_part = jnp.einsum("ryx,qyx->rq", h_next, h_next, precision=highest)
    numer_w_part = jnp.einsum("lyx,ryx->lr", x_band, h_next, precision=highest)
    numer_w, gram_h = lax.psum((numer_w_part, gram_h_part), "sp")
    w_next = w_band * numer_w / jnp.dot(w_band, gram_h, precision=highest)
    return (w_next[None], h_next)


def solution(mesh):
    in_specs = (
        P("bd", "sp", None, None),
        P("bd", "sp", None),
        P("bd", "sp", None),
        P("bd", None, None),
        P(None, None, "sp"),
    )
    out_specs = (P("bd", None, None), P(None, None, "sp"))

    def body(cube, *rest):
        suits = lax.axis_size("sp") == 8 and lax.axis_size("bd") == 4 and cube.shape[1] % GROUP == 0
        return (local if suits else local_any)(cube, *rest)

    return jax.shard_map(body, mesh=mesh, in_specs=in_specs, out_specs=out_specs, check_vma=False)
```

```python
import functools

import jax
import jax.numpy as jnp
from jax import lax
from jax.experimental import pallas as pl
from jax.experimental.pallas import tpu as pltpu
from jax.sharding import PartitionSpec as P

F32 = jnp.float32
BF16 = jnp.bfloat16
LANES = 128
GROUP = 16
PIECES = 16
FOLDED = 24
VMEM_LIMIT = 48 * 1024 * 1024


def split(value):
    high = value.astype(BF16)
    low = (value - high.astype(F32)).astype(BF16)
    return high, low


def dot(left, right):
    return lax.dot_general(left, right, (((1,), (0,)), ((), ())), preferred_element_type=F32)


def dot_nt(left, right):
    return lax.dot_general(left, right, (((1,), (1,)), ((), ())), preferred_element_type=F32)


def dot_exact(left, right):
    return lax.dot_general(
        left, right, (((1,), (0,)), ((), ())),
        precision=lax.Precision.HIGHEST, preferred_element_type=F32,
    )


def exchange_blocks(rows, block):
    lane = lax.broadcasted_iota(jnp.int32, rows[0].shape, 1)
    first_half = lane < 2 * block
    even = (lane // block) % 2 == 0
    v0, v1, v2, v3 = rows
    u0 = jnp.where(first_half, v0, pltpu.roll(v2, 2 * block, 1))
    u2 = jnp.where(first_half, pltpu.roll(v0, 2 * block, 1), v2)
    u1 = jnp.where(first_half, v1, pltpu.roll(v3, 2 * block, 1))
    u3 = jnp.where(first_half, pltpu.roll(v1, 2 * block, 1), v3)
    w0 = jnp.where(even, u0, pltpu.roll(u1, block, 1))
    w1 = jnp.where(even, pltpu.roll(u0, 3 * block, 1), u1)
    w2 = jnp.where(even, u2, pltpu.roll(u3, block, 1))
    w3 = jnp.where(even, pltpu.roll(u2, 3 * block, 1), u3)
    return w0, w1, w2, w3


def normalized_taps(taps_ref, reverse, work_ref, out_ref):
    taps = taps_ref.shape[0]
    planes = taps_ref.shape[2]
    work_ref[...] = jnp.zeros_like(work_ref)
    for tap in range(taps):
        row = taps - 1 - tap if reverse else tap
        work_ref[row:row + 1, 0:planes] = taps_ref[tap]
    values = work_ref[...]
    total = jnp.sum(values, axis=0, keepdims=True)
    total = jnp.where(total == 0.0, 1.0, total)
    out_ref[...] = jnp.transpose(values / total)


def column_table(row, margin):
    table = pltpu.roll(jnp.broadcast_to(row, (LANES, LANES)), 0, 1, stride=1, stride_axis=0)
    high = table.astype(BF16).astype(F32)
    src = lax.broadcasted_iota(jnp.int32, (GROUP, LANES), 0)
    dst = lax.broadcasted_iota(jnp.int32, (GROUP, LANES), 1)
    first, last = slice(0, GROUP), slice(LANES - GROUP, LANES)
    above = dst - src <= LANES // 2
    below = src + LANES - GROUP - dst <= LANES // 2
    empty = jnp.zeros((LANES - 2 * GROUP, LANES), F32)
    main, edge = [], []
    for part in (high, table - high):
        main.append(jnp.concatenate(
            [jnp.where(above, part[first], 0.0), part[GROUP:LANES - GROUP], jnp.where(below, part[last], 0.0)],
            axis=0).astype(BF16))
        edge.append(jnp.concatenate(
            [jnp.where(above, 0.0, part[first]), empty, jnp.where(below, 0.0, part[last])],
            axis=0).astype(BF16))
    return jnp.concatenate([jnp.concatenate(main, axis=1), jnp.concatenate(edge, axis=1)], axis=0)


def blur_plane(plane, row, margin):
    height = plane.shape[0]
    table = column_table(row, margin)
    left, right = plane[:, :LANES], plane[:, LANES:]
    lane = lax.broadcasted_iota(jnp.int32, left.shape, 1)
    main = jnp.concatenate([left, right], axis=0)
    edge = jnp.concatenate(
        [jnp.where(lane < LANES // 2, right, 0.0), jnp.where(lane < LANES // 2, 0.0, left)], axis=0)
    high, low = split(jnp.concatenate([main, edge], axis=1))
    product = dot(jnp.concatenate([high, low], axis=0), table)
    rows = 2 * height
    blocks = product[:rows, :LANES] + (product[:rows, LANES:] + product[rows:, :LANES])
    return jnp.concatenate([blocks[:height], blocks[height:]], axis=1)


def row_table(base, margin, height):
    high = base.astype(BF16).astype(F32)
    low = base - high
    plane = lax.broadcasted_iota(jnp.int32, (8, LANES), 0)
    lane = lax.broadcasted_iota(jnp.int32, (8, LANES), 1)
    per_vector = LANES // height
    own = lane // height == plane % per_vector
    masks = [own & (plane // per_vector == part) for part in range(8 * height // LANES)]

    def table(part):
        strips = []
        for row in range(height):
            rolled = pltpu.roll(part, (row - margin) % LANES, 1)
            strips.append(jnp.concatenate([jnp.where(mask, rolled, 0.0) for mask in masks], axis=1))
        return jnp.concatenate(strips, axis=0).astype(BF16)

    return table(high), table(low)


def fold(square):
    side = square.shape[0]
    rest = jnp.zeros((8, LANES - 2 * side), F32)
    return jnp.concatenate(
        [jnp.concatenate([square[first:first + 8], square[first + 8:first + 16], rest], axis=1)
         for first in range(0, side, 16)], axis=0)


def unfold(folded, side):
    blocks = []
    for first in range(0, folded.shape[0], 8):
        blocks += [folded[first:first + 8, :side], folded[first:first + 8, side:2 * side]]
    return jnp.concatenate(blocks, axis=0)


def in_vmem(count):
    return [pl.BlockSpec(memory_space=pltpu.VMEM)] * count


def band_gram(w_rows):
    high, low = split(w_rows)
    rank = w_rows.shape[0]
    padded = jnp.concatenate([high, jnp.zeros((2 * LANES - rank, high.shape[1]), BF16)], axis=0)
    padded_low = jnp.concatenate([low, jnp.zeros((2 * LANES - rank, low.shape[1]), BF16)], axis=0)
    both = dot_nt(jnp.concatenate([high, low], axis=0), padded)
    return both[:rank] + (both[rank:] + dot_nt(high, padded_low))


def blur_group(step, cube_ref, kx_ref, ky_ref, xh_ref, xl_ref, margin):
    height = cube_ref.shape[1]
    halves = []
    for half in range(GROUP // 8):
        done = []
        for k in range(8 * half, 8 * half + 8):
            plane = step * GROUP + k
            done.append(blur_plane(cube_ref[plane], kx_ref[pl.ds(plane, 1), :], margin))
        high, low = split(jnp.concatenate(done, axis=0))
        rows = ky_ref[pl.ds(pl.multiple_of(step * GROUP + 8 * half, 8), 8), :]
        table_high, table_low = row_table(rows, margin, height)
        result = dot(table_high, high) + (dot(table_low, high) + dot(table_high, low))
        halves.append(result.reshape(height, 8, result.shape[1]))
    high, low = split(jnp.concatenate(halves, axis=1))
    planes_here = pl.ds(pl.multiple_of(step * GROUP, GROUP), GROUP)
    xh_ref[:, planes_here, :] = high
    xl_ref[:, planes_here, :] = low


def blur_kernel(cube_hbm, taps_x_hbm, taps_y_hbm, w_hbm, xh_ref, xl_ref, w_here_ref, w_both_ref, keep_ref, give_ref,
                cube_ref, taps_x_ref, taps_y_ref, w_ref, sems, chunk_sems, work_ref, kx_ref, ky_ref):
    taps = taps_x_ref.shape[0]
    margin = (taps - 1) // 2
    height = cube_ref.shape[1]
    rank = w_ref.shape[0]
    groups = cube_ref.shape[0] // GROUP

    def chunk(step):
        here = pl.ds(step * GROUP, GROUP)
        return pltpu.make_async_copy(cube_hbm.at[here], cube_ref.at[here], chunk_sems.at[step])

    copies = [
        pltpu.make_async_copy(taps_x_hbm, taps_x_ref, sems.at[0]),
        pltpu.make_async_copy(taps_y_hbm, taps_y_ref, sems.at[1]),
        pltpu.make_async_copy(w_hbm, w_ref, sems.at[2]),
    ]
    for copy in copies:
        copy.start()
    for step in range(groups):
        chunk(step).start()
    copies[0].wait()
    normalized_taps(taps_x_ref, True, work_ref, kx_ref)
    kx_ref[...] = pltpu.roll(kx_ref[...], LANES - margin, 1)
    copies[1].wait()
    normalized_taps(taps_y_ref, False, work_ref, ky_ref)
    per_vector = LANES // height
    place = lax.broadcasted_iota(jnp.int32, (LANES, LANES), 0) % per_vector
    values = ky_ref[...]
    placed = values
    for k in range(1, per_vector):
        placed = jnp.where(place == k, pltpu.roll(values, k * height, 1), placed)
    ky_ref[...] = placed
    copies[2].wait()

    def body(step, carry):
        chunk(step).wait()
        blur_group(step, cube_ref, kx_ref, ky_ref, xh_ref, xl_ref, margin)
        return carry

    lax.fori_loop(0, groups, body, 0)
    gram = fold(band_gram(w_ref[...])[:, :rank])
    keep_ref[PIECES * rank:] = gram
    give_ref[PIECES * rank:] = gram
    planes = xh_ref.shape[1]
    band = w_ref.shape[1]
    shift = lax.rem(band - lax.axis_index("sp") * planes, band)
    w_here = pltpu.roll(w_ref[...], shift, 1)[:, :2 * LANES]
    w_here_ref[...] = w_here[:, :planes]
    lane = lax.broadcasted_iota(jnp.int32, w_here.shape, 1)
    w_here = jnp.where(lane < planes, w_here, 0.0)
    w_high = w_here.astype(BF16).astype(F32)
    w_both = jnp.concatenate([w_high + pltpu.roll(w_high, planes, 1), w_here - w_high], axis=0).astype(BF16)
    w_both_ref[...] = w_both
    project(xh_ref, xl_ref, w_both[:, :2 * planes], keep_ref, give_ref, 0)


def project(xh_ref, xl_ref, w_both, keep_ref, give_ref, chain):
    height = xh_ref.shape[0]
    rank = w_both.shape[0] // 2
    me_sp = lax.axis_index("sp")
    me_bd = lax.axis_index("bd")
    tall = height // lax.axis_size("bd")
    wide = 2 * LANES // lax.axis_size("sp")
    for rel_bd in (1, 3, 0, 2):
        first_row = lax.bitwise_xor(me_bd, rel_bd) * tall + 4 * chain
        sums = []
        for row in range(4):
            image = jnp.concatenate([xh_ref[first_row + row], xl_ref[first_row + row]], axis=0)
            both = dot(w_both, image)
            sums.append(both[:rank] + both[rank:])
        part_ref = (keep_ref, give_ref)[rel_bd % 2]
        for column in range(2):
            pieces = exchange_blocks(
                [value[:, column * LANES:(column + 1) * LANES] for value in sums], wide)
            for k in range(4):
                rel_sp = lax.bitwise_xor(me_sp, column * 4 + k)
                side = 3 - rel_sp % 2 if rel_bd // 2 else rel_sp % 2
                first = pl.multiple_of((side * 4 + rel_sp // 2) * rank, 8)
                part_ref[pl.ds(first, rank)] = pieces[k]


def project_kernel(xh_ref, xl_ref, w_both_ref, keep_ref, give_ref):
    planes = xh_ref.shape[1]
    project(xh_ref, xl_ref, w_both_ref[:, :2 * planes], keep_ref, give_ref, 1)


def project_call(x_high, x_low, w_both):
    part = jax.ShapeDtypeStruct((PIECES * w_both.shape[0] // 2, LANES), F32)
    return pl.pallas_call(
        project_kernel,
        out_shape=[part, part],
        in_specs=in_vmem(3),
        out_specs=in_vmem(2),
        compiler_params=pltpu.CompilerParams(vmem_limit_bytes=VMEM_LIMIT),
    )(x_high, x_low, w_both)


def blur_call(cube, taps_x, taps_y, w_rows):
    planes, height, length = cube.shape
    rank = w_rows.shape[0]
    first = jax.ShapeDtypeStruct((PIECES * rank + FOLDED, LANES), F32)
    image = (height, planes, length)
    mine = jax.ShapeDtypeStruct((rank, planes), F32)
    both = jax.ShapeDtypeStruct((2 * rank, 2 * LANES), BF16)
    in_hbm = [pltpu.with_memory_space_constraint(value, pltpu.HBM) for value in (cube, taps_x, taps_y, w_rows)]
    return pl.pallas_call(
        blur_kernel,
        out_shape=[jax.ShapeDtypeStruct(image, BF16)] * 2 + [mine, both, first, first],
        in_specs=[pl.BlockSpec(memory_space=pltpu.HBM)] * 4,
        out_specs=in_vmem(6),
        scratch_shapes=[pltpu.VMEM(value.shape, F32) for value in (cube, taps_x, taps_y, w_rows)]
        + [pltpu.SemaphoreType.DMA((3,)), pltpu.SemaphoreType.DMA((planes // GROUP,))]
        + [pltpu.VMEM((LANES, LANES), F32)] * 3,
        compiler_params=pltpu.CompilerParams(vmem_limit_bytes=VMEM_LIMIT),
    )(*in_hbm)


def ratio_kernel(mine_ref, other_ref, h_ref, out_ref):
    tall = h_ref.shape[0] // lax.axis_size("bd")
    first = pl.multiple_of(lax.axis_index("bd") * tall, tall)
    here = h_ref[pl.ds(first, tall)]
    here = jnp.transpose(here.reshape(-1, here.shape[2]))
    rows = mine_ref.shape[0]
    gram = unfold(mine_ref[rows - FOLDED:rows] + other_ref[rows - FOLDED:rows], here.shape[0])
    out_ref[...] = here / dot_exact(gram, here)


def ratio_call(mine, other, h_columns):
    piece = jax.ShapeDtypeStruct((h_columns.shape[2], 2 * LANES), F32)
    return pl.pallas_call(
        ratio_kernel,
        out_shape=piece,
        in_specs=in_vmem(3),
        compiler_params=pltpu.CompilerParams(vmem_limit_bytes=VMEM_LIMIT),
    )(mine, other, h_columns)


def accumulate(xh_ref, xl_ref, part_refs, all_ref, chain, total):
    height, planes, _ = xh_ref.shape
    me_sp = lax.axis_index("sp")
    me_bd = lax.axis_index("bd")
    bands = lax.axis_size("bd")
    pieces = lax.axis_size("sp")
    tall = height // bands
    wide = 2 * LANES // pieces
    for slot, part_ref in enumerate(part_refs):
        rel_bd = slot // 4 + 2 * ((slot // 2) % 2)
        for inner in range(4):
            rel_sp = slot % 2 + 2 * inner
            owner = lax.bitwise_xor(me_bd, rel_bd) * pieces + lax.bitwise_xor(me_sp, rel_sp)
            all_ref[owner] = part_ref[inner]
    for part in range(bands):
        first_row = part * tall + 4 * chain
        halves = [
            exchange_blocks([all_ref[part * pieces + column * 4 + k] for k in range(4)], wide)
            for column in range(2)]
        rows = jnp.concatenate([halves[column][row] for row in range(4) for column in range(2)], axis=1)
        high, low = split(rows)
        here = jnp.concatenate([high, low], axis=0)
        image = [
            jnp.concatenate([ref[first_row + row] for row in range(4)], axis=1) for ref in (xh_ref, xl_ref)]
        total = total + dot_nt(jnp.concatenate(image + [here], axis=0), here)
    return total


def first_kernel(xh_ref, xl_ref, *rest):
    part_refs = rest[:8]
    total_out, all_ref = rest[8:]
    total_out[...] = accumulate(xh_ref, xl_ref, part_refs, all_ref, 0, jnp.zeros(total_out.shape, F32))


def first_call(x_high, x_low, parts):
    _, planes, _ = x_high.shape
    rank = parts[0].shape[1]
    return pl.pallas_call(
        first_kernel,
        out_shape=jax.ShapeDtypeStruct((2 * (planes + rank), 2 * rank), F32),
        in_specs=in_vmem(2 + len(parts)),
        scratch_shapes=[pltpu.VMEM((32, rank, LANES), F32)],
        compiler_params=pltpu.CompilerParams(vmem_limit_bytes=VMEM_LIMIT),
    )(x_high, x_low, *parts)


def second_kernel(xh_ref, xl_ref, w_ref, total_ref, *rest):
    part_refs = rest[:8]
    w_out, all_ref = rest[8:]
    planes = xh_ref.shape[1]
    rank = w_ref.shape[0]
    total = accumulate(xh_ref, xl_ref, part_refs, all_ref, 1, total_ref[...])
    numer = total[:planes, :rank] + (total[:planes, rank:] + total[planes:2 * planes, :rank])
    gram = total[2 * planes:]
    gram = gram[:rank, :rank] + (gram[:rank, rank:] + gram[rank:, :rank])
    w_here = w_ref[...]
    w_out[...] = w_here * jnp.transpose(numer) / dot_exact(gram, w_here)


def second_call(x_high, x_low, w_here, total, parts):
    rank = w_here.shape[0]
    return pl.pallas_call(
        second_kernel,
        out_shape=jax.ShapeDtypeStruct(w_here.shape, F32),
        in_specs=in_vmem(4 + len(parts)),
        scratch_shapes=[pltpu.VMEM((32, rank, LANES), F32)],
        compiler_params=pltpu.CompilerParams(vmem_limit_bytes=VMEM_LIMIT),
    )(x_high, x_low, w_here, total, *parts)


def place_h_kernel(*refs):
    h_out = refs[-1]
    me_bd = lax.axis_index("bd")
    tall = h_out.shape[0] // lax.axis_size("bd")
    for chain in range(2):
        for rel_bd in range(4):
            piece = refs[4 * chain + rel_bd][0]
            first = lax.bitwise_xor(me_bd, rel_bd) * tall + 4 * chain
            h_out[pl.ds(first, 4)] = jnp.transpose(piece).reshape((4,) + h_out.shape[1:])


def place_h_call(parts, shape):
    return pl.pallas_call(
        place_h_kernel,
        out_shape=jax.ShapeDtypeStruct(shape, F32),
        in_specs=in_vmem(len(parts)),
        compiler_params=pltpu.CompilerParams(vmem_limit_bytes=VMEM_LIMIT),
    )(*parts)


def gather_w_kernel(*refs):
    part_refs = refs[:-2]
    out_ref, all_ref = refs[-2:]
    planes = out_ref.shape[1] // 8
    me_sp = lax.axis_index("sp")
    rel = 0
    for part_ref in part_refs:
        for inner in range(part_ref.shape[0]):
            all_ref[lax.bitwise_xor(me_sp, RING[rel]), :, 0:planes] = part_ref[inner]
            rel += 1
    for owner in range(8):
        out_ref[:, owner * planes:(owner + 1) * planes] = all_ref[owner][:, :planes]


RING = (0, 1, 2, 3, 4, 5, 6, 7)


def gather_w_call(parts):
    _, rank, planes = parts[0].shape
    return pl.pallas_call(
        gather_w_kernel,
        out_shape=jax.ShapeDtypeStruct((rank, planes * 8), F32),
        in_specs=in_vmem(len(parts)),
        scratch_shapes=[pltpu.VMEM((8, rank, LANES), F32)],
        compiler_params=pltpu.CompilerParams(vmem_limit_bytes=VMEM_LIMIT),
    )(*parts)


def send(value, mask_sp, mask_bd):
    bands = lax.axis_size("bd")
    pieces = lax.axis_size("sp")
    pairs = []
    for s in range(pieces):
        for b in range(bands):
            pairs.append((s * bands + b, (s ^ mask_sp) * bands + (b ^ mask_bd)))
    return lax.ppermute(value, ("sp", "bd"), pairs)


def around(values):
    return [send(values[k], k % 2, 2 * (k // 2)) for k in range(1, 4)]


def local(cube, taps_x, taps_y, factor_w, factor_h):
    w_rows = jnp.transpose(factor_w[0])
    taps_x = jnp.transpose(taps_x, (2, 0, 1))
    taps_y = jnp.transpose(taps_y, (2, 0, 1))
    h_columns = jnp.transpose(factor_h, (1, 2, 0))
    rank = w_rows.shape[0]
    x_high, x_low, w_here, w_both, keep_0, give_0 = blur_call(cube[0], taps_x, taps_y, w_rows)
    chains = []
    taken_0 = send(give_0, 0, 1)
    keep_1, give_1 = project_call(x_high, x_low, w_both)
    taken_0, keep_1, give_1 = lax.optimization_barrier((taken_0, keep_1, give_1))
    for keep, taken in ((keep_0, taken_0), (keep_1, send(give_1, 0, 1))):
        bounds = [place * 4 * rank for place in (0, 1, 3, 2)]
        sides = []
        for first in bounds:
            last = keep.shape[0] if first == max(bounds) else first + 4 * rank
            sides.append(keep[first:last] + taken[first:last])
        chains.append((sides, around(sides)))
    ratio = ratio_call(chains[0][0][2], chains[0][1][1], h_columns)
    numer = []
    for sides, others in chains:
        line = []
        for k in range(4):
            part = slice(k * rank, (k + 1) * rank)
            line.append((sides[0][part] + others[0][part]) + (others[1][part] + others[2][part]))
        line = [line[0]] + [send(line[k], 2 * k, 0) for k in range(1, 4)]
        numer.append((line[0] + line[1]) + (line[2] + line[3]))
    h_piece = ratio * jnp.concatenate(numer, axis=1)
    h_line = [h_piece] + [send(h_piece, 2 * k, 0) for k in range(1, 4)]
    chains = []
    for first in (0, LANES):
        mine = jnp.stack([value[:, first:first + LANES] for value in h_line])
        chains.append([mine] + around([mine] * 4))
    first_parts = chains[0] + [send(value, 0, 1) for value in chains[0]]
    total = first_call(x_high, x_low, first_parts)
    second_parts = chains[1] + [send(value, 0, 1) for value in chains[1]]
    w_piece = second_call(x_high, x_low, w_here, total, second_parts)
    own = [parts[k] for parts in (first_parts, second_parts) for k in (0, 4, 2, 6)]
    h_next = place_h_call(own, h_columns.shape)
    w_pair = jnp.stack([w_piece, send(w_piece, 1, 0)])
    w_next = gather_w_call([w_pair] + [send(w_pair, 2 * k, 0) for k in range(1, 4)])
    return jnp.transpose(w_next)[None], jnp.transpose(h_next, (2, 0, 1))


def normalized(kernel):
    return kernel / jnp.sum(kernel, axis=-1, keepdims=True)


def band_weights(kernel, size_in, size_out, offset):
    tap_count = kernel.shape[-1]
    in_index = lax.broadcasted_iota(jnp.int32, (size_in, size_out, tap_count), 0)
    out_index = lax.broadcasted_iota(jnp.int32, (size_in, size_out, tap_count), 1)
    tap_index = lax.broadcasted_iota(jnp.int32, (size_in, size_out, tap_count), 2)
    select = (tap_index == in_index - out_index + offset).astype(jnp.float32)
    return jnp.einsum("pk,iok->pio", kernel, select, precision=lax.Precision.HIGHEST)


def blur_rows(planes, kernel_y):
    margin = (kernel_y.shape[-1] - 1) // 2
    height = planes.shape[1]
    band_table = band_weights(kernel_y, height, height, margin)
    return jnp.einsum("piz,pio->poz", planes, band_table, precision=lax.Precision.HIGHEST)


def blur_columns(planes, kernel_x):
    margin = (kernel_x.shape[-1] - 1) // 2
    count, height, length = planes.shape
    blocks = planes.reshape(count, height, length // 128, 128)
    empty = jnp.zeros((count, height, 1, 128), jnp.float32)
    left_block = jnp.concatenate([empty, blocks[:, :, :-1]], axis=2)
    right_block = jnp.concatenate([blocks[:, :, 1:], empty], axis=2)
    window = jnp.concatenate([left_block, blocks, right_block], axis=3)
    band_table = band_weights(kernel_x, 384, 128, margin - 128)
    result = jnp.einsum("pybi,pio->pybo", window, band_table, precision=lax.Precision.HIGHEST)
    return result.reshape(count, height, length)


def local_any(cube, taps_x, taps_y, factor_w, factor_h):
    highest = lax.Precision.HIGHEST
    kernel_x = normalized(taps_x[0])
    kernel_y = normalized(taps_y[0])
    rows_done = blur_rows(cube[0], kernel_y)
    w_band = factor_w[0]
    blurred = blur_columns(rows_done, kernel_x)[None]
    moved = lax.all_to_all(blurred, "sp", split_axis=3, concat_axis=1, tiled=True)
    numer_part = jnp.einsum("lr,plyx->pryx", w_band, moved, precision=highest)
    gram_part = jnp.dot(w_band.T, w_band, precision=highest)
    numer_h, gram_w = lax.psum((numer_part[0], gram_part), "bd")
    h_next = factor_h * numer_h / jnp.einsum("rq,qyx->ryx", gram_w, factor_h, precision=highest)
    x_band = moved[0]
    gram_h_part = jnp.einsum("ryx,qyx->rq", h_next, h_next, precision=highest)
    numer_w_part = jnp.einsum("lyx,ryx->lr", x_band, h_next, precision=highest)
    numer_w, gram_h = lax.psum((numer_w_part, gram_h_part), "sp")
    w_next = w_band * numer_w / jnp.dot(w_band, gram_h, precision=highest)
    return (w_next[None], h_next)


def solution(mesh):
    in_specs = (
        P("bd", "sp", None, None),
        P("bd", "sp", None),
        P("bd", "sp", None),
        P("bd", None, None),
        P(None, None, "sp"),
    )
    out_specs = (P("bd", None, None), P(None, None, "sp"))

    def body(cube, *rest):
        suits = lax.axis_size("sp") == 8 and lax.axis_size("bd") == 4 and cube.shape[1] % GROUP == 0
        return (local if suits else local_any)(cube, *rest)

    return jax.shard_map(body, mesh=mesh, in_specs=in_specs, out_specs=out_specs, check_vma=False)
```

```python
import functools

import jax
import jax.numpy as jnp
from jax import lax
from jax.experimental import pallas as pl
from jax.experimental.pallas import tpu as pltpu
from jax.sharding import PartitionSpec as P

F32 = jnp.float32
BF16 = jnp.bfloat16
LANES = 128
GROUP = 16
PIECES = 32
FOLDED = 24
VMEM_LIMIT = 48 * 1024 * 1024


def split(value):
    high = value.astype(BF16)
    low = (value - high.astype(F32)).astype(BF16)
    return high, low


def dot(left, right):
    return lax.dot_general(left, right, (((1,), (0,)), ((), ())), preferred_element_type=F32)


def dot_nt(left, right):
    return lax.dot_general(left, right, (((1,), (1,)), ((), ())), preferred_element_type=F32)


def dot_exact(left, right):
    return lax.dot_general(
        left, right, (((1,), (0,)), ((), ())),
        precision=lax.Precision.HIGHEST, preferred_element_type=F32,
    )


def exchange_blocks(rows, block):
    lane = lax.broadcasted_iota(jnp.int32, rows[0].shape, 1)
    first_half = lane < 2 * block
    even = (lane // block) % 2 == 0
    v0, v1, v2, v3 = rows
    u0 = jnp.where(first_half, v0, pltpu.roll(v2, 2 * block, 1))
    u2 = jnp.where(first_half, pltpu.roll(v0, 2 * block, 1), v2)
    u1 = jnp.where(first_half, v1, pltpu.roll(v3, 2 * block, 1))
    u3 = jnp.where(first_half, pltpu.roll(v1, 2 * block, 1), v3)
    w0 = jnp.where(even, u0, pltpu.roll(u1, block, 1))
    w1 = jnp.where(even, pltpu.roll(u0, 3 * block, 1), u1)
    w2 = jnp.where(even, u2, pltpu.roll(u3, block, 1))
    w3 = jnp.where(even, pltpu.roll(u2, 3 * block, 1), u3)
    return w0, w1, w2, w3


def normalized_taps(taps_ref, reverse, work_ref, out_ref):
    taps = taps_ref.shape[0]
    planes = taps_ref.shape[2]
    work_ref[...] = jnp.zeros_like(work_ref)
    for tap in range(taps):
        row = taps - 1 - tap if reverse else tap
        work_ref[row:row + 1, 0:planes] = taps_ref[tap]
    values = work_ref[...]
    total = jnp.sum(values, axis=0, keepdims=True)
    total = jnp.where(total == 0.0, 1.0, total)
    out_ref[...] = jnp.transpose(values / total)


def column_table(row, margin):
    table = pltpu.roll(jnp.broadcast_to(row, (LANES, LANES)), 0, 1, stride=1, stride_axis=0)
    high = table.astype(BF16).astype(F32)
    src = lax.broadcasted_iota(jnp.int32, (GROUP, LANES), 0)
    dst = lax.broadcasted_iota(jnp.int32, (GROUP, LANES), 1)
    first, last = slice(0, GROUP), slice(LANES - GROUP, LANES)
    above = dst - src <= LANES // 2
    below = src + LANES - GROUP - dst <= LANES // 2
    empty = jnp.zeros((LANES - 2 * GROUP, LANES), F32)
    main, edge = [], []
    for part in (high, table - high):
        main.append(jnp.concatenate(
            [jnp.where(above, part[first], 0.0), part[GROUP:LANES - GROUP], jnp.where(below, part[last], 0.0)],
            axis=0).astype(BF16))
        edge.append(jnp.concatenate(
            [jnp.where(above, 0.0, part[first]), empty, jnp.where(below, 0.0, part[last])],
            axis=0).astype(BF16))
    return jnp.concatenate([jnp.concatenate(main, axis=1), jnp.concatenate(edge, axis=1)], axis=0)


def blur_plane(plane, row, margin):
    height = plane.shape[0]
    table = column_table(row, margin)
    left, right = plane[:, :LANES], plane[:, LANES:]
    lane = lax.broadcasted_iota(jnp.int32, left.shape, 1)
    main = jnp.concatenate([left, right], axis=0)
    edge = jnp.concatenate(
        [jnp.where(lane < LANES // 2, right, 0.0), jnp.where(lane < LANES // 2, 0.0, left)], axis=0)
    high, low = split(jnp.concatenate([main, edge], axis=1))
    product = dot(jnp.concatenate([high, low], axis=0), table)
    rows = 2 * height
    blocks = product[:rows, :LANES] + (product[:rows, LANES:] + product[rows:, :LANES])
    return jnp.concatenate([blocks[:height], blocks[height:]], axis=1)


def row_table(base, margin, height):
    high = base.astype(BF16).astype(F32)
    low = base - high
    plane = lax.broadcasted_iota(jnp.int32, (8, LANES), 0)
    lane = lax.broadcasted_iota(jnp.int32, (8, LANES), 1)
    per_vector = LANES // height
    own = lane // height == plane % per_vector
    masks = [own & (plane // per_vector == part) for part in range(8 * height // LANES)]

    def table(part):
        strips = []
        for row in range(height):
            rolled = pltpu.roll(part, (row - margin) % LANES, 1)
            strips.append(jnp.concatenate([jnp.where(mask, rolled, 0.0) for mask in masks], axis=1))
        return jnp.concatenate(strips, axis=0).astype(BF16)

    return table(high), table(low)


def fold(square):
    side = square.shape[0]
    rest = jnp.zeros((8, LANES - 2 * side), F32)
    return jnp.concatenate(
        [jnp.concatenate([square[first:first + 8], square[first + 8:first + 16], rest], axis=1)
         for first in range(0, side, 16)], axis=0)


def unfold(folded, side):
    blocks = []
    for first in range(0, folded.shape[0], 8):
        blocks += [folded[first:first + 8, :side], folded[first:first + 8, side:2 * side]]
    return jnp.concatenate(blocks, axis=0)


def in_vmem(count):
    return [pl.BlockSpec(memory_space=pltpu.VMEM)] * count


def band_gram(w_rows):
    high, low = split(w_rows)
    rank = w_rows.shape[0]
    padded = jnp.concatenate([high, jnp.zeros((2 * LANES - rank, high.shape[1]), BF16)], axis=0)
    padded_low = jnp.concatenate([low, jnp.zeros((2 * LANES - rank, low.shape[1]), BF16)], axis=0)
    both = dot_nt(jnp.concatenate([high, low], axis=0), padded)
    return both[:rank] + (both[rank:] + dot_nt(high, padded_low))


def blur_group(step, cube_ref, kx_ref, ky_ref, xh_ref, xl_ref, margin):
    height = cube_ref.shape[1]
    halves = []
    for half in range(GROUP // 8):
        done = []
        for k in range(8 * half, 8 * half + 8):
            plane = step * GROUP + k
            done.append(blur_plane(cube_ref[plane], kx_ref[pl.ds(plane, 1), :], margin))
        high, low = split(jnp.concatenate(done, axis=0))
        rows = ky_ref[pl.ds(pl.multiple_of(step * GROUP + 8 * half, 8), 8), :]
        table_high, table_low = row_table(rows, margin, height)
        result = dot(table_high, high) + (dot(table_low, high) + dot(table_high, low))
        halves.append(result.reshape(height, 8, result.shape[1]))
    high, low = split(jnp.concatenate(halves, axis=1))
    planes_here = pl.ds(pl.multiple_of(step * GROUP, GROUP), GROUP)
    xh_ref[:, planes_here, :] = high
    xl_ref[:, planes_here, :] = low


def blur_kernel(cube_hbm, taps_x_hbm, taps_y_hbm, w_hbm, xh_ref, xl_ref, w_here_ref, w_both_ref, part_ref,
                cube_ref, taps_x_ref, taps_y_ref, w_ref, sems, chunk_sems, work_ref, kx_ref, ky_ref):
    taps = taps_x_ref.shape[0]
    margin = (taps - 1) // 2
    height = cube_ref.shape[1]
    rank = w_ref.shape[0]
    groups = cube_ref.shape[0] // GROUP

    def chunk(step):
        here = pl.ds(step * GROUP, GROUP)
        return pltpu.make_async_copy(cube_hbm.at[here], cube_ref.at[here], chunk_sems.at[step])

    copies = [
        pltpu.make_async_copy(taps_x_hbm, taps_x_ref, sems.at[0]),
        pltpu.make_async_copy(taps_y_hbm, taps_y_ref, sems.at[1]),
        pltpu.make_async_copy(w_hbm, w_ref, sems.at[2]),
    ]
    for copy in copies:
        copy.start()
    for step in range(groups):
        chunk(step).start()
    copies[0].wait()
    normalized_taps(taps_x_ref, True, work_ref, kx_ref)
    kx_ref[...] = pltpu.roll(kx_ref[...], LANES - margin, 1)
    copies[1].wait()
    normalized_taps(taps_y_ref, False, work_ref, ky_ref)
    per_vector = LANES // height
    place = lax.broadcasted_iota(jnp.int32, (LANES, LANES), 0) % per_vector
    values = ky_ref[...]
    placed = values
    for k in range(1, per_vector):
        placed = jnp.where(place == k, pltpu.roll(values, k * height, 1), placed)
    ky_ref[...] = placed
    copies[2].wait()

    def body(step, carry):
        chunk(step).wait()
        blur_group(step, cube_ref, kx_ref, ky_ref, xh_ref, xl_ref, margin)
        return carry

    lax.fori_loop(0, groups, body, 0)
    gram = fold(band_gram(w_ref[...])[:, :rank])
    part_ref[PIECES * rank:] = gram
    planes = xh_ref.shape[1]
    band = w_ref.shape[1]
    shift = lax.rem(band - lax.axis_index("sp") * planes, band)
    w_here = pltpu.roll(w_ref[...], shift, 1)[:, :2 * LANES]
    w_here_ref[...] = w_here[:, :planes]
    lane = lax.broadcasted_iota(jnp.int32, w_here.shape, 1)
    w_here = jnp.where(lane < planes, w_here, 0.0)
    w_high = w_here.astype(BF16).astype(F32)
    w_both = jnp.concatenate([w_high + pltpu.roll(w_high, planes, 1), w_here - w_high], axis=0).astype(BF16)
    w_both_ref[...] = w_both
    project(xh_ref, xl_ref, w_both[:, :2 * planes], part_ref, 0)


def project(xh_ref, xl_ref, w_both, part_ref, chain):
    height = xh_ref.shape[0]
    rank = w_both.shape[0] // 2
    me_sp = lax.axis_index("sp")
    me_bd = lax.axis_index("bd")
    tall = height // lax.axis_size("bd")
    wide = 2 * LANES // lax.axis_size("sp")
    for side in range(4):
        rel_row, core = side // 2, side % 2
        first_row = (lax.bitwise_xor(me_bd // 2, rel_row) * 2 + core) * tall + 4 * chain
        sums = []
        for row in range(4):
            image = jnp.concatenate([xh_ref[first_row + row], xl_ref[first_row + row]], axis=0)
            both = dot(w_both, image)
            sums.append(both[:rank] + both[rank:])
        for column in range(2):
            pieces = exchange_blocks(
                [value[:, column * LANES:(column + 1) * LANES] for value in sums], wide)
            for k in range(4):
                rel_sp = lax.bitwise_xor(me_sp, column * 4 + k)
                place = 3 - rel_sp % 2 if rel_row else rel_sp % 2
                first = pl.multiple_of(((place * 4 + rel_sp // 2) * 2 + core) * rank, 8)
                part_ref[pl.ds(first, rank)] = pieces[k]


def project_kernel(xh_ref, xl_ref, w_both_ref, part_ref):
    planes = xh_ref.shape[1]
    project(xh_ref, xl_ref, w_both_ref[:, :2 * planes], part_ref, 1)


def project_call(x_high, x_low, w_both):
    part = jax.ShapeDtypeStruct((PIECES * w_both.shape[0] // 2, LANES), F32)
    return pl.pallas_call(
        project_kernel,
        out_shape=part,
        in_specs=in_vmem(3),
        out_specs=in_vmem(1)[0],
        compiler_params=pltpu.CompilerParams(vmem_limit_bytes=VMEM_LIMIT),
    )(x_high, x_low, w_both)


def blur_call(cube, taps_x, taps_y, w_rows):
    planes, height, length = cube.shape
    rank = w_rows.shape[0]
    first = jax.ShapeDtypeStruct((PIECES * rank + FOLDED, LANES), F32)
    image = (height, planes, length)
    mine = jax.ShapeDtypeStruct((rank, planes), F32)
    both = jax.ShapeDtypeStruct((2 * rank, 2 * LANES), BF16)
    in_hbm = [pltpu.with_memory_space_constraint(value, pltpu.HBM) for value in (cube, taps_x, taps_y, w_rows)]
    return pl.pallas_call(
        blur_kernel,
        out_shape=[jax.ShapeDtypeStruct(image, BF16)] * 2 + [mine, both, first],
        in_specs=[pl.BlockSpec(memory_space=pltpu.HBM)] * 4,
        out_specs=in_vmem(5),
        scratch_shapes=[pltpu.VMEM(value.shape, F32) for value in (cube, taps_x, taps_y, w_rows)]
        + [pltpu.SemaphoreType.DMA((3,)), pltpu.SemaphoreType.DMA((planes // GROUP,))]
        + [pltpu.VMEM((LANES, LANES), F32)] * 3,
        compiler_params=pltpu.CompilerParams(vmem_limit_bytes=VMEM_LIMIT),
    )(*in_hbm)


def ratio_kernel(mine_ref, other_ref, h_ref, out_ref):
    tall = h_ref.shape[0] // lax.axis_size("bd")
    rank = h_ref.shape[2]
    rows = mine_ref.shape[0]
    gram = unfold(mine_ref[rows - FOLDED:rows] + other_ref[rows - FOLDED:rows], rank)
    for core in range(2):
        first = pl.multiple_of((lax.axis_index("bd") // 2 * 2 + core) * tall, tall)
        here = h_ref[pl.ds(first, tall)]
        here = jnp.transpose(here.reshape(-1, rank))
        out_ref[core * rank:(core + 1) * rank] = here / dot_exact(gram, here)


def ratio_call(mine, other, h_columns):
    piece = jax.ShapeDtypeStruct((2 * h_columns.shape[2], 2 * LANES), F32)
    return pl.pallas_call(
        ratio_kernel,
        out_shape=piece,
        in_specs=in_vmem(3),
        compiler_params=pltpu.CompilerParams(vmem_limit_bytes=VMEM_LIMIT),
    )(mine, other, h_columns)


def pick(own, received):
    return jnp.where(lax.axis_index("bd") % 2 == 1, own, received)


def accumulate(xh_ref, xl_ref, part_refs, all_ref, chain, total):
    height, planes, _ = xh_ref.shape
    me_sp = lax.axis_index("sp")
    me_bd = lax.axis_index("bd")
    bands = lax.axis_size("bd")
    pieces = lax.axis_size("sp")
    tall = height // bands
    wide = 2 * LANES // pieces
    rank = all_ref.shape[1]
    for partner in range(4):
        row = lax.bitwise_xor(me_bd // 2, partner // 2)
        for inner in range(4):
            owner_sp = lax.bitwise_xor(me_sp, partner % 2 + 2 * inner)
            both = pick(part_refs[partner][inner], part_refs[4 + partner][inner])
            for core in range(2):
                all_ref[(2 * row + core) * pieces + owner_sp] = both[core * rank:(core + 1) * rank]
    for part in range(bands):
        first_row = part * tall + 4 * chain
        halves = [
            exchange_blocks([all_ref[part * pieces + column * 4 + k] for k in range(4)], wide)
            for column in range(2)]
        rows = jnp.concatenate([halves[column][row] for row in range(4) for column in range(2)], axis=1)
        high, low = split(rows)
        here = jnp.concatenate([high, low], axis=0)
        image = [
            jnp.concatenate([ref[first_row + row] for row in range(4)], axis=1) for ref in (xh_ref, xl_ref)]
        total = total + dot_nt(jnp.concatenate(image + [here], axis=0), here)
    return total


def first_kernel(xh_ref, xl_ref, *rest):
    part_refs = rest[:8]
    total_out, all_ref = rest[8:]
    total_out[...] = accumulate(xh_ref, xl_ref, part_refs, all_ref, 0, jnp.zeros(total_out.shape, F32))


def first_call(x_high, x_low, parts):
    _, planes, _ = x_high.shape
    rank = parts[0].shape[1] // 2
    return pl.pallas_call(
        first_kernel,
        out_shape=jax.ShapeDtypeStruct((2 * (planes + rank), 2 * rank), F32),
        in_specs=in_vmem(2 + len(parts)),
        scratch_shapes=[pltpu.VMEM((32, rank, LANES), F32)],
        compiler_params=pltpu.CompilerParams(vmem_limit_bytes=VMEM_LIMIT),
    )(x_high, x_low, *parts)


def second_kernel(xh_ref, xl_ref, w_ref, total_ref, *rest):
    part_refs = rest[:8]
    w_out, all_ref = rest[8:]
    planes = xh_ref.shape[1]
    rank = w_ref.shape[0]
    total = accumulate(xh_ref, xl_ref, part_refs, all_ref, 1, total_ref[...])
    numer = total[:planes, :rank] + (total[:planes, rank:] + total[planes:2 * planes, :rank])
    gram = total[2 * planes:]
    gram = gram[:rank, :rank] + (gram[:rank, rank:] + gram[rank:, :rank])
    w_here = w_ref[...]
    w_out[...] = w_here * jnp.transpose(numer) / dot_exact(gram, w_here)


def second_call(x_high, x_low, w_here, total, parts):
    rank = w_here.shape[0]
    return pl.pallas_call(
        second_kernel,
        out_shape=jax.ShapeDtypeStruct(w_here.shape, F32),
        in_specs=in_vmem(4 + len(parts)),
        scratch_shapes=[pltpu.VMEM((32, rank, LANES), F32)],
        compiler_params=pltpu.CompilerParams(vmem_limit_bytes=VMEM_LIMIT),
    )(x_high, x_low, w_here, total, *parts)


def place_h_kernel(*refs):
    h_out = refs[-1]
    me_bd = lax.axis_index("bd")
    tall = h_out.shape[0] // lax.axis_size("bd")
    rank = h_out.shape[2]
    for chain in range(2):
        for rel_row in range(2):
            own_ref, received_ref = refs[4 * chain + 2 * rel_row:4 * chain + 2 * rel_row + 2]
            both = pick(own_ref[0], received_ref[0])
            for core in range(2):
                first = (lax.bitwise_xor(me_bd // 2, rel_row) * 2 + core) * tall + 4 * chain
                piece = jnp.transpose(both[core * rank:(core + 1) * rank])
                h_out[pl.ds(first, 4)] = piece.reshape((4,) + h_out.shape[1:])


def place_h_call(parts, shape):
    return pl.pallas_call(
        place_h_kernel,
        out_shape=jax.ShapeDtypeStruct(shape, F32),
        in_specs=in_vmem(len(parts)),
        compiler_params=pltpu.CompilerParams(vmem_limit_bytes=VMEM_LIMIT),
    )(*parts)


def gather_w_kernel(*refs):
    part_refs = refs[:-2]
    out_ref, all_ref = refs[-2:]
    planes = out_ref.shape[1] // 8
    me_sp = lax.axis_index("sp")
    rel = 0
    for part_ref in part_refs:
        for inner in range(part_ref.shape[0]):
            all_ref[lax.bitwise_xor(me_sp, RING[rel]), :, 0:planes] = part_ref[inner]
            rel += 1
    for owner in range(8):
        out_ref[:, owner * planes:(owner + 1) * planes] = all_ref[owner][:, :planes]


RING = (0, 1, 2, 3, 4, 5, 6, 7)


def gather_w_call(parts):
    _, rank, planes = parts[0].shape
    return pl.pallas_call(
        gather_w_kernel,
        out_shape=jax.ShapeDtypeStruct((rank, planes * 8), F32),
        in_specs=in_vmem(len(parts)),
        scratch_shapes=[pltpu.VMEM((8, rank, LANES), F32)],
        compiler_params=pltpu.CompilerParams(vmem_limit_bytes=VMEM_LIMIT),
    )(*parts)


def send(value, mask_sp, mask_bd):
    bands = lax.axis_size("bd")
    pieces = lax.axis_size("sp")
    pairs = []
    for s in range(pieces):
        for b in range(bands):
            pairs.append((s * bands + b, (s ^ mask_sp) * bands + (b ^ mask_bd)))
    return lax.ppermute(value, ("sp", "bd"), pairs)


def send_odd(value, mask_sp, mask_bd):
    bands = lax.axis_size("bd")
    pieces = lax.axis_size("sp")
    pairs = []
    for s in range(pieces):
        for b in range(1, bands, 2):
            pairs.append((s * bands + b, (s ^ mask_sp) * bands + (b ^ mask_bd)))
    return lax.ppermute(value, ("sp", "bd"), pairs)


def send_core(value, source):
    count = lax.axis_size("bd") * lax.axis_size("sp")
    return lax.ppermute(value, ("sp", "bd"), [(d, d ^ 1) for d in range(source, count, 2)])


def around(value):
    return [send_odd(value[k], k % 2, 2 * (k // 2)) for k in range(1, 4)]


def local(cube, taps_x, taps_y, factor_w, factor_h):
    w_rows = jnp.transpose(factor_w[0])
    taps_x = jnp.transpose(taps_x, (2, 0, 1))
    taps_y = jnp.transpose(taps_y, (2, 0, 1))
    h_columns = jnp.transpose(factor_h, (1, 2, 0))
    rank = w_rows.shape[0]
    x_high, x_low, w_here, w_both, part_0 = blur_call(cube[0], taps_x, taps_y, w_rows)
    taken_0 = send_core(part_0, 0)
    part_1 = project_call(x_high, x_low, w_both)
    taken_0, part_1 = lax.optimization_barrier((taken_0, part_1))
    chains = []
    for part, taken in ((part_0, taken_0), (part_1, send_core(part_1, 0))):
        bounds = [place * 8 * rank for place in (0, 1, 3, 2)]
        sides = []
        for first in bounds:
            last = part.shape[0] if first == max(bounds) else first + 8 * rank
            sides.append(part[first:last] + taken[first:last])
        chains.append((sides, around(sides)))
    ratio = ratio_call(chains[0][0][2], chains[0][1][1], h_columns)
    line = []
    for k in range(4):
        here = slice(2 * k * rank, 2 * (k + 1) * rank)
        line.append(jnp.concatenate(
            [(sides[0][here] + others[0][here]) + (others[1][here] + others[2][here]) for sides, others in chains],
            axis=1))
    line = [line[0]] + [send_odd(line[k], 2 * k, 0) for k in (3, 2, 1)]
    h_piece = ratio * ((line[0] + line[1]) + (line[2] + line[3]))
    h_line = [h_piece] + [send_odd(h_piece, 2 * k, 0) for k in range(1, 4)]
    chains = []
    for first in (0, LANES):
        mine = jnp.stack([value[:, first:first + LANES] for value in h_line])
        own = [mine] + around([mine] * 4)
        chains.append(own + [send_core(value, 1) for value in own])
    total = first_call(x_high, x_low, chains[0])
    w_piece = second_call(x_high, x_low, w_here, total, chains[1])
    own = [parts[k] for parts in chains for k in (0, 4, 2, 6)]
    h_next = place_h_call(own, h_columns.shape)
    w_pair = jnp.stack([w_piece, send(w_piece, 1, 0)])
    w_next = gather_w_call([w_pair] + [send(w_pair, 2 * k, 0) for k in range(1, 4)])
    return jnp.transpose(w_next)[None], jnp.transpose(h_next, (2, 0, 1))


def normalized(kernel):
    return kernel / jnp.sum(kernel, axis=-1, keepdims=True)


def band_weights(kernel, size_in, size_out, offset):
    tap_count = kernel.shape[-1]
    in_index = lax.broadcasted_iota(jnp.int32, (size_in, size_out, tap_count), 0)
    out_index = lax.broadcasted_iota(jnp.int32, (size_in, size_out, tap_count), 1)
    tap_index = lax.broadcasted_iota(jnp.int32, (size_in, size_out, tap_count), 2)
    select = (tap_index == in_index - out_index + offset).astype(jnp.float32)
    return jnp.einsum("pk,iok->pio", kernel, select, precision=lax.Precision.HIGHEST)


def blur_rows(planes, kernel_y):
    margin = (kernel_y.shape[-1] - 1) // 2
    height = planes.shape[1]
    band_table = band_weights(kernel_y, height, height, margin)
    return jnp.einsum("piz,pio->poz", planes, band_table, precision=lax.Precision.HIGHEST)


def blur_columns(planes, kernel_x):
    margin = (kernel_x.shape[-1] - 1) // 2
    count, height, length = planes.shape
    blocks = planes.reshape(count, height, length // 128, 128)
    empty = jnp.zeros((count, height, 1, 128), jnp.float32)
    left_block = jnp.concatenate([empty, blocks[:, :, :-1]], axis=2)
    right_block = jnp.concatenate([blocks[:, :, 1:], empty], axis=2)
    window = jnp.concatenate([left_block, blocks, right_block], axis=3)
    band_table = band_weights(kernel_x, 384, 128, margin - 128)
    result = jnp.einsum("pybi,pio->pybo", window, band_table, precision=lax.Precision.HIGHEST)
    return result.reshape(count, height, length)


def local_any(cube, taps_x, taps_y, factor_w, factor_h):
    highest = lax.Precision.HIGHEST
    kernel_x = normalized(taps_x[0])
    kernel_y = normalized(taps_y[0])
    rows_done = blur_rows(cube[0], kernel_y)
    w_band = factor_w[0]
    blurred = blur_columns(rows_done, kernel_x)[None]
    moved = lax.all_to_all(blurred, "sp", split_axis=3, concat_axis=1, tiled=True)
    numer_part = jnp.einsum("lr,plyx->pryx", w_band, moved, precision=highest)
    gram_part = jnp.dot(w_band.T, w_band, precision=highest)
    numer_h, gram_w = lax.psum((numer_part[0], gram_part), "bd")
    h_next = factor_h * numer_h / jnp.einsum("rq,qyx->ryx", gram_w, factor_h, precision=highest)
    x_band = moved[0]
    gram_h_part = jnp.einsum("ryx,qyx->rq", h_next, h_next, precision=highest)
    numer_w_part = jnp.einsum("lyx,ryx->lr", x_band, h_next, precision=highest)
    numer_w, gram_h = lax.psum((numer_w_part, gram_h_part), "sp")
    w_next = w_band * numer_w / jnp.dot(w_band, gram_h, precision=highest)
    return (w_next[None], h_next)


def solution(mesh):
    in_specs = (
        P("bd", "sp", None, None),
        P("bd", "sp", None),
        P("bd", "sp", None),
        P("bd", None, None),
        P(None, None, "sp"),
    )
    out_specs = (P("bd", None, None), P(None, None, "sp"))

    def body(cube, *rest):
        suits = lax.axis_size("sp") == 8 and lax.axis_size("bd") == 4 and cube.shape[1] % GROUP == 0
        return (local if suits else local_any)(cube, *rest)

    return jax.shard_map(body, mesh=mesh, in_specs=in_specs, out_specs=out_specs, check_vma=False)
```

```python
import functools

import jax
import jax.numpy as jnp
from jax import lax
from jax.experimental import pallas as pl
from jax.experimental.pallas import tpu as pltpu
from jax.sharding import PartitionSpec as P

F32 = jnp.float32
BF16 = jnp.bfloat16
LANES = 128
GROUP = 16
PIECES = 16
FOLDED = 24
VMEM_LIMIT = 48 * 1024 * 1024


def split(value):
    high = value.astype(BF16)
    low = (value - high.astype(F32)).astype(BF16)
    return high, low


def dot(left, right):
    return lax.dot_general(left, right, (((1,), (0,)), ((), ())), preferred_element_type=F32)


def dot_nt(left, right):
    return lax.dot_general(left, right, (((1,), (1,)), ((), ())), preferred_element_type=F32)


def dot_exact(left, right):
    return lax.dot_general(
        left, right, (((1,), (0,)), ((), ())),
        precision=lax.Precision.HIGHEST, preferred_element_type=F32,
    )


def exchange_blocks(rows, block):
    lane = lax.broadcasted_iota(jnp.int32, rows[0].shape, 1)
    first_half = lane < 2 * block
    even = (lane // block) % 2 == 0
    v0, v1, v2, v3 = rows
    u0 = jnp.where(first_half, v0, pltpu.roll(v2, 2 * block, 1))
    u2 = jnp.where(first_half, pltpu.roll(v0, 2 * block, 1), v2)
    u1 = jnp.where(first_half, v1, pltpu.roll(v3, 2 * block, 1))
    u3 = jnp.where(first_half, pltpu.roll(v1, 2 * block, 1), v3)
    w0 = jnp.where(even, u0, pltpu.roll(u1, block, 1))
    w1 = jnp.where(even, pltpu.roll(u0, 3 * block, 1), u1)
    w2 = jnp.where(even, u2, pltpu.roll(u3, block, 1))
    w3 = jnp.where(even, pltpu.roll(u2, 3 * block, 1), u3)
    return w0, w1, w2, w3


def normalized_taps(taps_ref, reverse, work_ref, out_ref):
    taps = taps_ref.shape[0]
    planes = taps_ref.shape[2]
    work_ref[...] = jnp.zeros_like(work_ref)
    for tap in range(taps):
        row = taps - 1 - tap if reverse else tap
        work_ref[row:row + 1, 0:planes] = taps_ref[tap]
    values = work_ref[...]
    total = jnp.sum(values, axis=0, keepdims=True)
    total = jnp.where(total == 0.0, 1.0, total)
    out_ref[...] = jnp.transpose(values / total)


def column_table(row, margin):
    table = pltpu.roll(jnp.broadcast_to(row, (LANES, LANES)), 0, 1, stride=1, stride_axis=0)
    high = table.astype(BF16).astype(F32)
    src = lax.broadcasted_iota(jnp.int32, (GROUP, LANES), 0)
    dst = lax.broadcasted_iota(jnp.int32, (GROUP, LANES), 1)
    first, last = slice(0, GROUP), slice(LANES - GROUP, LANES)
    above = dst - src <= LANES // 2
    below = src + LANES - GROUP - dst <= LANES // 2
    empty = jnp.zeros((LANES - 2 * GROUP, LANES), F32)
    main, edge = [], []
    for part in (high, table - high):
        main.append(jnp.concatenate(
            [jnp.where(above, part[first], 0.0), part[GROUP:LANES - GROUP], jnp.where(below, part[last], 0.0)],
            axis=0).astype(BF16))
        edge.append(jnp.concatenate(
            [jnp.where(above, 0.0, part[first]), empty, jnp.where(below, 0.0, part[last])],
            axis=0).astype(BF16))
    return jnp.concatenate([jnp.concatenate(main, axis=1), jnp.concatenate(edge, axis=1)], axis=0)


def blur_plane(plane, row, margin):
    height = plane.shape[0]
    table = column_table(row, margin)
    left, right = plane[:, :LANES], plane[:, LANES:]
    lane = lax.broadcasted_iota(jnp.int32, left.shape, 1)
    main = jnp.concatenate([left, right], axis=0)
    edge = jnp.concatenate(
        [jnp.where(lane < LANES // 2, right, 0.0), jnp.where(lane < LANES // 2, 0.0, left)], axis=0)
    high, low = split(jnp.concatenate([main, edge], axis=1))
    product = dot(jnp.concatenate([high, low], axis=0), table)
    rows = 2 * height
    blocks = product[:rows, :LANES] + (product[:rows, LANES:] + product[rows:, :LANES])
    return jnp.concatenate([blocks[:height], blocks[height:]], axis=1)


def row_table(base, margin, height):
    high = base.astype(BF16).astype(F32)
    low = base - high
    plane = lax.broadcasted_iota(jnp.int32, (8, LANES), 0)
    lane = lax.broadcasted_iota(jnp.int32, (8, LANES), 1)
    per_vector = LANES // height
    own = lane // height == plane % per_vector
    masks = [own & (plane // per_vector == part) for part in range(8 * height // LANES)]

    def table(part):
        strips = []
        for row in range(height):
            rolled = pltpu.roll(part, (row - margin) % LANES, 1)
            strips.append(jnp.concatenate([jnp.where(mask, rolled, 0.0) for mask in masks], axis=1))
        return jnp.concatenate(strips, axis=0).astype(BF16)

    return table(high), table(low)


def fold(square):
    side = square.shape[0]
    rest = jnp.zeros((8, LANES - 2 * side), F32)
    return jnp.concatenate(
        [jnp.concatenate([square[first:first + 8], square[first + 8:first + 16], rest], axis=1)
         for first in range(0, side, 16)], axis=0)


def unfold(folded, side):
    blocks = []
    for first in range(0, folded.shape[0], 8):
        blocks += [folded[first:first + 8, :side], folded[first:first + 8, side:2 * side]]
    return jnp.concatenate(blocks, axis=0)


def in_vmem(count):
    return [pl.BlockSpec(memory_space=pltpu.VMEM)] * count


def band_gram(w_rows):
    high, low = split(w_rows)
    rank = w_rows.shape[0]
    padded = jnp.concatenate([high, jnp.zeros((2 * LANES - rank, high.shape[1]), BF16)], axis=0)
    padded_low = jnp.concatenate([low, jnp.zeros((2 * LANES - rank, low.shape[1]), BF16)], axis=0)
    both = dot_nt(jnp.concatenate([high, low], axis=0), padded)
    return both[:rank] + (both[rank:] + dot_nt(high, padded_low))


def blur_group(step, cube_ref, kx_ref, ky_ref, xh_ref, xl_ref, margin):
    height = cube_ref.shape[1]
    halves = []
    for half in range(GROUP // 8):
        done = []
        for k in range(8 * half, 8 * half + 8):
            plane = step * GROUP + k
            done.append(blur_plane(cube_ref[plane], kx_ref[pl.ds(plane, 1), :], margin))
        high, low = split(jnp.concatenate(done, axis=0))
        rows = ky_ref[pl.ds(pl.multiple_of(step * GROUP + 8 * half, 8), 8), :]
        table_high, table_low = row_table(rows, margin, height)
        result = dot(table_high, high) + (dot(table_low, high) + dot(table_high, low))
        halves.append(result.reshape(height, 8, result.shape[1]))
    high, low = split(jnp.concatenate(halves, axis=1))
    planes_here = pl.ds(pl.multiple_of(step * GROUP, GROUP), GROUP)
    xh_ref[:, planes_here, :] = high
    xl_ref[:, planes_here, :] = low


def blur_kernel(cube_hbm, taps_x_hbm, taps_y_hbm, w_hbm, xh_ref, xl_ref, w_here_ref, w_both_ref, keep_ref, give_ref,
                cube_ref, taps_x_ref, taps_y_ref, w_ref, sems, chunk_sems, work_ref, kx_ref, ky_ref):
    taps = taps_x_ref.shape[0]
    margin = (taps - 1) // 2
    height = cube_ref.shape[1]
    rank = w_ref.shape[0]
    groups = cube_ref.shape[0] // GROUP

    def chunk(step):
        here = pl.ds(step * GROUP, GROUP)
        return pltpu.make_async_copy(cube_hbm.at[here], cube_ref.at[here], chunk_sems.at[step])

    copies = [
        pltpu.make_async_copy(taps_x_hbm, taps_x_ref, sems.at[0]),
        pltpu.make_async_copy(taps_y_hbm, taps_y_ref, sems.at[1]),
        pltpu.make_async_copy(w_hbm, w_ref, sems.at[2]),
    ]
    for copy in copies:
        copy.start()
    for step in range(groups):
        chunk(step).start()
    copies[0].wait()
    normalized_taps(taps_x_ref, True, work_ref, kx_ref)
    kx_ref[...] = pltpu.roll(kx_ref[...], LANES - margin, 1)
    copies[1].wait()
    normalized_taps(taps_y_ref, False, work_ref, ky_ref)
    per_vector = LANES // height
    place = lax.broadcasted_iota(jnp.int32, (LANES, LANES), 0) % per_vector
    values = ky_ref[...]
    placed = values
    for k in range(1, per_vector):
        placed = jnp.where(place == k, pltpu.roll(values, k * height, 1), placed)
    ky_ref[...] = placed
    copies[2].wait()

    for step in range(groups):
        chunk(step).wait()
    for step in range(groups):
        blur_group(step, cube_ref, kx_ref, ky_ref, xh_ref, xl_ref, margin)
    gram = fold(band_gram(w_ref[...])[:, :rank])
    keep_ref[PIECES * rank:] = gram
    give_ref[PIECES * rank:] = gram
    planes = xh_ref.shape[1]
    band = w_ref.shape[1]
    shift = lax.rem(band - lax.axis_index("sp") * planes, band)
    w_here = pltpu.roll(w_ref[...], shift, 1)[:, :2 * LANES]
    w_here_ref[...] = w_here[:, :planes]
    lane = lax.broadcasted_iota(jnp.int32, w_here.shape, 1)
    w_here = jnp.where(lane < planes, w_here, 0.0)
    w_high = w_here.astype(BF16).astype(F32)
    w_both = jnp.concatenate([w_high + pltpu.roll(w_high, planes, 1), w_here - w_high], axis=0).astype(BF16)
    w_both_ref[...] = w_both
    project(xh_ref, xl_ref, w_both[:, :2 * planes], keep_ref, give_ref, 0)


def project(xh_ref, xl_ref, w_both, keep_ref, give_ref, chain):
    height = xh_ref.shape[0]
    rank = w_both.shape[0] // 2
    me_sp = lax.axis_index("sp")
    me_bd = lax.axis_index("bd")
    tall = height // lax.axis_size("bd")
    wide = 2 * LANES // lax.axis_size("sp")
    for rel_bd in (1, 3, 0, 2):
        first_row = lax.bitwise_xor(me_bd, rel_bd) * tall + 4 * chain
        sums = []
        for row in range(4):
            image = jnp.concatenate([xh_ref[first_row + row], xl_ref[first_row + row]], axis=0)
            both = dot(w_both, image)
            sums.append(both[:rank] + both[rank:])
        part_ref = (keep_ref, give_ref)[rel_bd % 2]
        for column in range(2):
            pieces = exchange_blocks(
                [value[:, column * LANES:(column + 1) * LANES] for value in sums], wide)
            for k in range(4):
                rel_sp = lax.bitwise_xor(me_sp, column * 4 + k)
                side = 3 - rel_sp % 2 if rel_bd // 2 else rel_sp % 2
                first = pl.multiple_of((side * 4 + rel_sp // 2) * rank, 8)
                part_ref[pl.ds(first, rank)] = pieces[k]


def project_kernel(xh_ref, xl_ref, w_both_ref, keep_ref, give_ref):
    planes = xh_ref.shape[1]
    project(xh_ref, xl_ref, w_both_ref[:, :2 * planes], keep_ref, give_ref, 1)


def project_call(x_high, x_low, w_both):
    part = jax.ShapeDtypeStruct((PIECES * w_both.shape[0] // 2, LANES), F32)
    return pl.pallas_call(
        project_kernel,
        out_shape=[part, part],
        in_specs=in_vmem(3),
        out_specs=in_vmem(2),
        compiler_params=pltpu.CompilerParams(vmem_limit_bytes=VMEM_LIMIT),
    )(x_high, x_low, w_both)


def blur_call(cube, taps_x, taps_y, w_rows):
    planes, height, length = cube.shape
    rank = w_rows.shape[0]
    first = jax.ShapeDtypeStruct((PIECES * rank + FOLDED, LANES), F32)
    image = (height, planes, length)
    mine = jax.ShapeDtypeStruct((rank, planes), F32)
    both = jax.ShapeDtypeStruct((2 * rank, 2 * LANES), BF16)
    in_hbm = [pltpu.with_memory_space_constraint(value, pltpu.HBM) for value in (cube, taps_x, taps_y, w_rows)]
    return pl.pallas_call(
        blur_kernel,
        out_shape=[jax.ShapeDtypeStruct(image, BF16)] * 2 + [mine, both, first, first],
        in_specs=[pl.BlockSpec(memory_space=pltpu.HBM)] * 4,
        out_specs=in_vmem(6),
        scratch_shapes=[pltpu.VMEM(value.shape, F32) for value in (cube, taps_x, taps_y, w_rows)]
        + [pltpu.SemaphoreType.DMA((3,)), pltpu.SemaphoreType.DMA((planes // GROUP,))]
        + [pltpu.VMEM((LANES, LANES), F32)] * 3,
        compiler_params=pltpu.CompilerParams(vmem_limit_bytes=VMEM_LIMIT),
    )(*in_hbm)


def ratio_kernel(mine_ref, other_ref, h_ref, out_ref):
    tall = h_ref.shape[0] // lax.axis_size("bd")
    first = pl.multiple_of(lax.axis_index("bd") * tall, tall)
    here = h_ref[pl.ds(first, tall)]
    here = jnp.transpose(here.reshape(-1, here.shape[2]))
    rows = mine_ref.shape[0]
    gram = unfold(mine_ref[rows - FOLDED:rows] + other_ref[rows - FOLDED:rows], here.shape[0])
    out_ref[...] = here / dot_exact(gram, here)


def ratio_call(mine, other, h_columns):
    piece = jax.ShapeDtypeStruct((h_columns.shape[2], 2 * LANES), F32)
    return pl.pallas_call(
        ratio_kernel,
        out_shape=piece,
        in_specs=in_vmem(3),
        compiler_params=pltpu.CompilerParams(vmem_limit_bytes=VMEM_LIMIT),
    )(mine, other, h_columns)


def accumulate(xh_ref, xl_ref, part_refs, all_ref, chain, total):
    height, planes, _ = xh_ref.shape
    me_sp = lax.axis_index("sp")
    me_bd = lax.axis_index("bd")
    bands = lax.axis_size("bd")
    pieces = lax.axis_size("sp")
    tall = height // bands
    wide = 2 * LANES // pieces
    for slot, part_ref in enumerate(part_refs):
        rel_bd = slot // 4 + 2 * ((slot // 2) % 2)
        for inner in range(4):
            rel_sp = slot % 2 + 2 * inner
            owner = lax.bitwise_xor(me_bd, rel_bd) * pieces + lax.bitwise_xor(me_sp, rel_sp)
            all_ref[owner] = part_ref[inner]
    for part in range(bands):
        first_row = part * tall + 4 * chain
        halves = [
            exchange_blocks([all_ref[part * pieces + column * 4 + k] for k in range(4)], wide)
            for column in range(2)]
        rows = jnp.concatenate([halves[column][row] for row in range(4) for column in range(2)], axis=1)
        high, low = split(rows)
        here = jnp.concatenate([high, low], axis=0)
        image = [
            jnp.concatenate([ref[first_row + row] for row in range(4)], axis=1) for ref in (xh_ref, xl_ref)]
        total = total + dot_nt(jnp.concatenate(image + [here], axis=0), here)
    return total


def first_kernel(xh_ref, xl_ref, *rest):
    part_refs = rest[:8]
    total_out, all_ref = rest[8:]
    total_out[...] = accumulate(xh_ref, xl_ref, part_refs, all_ref, 0, jnp.zeros(total_out.shape, F32))


def first_call(x_high, x_low, parts):
    _, planes, _ = x_high.shape
    rank = parts[0].shape[1]
    return pl.pallas_call(
        first_kernel,
        out_shape=jax.ShapeDtypeStruct((2 * (planes + rank), 2 * rank), F32),
        in_specs=in_vmem(2 + len(parts)),
        scratch_shapes=[pltpu.VMEM((32, rank, LANES), F32)],
        compiler_params=pltpu.CompilerParams(vmem_limit_bytes=VMEM_LIMIT),
    )(x_high, x_low, *parts)


def second_kernel(xh_ref, xl_ref, w_ref, total_ref, *rest):
    part_refs = rest[:8]
    w_out, all_ref = rest[8:]
    planes = xh_ref.shape[1]
    rank = w_ref.shape[0]
    total = accumulate(xh_ref, xl_ref, part_refs, all_ref, 1, total_ref[...])
    numer = total[:planes, :rank] + (total[:planes, rank:] + total[planes:2 * planes, :rank])
    gram = total[2 * planes:]
    gram = gram[:rank, :rank] + (gram[:rank, rank:] + gram[rank:, :rank])
    w_here = w_ref[...]
    w_out[...] = w_here * jnp.transpose(numer) / dot_exact(gram, w_here)


def second_call(x_high, x_low, w_here, total, parts):
    rank = w_here.shape[0]
    return pl.pallas_call(
        second_kernel,
        out_shape=jax.ShapeDtypeStruct(w_here.shape, F32),
        in_specs=in_vmem(4 + len(parts)),
        scratch_shapes=[pltpu.VMEM((32, rank, LANES), F32)],
        compiler_params=pltpu.CompilerParams(vmem_limit_bytes=VMEM_LIMIT),
    )(x_high, x_low, w_here, total, *parts)


def place_h_kernel(*refs):
    h_out = refs[-1]
    me_bd = lax.axis_index("bd")
    tall = h_out.shape[0] // lax.axis_size("bd")
    for chain in range(2):
        for rel_bd in range(4):
            piece = refs[4 * chain + rel_bd][0]
            first = lax.bitwise_xor(me_bd, rel_bd) * tall + 4 * chain
            h_out[pl.ds(first, 4)] = jnp.transpose(piece).reshape((4,) + h_out.shape[1:])


def place_h_call(parts, shape):
    return pl.pallas_call(
        place_h_kernel,
        out_shape=jax.ShapeDtypeStruct(shape, F32),
        in_specs=in_vmem(len(parts)),
        compiler_params=pltpu.CompilerParams(vmem_limit_bytes=VMEM_LIMIT),
    )(*parts)


def gather_w_kernel(*refs):
    part_refs = refs[:-2]
    out_ref, all_ref = refs[-2:]
    planes = out_ref.shape[1] // 8
    me_sp = lax.axis_index("sp")
    rel = 0
    for part_ref in part_refs:
        for inner in range(part_ref.shape[0]):
            all_ref[lax.bitwise_xor(me_sp, RING[rel]), :, 0:planes] = part_ref[inner]
            rel += 1
    for owner in range(8):
        out_ref[:, owner * planes:(owner + 1) * planes] = all_ref[owner][:, :planes]


RING = (0, 1, 2, 3, 4, 5, 6, 7)


def gather_w_call(parts):
    _, rank, planes = parts[0].shape
    return pl.pallas_call(
        gather_w_kernel,
        out_shape=jax.ShapeDtypeStruct((rank, planes * 8), F32),
        in_specs=in_vmem(len(parts)),
        scratch_shapes=[pltpu.VMEM((8, rank, LANES), F32)],
        compiler_params=pltpu.CompilerParams(vmem_limit_bytes=VMEM_LIMIT),
    )(*parts)


def send(value, mask_sp, mask_bd):
    bands = lax.axis_size("bd")
    pieces = lax.axis_size("sp")
    pairs = []
    for s in range(pieces):
        for b in range(bands):
            pairs.append((s * bands + b, (s ^ mask_sp) * bands + (b ^ mask_bd)))
    return lax.ppermute(value, ("sp", "bd"), pairs)


def around(values):
    return [send(values[k], k % 2, 2 * (k // 2)) for k in range(1, 4)]


def local(cube, taps_x, taps_y, factor_w, factor_h):
    w_rows = jnp.transpose(factor_w[0])
    taps_x = jnp.transpose(taps_x, (2, 0, 1))
    taps_y = jnp.transpose(taps_y, (2, 0, 1))
    h_columns = jnp.transpose(factor_h, (1, 2, 0))
    rank = w_rows.shape[0]
    x_high, x_low, w_here, w_both, keep_0, give_0 = blur_call(cube[0], taps_x, taps_y, w_rows)
    chains = []
    taken_0 = send(give_0, 0, 1)
    keep_1, give_1 = project_call(x_high, x_low, w_both)
    taken_0, keep_1, give_1 = lax.optimization_barrier((taken_0, keep_1, give_1))
    for keep, taken in ((keep_0, taken_0), (keep_1, send(give_1, 0, 1))):
        bounds = [place * 4 * rank for place in (0, 1, 3, 2)]
        sides = []
        for first in bounds:
            last = keep.shape[0] if first == max(bounds) else first + 4 * rank
            sides.append(keep[first:last] + taken[first:last])
        chains.append((sides, around(sides)))
    ratio = ratio_call(chains[0][0][2], chains[0][1][1], h_columns)
    line = []
    for k in range(4):
        part = slice(k * rank, (k + 1) * rank)
        line.append(jnp.concatenate(
            [(sides[0][part] + others[0][part]) + (others[1][part] + others[2][part]) for sides, others in chains],
            axis=1))
    line = [line[0]] + [send(line[k], 2 * k, 0) for k in (3, 2, 1)]
    h_piece = ratio * ((line[0] + line[1]) + (line[2] + line[3]))
    h_line = [h_piece] + [send(h_piece, 2 * k, 0) for k in range(1, 4)]
    chains = []
    for first in (0, LANES):
        mine = jnp.stack([value[:, first:first + LANES] for value in h_line])
        chains.append([mine] + around([mine] * 4))
    first_parts = chains[0] + [send(value, 0, 1) for value in chains[0]]
    total = first_call(x_high, x_low, first_parts)
    second_parts = chains[1] + [send(value, 0, 1) for value in chains[1]]
    w_piece = second_call(x_high, x_low, w_here, total, second_parts)
    own = [parts[k] for parts in (first_parts, second_parts) for k in (0, 4, 2, 6)]
    h_next = place_h_call(own, h_columns.shape)
    w_pair = jnp.stack([w_piece, send(w_piece, 1, 0)])
    w_next = gather_w_call([w_pair] + [send(w_pair, 2 * k, 0) for k in range(1, 4)])
    return jnp.transpose(w_next)[None], jnp.transpose(h_next, (2, 0, 1))


def normalized(kernel):
    return kernel / jnp.sum(kernel, axis=-1, keepdims=True)


def band_weights(kernel, size_in, size_out, offset):
    tap_count = kernel.shape[-1]
    in_index = lax.broadcasted_iota(jnp.int32, (size_in, size_out, tap_count), 0)
    out_index = lax.broadcasted_iota(jnp.int32, (size_in, size_out, tap_count), 1)
    tap_index = lax.broadcasted_iota(jnp.int32, (size_in, size_out, tap_count), 2)
    select = (tap_index == in_index - out_index + offset).astype(jnp.float32)
    return jnp.einsum("pk,iok->pio", kernel, select, precision=lax.Precision.HIGHEST)


def blur_rows(planes, kernel_y):
    margin = (kernel_y.shape[-1] - 1) // 2
    height = planes.shape[1]
    band_table = band_weights(kernel_y, height, height, margin)
    return jnp.einsum("piz,pio->poz", planes, band_table, precision=lax.Precision.HIGHEST)


def blur_columns(planes, kernel_x):
    margin = (kernel_x.shape[-1] - 1) // 2
    count, height, length = planes.shape
    blocks = planes.reshape(count, height, length // 128, 128)
    empty = jnp.zeros((count, height, 1, 128), jnp.float32)
    left_block = jnp.concatenate([empty, blocks[:, :, :-1]], axis=2)
    right_block = jnp.concatenate([blocks[:, :, 1:], empty], axis=2)
    window = jnp.concatenate([left_block, blocks, right_block], axis=3)
    band_table = band_weights(kernel_x, 384, 128, margin - 128)
    result = jnp.einsum("pybi,pio->pybo", window, band_table, precision=lax.Precision.HIGHEST)
    return result.reshape(count, height, length)


def local_any(cube, taps_x, taps_y, factor_w, factor_h):
    highest = lax.Precision.HIGHEST
    kernel_x = normalized(taps_x[0])
    kernel_y = normalized(taps_y[0])
    rows_done = blur_rows(cube[0], kernel_y)
    w_band = factor_w[0]
    blurred = blur_columns(rows_done, kernel_x)[None]
    moved = lax.all_to_all(blurred, "sp", split_axis=3, concat_axis=1, tiled=True)
    numer_part = jnp.einsum("lr,plyx->pryx", w_band, moved, precision=highest)
    gram_part = jnp.dot(w_band.T, w_band, precision=highest)
    numer_h, gram_w = lax.psum((numer_part[0], gram_part), "bd")
    h_next = factor_h * numer_h / jnp.einsum("rq,qyx->ryx", gram_w, factor_h, precision=highest)
    x_band = moved[0]
    gram_h_part = jnp.einsum("ryx,qyx->rq", h_next, h_next, precision=highest)
    numer_w_part = jnp.einsum("lyx,ryx->lr", x_band, h_next, precision=highest)
    numer_w, gram_h = lax.psum((numer_w_part, gram_h_part), "sp")
    w_next = w_band * numer_w / jnp.dot(w_band, gram_h, precision=highest)
    return (w_next[None], h_next)


def solution(mesh):
    in_specs = (
        P("bd", "sp", None, None),
        P("bd", "sp", None),
        P("bd", "sp", None),
        P("bd", None, None),
        P(None, None, "sp"),
    )
    out_specs = (P("bd", None, None), P(None, None, "sp"))

    def body(cube, *rest):
        suits = lax.axis_size("sp") == 8 and lax.axis_size("bd") == 4 and cube.shape[1] % GROUP == 0
        return (local if suits else local_any)(cube, *rest)

    return jax.shard_map(body, mesh=mesh, in_specs=in_specs, out_specs=out_specs, check_vma=False)
```

```python
import functools

import jax
import jax.numpy as jnp
from jax import lax
from jax.experimental import pallas as pl
from jax.experimental.pallas import tpu as pltpu
from jax.sharding import PartitionSpec as P

F32 = jnp.float32
BF16 = jnp.bfloat16
LANES = 128
GROUP = 16
PIECES = 16
FOLDED = 24
VMEM_LIMIT = 48 * 1024 * 1024


def split(value):
    high = value.astype(BF16)
    low = (value - high.astype(F32)).astype(BF16)
    return high, low


def dot(left, right):
    return lax.dot_general(left, right, (((1,), (0,)), ((), ())), preferred_element_type=F32)


def dot_nt(left, right):
    return lax.dot_general(left, right, (((1,), (1,)), ((), ())), preferred_element_type=F32)


def dot_exact(left, right):
    return lax.dot_general(
        left, right, (((1,), (0,)), ((), ())),
        precision=lax.Precision.HIGHEST, preferred_element_type=F32,
    )


def exchange_blocks(rows, block):
    lane = lax.broadcasted_iota(jnp.int32, rows[0].shape, 1)
    first_half = lane < 2 * block
    even = (lane // block) % 2 == 0
    v0, v1, v2, v3 = rows
    u0 = jnp.where(first_half, v0, pltpu.roll(v2, 2 * block, 1))
    u2 = jnp.where(first_half, pltpu.roll(v0, 2 * block, 1), v2)
    u1 = jnp.where(first_half, v1, pltpu.roll(v3, 2 * block, 1))
    u3 = jnp.where(first_half, pltpu.roll(v1, 2 * block, 1), v3)
    w0 = jnp.where(even, u0, pltpu.roll(u1, block, 1))
    w1 = jnp.where(even, pltpu.roll(u0, 3 * block, 1), u1)
    w2 = jnp.where(even, u2, pltpu.roll(u3, block, 1))
    w3 = jnp.where(even, pltpu.roll(u2, 3 * block, 1), u3)
    return w0, w1, w2, w3


def normalized_taps(taps_ref, reverse, work_ref, out_ref):
    taps = taps_ref.shape[0]
    planes = taps_ref.shape[2]
    work_ref[...] = jnp.zeros_like(work_ref)
    for tap in range(taps):
        row = taps - 1 - tap if reverse else tap
        work_ref[row:row + 1, 0:planes] = taps_ref[tap]
    values = work_ref[...]
    total = jnp.sum(values, axis=0, keepdims=True)
    total = jnp.where(total == 0.0, 1.0, total)
    out_ref[...] = jnp.transpose(values / total)


def column_table(row, margin):
    table = pltpu.roll(jnp.broadcast_to(row, (LANES, LANES)), 0, 1, stride=1, stride_axis=0)
    high = table.astype(BF16).astype(F32)
    src = lax.broadcasted_iota(jnp.int32, (GROUP, LANES), 0)
    dst = lax.broadcasted_iota(jnp.int32, (GROUP, LANES), 1)
    first, last = slice(0, GROUP), slice(LANES - GROUP, LANES)
    above = dst - src <= LANES // 2
    below = src + LANES - GROUP - dst <= LANES // 2
    empty = jnp.zeros((LANES - 2 * GROUP, LANES), F32)
    main, edge = [], []
    for part in (high, table - high):
        main.append(jnp.concatenate(
            [jnp.where(above, part[first], 0.0), part[GROUP:LANES - GROUP], jnp.where(below, part[last], 0.0)],
            axis=0).astype(BF16))
        edge.append(jnp.concatenate(
            [jnp.where(above, 0.0, part[first]), empty, jnp.where(below, 0.0, part[last])],
            axis=0).astype(BF16))
    return jnp.concatenate([jnp.concatenate(main, axis=1), jnp.concatenate(edge, axis=1)], axis=0)


def blur_plane(plane, row, margin):
    height = plane.shape[0]
    table = column_table(row, margin)
    left, right = plane[:, :LANES], plane[:, LANES:]
    lane = lax.broadcasted_iota(jnp.int32, left.shape, 1)
    main = jnp.concatenate([left, right], axis=0)
    edge = jnp.concatenate(
        [jnp.where(lane < LANES // 2, right, 0.0), jnp.where(lane < LANES // 2, 0.0, left)], axis=0)
    high, low = split(jnp.concatenate([main, edge], axis=1))
    product = dot(jnp.concatenate([high, low], axis=0), table)
    rows = 2 * height
    blocks = product[:rows, :LANES] + (product[:rows, LANES:] + product[rows:, :LANES])
    return jnp.concatenate([blocks[:height], blocks[height:]], axis=1)


def row_table(base, margin, height):
    high = base.astype(BF16).astype(F32)
    low = base - high
    plane = lax.broadcasted_iota(jnp.int32, (8, LANES), 0)
    lane = lax.broadcasted_iota(jnp.int32, (8, LANES), 1)
    per_vector = LANES // height
    own = lane // height == plane % per_vector
    masks = [own & (plane // per_vector == part) for part in range(8 * height // LANES)]

    def table(part):
        strips = []
        for row in range(height):
            rolled = pltpu.roll(part, (row - margin) % LANES, 1)
            strips.append(jnp.concatenate([jnp.where(mask, rolled, 0.0) for mask in masks], axis=1))
        return jnp.concatenate(strips, axis=0).astype(BF16)

    return table(high), table(low)


def fold(square):
    side = square.shape[0]
    rest = jnp.zeros((8, LANES - 2 * side), F32)
    return jnp.concatenate(
        [jnp.concatenate([square[first:first + 8], square[first + 8:first + 16], rest], axis=1)
         for first in range(0, side, 16)], axis=0)


def unfold(folded, side):
    blocks = []
    for first in range(0, folded.shape[0], 8):
        blocks += [folded[first:first + 8, :side], folded[first:first + 8, side:2 * side]]
    return jnp.concatenate(blocks, axis=0)


def in_vmem(count):
    return [pl.BlockSpec(memory_space=pltpu.VMEM)] * count


def band_gram(w_rows):
    high, low = split(w_rows)
    rank = w_rows.shape[0]
    padded = jnp.concatenate([high, jnp.zeros((2 * LANES - rank, high.shape[1]), BF16)], axis=0)
    padded_low = jnp.concatenate([low, jnp.zeros((2 * LANES - rank, low.shape[1]), BF16)], axis=0)
    both = dot_nt(jnp.concatenate([high, low], axis=0), padded)
    return both[:rank] + (both[rank:] + dot_nt(high, padded_low))


def blur_group(step, cube_ref, kx_ref, ky_ref, xh_ref, xl_ref, margin):
    height = cube_ref.shape[1]
    halves = []
    for half in range(GROUP // 8):
        done = []
        for k in range(8 * half, 8 * half + 8):
            plane = step * GROUP + k
            done.append(blur_plane(cube_ref[plane], kx_ref[pl.ds(plane, 1), :], margin))
        high, low = split(jnp.concatenate(done, axis=0))
        rows = ky_ref[pl.ds(pl.multiple_of(step * GROUP + 8 * half, 8), 8), :]
        table_high, table_low = row_table(rows, margin, height)
        result = dot(table_high, high) + (dot(table_low, high) + dot(table_high, low))
        halves.append(result.reshape(height, 8, result.shape[1]))
    high, low = split(jnp.concatenate(halves, axis=1))
    planes_here = pl.ds(pl.multiple_of(step * GROUP, GROUP), GROUP)
    xh_ref[:, planes_here, :] = high
    xl_ref[:, planes_here, :] = low


def blur_kernel(cube_hbm, taps_x_hbm, taps_y_hbm, w_hbm, xh_ref, xl_ref, w_here_ref, w_both_ref, keep_ref, give_ref,
                cube_ref, taps_x_ref, taps_y_ref, w_ref, sems, chunk_sems, work_ref, kx_ref, ky_ref):
    taps = taps_x_ref.shape[0]
    margin = (taps - 1) // 2
    height = cube_ref.shape[1]
    rank = w_ref.shape[0]
    groups = cube_ref.shape[0] // GROUP

    def chunk(step):
        here = pl.ds(step * GROUP, GROUP)
        return pltpu.make_async_copy(cube_hbm.at[here], cube_ref.at[here], chunk_sems.at[step])

    copies = [
        pltpu.make_async_copy(taps_x_hbm, taps_x_ref, sems.at[0]),
        pltpu.make_async_copy(taps_y_hbm, taps_y_ref, sems.at[1]),
        pltpu.make_async_copy(w_hbm, w_ref, sems.at[2]),
    ]
    for copy in copies:
        copy.start()
    for step in range(groups):
        chunk(step).start()
    copies[0].wait()
    normalized_taps(taps_x_ref, True, work_ref, kx_ref)
    kx_ref[...] = pltpu.roll(kx_ref[...], LANES - margin, 1)
    copies[1].wait()
    normalized_taps(taps_y_ref, False, work_ref, ky_ref)
    per_vector = LANES // height
    place = lax.broadcasted_iota(jnp.int32, (LANES, LANES), 0) % per_vector
    values = ky_ref[...]
    placed = values
    for k in range(1, per_vector):
        placed = jnp.where(place == k, pltpu.roll(values, k * height, 1), placed)
    ky_ref[...] = placed
    copies[2].wait()

    for step in range(groups):
        chunk(step).wait()
    for step in range(groups):
        blur_group(step, cube_ref, kx_ref, ky_ref, xh_ref, xl_ref, margin)
    gram = fold(band_gram(w_ref[...])[:, :rank])
    keep_ref[PIECES * rank:] = gram
    give_ref[PIECES * rank:] = gram
    planes = xh_ref.shape[1]
    band = w_ref.shape[1]
    shift = lax.rem(band - lax.axis_index("sp") * planes, band)
    w_here = pltpu.roll(w_ref[...], shift, 1)[:, :2 * LANES]
    w_here_ref[...] = w_here[:, :planes]
    lane = lax.broadcasted_iota(jnp.int32, w_here.shape, 1)
    w_here = jnp.where(lane < planes, w_here, 0.0)
    w_high = w_here.astype(BF16).astype(F32)
    w_both = jnp.concatenate([w_high + pltpu.roll(w_high, planes, 1), w_here - w_high], axis=0).astype(BF16)
    w_both_ref[...] = w_both
    project(xh_ref, xl_ref, w_both[:, :2 * planes], keep_ref, give_ref, 0)


def project(xh_ref, xl_ref, w_both, keep_ref, give_ref, chain):
    height = xh_ref.shape[0]
    rank = w_both.shape[0] // 2
    me_sp = lax.axis_index("sp")
    me_bd = lax.axis_index("bd")
    tall = height // lax.axis_size("bd")
    wide = 2 * LANES // lax.axis_size("sp")
    for rel_bd in (1, 3, 0, 2):
        first_row = lax.bitwise_xor(me_bd, rel_bd) * tall + 4 * chain
        sums = []
        for row in range(4):
            image = jnp.concatenate([xh_ref[first_row + row], xl_ref[first_row + row]], axis=0)
            both = dot(w_both, image)
            sums.append(both[:rank] + both[rank:])
        part_ref = (keep_ref, give_ref)[rel_bd % 2]
        for column in range(2):
            pieces = exchange_blocks(
                [value[:, column * LANES:(column + 1) * LANES] for value in sums], wide)
            for k in range(4):
                rel_sp = lax.bitwise_xor(me_sp, column * 4 + k)
                side = 3 - rel_sp % 2 if rel_bd // 2 else rel_sp % 2
                first = pl.multiple_of((side * 4 + rel_sp // 2) * rank, 8)
                part_ref[pl.ds(first, rank)] = pieces[k]


def project_kernel(xh_ref, xl_ref, w_both_ref, keep_ref, give_ref):
    planes = xh_ref.shape[1]
    project(xh_ref, xl_ref, w_both_ref[:, :2 * planes], keep_ref, give_ref, 1)


def project_call(x_high, x_low, w_both):
    part = jax.ShapeDtypeStruct((PIECES * w_both.shape[0] // 2, LANES), F32)
    return pl.pallas_call(
        project_kernel,
        out_shape=[part, part],
        in_specs=in_vmem(3),
        out_specs=in_vmem(2),
        compiler_params=pltpu.CompilerParams(vmem_limit_bytes=VMEM_LIMIT),
    )(x_high, x_low, w_both)


def blur_call(cube, taps_x, taps_y, w_rows):
    planes, height, length = cube.shape
    rank = w_rows.shape[0]
    first = jax.ShapeDtypeStruct((PIECES * rank + FOLDED, LANES), F32)
    image = (height, planes, length)
    mine = jax.ShapeDtypeStruct((rank, planes), F32)
    both = jax.ShapeDtypeStruct((2 * rank, 2 * LANES), BF16)
    in_hbm = [pltpu.with_memory_space_constraint(value, pltpu.HBM) for value in (cube, taps_x, taps_y, w_rows)]
    return pl.pallas_call(
        blur_kernel,
        out_shape=[jax.ShapeDtypeStruct(image, BF16)] * 2 + [mine, both, first, first],
        in_specs=[pl.BlockSpec(memory_space=pltpu.HBM)] * 4,
        out_specs=in_vmem(6),
        scratch_shapes=[pltpu.VMEM(value.shape, F32) for value in (cube, taps_x, taps_y, w_rows)]
        + [pltpu.SemaphoreType.DMA((3,)), pltpu.SemaphoreType.DMA((planes // GROUP,))]
        + [pltpu.VMEM((LANES, LANES), F32)] * 3,
        compiler_params=pltpu.CompilerParams(vmem_limit_bytes=VMEM_LIMIT),
    )(*in_hbm)


def ratio_kernel(mine_ref, other_ref, h_ref, out_ref):
    tall = h_ref.shape[0] // lax.axis_size("bd")
    first = pl.multiple_of(lax.axis_index("bd") * tall, tall)
    here = h_ref[pl.ds(first, tall)]
    here = jnp.transpose(here.reshape(-1, here.shape[2]))
    rows = mine_ref.shape[0]
    gram = unfold(mine_ref[rows - FOLDED:rows] + other_ref[rows - FOLDED:rows], here.shape[0])
    out_ref[...] = here / dot_exact(gram, here)


def ratio_call(mine, other, h_columns):
    piece = jax.ShapeDtypeStruct((h_columns.shape[2], 2 * LANES), F32)
    return pl.pallas_call(
        ratio_kernel,
        out_shape=piece,
        in_specs=in_vmem(3),
        compiler_params=pltpu.CompilerParams(vmem_limit_bytes=VMEM_LIMIT),
    )(mine, other, h_columns)


def accumulate(xh_ref, xl_ref, part_refs, all_ref, rel_core, total):
    height, planes, _ = xh_ref.shape
    me_sp = lax.axis_index("sp")
    me_bd = lax.axis_index("bd")
    pieces = lax.axis_size("sp")
    tall = height // lax.axis_size("bd")
    wide = 2 * LANES // pieces
    core = lax.bitwise_xor(me_bd % 2, rel_core)
    for partner, part_ref in enumerate(part_refs):
        row = lax.bitwise_xor(me_bd // 2, partner // 2)
        for inner in range(4):
            column = lax.bitwise_xor(me_sp, partner % 2 + 2 * inner)
            all_ref[row * pieces + column] = part_ref[inner]
    for row in range(2):
        for quarter in range(2):
            first_row = (2 * row + core) * tall + 4 * quarter
            halves = [
                exchange_blocks(
                    [all_ref[row * pieces + column * 4 + k][:, quarter * LANES:(quarter + 1) * LANES]
                     for k in range(4)], wide)
                for column in range(2)]
            rows = jnp.concatenate([halves[column][k] for k in range(4) for column in range(2)], axis=1)
            high, low = split(rows)
            here = jnp.concatenate([high, low], axis=0)
            image = [
                jnp.concatenate([ref[first_row + k] for k in range(4)], axis=1) for ref in (xh_ref, xl_ref)]
            total = total + dot_nt(jnp.concatenate(image + [here], axis=0), here)
    return total


def first_kernel(xh_ref, xl_ref, *rest):
    part_refs = rest[:4]
    total_out, all_ref = rest[4:]
    total_out[...] = accumulate(xh_ref, xl_ref, part_refs, all_ref, 0, jnp.zeros(total_out.shape, F32))


def first_call(x_high, x_low, parts):
    _, planes, _ = x_high.shape
    rank = parts[0].shape[1]
    return pl.pallas_call(
        first_kernel,
        out_shape=jax.ShapeDtypeStruct((2 * (planes + rank), 2 * rank), F32),
        in_specs=in_vmem(2 + len(parts)),
        scratch_shapes=[pltpu.VMEM((16, rank, 2 * LANES), F32)],
        compiler_params=pltpu.CompilerParams(vmem_limit_bytes=VMEM_LIMIT),
    )(x_high, x_low, *parts)


def second_kernel(xh_ref, xl_ref, w_ref, total_ref, *rest):
    part_refs = rest[:4]
    w_out, all_ref = rest[4:]
    planes = xh_ref.shape[1]
    rank = w_ref.shape[0]
    total = accumulate(xh_ref, xl_ref, part_refs, all_ref, 1, total_ref[...])
    numer = total[:planes, :rank] + (total[:planes, rank:] + total[planes:2 * planes, :rank])
    gram = total[2 * planes:]
    gram = gram[:rank, :rank] + (gram[:rank, rank:] + gram[rank:, :rank])
    w_here = w_ref[...]
    w_out[...] = w_here * jnp.transpose(numer) / dot_exact(gram, w_here)


def second_call(x_high, x_low, w_here, total, parts):
    rank = w_here.shape[0]
    return pl.pallas_call(
        second_kernel,
        out_shape=jax.ShapeDtypeStruct(w_here.shape, F32),
        in_specs=in_vmem(4 + len(parts)),
        scratch_shapes=[pltpu.VMEM((16, rank, 2 * LANES), F32)],
        compiler_params=pltpu.CompilerParams(vmem_limit_bytes=VMEM_LIMIT),
    )(x_high, x_low, w_here, total, *parts)


def place_h_kernel(*refs):
    h_out = refs[-1]
    me_bd = lax.axis_index("bd")
    tall = h_out.shape[0] // lax.axis_size("bd")
    for rel_bd in range(4):
        piece = refs[rel_bd][0]
        first = lax.bitwise_xor(me_bd, rel_bd) * tall
        h_out[pl.ds(first, tall)] = jnp.transpose(piece).reshape((tall,) + h_out.shape[1:])


def place_h_call(parts, shape):
    return pl.pallas_call(
        place_h_kernel,
        out_shape=jax.ShapeDtypeStruct(shape, F32),
        in_specs=in_vmem(len(parts)),
        compiler_params=pltpu.CompilerParams(vmem_limit_bytes=VMEM_LIMIT),
    )(*parts)


def gather_w_kernel(*refs):
    part_refs = refs[:-2]
    out_ref, all_ref = refs[-2:]
    planes = out_ref.shape[1] // 8
    me_sp = lax.axis_index("sp")
    rel = 0
    for part_ref in part_refs:
        for inner in range(part_ref.shape[0]):
            all_ref[lax.bitwise_xor(me_sp, RING[rel]), :, 0:planes] = part_ref[inner]
            rel += 1
    for owner in range(8):
        out_ref[:, owner * planes:(owner + 1) * planes] = all_ref[owner][:, :planes]


RING = (0, 1, 2, 3, 4, 5, 6, 7)


def gather_w_call(parts):
    _, rank, planes = parts[0].shape
    return pl.pallas_call(
        gather_w_kernel,
        out_shape=jax.ShapeDtypeStruct((rank, planes * 8), F32),
        in_specs=in_vmem(len(parts)),
        scratch_shapes=[pltpu.VMEM((8, rank, LANES), F32)],
        compiler_params=pltpu.CompilerParams(vmem_limit_bytes=VMEM_LIMIT),
    )(*parts)


def send(value, mask_sp, mask_bd):
    bands = lax.axis_size("bd")
    pieces = lax.axis_size("sp")
    pairs = []
    for s in range(pieces):
        for b in range(bands):
            pairs.append((s * bands + b, (s ^ mask_sp) * bands + (b ^ mask_bd)))
    return lax.ppermute(value, ("sp", "bd"), pairs)


def around(values):
    return [send(values[k], k % 2, 2 * (k // 2)) for k in range(1, 4)]


def local(cube, taps_x, taps_y, factor_w, factor_h):
    w_rows = jnp.transpose(factor_w[0])
    taps_x = jnp.transpose(taps_x, (2, 0, 1))
    taps_y = jnp.transpose(taps_y, (2, 0, 1))
    h_columns = jnp.transpose(factor_h, (1, 2, 0))
    rank = w_rows.shape[0]
    x_high, x_low, w_here, w_both, keep_0, give_0 = blur_call(cube[0], taps_x, taps_y, w_rows)
    chains = []
    taken_0 = send(give_0, 0, 1)
    keep_1, give_1 = project_call(x_high, x_low, w_both)
    taken_0, keep_1, give_1 = lax.optimization_barrier((taken_0, keep_1, give_1))
    for keep, taken in ((keep_0, taken_0), (keep_1, send(give_1, 0, 1))):
        bounds = [place * 4 * rank for place in (0, 1, 3, 2)]
        sides = []
        for first in bounds:
            last = keep.shape[0] if first == max(bounds) else first + 4 * rank
            sides.append(keep[first:last] + taken[first:last])
        chains.append((sides, around(sides)))
    ratio = ratio_call(chains[0][0][2], chains[0][1][1], h_columns)
    line = []
    for k in range(4):
        part = slice(k * rank, (k + 1) * rank)
        line.append(jnp.concatenate(
            [(sides[0][part] + others[0][part]) + (others[1][part] + others[2][part]) for sides, others in chains],
            axis=1))
    line = [line[0]] + [send(line[k], 2 * k, 0) for k in (3, 2, 1)]
    h_piece = ratio * ((line[0] + line[1]) + (line[2] + line[3]))
    h_line = [h_piece] + [send(h_piece, 2 * k, 0) for k in range(1, 4)]
    mine = jnp.stack(h_line)
    first_parts = [mine] + around([mine] * 4)
    second_parts = [send(value, 0, 1) for value in first_parts]
    total = first_call(x_high, x_low, first_parts)
    w_piece = second_call(x_high, x_low, w_here, total, second_parts)
    own = [parts[k] for k in (0, 2) for parts in (first_parts, second_parts)]
    h_next = place_h_call(own, h_columns.shape)
    w_pair = jnp.stack([w_piece, send(w_piece, 1, 0)])
    w_next = gather_w_call([w_pair] + [send(w_pair, 2 * k, 0) for k in range(1, 4)])
    return jnp.transpose(w_next)[None], jnp.transpose(h_next, (2, 0, 1))


def normalized(kernel):
    return kernel / jnp.sum(kernel, axis=-1, keepdims=True)


def band_weights(kernel, size_in, size_out, offset):
    tap_count = kernel.shape[-1]
    in_index = lax.broadcasted_iota(jnp.int32, (size_in, size_out, tap_count), 0)
    out_index = lax.broadcasted_iota(jnp.int32, (size_in, size_out, tap_count), 1)
    tap_index = lax.broadcasted_iota(jnp.int32, (size_in, size_out, tap_count), 2)
    select = (tap_index == in_index - out_index + offset).astype(jnp.float32)
    return jnp.einsum("pk,iok->pio", kernel, select, precision=lax.Precision.HIGHEST)


def blur_rows(planes, kernel_y):
    margin = (kernel_y.shape[-1] - 1) // 2
    height = planes.shape[1]
    band_table = band_weights(kernel_y, height, height, margin)
    return jnp.einsum("piz,pio->poz", planes, band_table, precision=lax.Precision.HIGHEST)


def blur_columns(planes, kernel_x):
    margin = (kernel_x.shape[-1] - 1) // 2
    count, height, length = planes.shape
    blocks = planes.reshape(count, height, length // 128, 128)
    empty = jnp.zeros((count, height, 1, 128), jnp.float32)
    left_block = jnp.concatenate([empty, blocks[:, :, :-1]], axis=2)
    right_block = jnp.concatenate([blocks[:, :, 1:], empty], axis=2)
    window = jnp.concatenate([left_block, blocks, right_block], axis=3)
    band_table = band_weights(kernel_x, 384, 128, margin - 128)
    result = jnp.einsum("pybi,pio->pybo", window, band_table, precision=lax.Precision.HIGHEST)
    return result.reshape(count, height, length)


def local_any(cube, taps_x, taps_y, factor_w, factor_h):
    highest = lax.Precision.HIGHEST
    kernel_x = normalized(taps_x[0])
    kernel_y = normalized(taps_y[0])
    rows_done = blur_rows(cube[0], kernel_y)
    w_band = factor_w[0]
    blurred = blur_columns(rows_done, kernel_x)[None]
    moved = lax.all_to_all(blurred, "sp", split_axis=3, concat_axis=1, tiled=True)
    numer_part = jnp.einsum("lr,plyx->pryx", w_band, moved, precision=highest)
    gram_part = jnp.dot(w_band.T, w_band, precision=highest)
    numer_h, gram_w = lax.psum((numer_part[0], gram_part), "bd")
    h_next = factor_h * numer_h / jnp.einsum("rq,qyx->ryx", gram_w, factor_h, precision=highest)
    x_band = moved[0]
    gram_h_part = jnp.einsum("ryx,qyx->rq", h_next, h_next, precision=highest)
    numer_w_part = jnp.einsum("lyx,ryx->lr", x_band, h_next, precision=highest)
    numer_w, gram_h = lax.psum((numer_w_part, gram_h_part), "sp")
    w_next = w_band * numer_w / jnp.dot(w_band, gram_h, precision=highest)
    return (w_next[None], h_next)


def solution(mesh):
    in_specs = (
        P("bd", "sp", None, None),
        P("bd", "sp", None),
        P("bd", "sp", None),
        P("bd", None, None),
        P(None, None, "sp"),
    )
    out_specs = (P("bd", None, None), P(None, None, "sp"))

    def body(cube, *rest):
        suits = lax.axis_size("sp") == 8 and lax.axis_size("bd") == 4 and cube.shape[1] % GROUP == 0
        return (local if suits else local_any)(cube, *rest)

    return jax.shard_map(body, mesh=mesh, in_specs=in_specs, out_specs=out_specs, check_vma=False)
```

```python
import functools

import jax
import jax.numpy as jnp
from jax import lax
from jax.experimental import pallas as pl
from jax.experimental.pallas import tpu as pltpu
from jax.sharding import PartitionSpec as P

F32 = jnp.float32
BF16 = jnp.bfloat16
LANES = 128
GROUP = 16
PIECES = 16
FOLDED = 24
VMEM_LIMIT = 48 * 1024 * 1024


def split(value):
    high = value.astype(BF16)
    low = (value - high.astype(F32)).astype(BF16)
    return high, low


def dot(left, right):
    return lax.dot_general(left, right, (((1,), (0,)), ((), ())), preferred_element_type=F32)


def dot_nt(left, right):
    return lax.dot_general(left, right, (((1,), (1,)), ((), ())), preferred_element_type=F32)


def dot_exact(left, right):
    return lax.dot_general(
        left, right, (((1,), (0,)), ((), ())),
        precision=lax.Precision.HIGHEST, preferred_element_type=F32,
    )


def exchange_blocks(rows, block):
    lane = lax.broadcasted_iota(jnp.int32, rows[0].shape, 1)
    first_half = lane < 2 * block
    even = (lane // block) % 2 == 0
    v0, v1, v2, v3 = rows
    u0 = jnp.where(first_half, v0, pltpu.roll(v2, 2 * block, 1))
    u2 = jnp.where(first_half, pltpu.roll(v0, 2 * block, 1), v2)
    u1 = jnp.where(first_half, v1, pltpu.roll(v3, 2 * block, 1))
    u3 = jnp.where(first_half, pltpu.roll(v1, 2 * block, 1), v3)
    w0 = jnp.where(even, u0, pltpu.roll(u1, block, 1))
    w1 = jnp.where(even, pltpu.roll(u0, 3 * block, 1), u1)
    w2 = jnp.where(even, u2, pltpu.roll(u3, block, 1))
    w3 = jnp.where(even, pltpu.roll(u2, 3 * block, 1), u3)
    return w0, w1, w2, w3


def normalized_taps(taps_ref, reverse, work_ref, out_ref):
    taps = taps_ref.shape[0]
    planes = taps_ref.shape[2]
    work_ref[...] = jnp.zeros_like(work_ref)
    for tap in range(taps):
        row = taps - 1 - tap if reverse else tap
        work_ref[row:row + 1, 0:planes] = taps_ref[tap]
    values = work_ref[...]
    total = jnp.sum(values, axis=0, keepdims=True)
    total = jnp.where(total == 0.0, 1.0, total)
    out_ref[...] = jnp.transpose(values / total)


def column_table(row, margin):
    table = pltpu.roll(jnp.broadcast_to(row, (LANES, LANES)), 0, 1, stride=1, stride_axis=0)
    high = table.astype(BF16).astype(F32)
    src = lax.broadcasted_iota(jnp.int32, (GROUP, LANES), 0)
    dst = lax.broadcasted_iota(jnp.int32, (GROUP, LANES), 1)
    first, last = slice(0, GROUP), slice(LANES - GROUP, LANES)
    above = dst - src <= LANES // 2
    below = src + LANES - GROUP - dst <= LANES // 2
    empty = jnp.zeros((LANES - 2 * GROUP, LANES), F32)
    main, edge = [], []
    for part in (high, table - high):
        main.append(jnp.concatenate(
            [jnp.where(above, part[first], 0.0), part[GROUP:LANES - GROUP], jnp.where(below, part[last], 0.0)],
            axis=0).astype(BF16))
        edge.append(jnp.concatenate(
            [jnp.where(above, 0.0, part[first]), empty, jnp.where(below, 0.0, part[last])],
            axis=0).astype(BF16))
    return jnp.concatenate([jnp.concatenate(main, axis=1), jnp.concatenate(edge, axis=1)], axis=0)


def blur_plane(plane, row, margin):
    height = plane.shape[0]
    table = column_table(row, margin)
    left, right = plane[:, :LANES], plane[:, LANES:]
    lane = lax.broadcasted_iota(jnp.int32, left.shape, 1)
    main = jnp.concatenate([left, right], axis=0)
    edge = jnp.concatenate(
        [jnp.where(lane < LANES // 2, right, 0.0), jnp.where(lane < LANES // 2, 0.0, left)], axis=0)
    high, low = split(jnp.concatenate([main, edge], axis=1))
    product = dot(jnp.concatenate([high, low], axis=0), table)
    rows = 2 * height
    blocks = product[:rows, :LANES] + (product[:rows, LANES:] + product[rows:, :LANES])
    return jnp.concatenate([blocks[:height], blocks[height:]], axis=1)


def row_table(base, margin, height):
    high = base.astype(BF16).astype(F32)
    low = base - high
    plane = lax.broadcasted_iota(jnp.int32, (8, LANES), 0)
    lane = lax.broadcasted_iota(jnp.int32, (8, LANES), 1)
    per_vector = LANES // height
    own = lane // height == plane % per_vector
    masks = [own & (plane // per_vector == part) for part in range(8 * height // LANES)]

    def table(part):
        strips = []
        for row in range(height):
            rolled = pltpu.roll(part, (row - margin) % LANES, 1)
            strips.append(jnp.concatenate([jnp.where(mask, rolled, 0.0) for mask in masks], axis=1))
        return jnp.concatenate(strips, axis=0).astype(BF16)

    return table(high), table(low)


def fold(square):
    side = square.shape[0]
    rest = jnp.zeros((8, LANES - 2 * side), F32)
    return jnp.concatenate(
        [jnp.concatenate([square[first:first + 8], square[first + 8:first + 16], rest], axis=1)
         for first in range(0, side, 16)], axis=0)


def unfold(folded, side):
    blocks = []
    for first in range(0, folded.shape[0], 8):
        blocks += [folded[first:first + 8, :side], folded[first:first + 8, side:2 * side]]
    return jnp.concatenate(blocks, axis=0)


def in_vmem(count):
    return [pl.BlockSpec(memory_space=pltpu.VMEM)] * count


def band_gram(w_rows):
    high, low = split(w_rows)
    rank = w_rows.shape[0]
    padded = jnp.concatenate([high, jnp.zeros((2 * LANES - rank, high.shape[1]), BF16)], axis=0)
    padded_low = jnp.concatenate([low, jnp.zeros((2 * LANES - rank, low.shape[1]), BF16)], axis=0)
    both = dot_nt(jnp.concatenate([high, low], axis=0), padded)
    return both[:rank] + (both[rank:] + dot_nt(high, padded_low))


def blur_group(step, cube_ref, kx_ref, ky_ref, xh_ref, xl_ref, margin):
    height = cube_ref.shape[1]
    halves = []
    for half in range(GROUP // 8):
        done = []
        for k in range(8 * half, 8 * half + 8):
            plane = step * GROUP + k
            done.append(blur_plane(cube_ref[plane], kx_ref[pl.ds(plane, 1), :], margin))
        high, low = split(jnp.concatenate(done, axis=0))
        rows = ky_ref[pl.ds(pl.multiple_of(step * GROUP + 8 * half, 8), 8), :]
        table_high, table_low = row_table(rows, margin, height)
        result = dot(table_high, high) + (dot(table_low, high) + dot(table_high, low))
        halves.append(result.reshape(height, 8, result.shape[1]))
    high, low = split(jnp.concatenate(halves, axis=1))
    planes_here = pl.ds(pl.multiple_of(step * GROUP, GROUP), GROUP)
    xh_ref[:, planes_here, :] = high
    xl_ref[:, planes_here, :] = low


def blur_kernel(cube_hbm, taps_x_hbm, taps_y_hbm, w_hbm, xh_ref, xl_ref, w_here_ref, w_both_ref, keep_ref, give_ref,
                cube_ref, taps_x_ref, taps_y_ref, w_ref, sems, chunk_sems, work_ref, kx_ref, ky_ref):
    taps = taps_x_ref.shape[0]
    margin = (taps - 1) // 2
    height = cube_ref.shape[1]
    rank = w_ref.shape[0]
    groups = cube_ref.shape[0] // GROUP

    def chunk(step):
        here = pl.ds(step * GROUP, GROUP)
        return pltpu.make_async_copy(cube_hbm.at[here], cube_ref.at[here], chunk_sems.at[step])

    copies = [
        pltpu.make_async_copy(taps_x_hbm, taps_x_ref, sems.at[0]),
        pltpu.make_async_copy(taps_y_hbm, taps_y_ref, sems.at[1]),
        pltpu.make_async_copy(w_hbm, w_ref, sems.at[2]),
    ]
    for copy in copies:
        copy.start()
    for step in range(groups):
        chunk(step).start()
    copies[0].wait()
    normalized_taps(taps_x_ref, True, work_ref, kx_ref)
    kx_ref[...] = pltpu.roll(kx_ref[...], LANES - margin, 1)
    copies[1].wait()
    normalized_taps(taps_y_ref, False, work_ref, ky_ref)
    per_vector = LANES // height
    place = lax.broadcasted_iota(jnp.int32, (LANES, LANES), 0) % per_vector
    values = ky_ref[...]
    placed = values
    for k in range(1, per_vector):
        placed = jnp.where(place == k, pltpu.roll(values, k * height, 1), placed)
    ky_ref[...] = placed
    copies[2].wait()

    for step in range(groups):
        chunk(step).wait()
    for step in range(groups):
        blur_group(step, cube_ref, kx_ref, ky_ref, xh_ref, xl_ref, margin)
    gram = fold(band_gram(w_ref[...])[:, :rank])
    keep_ref[PIECES * rank:] = gram
    give_ref[PIECES * rank:] = gram
    planes = xh_ref.shape[1]
    band = w_ref.shape[1]
    shift = lax.rem(band - lax.axis_index("sp") * planes, band)
    w_here = pltpu.roll(w_ref[...], shift, 1)[:, :2 * LANES]
    w_here_ref[...] = w_here[:, :planes]
    lane = lax.broadcasted_iota(jnp.int32, w_here.shape, 1)
    w_here = jnp.where(lane < planes, w_here, 0.0)
    w_high = w_here.astype(BF16).astype(F32)
    w_both = jnp.concatenate([w_high + pltpu.roll(w_high, planes, 1), w_here - w_high], axis=0).astype(BF16)
    w_both_ref[...] = w_both
    project(xh_ref, xl_ref, w_both[:, :2 * planes], keep_ref, give_ref, 0)


def project(xh_ref, xl_ref, w_both, keep_ref, give_ref, chain):
    height = xh_ref.shape[0]
    rank = w_both.shape[0] // 2
    me_sp = lax.axis_index("sp")
    me_bd = lax.axis_index("bd")
    tall = height // lax.axis_size("bd")
    wide = 2 * LANES // lax.axis_size("sp")
    for rel_bd in (1, 3, 0, 2):
        first_row = lax.bitwise_xor(me_bd, rel_bd) * tall + 4 * chain
        sums = []
        for row in range(4):
            image = jnp.concatenate([xh_ref[first_row + row], xl_ref[first_row + row]], axis=0)
            both = dot(w_both, image)
            sums.append(both[:rank] + both[rank:])
        part_ref = (keep_ref, give_ref)[rel_bd % 2]
        for column in range(2):
            pieces = exchange_blocks(
                [value[:, column * LANES:(column + 1) * LANES] for value in sums], wide)
            for k in range(4):
                rel_sp = lax.bitwise_xor(me_sp, column * 4 + k)
                side = 3 - rel_sp % 2 if rel_bd // 2 else rel_sp % 2
                first = pl.multiple_of((side * 4 + rel_sp // 2) * rank, 8)
                part_ref[pl.ds(first, rank)] = pieces[k]


def project_kernel(xh_ref, xl_ref, w_both_ref, keep_ref, give_ref):
    planes = xh_ref.shape[1]
    project(xh_ref, xl_ref, w_both_ref[:, :2 * planes], keep_ref, give_ref, 1)


def project_call(x_high, x_low, w_both):
    part = jax.ShapeDtypeStruct((PIECES * w_both.shape[0] // 2, LANES), F32)
    return pl.pallas_call(
        project_kernel,
        out_shape=[part, part],
        in_specs=in_vmem(3),
        out_specs=in_vmem(2),
        compiler_params=pltpu.CompilerParams(vmem_limit_bytes=VMEM_LIMIT),
    )(x_high, x_low, w_both)


def blur_call(cube, taps_x, taps_y, w_rows):
    planes, height, length = cube.shape
    rank = w_rows.shape[0]
    first = jax.ShapeDtypeStruct((PIECES * rank + FOLDED, LANES), F32)
    image = (height, planes, length)
    mine = jax.ShapeDtypeStruct((rank, planes), F32)
    both = jax.ShapeDtypeStruct((2 * rank, 2 * LANES), BF16)
    in_hbm = [pltpu.with_memory_space_constraint(value, pltpu.HBM) for value in (cube, taps_x, taps_y, w_rows)]
    return pl.pallas_call(
        blur_kernel,
        out_shape=[jax.ShapeDtypeStruct(image, BF16)] * 2 + [mine, both, first, first],
        in_specs=[pl.BlockSpec(memory_space=pltpu.HBM)] * 4,
        out_specs=in_vmem(6),
        scratch_shapes=[pltpu.VMEM(value.shape, F32) for value in (cube, taps_x, taps_y, w_rows)]
        + [pltpu.SemaphoreType.DMA((3,)), pltpu.SemaphoreType.DMA((planes // GROUP,))]
        + [pltpu.VMEM((LANES, LANES), F32)] * 3,
        compiler_params=pltpu.CompilerParams(vmem_limit_bytes=VMEM_LIMIT),
    )(*in_hbm)


def ratio_kernel(mine_ref, other_ref, h_ref, out_ref):
    tall = h_ref.shape[0] // lax.axis_size("bd")
    first = pl.multiple_of(lax.axis_index("bd") * tall, tall)
    here = h_ref[pl.ds(first, tall)]
    here = jnp.transpose(here.reshape(-1, here.shape[2]))
    rows = mine_ref.shape[0]
    folded = mine_ref[rows - 16:rows] + other_ref[rows - 16:rows]
    folded = jnp.concatenate([folded[:8, :LANES], folded[:8, LANES:], folded[8:, :LANES]], axis=0)
    gram = unfold(folded, here.shape[0])
    out_ref[...] = here / dot_exact(gram, here)


def ratio_call(mine, other, h_columns):
    piece = jax.ShapeDtypeStruct((h_columns.shape[2], 2 * LANES), F32)
    return pl.pallas_call(
        ratio_kernel,
        out_shape=piece,
        in_specs=in_vmem(3),
        compiler_params=pltpu.CompilerParams(vmem_limit_bytes=VMEM_LIMIT),
    )(mine, other, h_columns)


def accumulate(xh_ref, xl_ref, part_refs, all_ref, rel_core, total):
    height, planes, _ = xh_ref.shape
    me_sp = lax.axis_index("sp")
    me_bd = lax.axis_index("bd")
    pieces = lax.axis_size("sp")
    tall = height // lax.axis_size("bd")
    wide = 2 * LANES // pieces
    core = lax.bitwise_xor(me_bd % 2, rel_core)
    for partner, part_ref in enumerate(part_refs):
        row = lax.bitwise_xor(me_bd // 2, partner // 2)
        for inner in range(4):
            column = lax.bitwise_xor(me_sp, partner % 2 + 2 * inner)
            all_ref[row * pieces + column] = part_ref[inner]
    for row in range(2):
        for quarter in range(2):
            first_row = (2 * row + core) * tall + 4 * quarter
            halves = [
                exchange_blocks(
                    [all_ref[row * pieces + column * 4 + k][:, quarter * LANES:(quarter + 1) * LANES]
                     for k in range(4)], wide)
                for column in range(2)]
            rows = jnp.concatenate([halves[column][k] for k in range(4) for column in range(2)], axis=1)
            high, low = split(rows)
            here = jnp.concatenate([high, low], axis=0)
            image = [
                jnp.concatenate([ref[first_row + k] for k in range(4)], axis=1) for ref in (xh_ref, xl_ref)]
            total = total + dot_nt(jnp.concatenate(image + [here], axis=0), here)
    return total


def first_kernel(xh_ref, xl_ref, *rest):
    part_refs = rest[:4]
    total_out, all_ref = rest[4:]
    total_out[...] = accumulate(xh_ref, xl_ref, part_refs, all_ref, 0, jnp.zeros(total_out.shape, F32))


def first_call(x_high, x_low, parts):
    _, planes, _ = x_high.shape
    rank = parts[0].shape[1]
    return pl.pallas_call(
        first_kernel,
        out_shape=jax.ShapeDtypeStruct((2 * (planes + rank), 2 * rank), F32),
        in_specs=in_vmem(2 + len(parts)),
        scratch_shapes=[pltpu.VMEM((16, rank, 2 * LANES), F32)],
        compiler_params=pltpu.CompilerParams(vmem_limit_bytes=VMEM_LIMIT),
    )(x_high, x_low, *parts)


def second_kernel(xh_ref, xl_ref, w_ref, total_ref, *rest):
    part_refs = rest[:4]
    w_out, all_ref = rest[4:]
    planes = xh_ref.shape[1]
    rank = w_ref.shape[0]
    total = accumulate(xh_ref, xl_ref, part_refs, all_ref, 1, total_ref[...])
    numer = total[:planes, :rank] + (total[:planes, rank:] + total[planes:2 * planes, :rank])
    gram = total[2 * planes:]
    gram = gram[:rank, :rank] + (gram[:rank, rank:] + gram[rank:, :rank])
    w_here = w_ref[...]
    w_out[...] = w_here * jnp.transpose(numer) / dot_exact(gram, w_here)


def second_call(x_high, x_low, w_here, total, parts):
    rank = w_here.shape[0]
    return pl.pallas_call(
        second_kernel,
        out_shape=jax.ShapeDtypeStruct(w_here.shape, F32),
        in_specs=in_vmem(4 + len(parts)),
        scratch_shapes=[pltpu.VMEM((16, rank, 2 * LANES), F32)],
        compiler_params=pltpu.CompilerParams(vmem_limit_bytes=VMEM_LIMIT),
    )(x_high, x_low, w_here, total, *parts)


def place_h_kernel(*refs):
    h_out = refs[-1]
    me_bd = lax.axis_index("bd")
    tall = h_out.shape[0] // lax.axis_size("bd")
    for rel_bd in range(4):
        piece = refs[rel_bd][0]
        first = lax.bitwise_xor(me_bd, rel_bd) * tall
        h_out[pl.ds(first, tall)] = jnp.transpose(piece).reshape((tall,) + h_out.shape[1:])


def place_h_call(parts, shape):
    return pl.pallas_call(
        place_h_kernel,
        out_shape=jax.ShapeDtypeStruct(shape, F32),
        in_specs=in_vmem(len(parts)),
        compiler_params=pltpu.CompilerParams(vmem_limit_bytes=VMEM_LIMIT),
    )(*parts)


def gather_w_kernel(*refs):
    part_refs = refs[:-2]
    out_ref, all_ref = refs[-2:]
    planes = out_ref.shape[1] // 8
    me_sp = lax.axis_index("sp")
    rel = 0
    for part_ref in part_refs:
        for inner in range(part_ref.shape[0]):
            all_ref[lax.bitwise_xor(me_sp, RING[rel]), :, 0:planes] = part_ref[inner]
            rel += 1
    for owner in range(8):
        out_ref[:, owner * planes:(owner + 1) * planes] = all_ref[owner][:, :planes]


RING = (0, 1, 2, 3, 4, 5, 6, 7)


def gather_w_call(parts):
    _, rank, planes = parts[0].shape
    return pl.pallas_call(
        gather_w_kernel,
        out_shape=jax.ShapeDtypeStruct((rank, planes * 8), F32),
        in_specs=in_vmem(len(parts)),
        scratch_shapes=[pltpu.VMEM((8, rank, LANES), F32)],
        compiler_params=pltpu.CompilerParams(vmem_limit_bytes=VMEM_LIMIT),
    )(*parts)


def send(value, mask_sp, mask_bd):
    bands = lax.axis_size("bd")
    pieces = lax.axis_size("sp")
    pairs = []
    for s in range(pieces):
        for b in range(bands):
            pairs.append((s * bands + b, (s ^ mask_sp) * bands + (b ^ mask_bd)))
    return lax.ppermute(value, ("sp", "bd"), pairs)


def around(values):
    return [send(values[k], k % 2, 2 * (k // 2)) for k in range(1, 4)]


def local(cube, taps_x, taps_y, factor_w, factor_h):
    w_rows = jnp.transpose(factor_w[0])
    taps_x = jnp.transpose(taps_x, (2, 0, 1))
    taps_y = jnp.transpose(taps_y, (2, 0, 1))
    h_columns = jnp.transpose(factor_h, (1, 2, 0))
    rank = w_rows.shape[0]
    x_high, x_low, w_here, w_both, keep_0, give_0 = blur_call(cube[0], taps_x, taps_y, w_rows)
    taken_0 = send(give_0, 0, 1)
    keep_1, give_1 = project_call(x_high, x_low, w_both)
    taken_0, keep_1, give_1 = lax.optimization_barrier((taken_0, keep_1, give_1))
    taken_1 = send(give_1, 0, 1)
    sides = []
    for place in (0, 1, 3, 2):
        here = slice(place * 4 * rank, (place + 1) * 4 * rank)
        sides.append(jnp.concatenate([keep_0[here] + taken_0[here], keep_1[here] + taken_1[here]], axis=1))
    gram = keep_0[PIECES * rank:] + taken_0[PIECES * rank:]
    gram = jnp.concatenate([gram, jnp.zeros_like(gram[:8])], axis=0)
    gram = jnp.concatenate(
        [jnp.concatenate([gram[first:first + 8], gram[first + 8:first + 16]], axis=1) for first in (0, 16)], axis=0)
    sides[2] = jnp.concatenate([sides[2], gram], axis=0)
    others = around(sides)
    ratio = ratio_call(sides[2], others[1], h_columns)
    line = []
    for k in range(4):
        part = slice(k * rank, (k + 1) * rank)
        line.append((sides[0][part] + others[0][part]) + (others[1][part] + others[2][part]))
    line = [line[0]] + [send(line[k], 2 * k, 0) for k in range(1, 4)]
    h_piece = ratio * ((line[0] + line[1]) + (line[2] + line[3]))
    h_line = [h_piece] + [send(h_piece, 2 * k, 0) for k in range(1, 4)]
    mine = jnp.stack(h_line)
    first_parts = [mine] + around([mine] * 4)
    second_parts = [send(value, 0, 1) for value in first_parts]
    total = first_call(x_high, x_low, first_parts)
    w_piece = second_call(x_high, x_low, w_here, total, second_parts)
    own = [parts[k] for k in (0, 2) for parts in (first_parts, second_parts)]
    h_next = place_h_call(own, h_columns.shape)
    w_pair = jnp.stack([w_piece, send(w_piece, 1, 0)])
    w_next = gather_w_call([w_pair] + [send(w_pair, 2 * k, 0) for k in range(1, 4)])
    return jnp.transpose(w_next)[None], jnp.transpose(h_next, (2, 0, 1))


def normalized(kernel):
    return kernel / jnp.sum(kernel, axis=-1, keepdims=True)


def band_weights(kernel, size_in, size_out, offset):
    tap_count = kernel.shape[-1]
    in_index = lax.broadcasted_iota(jnp.int32, (size_in, size_out, tap_count), 0)
    out_index = lax.broadcasted_iota(jnp.int32, (size_in, size_out, tap_count), 1)
    tap_index = lax.broadcasted_iota(jnp.int32, (size_in, size_out, tap_count), 2)
    select = (tap_index == in_index - out_index + offset).astype(jnp.float32)
    return jnp.einsum("pk,iok->pio", kernel, select, precision=lax.Precision.HIGHEST)


def blur_rows(planes, kernel_y):
    margin = (kernel_y.shape[-1] - 1) // 2
    height = planes.shape[1]
    band_table = band_weights(kernel_y, height, height, margin)
    return jnp.einsum("piz,pio->poz", planes, band_table, precision=lax.Precision.HIGHEST)


def blur_columns(planes, kernel_x):
    margin = (kernel_x.shape[-1] - 1) // 2
    count, height, length = planes.shape
    blocks = planes.reshape(count, height, length // 128, 128)
    empty = jnp.zeros((count, height, 1, 128), jnp.float32)
    left_block = jnp.concatenate([empty, blocks[:, :, :-1]], axis=2)
    right_block = jnp.concatenate([blocks[:, :, 1:], empty], axis=2)
    window = jnp.concatenate([left_block, blocks, right_block], axis=3)
    band_table = band_weights(kernel_x, 384, 128, margin - 128)
    result = jnp.einsum("pybi,pio->pybo", window, band_table, precision=lax.Precision.HIGHEST)
    return result.reshape(count, height, length)


def local_any(cube, taps_x, taps_y, factor_w, factor_h):
    highest = lax.Precision.HIGHEST
    kernel_x = normalized(taps_x[0])
    kernel_y = normalized(taps_y[0])
    rows_done = blur_rows(cube[0], kernel_y)
    w_band = factor_w[0]
    blurred = blur_columns(rows_done, kernel_x)[None]
    moved = lax.all_to_all(blurred, "sp", split_axis=3, concat_axis=1, tiled=True)
    numer_part = jnp.einsum("lr,plyx->pryx", w_band, moved, precision=highest)
    gram_part = jnp.dot(w_band.T, w_band, precision=highest)
    numer_h, gram_w = lax.psum((numer_part[0], gram_part), "bd")
    h_next = factor_h * numer_h / jnp.einsum("rq,qyx->ryx", gram_w, factor_h, precision=highest)
    x_band = moved[0]
    gram_h_part = jnp.einsum("ryx,qyx->rq", h_next, h_next, precision=highest)
    numer_w_part = jnp.einsum("lyx,ryx->lr", x_band, h_next, precision=highest)
    numer_w, gram_h = lax.psum((numer_w_part, gram_h_part), "sp")
    w_next = w_band * numer_w / jnp.dot(w_band, gram_h, precision=highest)
    return (w_next[None], h_next)


def solution(mesh):
    in_specs = (
        P("bd", "sp", None, None),
        P("bd", "sp", None),
        P("bd", "sp", None),
        P("bd", None, None),
        P(None, None, "sp"),
    )
    out_specs = (P("bd", None, None), P(None, None, "sp"))

    def body(cube, *rest):
        suits = lax.axis_size("sp") == 8 and lax.axis_size("bd") == 4 and cube.shape[1] % GROUP == 0
        return (local if suits else local_any)(cube, *rest)

    return jax.shard_map(body, mesh=mesh, in_specs=in_specs, out_specs=out_specs, check_vma=False)
```

```python
import functools

import jax
import jax.numpy as jnp
from jax import lax
from jax.experimental import pallas as pl
from jax.experimental.pallas import tpu as pltpu
from jax.sharding import PartitionSpec as P

F32 = jnp.float32
BF16 = jnp.bfloat16
LANES = 128
GROUP = 16
PIECES = 16
FOLDED = 24
VMEM_LIMIT = 48 * 1024 * 1024


def split(value):
    high = value.astype(BF16)
    low = (value - high.astype(F32)).astype(BF16)
    return high, low


def dot(left, right):
    return lax.dot_general(left, right, (((1,), (0,)), ((), ())), preferred_element_type=F32)


def dot_nt(left, right):
    return lax.dot_general(left, right, (((1,), (1,)), ((), ())), preferred_element_type=F32)


def dot_exact(left, right):
    return lax.dot_general(
        left, right, (((1,), (0,)), ((), ())),
        precision=lax.Precision.HIGHEST, preferred_element_type=F32,
    )


def exchange_blocks(rows, block):
    lane = lax.broadcasted_iota(jnp.int32, rows[0].shape, 1)
    first_half = lane < 2 * block
    even = (lane // block) % 2 == 0
    v0, v1, v2, v3 = rows
    u0 = jnp.where(first_half, v0, pltpu.roll(v2, 2 * block, 1))
    u2 = jnp.where(first_half, pltpu.roll(v0, 2 * block, 1), v2)
    u1 = jnp.where(first_half, v1, pltpu.roll(v3, 2 * block, 1))
    u3 = jnp.where(first_half, pltpu.roll(v1, 2 * block, 1), v3)
    w0 = jnp.where(even, u0, pltpu.roll(u1, block, 1))
    w1 = jnp.where(even, pltpu.roll(u0, 3 * block, 1), u1)
    w2 = jnp.where(even, u2, pltpu.roll(u3, block, 1))
    w3 = jnp.where(even, pltpu.roll(u2, 3 * block, 1), u3)
    return w0, w1, w2, w3


def normalized_taps(taps_ref, reverse, work_ref, out_ref):
    taps = taps_ref.shape[0]
    planes = taps_ref.shape[2]
    work_ref[...] = jnp.zeros_like(work_ref)
    for tap in range(taps):
        row = taps - 1 - tap if reverse else tap
        work_ref[row:row + 1, 0:planes] = taps_ref[tap]
    values = work_ref[...]
    total = jnp.sum(values, axis=0, keepdims=True)
    total = jnp.where(total == 0.0, 1.0, total)
    out_ref[...] = jnp.transpose(values / total)


def column_table(row, margin):
    table = pltpu.roll(jnp.broadcast_to(row, (LANES, LANES)), 0, 1, stride=1, stride_axis=0)
    high = table.astype(BF16).astype(F32)
    src = lax.broadcasted_iota(jnp.int32, (GROUP, LANES), 0)
    dst = lax.broadcasted_iota(jnp.int32, (GROUP, LANES), 1)
    first, last = slice(0, GROUP), slice(LANES - GROUP, LANES)
    above = dst - src <= LANES // 2
    below = src + LANES - GROUP - dst <= LANES // 2
    empty = jnp.zeros((LANES - 2 * GROUP, LANES), F32)
    main, edge = [], []
    for part in (high, table - high):
        main.append(jnp.concatenate(
            [jnp.where(above, part[first], 0.0), part[GROUP:LANES - GROUP], jnp.where(below, part[last], 0.0)],
            axis=0).astype(BF16))
        edge.append(jnp.concatenate(
            [jnp.where(above, 0.0, part[first]), empty, jnp.where(below, 0.0, part[last])],
            axis=0).astype(BF16))
    return jnp.concatenate([jnp.concatenate(main, axis=1), jnp.concatenate(edge, axis=1)], axis=0)


def blur_plane(plane, row, margin):
    height = plane.shape[0]
    table = column_table(row, margin)
    left, right = plane[:, :LANES], plane[:, LANES:]
    lane = lax.broadcasted_iota(jnp.int32, left.shape, 1)
    main = jnp.concatenate([left, right], axis=0)
    edge = jnp.concatenate(
        [jnp.where(lane < LANES // 2, right, 0.0), jnp.where(lane < LANES // 2, 0.0, left)], axis=0)
    high, low = split(jnp.concatenate([main, edge], axis=1))
    product = dot(jnp.concatenate([high, low], axis=0), table)
    rows = 2 * height
    blocks = product[:rows, :LANES] + (product[:rows, LANES:] + product[rows:, :LANES])
    return jnp.concatenate([blocks[:height], blocks[height:]], axis=1)


def blur_rows_of(images, rows, margin):
    height = images[0].shape[0]
    sub = lax.broadcasted_iota(jnp.int32, (8, LANES), 0)
    lane = lax.broadcasted_iota(jnp.int32, (8, LANES), 1)
    lower = sub < 4
    own = lane // height == sub % 4
    moved = pltpu.roll(pltpu.roll(rows, 4, 0), 1, 1)
    results = []
    for group, base in ((0, jnp.where(lower, rows, moved)), (1, jnp.where(lower, moved, rows))):
        high = base.astype(BF16).astype(F32)
        strips = [
            jnp.where(own, pltpu.roll(part, (2 * pair - margin) % LANES, 1), 0.0)
            for part in (high, base - high) for pair in range(height // 2)]
        table = jnp.concatenate(strips, axis=0).astype(BF16)
        table = jnp.concatenate([table, table], axis=1)
        image = jnp.concatenate(split(jnp.concatenate(images[4 * group:4 * group + 4], axis=0)), axis=0)
        product = dot(table, image)
        half = product.shape[0] // 2
        results.append(product[:half] + product[half:])
    lower = lax.broadcasted_iota(jnp.int32, (8, results[0].shape[1]), 0) < 4
    out = []
    for pair in range(height // 2):
        here = slice(8 * pair, 8 * pair + 8)
        one, two = results[0][here], results[1][here]
        out.append(jnp.where(lower, one, two))
        out.append(pltpu.roll(jnp.where(lower, two, one), 4, 0))
    return jnp.concatenate(out, axis=0).reshape(height, 8, results[0].shape[1])


def fold(square):
    side = square.shape[0]
    rest = jnp.zeros((8, LANES - 2 * side), F32)
    return jnp.concatenate(
        [jnp.concatenate([square[first:first + 8], square[first + 8:first + 16], rest], axis=1)
         for first in range(0, side, 16)], axis=0)


def unfold(folded, side):
    blocks = []
    for first in range(0, folded.shape[0], 8):
        blocks += [folded[first:first + 8, :side], folded[first:first + 8, side:2 * side]]
    return jnp.concatenate(blocks, axis=0)


def in_vmem(count):
    return [pl.BlockSpec(memory_space=pltpu.VMEM)] * count


def band_gram(w_rows):
    high, low = split(w_rows)
    rank = w_rows.shape[0]
    padded = jnp.concatenate([high, jnp.zeros((2 * LANES - rank, high.shape[1]), BF16)], axis=0)
    padded_low = jnp.concatenate([low, jnp.zeros((2 * LANES - rank, low.shape[1]), BF16)], axis=0)
    both = dot_nt(jnp.concatenate([high, low], axis=0), padded)
    return both[:rank] + (both[rank:] + dot_nt(high, padded_low))


def blur_group(step, cube_ref, kx_ref, ky_ref, xh_ref, xl_ref, margin):
    halves = []
    for half in range(GROUP // 8):
        done = []
        for k in range(8 * half, 8 * half + 8):
            plane = step * GROUP + k
            done.append(blur_plane(cube_ref[plane], kx_ref[pl.ds(plane, 1), :], margin))
        rows = ky_ref[pl.ds(pl.multiple_of(step * GROUP + 8 * half, 8), 8), :]
        halves.append(blur_rows_of(done, rows, margin))
    high, low = split(jnp.concatenate(halves, axis=1))
    planes_here = pl.ds(pl.multiple_of(step * GROUP, GROUP), GROUP)
    xh_ref[:, planes_here, :] = high
    xl_ref[:, planes_here, :] = low


def blur_kernel(cube_hbm, taps_x_hbm, taps_y_hbm, w_hbm, xh_ref, xl_ref, w_here_ref, w_both_ref, keep_ref, give_ref,
                cube_ref, taps_x_ref, taps_y_ref, w_ref, sems, chunk_sems, work_ref, kx_ref, ky_ref):
    taps = taps_x_ref.shape[0]
    margin = (taps - 1) // 2
    height = cube_ref.shape[1]
    rank = w_ref.shape[0]
    groups = cube_ref.shape[0] // GROUP

    def chunk(step):
        here = pl.ds(step * GROUP, GROUP)
        return pltpu.make_async_copy(cube_hbm.at[here], cube_ref.at[here], chunk_sems.at[step])

    copies = [
        pltpu.make_async_copy(taps_x_hbm, taps_x_ref, sems.at[0]),
        pltpu.make_async_copy(taps_y_hbm, taps_y_ref, sems.at[1]),
        pltpu.make_async_copy(w_hbm, w_ref, sems.at[2]),
    ]
    for copy in copies:
        copy.start()
    for step in range(groups):
        chunk(step).start()
    copies[0].wait()
    normalized_taps(taps_x_ref, True, work_ref, kx_ref)
    kx_ref[...] = pltpu.roll(kx_ref[...], LANES - margin, 1)
    copies[1].wait()
    normalized_taps(taps_y_ref, False, work_ref, ky_ref)
    per_vector = LANES // height
    place = lax.broadcasted_iota(jnp.int32, (LANES, LANES), 0) % per_vector
    values = ky_ref[...]
    placed = values
    for k in range(1, per_vector):
        placed = jnp.where(place == k, pltpu.roll(values, k * height, 1), placed)
    ky_ref[...] = placed
    copies[2].wait()

    for step in range(groups):
        chunk(step).wait()
    for step in range(groups):
        blur_group(step, cube_ref, kx_ref, ky_ref, xh_ref, xl_ref, margin)
    gram = fold(band_gram(w_ref[...])[:, :rank])
    keep_ref[PIECES * rank:] = gram
    give_ref[PIECES * rank:] = gram
    planes = xh_ref.shape[1]
    band = w_ref.shape[1]
    shift = lax.rem(band - lax.axis_index("sp") * planes, band)
    w_here = pltpu.roll(w_ref[...], shift, 1)[:, :2 * LANES]
    w_here_ref[...] = w_here[:, :planes]
    lane = lax.broadcasted_iota(jnp.int32, w_here.shape, 1)
    w_here = jnp.where(lane < planes, w_here, 0.0)
    w_high = w_here.astype(BF16).astype(F32)
    w_both = jnp.concatenate([w_high + pltpu.roll(w_high, planes, 1), w_here - w_high], axis=0).astype(BF16)
    w_both_ref[...] = w_both
    project(xh_ref, xl_ref, w_both[:, :2 * planes], keep_ref, give_ref, 0)


def project(xh_ref, xl_ref, w_both, keep_ref, give_ref, chain):
    height = xh_ref.shape[0]
    rank = w_both.shape[0] // 2
    me_sp = lax.axis_index("sp")
    me_bd = lax.axis_index("bd")
    tall = height // lax.axis_size("bd")
    wide = 2 * LANES // lax.axis_size("sp")
    for rel_bd in (1, 3, 0, 2):
        first_row = lax.bitwise_xor(me_bd, rel_bd) * tall + 4 * chain
        sums = []
        for row in range(4):
            image = jnp.concatenate([xh_ref[first_row + row], xl_ref[first_row + row]], axis=0)
            both = dot(w_both, image)
            sums.append(both[:rank] + both[rank:])
        part_ref = (keep_ref, give_ref)[rel_bd % 2]
        for column in range(2):
            pieces = exchange_blocks(
                [value[:, column * LANES:(column + 1) * LANES] for value in sums], wide)
            for k in range(4):
                rel_sp = lax.bitwise_xor(me_sp, column * 4 + k)
                side = 3 - rel_sp % 2 if rel_bd // 2 else rel_sp % 2
                first = pl.multiple_of((side * 4 + rel_sp // 2) * rank, 8)
                part_ref[pl.ds(first, rank)] = pieces[k]


def project_kernel(xh_ref, xl_ref, w_both_ref, keep_ref, give_ref):
    planes = xh_ref.shape[1]
    project(xh_ref, xl_ref, w_both_ref[:, :2 * planes], keep_ref, give_ref, 1)


def project_call(x_high, x_low, w_both):
    part = jax.ShapeDtypeStruct((PIECES * w_both.shape[0] // 2, LANES), F32)
    return pl.pallas_call(
        project_kernel,
        out_shape=[part, part],
        in_specs=in_vmem(3),
        out_specs=in_vmem(2),
        compiler_params=pltpu.CompilerParams(vmem_limit_bytes=VMEM_LIMIT),
    )(x_high, x_low, w_both)


def blur_call(cube, taps_x, taps_y, w_rows):
    planes, height, length = cube.shape
    rank = w_rows.shape[0]
    first = jax.ShapeDtypeStruct((PIECES * rank + FOLDED, LANES), F32)
    image = (height, planes, length)
    mine = jax.ShapeDtypeStruct((rank, planes), F32)
    both = jax.ShapeDtypeStruct((2 * rank, 2 * LANES), BF16)
    in_hbm = [pltpu.with_memory_space_constraint(value, pltpu.HBM) for value in (cube, taps_x, taps_y, w_rows)]
    return pl.pallas_call(
        blur_kernel,
        out_shape=[jax.ShapeDtypeStruct(image, BF16)] * 2 + [mine, both, first, first],
        in_specs=[pl.BlockSpec(memory_space=pltpu.HBM)] * 4,
        out_specs=in_vmem(6),
        scratch_shapes=[pltpu.VMEM(value.shape, F32) for value in (cube, taps_x, taps_y, w_rows)]
        + [pltpu.SemaphoreType.DMA((3,)), pltpu.SemaphoreType.DMA((planes // GROUP,))]
        + [pltpu.VMEM((LANES, LANES), F32)] * 3,
        compiler_params=pltpu.CompilerParams(vmem_limit_bytes=VMEM_LIMIT),
    )(*in_hbm)


def ratio_kernel(mine_ref, other_ref, h_ref, out_ref):
    tall = h_ref.shape[0] // lax.axis_size("bd")
    first = pl.multiple_of(lax.axis_index("bd") * tall, tall)
    here = h_ref[pl.ds(first, tall)]
    here = jnp.transpose(here.reshape(-1, here.shape[2]))
    rows = mine_ref.shape[0]
    gram = unfold(mine_ref[rows - FOLDED:rows] + other_ref[rows - FOLDED:rows], here.shape[0])
    out_ref[...] = here / dot_exact(gram, here)


def ratio_call(mine, other, h_columns):
    piece = jax.ShapeDtypeStruct((h_columns.shape[2], 2 * LANES), F32)
    return pl.pallas_call(
        ratio_kernel,
        out_shape=piece,
        in_specs=in_vmem(3),
        compiler_params=pltpu.CompilerParams(vmem_limit_bytes=VMEM_LIMIT),
    )(mine, other, h_columns)


def accumulate(xh_ref, xl_ref, part_refs, all_ref, rel_core, total):
    height, planes, _ = xh_ref.shape
    me_sp = lax.axis_index("sp")
    me_bd = lax.axis_index("bd")
    pieces = lax.axis_size("sp")
    tall = height // lax.axis_size("bd")
    wide = 2 * LANES // pieces
    core = lax.bitwise_xor(me_bd % 2, rel_core)
    for partner, part_ref in enumerate(part_refs):
        row = lax.bitwise_xor(me_bd // 2, partner // 2)
        for inner in range(4):
            column = lax.bitwise_xor(me_sp, partner % 2 + 2 * inner)
            all_ref[row * pieces + column] = part_ref[inner]
    for row in range(2):
        for quarter in range(2):
            first_row = (2 * row + core) * tall + 4 * quarter
            halves = [
                exchange_blocks(
                    [all_ref[row * pieces + column * 4 + k][:, quarter * LANES:(quarter + 1) * LANES]
                     for k in range(4)], wide)
                for column in range(2)]
            rows = jnp.concatenate([halves[column][k] for k in range(4) for column in range(2)], axis=1)
            high, low = split(rows)
            here = jnp.concatenate([high, low], axis=0)
            image = [
                jnp.concatenate([ref[first_row + k] for k in range(4)], axis=1) for ref in (xh_ref, xl_ref)]
            total = total + dot_nt(jnp.concatenate(image + [here], axis=0), here)
    return total


def first_kernel(xh_ref, xl_ref, *rest):
    part_refs = rest[:4]
    total_out, all_ref = rest[4:]
    total_out[...] = accumulate(xh_ref, xl_ref, part_refs, all_ref, 0, jnp.zeros(total_out.shape, F32))


def first_call(x_high, x_low, parts):
    _, planes, _ = x_high.shape
    rank = parts[0].shape[1]
    return pl.pallas_call(
        first_kernel,
        out_shape=jax.ShapeDtypeStruct((2 * (planes + rank), 2 * rank), F32),
        in_specs=in_vmem(2 + len(parts)),
        scratch_shapes=[pltpu.VMEM((16, rank, 2 * LANES), F32)],
        compiler_params=pltpu.CompilerParams(vmem_limit_bytes=VMEM_LIMIT),
    )(x_high, x_low, *parts)


def second_kernel(xh_ref, xl_ref, w_ref, total_ref, *rest):
    part_refs = rest[:4]
    w_out, all_ref = rest[4:]
    planes = xh_ref.shape[1]
    rank = w_ref.shape[0]
    total = accumulate(xh_ref, xl_ref, part_refs, all_ref, 1, total_ref[...])
    numer = total[:planes, :rank] + (total[:planes, rank:] + total[planes:2 * planes, :rank])
    gram = total[2 * planes:]
    gram = gram[:rank, :rank] + (gram[:rank, rank:] + gram[rank:, :rank])
    w_here = w_ref[...]
    gram_high, gram_low = split(gram)
    w_high, w_low = split(w_here)
    both = dot(jnp.concatenate([gram_high, gram_low], axis=0), w_high)
    denominator = both[:rank] + (both[rank:] + dot(gram_high, w_low))
    w_out[...] = w_here * jnp.transpose(numer) / denominator


def second_call(x_high, x_low, w_here, total, parts):
    rank = w_here.shape[0]
    return pl.pallas_call(
        second_kernel,
        out_shape=jax.ShapeDtypeStruct(w_here.shape, F32),
        in_specs=in_vmem(4 + len(parts)),
        scratch_shapes=[pltpu.VMEM((16, rank, 2 * LANES), F32)],
        compiler_params=pltpu.CompilerParams(vmem_limit_bytes=VMEM_LIMIT),
    )(x_high, x_low, w_here, total, *parts)


def place_h_kernel(*refs):
    h_out = refs[-1]
    me_bd = lax.axis_index("bd")
    tall = h_out.shape[0] // lax.axis_size("bd")
    for rel_bd in range(4):
        piece = refs[rel_bd][0]
        first = lax.bitwise_xor(me_bd, rel_bd) * tall
        h_out[pl.ds(first, tall)] = jnp.transpose(piece).reshape((tall,) + h_out.shape[1:])


def place_h_call(parts, shape):
    return pl.pallas_call(
        place_h_kernel,
        out_shape=jax.ShapeDtypeStruct(shape, F32),
        in_specs=in_vmem(len(parts)),
        compiler_params=pltpu.CompilerParams(vmem_limit_bytes=VMEM_LIMIT),
    )(*parts)


def gather_w_kernel(*refs):
    part_refs = refs[:-2]
    out_ref, all_ref = refs[-2:]
    planes = out_ref.shape[1] // 8
    me_sp = lax.axis_index("sp")
    rel = 0
    for part_ref in part_refs:
        for inner in range(part_ref.shape[0]):
            all_ref[lax.bitwise_xor(me_sp, RING[rel]), :, 0:planes] = part_ref[inner]
            rel += 1
    for owner in range(8):
        out_ref[:, owner * planes:(owner + 1) * planes] = all_ref[owner][:, :planes]


RING = (0, 1, 2, 3, 4, 5, 6, 7)


def gather_w_call(parts):
    _, rank, planes = parts[0].shape
    return pl.pallas_call(
        gather_w_kernel,
        out_shape=jax.ShapeDtypeStruct((rank, planes * 8), F32),
        in_specs=in_vmem(len(parts)),
        scratch_shapes=[pltpu.VMEM((8, rank, LANES), F32)],
        compiler_params=pltpu.CompilerParams(vmem_limit_bytes=VMEM_LIMIT),
    )(*parts)


def send(value, mask_sp, mask_bd):
    bands = lax.axis_size("bd")
    pieces = lax.axis_size("sp")
    pairs = []
    for s in range(pieces):
        for b in range(bands):
            pairs.append((s * bands + b, (s ^ mask_sp) * bands + (b ^ mask_bd)))
    return lax.ppermute(value, ("sp", "bd"), pairs)


def around(values):
    return [send(values[k], k % 2, 2 * (k // 2)) for k in range(1, 4)]


def local(cube, taps_x, taps_y, factor_w, factor_h):
    w_rows = jnp.transpose(factor_w[0])
    taps_x = jnp.transpose(taps_x, (2, 0, 1))
    taps_y = jnp.transpose(taps_y, (2, 0, 1))
    h_columns = jnp.transpose(factor_h, (1, 2, 0))
    rank = w_rows.shape[0]
    x_high, x_low, w_here, w_both, keep_0, give_0 = blur_call(cube[0], taps_x, taps_y, w_rows)
    chains = []
    taken_0 = send(give_0, 0, 1)
    keep_1, give_1 = project_call(x_high, x_low, w_both)
    taken_0, keep_1, give_1 = lax.optimization_barrier((taken_0, keep_1, give_1))
    for keep, taken in ((keep_0, taken_0), (keep_1, send(give_1, 0, 1))):
        bounds = [place * 4 * rank for place in (0, 1, 3, 2)]
        sides = []
        for first in bounds:
            last = keep.shape[0] if first == max(bounds) else first + 4 * rank
            sides.append(keep[first:last] + taken[first:last])
        chains.append((sides, around(sides)))
    ratio = ratio_call(chains[0][0][2], chains[0][1][1], h_columns)
    line = []
    for k in range(4):
        part = slice(k * rank, (k + 1) * rank)
        line.append(jnp.concatenate(
            [(sides[0][part] + others[0][part]) + (others[1][part] + others[2][part]) for sides, others in chains],
            axis=1))
    line = [line[0]] + [send(line[k], 2 * k, 0) for k in (3, 2, 1)]
    h_piece = ratio * ((line[0] + line[1]) + (line[2] + line[3]))
    h_line = [h_piece] + [send(h_piece, 2 * k, 0) for k in range(1, 4)]
    mine = jnp.stack(h_line)
    first_parts = [mine] + around([mine] * 4)
    second_parts = [send(value, 0, 1) for value in first_parts]
    total = first_call(x_high, x_low, first_parts)
    w_piece = second_call(x_high, x_low, w_here, total, second_parts)
    own = [parts[k] for k in (0, 2) for parts in (first_parts, second_parts)]
    h_next = place_h_call(own, h_columns.shape)
    w_pair = jnp.stack([w_piece, send(w_piece, 1, 0)])
    w_next = gather_w_call([w_pair] + [send(w_pair, 2 * k, 0) for k in range(1, 4)])
    return jnp.transpose(w_next)[None], jnp.transpose(h_next, (2, 0, 1))


def normalized(kernel):
    return kernel / jnp.sum(kernel, axis=-1, keepdims=True)


def band_weights(kernel, size_in, size_out, offset):
    tap_count = kernel.shape[-1]
    in_index = lax.broadcasted_iota(jnp.int32, (size_in, size_out, tap_count), 0)
    out_index = lax.broadcasted_iota(jnp.int32, (size_in, size_out, tap_count), 1)
    tap_index = lax.broadcasted_iota(jnp.int32, (size_in, size_out, tap_count), 2)
    select = (tap_index == in_index - out_index + offset).astype(jnp.float32)
    return jnp.einsum("pk,iok->pio", kernel, select, precision=lax.Precision.HIGHEST)


def blur_rows(planes, kernel_y):
    margin = (kernel_y.shape[-1] - 1) // 2
    height = planes.shape[1]
    band_table = band_weights(kernel_y, height, height, margin)
    return jnp.einsum("piz,pio->poz", planes, band_table, precision=lax.Precision.HIGHEST)


def blur_columns(planes, kernel_x):
    margin = (kernel_x.shape[-1] - 1) // 2
    count, height, length = planes.shape
    blocks = planes.reshape(count, height, length // 128, 128)
    empty = jnp.zeros((count, height, 1, 128), jnp.float32)
    left_block = jnp.concatenate([empty, blocks[:, :, :-1]], axis=2)
    right_block = jnp.concatenate([blocks[:, :, 1:], empty], axis=2)
    window = jnp.concatenate([left_block, blocks, right_block], axis=3)
    band_table = band_weights(kernel_x, 384, 128, margin - 128)
    result = jnp.einsum("pybi,pio->pybo", window, band_table, precision=lax.Precision.HIGHEST)
    return result.reshape(count, height, length)


def local_any(cube, taps_x, taps_y, factor_w, factor_h):
    highest = lax.Precision.HIGHEST
    kernel_x = normalized(taps_x[0])
    kernel_y = normalized(taps_y[0])
    rows_done = blur_rows(cube[0], kernel_y)
    w_band = factor_w[0]
    blurred = blur_columns(rows_done, kernel_x)[None]
    moved = lax.all_to_all(blurred, "sp", split_axis=3, concat_axis=1, tiled=True)
    numer_part = jnp.einsum("lr,plyx->pryx", w_band, moved, precision=highest)
    gram_part = jnp.dot(w_band.T, w_band, precision=highest)
    numer_h, gram_w = lax.psum((numer_part[0], gram_part), "bd")
    h_next = factor_h * numer_h / jnp.einsum("rq,qyx->ryx", gram_w, factor_h, precision=highest)
    x_band = moved[0]
    gram_h_part = jnp.einsum("ryx,qyx->rq", h_next, h_next, precision=highest)
    numer_w_part = jnp.einsum("lyx,ryx->lr", x_band, h_next, precision=highest)
    numer_w, gram_h = lax.psum((numer_w_part, gram_h_part), "sp")
    w_next = w_band * numer_w / jnp.dot(w_band, gram_h, precision=highest)
    return (w_next[None], h_next)


def solution(mesh):
    in_specs = (
        P("bd", "sp", None, None),
        P("bd", "sp", None),
        P("bd", "sp", None),
        P("bd", None, None),
        P(None, None, "sp"),
    )
    out_specs = (P("bd", None, None), P(None, None, "sp"))

    def body(cube, *rest):
        suits = lax.axis_size("sp") == 8 and lax.axis_size("bd") == 4 and cube.shape[1:] == (96, 32, 2 * LANES)
        return (local if suits else local_any)(cube, *rest)

    return jax.shard_map(body, mesh=mesh, in_specs=in_specs, out_specs=out_specs, check_vma=False)
```

```python
import functools

import jax
import jax.numpy as jnp
from jax import lax
from jax.experimental import pallas as pl
from jax.experimental.pallas import tpu as pltpu
from jax.sharding import PartitionSpec as P

F32 = jnp.float32
BF16 = jnp.bfloat16
LANES = 128
GROUP = 16
PIECES = 16
FOLDED = 24
VMEM_LIMIT = 48 * 1024 * 1024


def split(value):
    high = value.astype(BF16)
    low = (value - high.astype(F32)).astype(BF16)
    return high, low


def dot(left, right):
    return lax.dot_general(left, right, (((1,), (0,)), ((), ())), preferred_element_type=F32)


def dot_nt(left, right):
    return lax.dot_general(left, right, (((1,), (1,)), ((), ())), preferred_element_type=F32)


def dot_exact(left, right):
    return lax.dot_general(
        left, right, (((1,), (0,)), ((), ())),
        precision=lax.Precision.HIGHEST, preferred_element_type=F32,
    )


def exchange_blocks(rows, block):
    lane = lax.broadcasted_iota(jnp.int32, rows[0].shape, 1)
    first_half = lane < 2 * block
    even = (lane // block) % 2 == 0
    v0, v1, v2, v3 = rows
    u0 = jnp.where(first_half, v0, pltpu.roll(v2, 2 * block, 1))
    u2 = jnp.where(first_half, pltpu.roll(v0, 2 * block, 1), v2)
    u1 = jnp.where(first_half, v1, pltpu.roll(v3, 2 * block, 1))
    u3 = jnp.where(first_half, pltpu.roll(v1, 2 * block, 1), v3)
    w0 = jnp.where(even, u0, pltpu.roll(u1, block, 1))
    w1 = jnp.where(even, pltpu.roll(u0, 3 * block, 1), u1)
    w2 = jnp.where(even, u2, pltpu.roll(u3, block, 1))
    w3 = jnp.where(even, pltpu.roll(u2, 3 * block, 1), u3)
    return w0, w1, w2, w3


def normalized_taps(taps_ref, reverse, work_ref, out_ref):
    taps = taps_ref.shape[0]
    planes = taps_ref.shape[2]
    work_ref[...] = jnp.zeros_like(work_ref)
    for tap in range(taps):
        row = taps - 1 - tap if reverse else tap
        work_ref[row:row + 1, 0:planes] = taps_ref[tap]
    values = work_ref[...]
    total = jnp.sum(values, axis=0, keepdims=True)
    total = jnp.where(total == 0.0, 1.0, total)
    out_ref[...] = jnp.transpose(values / total)


def column_table(row, margin):
    table = pltpu.roll(jnp.broadcast_to(row, (LANES, LANES)), 0, 1, stride=1, stride_axis=0)
    high = table.astype(BF16).astype(F32)
    src = lax.broadcasted_iota(jnp.int32, (GROUP, LANES), 0)
    dst = lax.broadcasted_iota(jnp.int32, (GROUP, LANES), 1)
    first, last = slice(0, GROUP), slice(LANES - GROUP, LANES)
    above = dst - src <= LANES // 2
    below = src + LANES - GROUP - dst <= LANES // 2
    empty = jnp.zeros((LANES - 2 * GROUP, LANES), F32)
    main, edge = [], []
    for part in (high, table - high):
        main.append(jnp.concatenate(
            [jnp.where(above, part[first], 0.0), part[GROUP:LANES - GROUP], jnp.where(below, part[last], 0.0)],
            axis=0).astype(BF16))
        edge.append(jnp.concatenate(
            [jnp.where(above, 0.0, part[first]), empty, jnp.where(below, 0.0, part[last])],
            axis=0).astype(BF16))
    return jnp.concatenate([jnp.concatenate(main, axis=1), jnp.concatenate(edge, axis=1)], axis=0)


def blur_plane(plane, row, margin):
    height = plane.shape[0]
    table = column_table(row, margin)
    left, right = plane[:, :LANES], plane[:, LANES:]
    lane = lax.broadcasted_iota(jnp.int32, left.shape, 1)
    main = jnp.concatenate([left, right], axis=0)
    edge = jnp.concatenate(
        [jnp.where(lane < LANES // 2, right, 0.0), jnp.where(lane < LANES // 2, 0.0, left)], axis=0)
    high, low = split(jnp.concatenate([main, edge], axis=1))
    product = dot(jnp.concatenate([high, low], axis=0), table)
    rows = 2 * height
    blocks = product[:rows, :LANES] + (product[:rows, LANES:] + product[rows:, :LANES])
    return jnp.concatenate([blocks[:height], blocks[height:]], axis=1)


def blur_rows_of(images, rows, margin):
    height = images[0].shape[0]
    sub = lax.broadcasted_iota(jnp.int32, (8, LANES), 0)
    lane = lax.broadcasted_iota(jnp.int32, (8, LANES), 1)
    lower = sub < 4
    own = lane // height == sub % 4
    moved = pltpu.roll(pltpu.roll(rows, 4, 0), 1, 1)
    results = []
    for group, base in ((0, jnp.where(lower, rows, moved)), (1, jnp.where(lower, moved, rows))):
        high = base.astype(BF16).astype(F32)
        strips = [
            jnp.where(own, pltpu.roll(part, (2 * pair - margin) % LANES, 1), 0.0)
            for part in (high, base - high) for pair in range(height // 2)]
        table = jnp.concatenate(strips, axis=0).astype(BF16)
        table = jnp.concatenate([table, table], axis=1)
        image = jnp.concatenate(split(jnp.concatenate(images[4 * group:4 * group + 4], axis=0)), axis=0)
        product = dot(table, image)
        half = product.shape[0] // 2
        results.append(product[:half] + product[half:])
    lower = lax.broadcasted_iota(jnp.int32, (8, results[0].shape[1]), 0) < 4
    out = []
    for pair in range(height // 2):
        here = slice(8 * pair, 8 * pair + 8)
        one, two = results[0][here], results[1][here]
        out.append(jnp.where(lower, one, two))
        out.append(pltpu.roll(jnp.where(lower, two, one), 4, 0))
    return jnp.concatenate(out, axis=0).reshape(height, 8, results[0].shape[1])


def fold(square):
    side = square.shape[0]
    rest = jnp.zeros((8, LANES - 2 * side), F32)
    return jnp.concatenate(
        [jnp.concatenate([square[first:first + 8], square[first + 8:first + 16], rest], axis=1)
         for first in range(0, side, 16)], axis=0)


def unfold(folded, side):
    blocks = []
    for first in range(0, folded.shape[0], 8):
        blocks += [folded[first:first + 8, :side], folded[first:first + 8, side:2 * side]]
    return jnp.concatenate(blocks, axis=0)


def in_vmem(count):
    return [pl.BlockSpec(memory_space=pltpu.VMEM)] * count


def band_gram(w_rows):
    high, low = split(w_rows)
    rank = w_rows.shape[0]
    padded = jnp.concatenate([high, jnp.zeros((2 * LANES - rank, high.shape[1]), BF16)], axis=0)
    padded_low = jnp.concatenate([low, jnp.zeros((2 * LANES - rank, low.shape[1]), BF16)], axis=0)
    both = dot_nt(jnp.concatenate([high, low], axis=0), padded)
    return both[:rank] + (both[rank:] + dot_nt(high, padded_low))


def blur_group(step, cube_ref, kx_ref, ky_ref, xh_ref, xl_ref, margin):
    halves = []
    for half in range(GROUP // 8):
        done = []
        for k in range(8 * half, 8 * half + 8):
            plane = step * GROUP + k
            done.append(blur_plane(cube_ref[plane], kx_ref[pl.ds(plane, 1), :], margin))
        rows = ky_ref[pl.ds(pl.multiple_of(step * GROUP + 8 * half, 8), 8), :]
        halves.append(blur_rows_of(done, rows, margin))
    high, low = split(jnp.concatenate(halves, axis=1))
    planes_here = pl.ds(pl.multiple_of(step * GROUP, GROUP), GROUP)
    xh_ref[:, planes_here, :] = high
    xl_ref[:, planes_here, :] = low


def blur_kernel(cube_hbm, taps_x_hbm, taps_y_hbm, w_hbm, xh_ref, xl_ref, w_here_ref, w_both_ref, give_ref,
                cube_ref, taps_x_ref, taps_y_ref, w_ref, sems, chunk_sems, work_ref, kx_ref, ky_ref):
    taps = taps_x_ref.shape[0]
    margin = (taps - 1) // 2
    height = cube_ref.shape[1]
    rank = w_ref.shape[0]
    groups = cube_ref.shape[0] // GROUP

    def chunk(step):
        here = pl.ds(step * GROUP, GROUP)
        return pltpu.make_async_copy(cube_hbm.at[here], cube_ref.at[here], chunk_sems.at[step])

    copies = [
        pltpu.make_async_copy(taps_x_hbm, taps_x_ref, sems.at[0]),
        pltpu.make_async_copy(taps_y_hbm, taps_y_ref, sems.at[1]),
        pltpu.make_async_copy(w_hbm, w_ref, sems.at[2]),
    ]
    for copy in copies:
        copy.start()
    for step in range(groups):
        chunk(step).start()
    copies[0].wait()
    normalized_taps(taps_x_ref, True, work_ref, kx_ref)
    kx_ref[...] = pltpu.roll(kx_ref[...], LANES - margin, 1)
    copies[1].wait()
    normalized_taps(taps_y_ref, False, work_ref, ky_ref)
    per_vector = LANES // height
    place = lax.broadcasted_iota(jnp.int32, (LANES, LANES), 0) % per_vector
    values = ky_ref[...]
    placed = values
    for k in range(1, per_vector):
        placed = jnp.where(place == k, pltpu.roll(values, k * height, 1), placed)
    ky_ref[...] = placed
    copies[2].wait()

    for step in range(groups):
        chunk(step).wait()
    for step in range(groups):
        blur_group(step, cube_ref, kx_ref, ky_ref, xh_ref, xl_ref, margin)
    gram = fold(band_gram(w_ref[...])[:, :rank])
    give_ref[PIECES * rank:] = gram
    planes = xh_ref.shape[1]
    band = w_ref.shape[1]
    shift = lax.rem(band - lax.axis_index("sp") * planes, band)
    w_here = pltpu.roll(w_ref[...], shift, 1)[:, :2 * LANES]
    w_here_ref[...] = w_here[:, :planes]
    lane = lax.broadcasted_iota(jnp.int32, w_here.shape, 1)
    w_here = jnp.where(lane < planes, w_here, 0.0)
    w_high = w_here.astype(BF16).astype(F32)
    w_both = jnp.concatenate([w_high + pltpu.roll(w_high, planes, 1), w_here - w_high], axis=0).astype(BF16)
    w_both_ref[...] = w_both
    project(xh_ref, xl_ref, w_both[:, :2 * planes], give_ref, 0, 1)


def project(xh_ref, xl_ref, w_both, part_ref, chain, rel_core):
    height = xh_ref.shape[0]
    rank = w_both.shape[0] // 2
    me_sp = lax.axis_index("sp")
    me_bd = lax.axis_index("bd")
    tall = height // lax.axis_size("bd")
    wide = 2 * LANES // lax.axis_size("sp")
    for rel_bd in (rel_core, rel_core + 2):
        first_row = lax.bitwise_xor(me_bd, rel_bd) * tall + 4 * chain
        sums = []
        for row in range(4):
            image = jnp.concatenate([xh_ref[first_row + row], xl_ref[first_row + row]], axis=0)
            both = dot(w_both, image)
            sums.append(both[:rank] + both[rank:])
        for column in range(2):
            pieces = exchange_blocks(
                [value[:, column * LANES:(column + 1) * LANES] for value in sums], wide)
            for k in range(4):
                rel_sp = lax.bitwise_xor(me_sp, column * 4 + k)
                side = 3 - rel_sp % 2 if rel_bd // 2 else rel_sp % 2
                first = pl.multiple_of((side * 4 + rel_sp // 2) * rank, 8)
                part_ref[pl.ds(first, rank)] = pieces[k]


def project_kernel(xh_ref, xl_ref, w_both_ref, first_ref, keep_0, keep_1, give_1):
    w_both = w_both_ref[:, :2 * xh_ref.shape[1]]
    end = first_ref.shape[0] - FOLDED
    keep_0[end:] = first_ref[end:]
    project(xh_ref, xl_ref, w_both, give_1, 1, 1)
    project(xh_ref, xl_ref, w_both, keep_0, 0, 0)
    project(xh_ref, xl_ref, w_both, keep_1, 1, 0)


def project_call(x_high, x_low, w_both, first):
    part = jax.ShapeDtypeStruct((PIECES * w_both.shape[0] // 2, LANES), F32)
    return pl.pallas_call(
        project_kernel,
        out_shape=[jax.ShapeDtypeStruct(first.shape, F32), part, part],
        in_specs=in_vmem(4),
        out_specs=in_vmem(3),
        compiler_params=pltpu.CompilerParams(vmem_limit_bytes=VMEM_LIMIT),
    )(x_high, x_low, w_both, first)


def blur_call(cube, taps_x, taps_y, w_rows):
    planes, height, length = cube.shape
    rank = w_rows.shape[0]
    first = jax.ShapeDtypeStruct((PIECES * rank + FOLDED, LANES), F32)
    image = (height, planes, length)
    mine = jax.ShapeDtypeStruct((rank, planes), F32)
    both = jax.ShapeDtypeStruct((2 * rank, 2 * LANES), BF16)
    in_hbm = [pltpu.with_memory_space_constraint(value, pltpu.HBM) for value in (cube, taps_x, taps_y, w_rows)]
    return pl.pallas_call(
        blur_kernel,
        out_shape=[jax.ShapeDtypeStruct(image, BF16)] * 2 + [mine, both, first],
        in_specs=[pl.BlockSpec(memory_space=pltpu.HBM)] * 4,
        out_specs=in_vmem(5),
        scratch_shapes=[pltpu.VMEM(value.shape, F32) for value in (cube, taps_x, taps_y, w_rows)]
        + [pltpu.SemaphoreType.DMA((3,)), pltpu.SemaphoreType.DMA((planes // GROUP,))]
        + [pltpu.VMEM((LANES, LANES), F32)] * 3,
        compiler_params=pltpu.CompilerParams(vmem_limit_bytes=VMEM_LIMIT),
    )(*in_hbm)


def ratio_kernel(mine_ref, other_ref, h_ref, out_ref):
    tall = h_ref.shape[0] // lax.axis_size("bd")
    first = pl.multiple_of(lax.axis_index("bd") * tall, tall)
    here = h_ref[pl.ds(first, tall)]
    here = jnp.transpose(here.reshape(-1, here.shape[2]))
    rows = mine_ref.shape[0]
    gram = unfold(mine_ref[rows - FOLDED:rows] + other_ref[rows - FOLDED:rows], here.shape[0])
    out_ref[...] = here / dot_exact(gram, here)


def ratio_call(mine, other, h_columns):
    piece = jax.ShapeDtypeStruct((h_columns.shape[2], 2 * LANES), F32)
    return pl.pallas_call(
        ratio_kernel,
        out_shape=piece,
        in_specs=in_vmem(3),
        compiler_params=pltpu.CompilerParams(vmem_limit_bytes=VMEM_LIMIT),
    )(mine, other, h_columns)


def accumulate(xh_ref, xl_ref, part_refs, all_ref, rel_core, total):
    height, planes, _ = xh_ref.shape
    me_sp = lax.axis_index("sp")
    me_bd = lax.axis_index("bd")
    pieces = lax.axis_size("sp")
    tall = height // lax.axis_size("bd")
    wide = 2 * LANES // pieces
    core = lax.bitwise_xor(me_bd % 2, rel_core)
    for partner, part_ref in enumerate(part_refs):
        row = lax.bitwise_xor(me_bd // 2, partner // 2)
        for inner in range(4):
            column = lax.bitwise_xor(me_sp, partner % 2 + 2 * inner)
            all_ref[row * pieces + column] = part_ref[inner]
    for row in range(2):
        for quarter in range(2):
            first_row = (2 * row + core) * tall + 4 * quarter
            halves = [
                exchange_blocks(
                    [all_ref[row * pieces + column * 4 + k][:, quarter * LANES:(quarter + 1) * LANES]
                     for k in range(4)], wide)
                for column in range(2)]
            rows = jnp.concatenate([halves[column][k] for k in range(4) for column in range(2)], axis=1)
            high, low = split(rows)
            here = jnp.concatenate([high, low], axis=0)
            image = [
                jnp.concatenate([ref[first_row + k] for k in range(4)], axis=1) for ref in (xh_ref, xl_ref)]
            total = total + dot_nt(jnp.concatenate(image + [here], axis=0), here)
    return total


def first_kernel(xh_ref, xl_ref, *rest):
    part_refs = rest[:4]
    total_out, all_ref = rest[4:]
    total_out[...] = accumulate(xh_ref, xl_ref, part_refs, all_ref, 0, jnp.zeros(total_out.shape, F32))


def first_call(x_high, x_low, parts):
    _, planes, _ = x_high.shape
    rank = parts[0].shape[1]
    return pl.pallas_call(
        first_kernel,
        out_shape=jax.ShapeDtypeStruct((2 * (planes + rank), 2 * rank), F32),
        in_specs=in_vmem(2 + len(parts)),
        scratch_shapes=[pltpu.VMEM((16, rank, 2 * LANES), F32)],
        compiler_params=pltpu.CompilerParams(vmem_limit_bytes=VMEM_LIMIT),
    )(x_high, x_low, *parts)


def second_kernel(xh_ref, xl_ref, w_ref, total_ref, *rest):
    part_refs = rest[:4]
    w_out, all_ref = rest[4:]
    planes = xh_ref.shape[1]
    rank = w_ref.shape[0]
    total = accumulate(xh_ref, xl_ref, part_refs, all_ref, 1, total_ref[...])
    numer = total[:planes, :rank] + (total[:planes, rank:] + total[planes:2 * planes, :rank])
    gram = total[2 * planes:]
    gram = gram[:rank, :rank] + (gram[:rank, rank:] + gram[rank:, :rank])
    w_here = w_ref[...]
    gram_high, gram_low = split(gram)
    w_high, w_low = split(w_here)
    both = dot(jnp.concatenate([gram_high, gram_low], axis=0), w_high)
    denominator = both[:rank] + (both[rank:] + dot(gram_high, w_low))
    w_out[...] = w_here * jnp.transpose(numer) / denominator


def second_call(x_high, x_low, w_here, total, parts):
    rank = w_here.shape[0]
    return pl.pallas_call(
        second_kernel,
        out_shape=jax.ShapeDtypeStruct(w_here.shape, F32),
        in_specs=in_vmem(4 + len(parts)),
        scratch_shapes=[pltpu.VMEM((16, rank, 2 * LANES), F32)],
        compiler_params=pltpu.CompilerParams(vmem_limit_bytes=VMEM_LIMIT),
    )(x_high, x_low, w_here, total, *parts)


def place_h_kernel(*refs):
    h_out = refs[-1]
    me_bd = lax.axis_index("bd")
    tall = h_out.shape[0] // lax.axis_size("bd")
    for rel_bd in range(4):
        piece = refs[rel_bd][0]
        first = lax.bitwise_xor(me_bd, rel_bd) * tall
        h_out[pl.ds(first, tall)] = jnp.transpose(piece).reshape((tall,) + h_out.shape[1:])


def place_h_call(parts, shape):
    return pl.pallas_call(
        place_h_kernel,
        out_shape=jax.ShapeDtypeStruct(shape, F32),
        in_specs=in_vmem(len(parts)),
        compiler_params=pltpu.CompilerParams(vmem_limit_bytes=VMEM_LIMIT),
    )(*parts)


def gather_w_kernel(*refs):
    part_refs = refs[:-2]
    out_ref, all_ref = refs[-2:]
    planes = out_ref.shape[1] // 8
    me_sp = lax.axis_index("sp")
    rel = 0
    for part_ref in part_refs:
        for inner in range(part_ref.shape[0]):
            all_ref[lax.bitwise_xor(me_sp, RING[rel]), :, 0:planes] = part_ref[inner]
            rel += 1
    for owner in range(8):
        out_ref[:, owner * planes:(owner + 1) * planes] = all_ref[owner][:, :planes]


RING = (0, 1, 2, 3, 4, 5, 6, 7)


def gather_w_call(parts):
    _, rank, planes = parts[0].shape
    return pl.pallas_call(
        gather_w_kernel,
        out_shape=jax.ShapeDtypeStruct((rank, planes * 8), F32),
        in_specs=in_vmem(len(parts)),
        scratch_shapes=[pltpu.VMEM((8, rank, LANES), F32)],
        compiler_params=pltpu.CompilerParams(vmem_limit_bytes=VMEM_LIMIT),
    )(*parts)


def send(value, mask_sp, mask_bd):
    bands = lax.axis_size("bd")
    pieces = lax.axis_size("sp")
    pairs = []
    for s in range(pieces):
        for b in range(bands):
            pairs.append((s * bands + b, (s ^ mask_sp) * bands + (b ^ mask_bd)))
    return lax.ppermute(value, ("sp", "bd"), pairs)


def around(values):
    return [send(values[k], k % 2, 2 * (k // 2)) for k in range(1, 4)]


def local(cube, taps_x, taps_y, factor_w, factor_h):
    w_rows = jnp.transpose(factor_w[0])
    taps_x = jnp.transpose(taps_x, (2, 0, 1))
    taps_y = jnp.transpose(taps_y, (2, 0, 1))
    h_columns = jnp.transpose(factor_h, (1, 2, 0))
    rank = w_rows.shape[0]
    x_high, x_low, w_here, w_both, give_0 = blur_call(cube[0], taps_x, taps_y, w_rows)
    chains = []
    taken_0 = send(give_0, 0, 1)
    keep_0, keep_1, give_1 = project_call(x_high, x_low, w_both, give_0)
    taken_0, keep_0, keep_1, give_1 = lax.optimization_barrier((taken_0, keep_0, keep_1, give_1))
    for keep, taken in ((keep_0, taken_0), (keep_1, send(give_1, 0, 1))):
        bounds = [place * 4 * rank for place in (0, 1, 3, 2)]
        sides = []
        for first in bounds:
            last = keep.shape[0] if first == max(bounds) else first + 4 * rank
            sides.append(keep[first:last] + taken[first:last])
        chains.append((sides, around(sides)))
    ratio = ratio_call(chains[0][0][2], chains[0][1][1], h_columns)
    line = []
    for k in range(4):
        part = slice(k * rank, (k + 1) * rank)
        line.append(jnp.concatenate(
            [(sides[0][part] + others[2][part]) + (others[1][part] + others[0][part]) for sides, others in chains],
            axis=1))
    line = [line[0]] + [send(line[k], 2 * k, 0) for k in range(1, 4)]
    h_piece = ratio * ((line[0] + line[1]) + (line[2] + line[3]))
    h_line = [h_piece] + [send(h_piece, 2 * k, 0) for k in (3, 2, 1)][::-1]
    mine = jnp.stack(h_line)
    first_parts = [mine] + [send(mine, k % 2, 2 * (k // 2)) for k in (3, 2, 1)][::-1]
    second_parts = [send(value, 0, 1) for value in first_parts]
    total = first_call(x_high, x_low, first_parts)
    w_piece = second_call(x_high, x_low, w_here, total, second_parts)
    own = [parts[k] for k in (0, 2) for parts in (first_parts, second_parts)]
    h_next = place_h_call(own, h_columns.shape)
    w_pair = jnp.stack([w_piece, send(w_piece, 1, 0)])
    w_next = gather_w_call([w_pair] + [send(w_pair, 2 * k, 0) for k in (3, 2, 1)][::-1])
    return jnp.transpose(w_next)[None], jnp.transpose(h_next, (2, 0, 1))


def normalized(kernel):
    return kernel / jnp.sum(kernel, axis=-1, keepdims=True)


def band_weights(kernel, size_in, size_out, offset):
    tap_count = kernel.shape[-1]
    in_index = lax.broadcasted_iota(jnp.int32, (size_in, size_out, tap_count), 0)
    out_index = lax.broadcasted_iota(jnp.int32, (size_in, size_out, tap_count), 1)
    tap_index = lax.broadcasted_iota(jnp.int32, (size_in, size_out, tap_count), 2)
    select = (tap_index == in_index - out_index + offset).astype(jnp.float32)
    return jnp.einsum("pk,iok->pio", kernel, select, precision=lax.Precision.HIGHEST)


def blur_rows(planes, kernel_y):
    margin = (kernel_y.shape[-1] - 1) // 2
    height = planes.shape[1]
    band_table = band_weights(kernel_y, height, height, margin)
    return jnp.einsum("piz,pio->poz", planes, band_table, precision=lax.Precision.HIGHEST)


def blur_columns(planes, kernel_x):
    margin = (kernel_x.shape[-1] - 1) // 2
    count, height, length = planes.shape
    blocks = planes.reshape(count, height, length // 128, 128)
    empty = jnp.zeros((count, height, 1, 128), jnp.float32)
    left_block = jnp.concatenate([empty, blocks[:, :, :-1]], axis=2)
    right_block = jnp.concatenate([blocks[:, :, 1:], empty], axis=2)
    window = jnp.concatenate([left_block, blocks, right_block], axis=3)
    band_table = band_weights(kernel_x, 384, 128, margin - 128)
    result = jnp.einsum("pybi,pio->pybo", window, band_table, precision=lax.Precision.HIGHEST)
    return result.reshape(count, height, length)


def local_any(cube, taps_x, taps_y, factor_w, factor_h):
    highest = lax.Precision.HIGHEST
    kernel_x = normalized(taps_x[0])
    kernel_y = normalized(taps_y[0])
    rows_done = blur_rows(cube[0], kernel_y)
    w_band = factor_w[0]
    blurred = blur_columns(rows_done, kernel_x)[None]
    moved = lax.all_to_all(blurred, "sp", split_axis=3, concat_axis=1, tiled=True)
    numer_part = jnp.einsum("lr,plyx->pryx", w_band, moved, precision=highest)
    gram_part = jnp.dot(w_band.T, w_band, precision=highest)
    numer_h, gram_w = lax.psum((numer_part[0], gram_part), "bd")
    h_next = factor_h * numer_h / jnp.einsum("rq,qyx->ryx", gram_w, factor_h, precision=highest)
    x_band = moved[0]
    gram_h_part = jnp.einsum("ryx,qyx->rq", h_next, h_next, precision=highest)
    numer_w_part = jnp.einsum("lyx,ryx->lr", x_band, h_next, precision=highest)
    numer_w, gram_h = lax.psum((numer_w_part, gram_h_part), "sp")
    w_next = w_band * numer_w / jnp.dot(w_band, gram_h, precision=highest)
    return (w_next[None], h_next)


def solution(mesh):
    in_specs = (
        P("bd", "sp", None, None),
        P("bd", "sp", None),
        P("bd", "sp", None),
        P("bd", None, None),
        P(None, None, "sp"),
    )
    out_specs = (P("bd", None, None), P(None, None, "sp"))

    def body(cube, *rest):
        suits = lax.axis_size("sp") == 8 and lax.axis_size("bd") == 4 and cube.shape[1:] == (96, 32, 2 * LANES)
        return (local if suits else local_any)(cube, *rest)

    return jax.shard_map(body, mesh=mesh, in_specs=in_specs, out_specs=out_specs, check_vma=False)
```
